256 devices in a mesh: band: 64 (over z_lo, y, x), dom: 4 (over z_hi, core).
Axes of the slice: x: 4, y: 4, z: 8 (z_hi: 2, z_lo: 4; z = z_hi * 4 + z_lo), core: 2. Of those that a mesh axis runs over, the one named last changes fastest.
Arguments:
- orbitals: float32 [128, 128, 16, 128], P('band', 'dom'), may hold values from -6 to 6
- potential: float32 [128, 16, 128], P('dom'), may hold values from -1 to 0
- subspace: float32 [128, 128], P('band'), may hold values from -0.4 to 2.4, as said below
Outputs:
- rotated: float32 [128, 262144], P(None, ('dom', 'band'))
The draws below stay inside these ranges and needn't reach their ends.
Inputs may be any that keep to these rules, and one draw needn't show every extreme that they name: `subspace`: diagonal entries between 0.7 and 2.3, off-diagonal entries small and independent.
All inputs are finite; a program needn't handle non-finite values.
Results may differ from the reference program's by a relative error of at most 0.00012.
Values sent between devices are 32-bit elements; how exact they have to be, the bound alone decides.
A program may use at most 128 MiB of HBM per device.

```python
import math
import jax
import jax.numpy as jnp
from jax import lax

ORB = 128
NY = 16
NZ = 128
DEG = 3
NX = 128


def draw_subspace(key, part):
    key = jax.random.fold_in(key, 7)
    first_key, second_key = jax.random.split(key)
    diagonal = jax.random.uniform(first_key, (ORB,), jnp.float32, 1.0, 2.0)
    spread_part = jnp.clip(jax.random.normal(second_key, (ORB, ORB), jnp.float32), -4.0, 4.0) * (0.7 / math.sqrt(ORB))
    return spread_part + jnp.diag(diagonal)


def block_levels(own_key, dims, cuts, smallest, high):
    gain = 1.0
    for axis_at, blocks in cuts:
        draws = jax.random.uniform(jax.random.fold_in(jax.random.fold_in(own_key, 6), axis_at), (blocks,), jnp.float32, smallest / len(cuts), high / len(cuts))
        gain = gain * jnp.repeat(jnp.exp(draws), dims[axis_at] // blocks).reshape((-1,) + (1,) * (len(dims) - 1 - axis_at))
    return gain


def centred(rng, dims, deviation, most, pieces=(), kind=jnp.bfloat16):
    gain = block_levels(rng, dims, pieces, -0.22, 0.18) if pieces else 1.0
    result = jax.random.normal(rng, dims, jnp.float32) * deviation * gain
    return jnp.minimum(jnp.maximum(result, -most), most).astype(kind)


def setup_inputs(seed: int = 0) -> dict:
    key_list = jax.random.split(jax.random.key(seed), 4)
    return {
        "orbitals": centred(key_list[0], (ORB, NX, NY, NZ), 1.0, 6.0, ((0, 64), (1, 4)), jnp.float32),
        "potential": jnp.clip(-1.0 + 1.0 * jax.random.uniform(key_list[1], (NX, NY, NZ), jnp.float32) ** block_levels(key_list[1], (NX, NY, NZ), ((0, 4),), -0.2, 0.2), -1.0, 0.0),
        "subspace": draw_subspace(jax.random.fold_in(key_list[3], 71), 0),
    }


upper_edge = 10.7
lower_edge = 1.5
bottom_edge = -1.0


def stencil_weights():
    factor_square = math.factorial(6) ** 2
    side_weights = []
    for offset in range(1, 7):
        side_weights.append(2.0 * (-1.0) ** (offset + 1) * factor_square / (offset * offset * math.factorial(6 - offset) * math.factorial(6 + offset)))
    center_weight = -2.0 * sum(side_weights)
    return center_weight, side_weights


def filter_scalars(pass_count):
    half_width = (upper_edge - lower_edge) / 2.0
    sigma_now = half_width / (bottom_edge - (upper_edge + lower_edge) / 2.0)
    gamma_value = 2.0 / sigma_now
    scalars = [(sigma_now / half_width, 0.0)]
    for pass_index in range(pass_count - 1):
        sigma_next = 1.0 / (gamma_value - sigma_now)
        scalars.append((2.0 * sigma_next / half_width, sigma_now * sigma_next))
        sigma_now = sigma_next
    return scalars


def apply_hamiltonian(padded, potential):
    center_weight, side_weights = stencil_weights()
    planes = padded.shape[1] - 12
    middle = padded[:, 6:6 + planes]
    laplace = (3.0 * center_weight) * middle
    for offset in range(1, 7):
        beside_all = padded[:, 6 + offset:6 + offset + planes] + padded[:, 6 - offset:6 - offset + planes]
        beside_all = beside_all + jnp.roll(middle, offset, 2) + jnp.roll(middle, -offset, 2)
        beside_all = beside_all + jnp.roll(middle, offset, 3) + jnp.roll(middle, -offset, 3)
        laplace = laplace + side_weights[offset - 1] * beside_all
    return -0.5 * laplace + potential[None] * middle, middle


def wrap_pad(field, rim_width):
    return jnp.concatenate([field[:, -rim_width:], field, field[:, :rim_width]], axis=1)


def reference(orbitals, potential, subspace):
    centre = (upper_edge + lower_edge) / 2.0

    def filter_one(single):
        current = single[None]
        previous = None
        for scale_apply, weight_prev in filter_scalars(DEG):
            applied, middle = apply_hamiltonian(wrap_pad(current, 6), potential)
            renewed = (applied - centre * middle) * scale_apply
            if previous is not None:
                renewed = renewed - weight_prev * previous
            previous = middle
            current = renewed
        return current[0]

    filtered = lax.map(filter_one, orbitals)
    flattened = filtered.reshape(ORB, -1)
    return jnp.dot(subspace.T, flattened, precision=lax.Precision.HIGHEST, preferred_element_type=jnp.float32)
```

```python
import functools
import math

import jax
import jax.numpy as jnp
from jax import lax
from jax.experimental import pallas as pl
from jax.experimental.pallas import tpu as pltpu
from jax.sharding import PartitionSpec as P

DEG = 3
REACH = 6
MESH = pl.DeviceIdType.MESH

upper_edge = 10.7
lower_edge = 1.5
bottom_edge = -1.0


def stencil_weights():
    factor_square = math.factorial(6) ** 2
    side_weights = []
    for offset in range(1, 7):
        side_weights.append(
            2.0
            * (-1.0) ** (offset + 1)
            * factor_square
            / (offset * offset * math.factorial(6 - offset) * math.factorial(6 + offset))
        )
    center_weight = -2.0 * sum(side_weights)
    return (center_weight, side_weights)


def filter_scalars(pass_count):
    half_width = (upper_edge - lower_edge) / 2.0
    sigma_now = half_width / (bottom_edge - (upper_edge + lower_edge) / 2.0)
    gamma_value = 2.0 / sigma_now
    scalars = [(sigma_now / half_width, 0.0)]
    for pass_index in range(pass_count - 1):
        sigma_next = 1.0 / (gamma_value - sigma_now)
        scalars.append((2.0 * sigma_next / half_width, sigma_now * sigma_next))
        sigma_now = sigma_next
    return scalars


def row_weights(side):
    rows = lax.broadcasted_iota(jnp.int32, (8, 128), 0)
    weight = lambda k: side[k - 1] if 1 <= k <= REACH else 0.0
    pairs = []
    for r in range(1, 8):
        inside = rows >= r
        near, far = weight(r), weight(8 - r)
        pairs.append((jnp.where(inside, near, far), jnp.where(inside, far, near)))
    return pairs


def filtered_block(window, pot, before, scale, weight, pairs):
    center_weight, side = stencil_weights()
    side = [-0.5 * scale * w for w in side]
    n = window.shape[0] - 2 * REACH
    mid = window[REACH : REACH + n]
    diag = (-1.5 * center_weight - (upper_edge + lower_edge) / 2.0) * scale
    total = (pot * scale + diag) * mid
    for k in range(1, REACH + 1):
        beside = window[REACH + k : REACH + k + n] + window[REACH - k : REACH - k + n]
        beside = beside + pltpu.roll(mid, k, 3) + pltpu.roll(mid, 128 - k, 3)
        total = total + side[k - 1] * beside
    low, high = mid[:, 0], mid[:, 1]
    low_sum, high_sum = total[:, 0], total[:, 1]
    for r in range(1, 8):
        own, other = pairs[r - 1]
        low_turned, high_turned = pltpu.roll(low, r, 1), pltpu.roll(high, r, 1)
        low_sum = low_sum + own * low_turned + other * high_turned
        high_sum = high_sum + own * high_turned + other * low_turned
    if before is not None:
        low_sum = low_sum - weight * before[:, 0]
        high_sum = high_sum - weight * before[:, 1]
    return low_sum, high_sum


def filter_kernel(
    bands, doms, orb, pot, sub, recv, rows, p0, p1, p2, out, pot_v,
    halo_send, halo_recv, move_sem, all_send, all_recv, row_send, row_recv,
):
    orbs, planes = orb.shape[0], orb.shape[1]
    band, dom = lax.axis_index("band"), lax.axis_index("dom")
    up, down = lax.rem(dom + 1, doms), lax.rem(dom + doms - 1, doms)
    scalars = filter_scalars(DEG)
    levels = (p0, p1, p2)
    step = 4
    edge = 8

    load = pltpu.make_async_copy(orb, p0.at[:, pl.ds(REACH, planes)], move_sem.at[0])
    load.start()
    load_pot = pltpu.make_async_copy(pot, pot_v, move_sem.at[1])
    load_pot.start()

    barrier = pltpu.get_barrier_semaphore()
    for peer in (up, down):
        pl.semaphore_signal(barrier, inc=1, device_id={"dom": peer}, device_id_type=MESH)

    def greet(i, c):
        pl.semaphore_signal(
            barrier, inc=1, device_id={"band": lax.rem(band + i, bands)}, device_id_type=MESH
        )
        return c

    lax.fori_loop(1, bands, greet, 0)
    pl.semaphore_wait(barrier, bands + 1)

    def halo(level, source, first, last):
        target = levels[level]
        copies = []
        for at, (begin, place, peer) in enumerate(((last, 0, up), (first, REACH + planes, down))):
            copies.append(
                pltpu.make_async_remote_copy(
                    src_ref=source.at[:, pl.ds(begin, REACH)],
                    dst_ref=target.at[:, pl.ds(place, REACH)],
                    send_sem=halo_send.at[level, at],
                    recv_sem=halo_recv.at[level, at],
                    device_id={"dom": peer},
                    device_id_type=MESH,
                )
            )
        for copy in copies:
            copy.start()
        return copies

    copies = halo(0, orb, 0, planes - REACH)

    own_rows = pltpu.make_async_copy(sub, rows.at[band], move_sem.at[2])
    own_rows.start()

    def send_rows(i, c):
        pltpu.make_async_remote_copy(
            src_ref=sub,
            dst_ref=rows.at[band],
            send_sem=row_send,
            recv_sem=row_recv,
            device_id={"band": lax.rem(band + i, bands)},
            device_id_type=MESH,
        ).start()
        return c

    lax.fori_loop(1, bands, send_rows, 0)

    load.wait()
    load_pot.wait()
    pairs_unit = row_weights(stencil_weights()[1])

    def apply(level, begin, blocks):
        scale, weight = scalars[level]
        source = levels[level]
        pairs = [(-0.5 * scale * a, -0.5 * scale * b) for a, b in pairs_unit]

        def body(i, c):
            at = begin + i * step
            for o in range(orbs):
                before = None
                if level > 0:
                    before = levels[level - 1][o, pl.ds(at + REACH, step)]
                window = source[o, pl.ds(at, step + 2 * REACH)]
                low, high = filtered_block(
                    window, pot_v[pl.ds(at, step)], before, scale, weight, pairs
                )
                if level < DEG - 1:
                    levels[level + 1][o, pl.ds(at + REACH, step), 0] = low
                    levels[level + 1][o, pl.ds(at + REACH, step), 1] = high
                else:
                    out[pl.ds(at, step), 0, o] = low
                    out[pl.ds(at, step), 1, o] = high
            return c

        lax.fori_loop(0, blocks, body, 0)

    for level in range(DEG):
        apply(level, edge, (planes - 2 * edge) // step)
        for copy in copies:
            copy.wait_recv()
        apply(level, 0, edge // step)
        apply(level, planes - edge, edge // step)
        sent = copies
        if level < DEG - 1:
            copies = halo(level + 1, levels[level + 1], REACH, planes)
        for copy in sent:
            copy.wait_send()

    own = pltpu.make_async_copy(
        out.at[lax.div(band, 2), lax.rem(band, 2)], recv.at[band], move_sem.at[3]
    )
    own.start()

    def send(i, c):
        peer = lax.rem(band + i, bands)
        pltpu.make_async_remote_copy(
            src_ref=out.at[lax.div(peer, 2), lax.rem(peer, 2)],
            dst_ref=recv.at[band],
            send_sem=all_send,
            recv_sem=all_recv,
            device_id={"band": peer},
            device_id_type=MESH,
        ).start()
        return c

    lax.fori_loop(1, bands, send, 0)
    own_rows.wait()
    own.wait()
    for ref, sem_a, sem_b in ((rows, row_send, row_recv), (recv, all_send, all_recv)):
        whole = ref.at[pl.ds(0, bands - 1)]
        pltpu.make_async_copy(whole, whole, sem_a).wait()
        pltpu.make_async_copy(whole, whole, sem_b).wait()


def rotate_kernel(recv, rows, out):
    bands = rows.shape[0]
    matrix = jnp.concatenate([rows[:, 0], rows[:, 1]], axis=0)
    for r in range(8):
        values = jnp.concatenate([recv[:, 0, r], recv[:, 1, r]], axis=0)
        out[:, pl.ds(r * 128, 128)] = lax.dot_general(
            matrix,
            values,
            (((0,), (0,)), ((), ())),
            precision=lax.Precision.HIGHEST,
            preferred_element_type=jnp.float32,
        )


def per_device(bands, doms, orbitals, potential, subspace):
    orbs, planes = orbitals.shape[0], orbitals.shape[1]
    orb = orbitals.reshape(orbs, planes, 2, 8, 128)
    pot = potential.reshape(planes, 2, 8, 128)
    padded = pltpu.VMEM((orbs, planes + 2 * REACH, 2, 8, 128), jnp.float32)
    dma = pltpu.SemaphoreType.DMA
    recv, rows = pl.pallas_call(
        functools.partial(filter_kernel, bands, doms),
        out_shape=(
            jax.ShapeDtypeStruct((bands, orbs, 8, 128), jnp.float32),
            jax.ShapeDtypeStruct((bands, orbs, 128), jnp.float32),
        ),
        in_specs=[pl.BlockSpec(memory_space=pl.ANY)] * 3,
        out_specs=(pl.BlockSpec(memory_space=pl.ANY),) * 2,
        scratch_shapes=[
            padded,
            padded,
            padded,
            pltpu.VMEM((planes, 2, orbs, 8, 128), jnp.float32),
            pltpu.VMEM((planes, 2, 8, 128), jnp.float32),
            dma((DEG, 2)),
            dma((DEG, 2)),
            dma((4,)),
            dma,
            dma,
            dma,
            dma,
        ],
        compiler_params=pltpu.CompilerParams(
            collective_id=0, has_side_effects=True, vmem_limit_bytes=32 * 2**20
        ),
        name="filter",
    )(orb, pot, subspace)
    return pl.pallas_call(
        rotate_kernel,
        out_shape=jax.ShapeDtypeStruct((bands * orbs, 1024), jnp.float32),
        in_specs=[pl.BlockSpec(memory_space=pltpu.VMEM)] * 2,
        out_specs=pl.BlockSpec(memory_space=pltpu.VMEM),
        name="rotate",
    )(recv, rows)


def solution(mesh):
    in_specs = (P("band", "dom", None, None), P("dom", None, None), P("band", None))
    out_specs = P(None, ("dom", "band"))
    return jax.shard_map(
        functools.partial(per_device, mesh.shape["band"], mesh.shape["dom"]),
        mesh=mesh,
        in_specs=in_specs,
        out_specs=out_specs,
        check_vma=False,
    )
```

```python
import functools
import math

import jax
import jax.numpy as jnp
from jax import lax
from jax.experimental import pallas as pl
from jax.experimental.pallas import tpu as pltpu
from jax.sharding import PartitionSpec as P

DEG = 3
REACH = 6
MESH = pl.DeviceIdType.MESH

upper_edge = 10.7
lower_edge = 1.5
bottom_edge = -1.0


def stencil_weights():
    factor_square = math.factorial(6) ** 2
    side_weights = []
    for offset in range(1, 7):
        side_weights.append(
            2.0
            * (-1.0) ** (offset + 1)
            * factor_square
            / (offset * offset * math.factorial(6 - offset) * math.factorial(6 + offset))
        )
    center_weight = -2.0 * sum(side_weights)
    return (center_weight, side_weights)


def filter_scalars(pass_count):
    half_width = (upper_edge - lower_edge) / 2.0
    sigma_now = half_width / (bottom_edge - (upper_edge + lower_edge) / 2.0)
    gamma_value = 2.0 / sigma_now
    scalars = [(sigma_now / half_width, 0.0)]
    for pass_index in range(pass_count - 1):
        sigma_next = 1.0 / (gamma_value - sigma_now)
        scalars.append((2.0 * sigma_next / half_width, sigma_now * sigma_next))
        sigma_now = sigma_next
    return scalars


def row_weights(side):
    rows = lax.broadcasted_iota(jnp.int32, (8, 128), 0)
    weight = lambda k: side[k - 1] if 1 <= k <= REACH else 0.0
    pairs = []
    for r in range(1, 8):
        inside = rows >= r
        near, far = weight(r), weight(8 - r)
        pairs.append((jnp.where(inside, near, far), jnp.where(inside, far, near)))
    return pairs


def filtered_block(window, pot, before, scale, weight, pairs):
    center_weight, side = stencil_weights()
    side = [-0.5 * scale * w for w in side]
    n = window.shape[0] - 2 * REACH
    mid = window[REACH : REACH + n]
    diag = (-1.5 * center_weight - (upper_edge + lower_edge) / 2.0) * scale
    total = (pot * scale + diag) * mid
    for k in range(1, REACH + 1):
        beside = window[REACH + k : REACH + k + n] + window[REACH - k : REACH - k + n]
        beside = beside + pltpu.roll(mid, k, 3) + pltpu.roll(mid, 128 - k, 3)
        total = total + side[k - 1] * beside
    low, high = mid[:, 0], mid[:, 1]
    low_sum, high_sum = total[:, 0], total[:, 1]
    for r in range(1, 8):
        own, other = pairs[r - 1]
        low_turned, high_turned = pltpu.roll(low, r, 1), pltpu.roll(high, r, 1)
        low_sum = low_sum + own * low_turned + other * high_turned
        high_sum = high_sum + own * high_turned + other * low_turned
    if before is not None:
        low_sum = low_sum - weight * before[:, 0]
        high_sum = high_sum - weight * before[:, 1]
    return low_sum, high_sum


def filter_kernel(
    bands, doms, lines, orb, pot, sub, recv, rows, p0, p1, p2, out, pot_v, held,
    near_send, near_recv, far_send, far_recv, pass_send, pass_recv,
    move_sem, all_send, all_recv, row_send, row_recv,
):
    orbs, planes = orb.shape[0], orb.shape[1]
    band, dom = lax.axis_index("band"), lax.axis_index("dom")
    core = lax.rem(dom, 2)
    half = lax.div(dom, 2)
    floor = bands // lines
    z = half * lines + lax.div(band, floor)

    def chip_along(shift, core_there):
        there = lax.rem(z + shift + 2 * lines, 2 * lines)
        return {
            "band": lax.rem(there, lines) * floor + lax.rem(band, floor),
            "dom": lax.div(there, lines) * 2 + core_there,
        }

    hop = (2 * core - 1) * (lines // 2)
    sibling = {"dom": dom + 1 - 2 * core}
    relay_to = chip_along(hop, core)
    relay_from = chip_along(-hop, core)
    across = chip_along(hop, 1 - core)
    scalars = filter_scalars(DEG)
    levels = (p0, p1, p2)
    step = 4
    edge = 8

    load = pltpu.make_async_copy(orb, p0.at[:, pl.ds(REACH, planes)], move_sem.at[0])
    load.start()
    load_pot = pltpu.make_async_copy(pot, pot_v, move_sem.at[1])
    load_pot.start()

    barrier = pltpu.get_barrier_semaphore()
    for peer in (sibling, relay_from, across):
        pl.semaphore_signal(barrier, inc=1, device_id=peer, device_id_type=MESH)

    def greet(i, c):
        pl.semaphore_signal(
            barrier, inc=1, device_id={"band": lax.rem(band + i, bands)}, device_id_type=MESH
        )
        return c

    lax.fori_loop(1, bands, greet, 0)
    pl.semaphore_wait(barrier, bands + 2)

    def remote(src, dst, send_sem, recv_sem, peer):
        return pltpu.make_async_remote_copy(
            src_ref=src, dst_ref=dst, send_sem=send_sem, recv_sem=recv_sem,
            device_id=peer, device_id_type=MESH,
        )

    def halo(level, o, source, offset):
        target = levels[level]
        last = planes - REACH
        far = remote(
            source.at[o, pl.ds(offset + core * last, REACH)], held.at[level, o],
            pass_send.at[level, o], pass_recv.at[level, o], relay_to,
        )
        near = remote(
            source.at[o, pl.ds(offset + (1 - core) * last, REACH)],
            target.at[o, pl.ds(core * (planes + REACH), REACH)],
            near_send.at[level, o], near_recv.at[level, o], sibling,
        )
        onward = remote(
            held.at[level, o], target.at[o, pl.ds((1 - core) * (planes + REACH), REACH)],
            far_send.at[level, o], far_recv.at[level, o], across,
        )
        far.start()
        near.start()
        return far, near, onward

    copies = [halo(0, o, orb, 0) for o in range(orbs)]

    own_rows = pltpu.make_async_copy(sub, rows.at[band], move_sem.at[2])
    own_rows.start()

    def send_rows(i, c):
        remote(sub, rows.at[band], row_send, row_recv, {"band": lax.rem(band + i, bands)}).start()
        return c

    lax.fori_loop(1, bands, send_rows, 0)

    load.wait()
    load_pot.wait()
    pairs_unit = row_weights(stencil_weights()[1])

    def apply(level, o, begin, blocks):
        scale, weight = scalars[level]
        source = levels[level]
        pairs = [(-0.5 * scale * a, -0.5 * scale * b) for a, b in pairs_unit]

        def body(i, c):
            at = begin + i * step
            before = None
            if level > 0:
                before = levels[level - 1][o, pl.ds(at + REACH, step)]
            window = source[o, pl.ds(at, step + 2 * REACH)]
            low, high = filtered_block(
                window, pot_v[pl.ds(at, step)], before, scale, weight, pairs
            )
            if level < DEG - 1:
                levels[level + 1][o, pl.ds(at + REACH, step), 0] = low
                levels[level + 1][o, pl.ds(at + REACH, step), 1] = high
            else:
                out[o, pl.ds(at, step), 0] = low
                out[o, pl.ds(at, step), 1] = high
            return c

        lax.fori_loop(0, blocks, body, 0)

    def spread(o):
        own = pltpu.make_async_copy(
            out.at[o, lax.div(band, 2), lax.rem(band, 2)], recv.at[band, o], move_sem.at[3 + o]
        )
        own.start()

        def send(i, c):
            peer = lax.rem(band + i, bands)
            remote(
                out.at[o, lax.div(peer, 2), lax.rem(peer, 2)], recv.at[band, o],
                all_send, all_recv, {"band": peer},
            ).start()
            return c

        lax.fori_loop(1, bands, send, 0)
        return own

    owns, sent = [], []
    for level in range(DEG):
        for o in range(orbs):
            apply(level, o, edge, (planes - 2 * edge) // step)
        for far, near, onward in copies:
            far.wait_recv()
            onward.start()
        following = []
        for o, (far, near, onward) in enumerate(copies):
            near.wait_recv()
            onward.wait_recv()
            apply(level, o, 0, edge // step)
            apply(level, o, planes - edge, edge // step)
            if level < DEG - 1:
                following.append(halo(level + 1, o, levels[level + 1], REACH))
            else:
                owns.append(spread(o))
        sent += copies
        copies = following

    for group in sent:
        for copy in group:
            copy.wait_send()
    own_rows.wait()
    for own in owns:
        own.wait()
    for ref, sem_a, sem_b in ((rows, row_send, row_recv), (recv, all_send, all_recv)):
        whole = ref.at[pl.ds(0, bands - 1)]
        pltpu.make_async_copy(whole, whole, sem_a).wait()
        pltpu.make_async_copy(whole, whole, sem_b).wait()


def two_parts(values):
    high = values.astype(jnp.bfloat16)
    return high, (values - high.astype(jnp.float32)).astype(jnp.bfloat16)


def rotate_kernel(recv, rows, out, recv_v, rows_v, out_v, sems):
    load = pltpu.make_async_copy(recv, recv_v, sems.at[0])
    load_rows = pltpu.make_async_copy(rows, rows_v, sems.at[1])
    load.start()
    load_rows.start()
    load_rows.wait()
    high, low = two_parts(jnp.concatenate([rows_v[:, 0], rows_v[:, 1]], axis=0).T)
    matrix = jnp.concatenate([high, high, low], axis=1)
    load.wait()
    width = 256
    stores = []
    for at in range(0, 8 * 128, width):
        columns = []
        for r in range(at // 128, (at + width) // 128):
            values = jnp.concatenate([recv_v[:, 0, r], recv_v[:, 1, r]], axis=0)
            high, low = two_parts(values)
            columns.append(jnp.concatenate([high, low, high], axis=0))
        out_v[:, pl.ds(at, width)] = jnp.dot(
            matrix, jnp.concatenate(columns, axis=1), preferred_element_type=jnp.float32
        )
        store = pltpu.make_async_copy(
            out_v.at[:, pl.ds(at, width)], out.at[:, pl.ds(at, width)], sems.at[2 + at // width]
        )
        store.start()
        stores.append(store)
    for store in stores:
        store.wait()


def per_device(bands, doms, lines, orbitals, potential, subspace):
    orbs, planes = orbitals.shape[0], orbitals.shape[1]
    orb = orbitals.reshape(orbs, planes, 2, 8, 128)
    pot = potential.reshape(planes, 2, 8, 128)
    f32 = jnp.float32
    padded = pltpu.VMEM((orbs, planes + 2 * REACH, 2, 8, 128), f32)
    dma = pltpu.SemaphoreType.DMA
    anywhere = pl.BlockSpec(memory_space=pl.ANY)
    recv, rows = pl.pallas_call(
        functools.partial(filter_kernel, bands, doms, lines),
        out_shape=(
            jax.ShapeDtypeStruct((bands, orbs, 8, 128), f32),
            jax.ShapeDtypeStruct((bands, orbs, 128), f32),
        ),
        in_specs=[anywhere] * 3,
        out_specs=(anywhere,) * 2,
        scratch_shapes=[
            padded,
            padded,
            padded,
            pltpu.VMEM((orbs, planes, 2, 8, 128), f32),
            pltpu.VMEM((planes, 2, 8, 128), f32),
            pltpu.VMEM((DEG, orbs, REACH, 2, 8, 128), f32),
            dma((DEG, orbs)),
            dma((DEG, orbs)),
            dma((DEG, orbs)),
            dma((DEG, orbs)),
            dma((DEG, orbs)),
            dma((DEG, orbs)),
            dma((3 + orbs,)),
            dma,
            dma,
            dma,
            dma,
        ],
        compiler_params=pltpu.CompilerParams(
            collective_id=0, has_side_effects=True, vmem_limit_bytes=60 * 2**20
        ),
        name="filter",
    )(orb, pot, subspace)
    return pl.pallas_call(
        rotate_kernel,
        out_shape=jax.ShapeDtypeStruct((bands * orbs, 1024), f32),
        in_specs=[anywhere] * 2,
        out_specs=anywhere,
        scratch_shapes=[
            pltpu.VMEM((bands, orbs, 8, 128), f32),
            pltpu.VMEM((bands, orbs, 128), f32),
            pltpu.VMEM((bands * orbs, 1024), f32),
            dma((6,)),
        ],
        compiler_params=pltpu.CompilerParams(vmem_limit_bytes=60 * 2**20),
        name="rotate",
    )(recv, rows)


def solution(mesh):
    in_specs = (P("band", "dom", None, None), P("dom", None, None), P("band", None))
    out_specs = P(None, ("dom", "band"))
    return jax.shard_map(
        functools.partial(per_device, mesh.shape["band"], mesh.shape["dom"], 4),
        mesh=mesh,
        in_specs=in_specs,
        out_specs=out_specs,
        check_vma=False,
    )
```

```python
import functools
import math

import jax
import jax.numpy as jnp
from jax import lax
from jax.experimental import pallas as pl
from jax.experimental.pallas import tpu as pltpu
from jax.sharding import PartitionSpec as P

DEG = 3
REACH = 6
MESH = pl.DeviceIdType.MESH

upper_edge = 10.7
lower_edge = 1.5
bottom_edge = -1.0


def stencil_weights():
    factor_square = math.factorial(6) ** 2
    side_weights = []
    for offset in range(1, 7):
        side_weights.append(
            2.0
            * (-1.0) ** (offset + 1)
            * factor_square
            / (offset * offset * math.factorial(6 - offset) * math.factorial(6 + offset))
        )
    center_weight = -2.0 * sum(side_weights)
    return (center_weight, side_weights)


def filter_scalars(pass_count):
    half_width = (upper_edge - lower_edge) / 2.0
    sigma_now = half_width / (bottom_edge - (upper_edge + lower_edge) / 2.0)
    gamma_value = 2.0 / sigma_now
    scalars = [(sigma_now / half_width, 0.0)]
    for pass_index in range(pass_count - 1):
        sigma_next = 1.0 / (gamma_value - sigma_now)
        scalars.append((2.0 * sigma_next / half_width, sigma_now * sigma_next))
        sigma_now = sigma_next
    return scalars


def row_weights(side):
    rows = lax.broadcasted_iota(jnp.int32, (8, 128), 0)
    weight = lambda k: side[k - 1] if 1 <= k <= REACH else 0.0
    pairs = []
    for r in range(1, 8):
        inside = rows >= r
        near, far = weight(r), weight(8 - r)
        pairs.append((jnp.where(inside, near, far), jnp.where(inside, far, near)))
    return pairs


def filtered_block(window, pot, before, scale, weight, pairs):
    center_weight, side = stencil_weights()
    side = [-0.5 * scale * w for w in side]
    n = window.shape[0] - 2 * REACH
    mid = window[REACH : REACH + n]
    diag = (-1.5 * center_weight - (upper_edge + lower_edge) / 2.0) * scale
    total = (pot * scale + diag) * mid
    for k in range(1, REACH + 1):
        beside = window[REACH + k : REACH + k + n] + window[REACH - k : REACH - k + n]
        beside = beside + pltpu.roll(mid, k, 3) + pltpu.roll(mid, 128 - k, 3)
        total = total + side[k - 1] * beside
    low, high = mid[:, 0], mid[:, 1]
    low_sum, high_sum = total[:, 0], total[:, 1]
    for r in range(1, 8):
        own, other = pairs[r - 1]
        low_turned, high_turned = pltpu.roll(low, r, 1), pltpu.roll(high, r, 1)
        low_sum = low_sum + own * low_turned + other * high_turned
        high_sum = high_sum + own * high_turned + other * low_turned
    if before is not None:
        low_sum = low_sum - weight * before[:, 0]
        high_sum = high_sum - weight * before[:, 1]
    return low_sum, high_sum


def filter_kernel(
    doms, orb, pot, out, p0, p1, p2, p3, pot_v, halo_send, halo_recv, move_sem
):
    orbs, planes = orb.shape[0], orb.shape[1]
    dom = lax.axis_index("dom")
    up, down = lax.rem(dom + 1, doms), lax.rem(dom + doms - 1, doms)
    scalars = filter_scalars(DEG)
    levels = (p0, p1, p2)
    step = 4
    edge = 8

    barrier = pltpu.get_barrier_semaphore()
    for peer in (up, down):
        pl.semaphore_signal(barrier, inc=1, device_id={"dom": peer}, device_id_type=MESH)
    load = pltpu.make_async_copy(orb, p0.at[:, pl.ds(REACH, planes)], move_sem.at[0])
    load.start()
    load_pot = pltpu.make_async_copy(pot, pot_v, move_sem.at[1])
    load_pot.start()
    pairs_unit = row_weights(stencil_weights()[1])

    def halo(level, source, first, last):
        target = levels[level]
        copies = []
        for at, (begin, place, peer) in enumerate(((last, 0, up), (first, REACH + planes, down))):
            copies.append(
                pltpu.make_async_remote_copy(
                    src_ref=source.at[:, pl.ds(begin, REACH)],
                    dst_ref=target.at[:, pl.ds(place, REACH)],
                    send_sem=halo_send.at[level, at],
                    recv_sem=halo_recv.at[level, at],
                    device_id={"dom": peer},
                    device_id_type=MESH,
                )
            )
        for copy in copies:
            copy.start()
        return copies

    pl.semaphore_wait(barrier, 2)
    copies = halo(0, orb, 0, planes - REACH)
    load.wait()
    load_pot.wait()

    def apply(level, begin, blocks):
        scale, weight = scalars[level]
        source = levels[level]
        pairs = [(-0.5 * scale * a, -0.5 * scale * b) for a, b in pairs_unit]

        def body(i, c):
            at = begin + i * step
            for o in range(orbs):
                before = None
                if level > 0:
                    before = levels[level - 1][o, pl.ds(at + REACH, step)]
                window = source[o, pl.ds(at, step + 2 * REACH)]
                low, high = filtered_block(
                    window, pot_v[pl.ds(at, step)], before, scale, weight, pairs
                )
                if level < DEG - 1:
                    levels[level + 1][o, pl.ds(at + REACH, step), 0] = low
                    levels[level + 1][o, pl.ds(at + REACH, step), 1] = high
                else:
                    p3[pl.ds(at, step), 0, o] = low
                    p3[pl.ds(at, step), 1, o] = high
            return c

        lax.fori_loop(0, blocks, body, 0)

    def store(number, begin, count):
        part = pl.ds(begin, count)
        copy = pltpu.make_async_copy(p3.at[part], out.at[part], move_sem.at[number])
        copy.start()
        return copy

    sent, stores = [], []
    for level in range(DEG):
        apply(level, edge, (planes - 2 * edge) // step)
        if level == DEG - 1:
            stores.append(store(2, edge, planes - 2 * edge))
        for copy in copies:
            copy.wait_recv()
        apply(level, 0, edge // step)
        apply(level, planes - edge, edge // step)
        sent += copies
        if level < DEG - 1:
            copies = halo(level + 1, levels[level + 1], REACH, planes)
    stores.append(store(3, 0, edge))
    stores.append(store(4, planes - edge, edge))
    for copy in sent:
        copy.wait_send()
    for copy in stores:
        copy.wait()


def spread_kernel(bands, parts, sub, recv, rows, move_sem, all_send, all_recv, row_send, row_recv):
    band = lax.axis_index("band")
    barrier = pltpu.get_barrier_semaphore()

    def greet(i, c):
        pl.semaphore_signal(
            barrier, inc=1, device_id={"band": lax.rem(band + i, bands)}, device_id_type=MESH
        )
        return c

    lax.fori_loop(1, bands, greet, 0)
    own = pltpu.make_async_copy(parts.at[band], recv.at[band], move_sem.at[0])
    own.start()
    own_rows = pltpu.make_async_copy(sub, rows.at[band], move_sem.at[1])
    own_rows.start()
    pl.semaphore_wait(barrier, bands - 1)

    def send(i, c):
        peer = lax.rem(band + i, bands)
        pltpu.make_async_remote_copy(
            src_ref=parts.at[peer], dst_ref=recv.at[band], send_sem=all_send, recv_sem=all_recv,
            device_id={"band": peer}, device_id_type=MESH,
        ).start()
        pltpu.make_async_remote_copy(
            src_ref=sub, dst_ref=rows.at[band], send_sem=row_send, recv_sem=row_recv,
            device_id={"band": peer}, device_id_type=MESH,
        ).start()
        return c

    lax.fori_loop(1, bands, send, 0)
    own.wait()
    own_rows.wait()
    for ref, sem_a, sem_b in ((rows, row_send, row_recv), (recv, all_send, all_recv)):
        whole = ref.at[pl.ds(0, bands - 1)]
        pltpu.make_async_copy(whole, whole, sem_a).wait()
        pltpu.make_async_copy(whole, whole, sem_b).wait()


def two_parts(values):
    high = values.astype(jnp.bfloat16)
    return high, (values - high.astype(jnp.float32)).astype(jnp.bfloat16)


def rotate_kernel(recv, rows, out, recv_v, rows_v, out_v, sems):
    load = pltpu.make_async_copy(recv, recv_v, sems.at[0])
    load_rows = pltpu.make_async_copy(rows, rows_v, sems.at[1])
    load.start()
    load_rows.start()
    load_rows.wait()
    high, low = two_parts(jnp.concatenate([rows_v[:, 0], rows_v[:, 1]], axis=0).T)
    matrix = jnp.concatenate([high, high, low], axis=1)
    load.wait()
    width = 256
    stores = []
    for at in range(0, 8 * 128, width):
        columns = []
        for r in range(at // 128, (at + width) // 128):
            values = jnp.concatenate([recv_v[:, 0, r], recv_v[:, 1, r]], axis=0)
            high, low = two_parts(values)
            columns.append(jnp.concatenate([high, low, high], axis=0))
        out_v[:, pl.ds(at, width)] = jnp.dot(
            matrix, jnp.concatenate(columns, axis=1), preferred_element_type=jnp.float32
        )
        store = pltpu.make_async_copy(
            out_v.at[:, pl.ds(at, width)], out.at[:, pl.ds(at, width)], sems.at[2 + at // width]
        )
        store.start()
        stores.append(store)
    for store in stores:
        store.wait()


def per_device(bands, doms, orbitals, potential, subspace):
    orbs, planes = orbitals.shape[0], orbitals.shape[1]
    orb = orbitals.reshape(orbs, planes, 2, 8, 128)
    pot = potential.reshape(planes, 2, 8, 128)
    f32 = jnp.float32
    padded = pltpu.VMEM((orbs, planes + 2 * REACH, 2, 8, 128), f32)
    dma = pltpu.SemaphoreType.DMA
    anywhere = pl.BlockSpec(memory_space=pl.ANY)
    filtered = pl.pallas_call(
        functools.partial(filter_kernel, doms),
        out_shape=jax.ShapeDtypeStruct((planes, 2, orbs, 8, 128), f32),
        in_specs=[anywhere] * 2,
        out_specs=anywhere,
        scratch_shapes=[
            padded,
            padded,
            padded,
            pltpu.VMEM((planes, 2, orbs, 8, 128), f32),
            pltpu.VMEM((planes, 2, 8, 128), f32),
            dma((DEG, 2)),
            dma((DEG, 2)),
            dma((5,)),
        ],
        compiler_params=pltpu.CompilerParams(
            collective_id=0, has_side_effects=True, vmem_limit_bytes=60 * 2**20
        ),
        name="filter",
    )(orb, pot)
    recv, rows = pl.pallas_call(
        functools.partial(spread_kernel, bands),
        out_shape=(
            jax.ShapeDtypeStruct((bands, orbs, 8, 128), f32),
            jax.ShapeDtypeStruct((bands, orbs, 128), f32),
        ),
        in_specs=[anywhere] * 2,
        out_specs=(anywhere,) * 2,
        scratch_shapes=[dma((2,)), dma, dma, dma, dma],
        compiler_params=pltpu.CompilerParams(
            collective_id=1, has_side_effects=True, vmem_limit_bytes=60 * 2**20
        ),
        name="spread",
    )(filtered.reshape(bands, orbs, 8, 128), subspace)
    return pl.pallas_call(
        rotate_kernel,
        out_shape=jax.ShapeDtypeStruct((bands * orbs, 1024), f32),
        in_specs=[anywhere] * 2,
        out_specs=anywhere,
        scratch_shapes=[
            pltpu.VMEM((bands, orbs, 8, 128), f32),
            pltpu.VMEM((bands, orbs, 128), f32),
            pltpu.VMEM((bands * orbs, 1024), f32),
            dma((6,)),
        ],
        compiler_params=pltpu.CompilerParams(vmem_limit_bytes=60 * 2**20),
        name="rotate",
    )(recv, rows)


def solution(mesh):
    in_specs = (P("band", "dom", None, None), P("dom", None, None), P("band", None))
    out_specs = P(None, ("dom", "band"))
    return jax.shard_map(
        functools.partial(per_device, mesh.shape["band"], mesh.shape["dom"]),
        mesh=mesh,
        in_specs=in_specs,
        out_specs=out_specs,
        check_vma=False,
    )
```

```python
import functools
import math

import jax
import jax.numpy as jnp
from jax import lax
from jax.experimental import pallas as pl
from jax.experimental.pallas import tpu as pltpu
from jax.sharding import PartitionSpec as P

DEG = 3
REACH = 6
MESH = pl.DeviceIdType.MESH

upper_edge = 10.7
lower_edge = 1.5
bottom_edge = -1.0


def stencil_weights():
    factor_square = math.factorial(6) ** 2
    side_weights = []
    for offset in range(1, 7):
        side_weights.append(
            2.0
            * (-1.0) ** (offset + 1)
            * factor_square
            / (offset * offset * math.factorial(6 - offset) * math.factorial(6 + offset))
        )
    center_weight = -2.0 * sum(side_weights)
    return (center_weight, side_weights)


def filter_scalars(pass_count):
    half_width = (upper_edge - lower_edge) / 2.0
    sigma_now = half_width / (bottom_edge - (upper_edge + lower_edge) / 2.0)
    gamma_value = 2.0 / sigma_now
    scalars = [(sigma_now / half_width, 0.0)]
    for pass_index in range(pass_count - 1):
        sigma_next = 1.0 / (gamma_value - sigma_now)
        scalars.append((2.0 * sigma_next / half_width, sigma_now * sigma_next))
        sigma_now = sigma_next
    return scalars


def two_parts(values):
    high = values.astype(jnp.bfloat16)
    return high, (values - high.astype(jnp.float32)).astype(jnp.bfloat16)


def lane_matrix():
    rows = lax.broadcasted_iota(jnp.int32, (128, 128), 0)
    columns = lax.broadcasted_iota(jnp.int32, (128, 128), 1)
    apart = jnp.abs(rows - columns)
    apart = jnp.minimum(apart, 128 - apart)
    matrix = jnp.zeros((128, 128), jnp.float32)
    for k, w in enumerate(stencil_weights()[1], 1):
        matrix = jnp.where(apart == k, jnp.float32(w), matrix)
    high, low = two_parts(matrix)
    return jnp.concatenate([high, high, low], axis=0)


def row_weights():
    side = stencil_weights()[1]
    weight = lambda k: side[k - 1] if 1 <= k <= REACH else 0.0
    rows = lax.broadcasted_iota(jnp.int32, (8, 128), 0)
    cyclic, negacyclic = {}, {}
    for r in range(1, 8):
        cyclic[r] = 0.5 * (weight(r) + weight(8 - r))
        if r != 4:
            w = 0.5 * (weight(r) - weight(8 - r))
            negacyclic[r] = jnp.where(rows >= r, jnp.float32(w), jnp.float32(-w))
    return cyclic, negacyclic


def filtered_block(window, pot, before, scale, weight, lanes, cyclic, negacyclic):
    center_weight, side = stencil_weights()
    n = window.shape[0] - 2 * REACH
    mid = window[REACH : REACH + n]
    high, low = two_parts(mid.reshape(n * 16, 128))
    total = jnp.dot(
        jnp.concatenate([high, low, high], axis=1), lanes, preferred_element_type=jnp.float32
    ).reshape(n, 2, 8, 128)
    for k in range(1, REACH + 1):
        beside = window[REACH + k : REACH + k + n] + window[REACH - k : REACH - k + n]
        total = total + side[k - 1] * beside
    both, apart = mid[:, 0] + mid[:, 1], mid[:, 0] - mid[:, 1]
    even = cyclic[4] * pltpu.roll(both, 4, 1)
    for r in range(1, 4):
        even = even + cyclic[r] * (pltpu.roll(both, r, 1) + pltpu.roll(both, 8 - r, 1))
    odd = None
    for r, w in negacyclic.items():
        term = w * pltpu.roll(apart, r, 1)
        odd = term if odd is None else odd + term
    diag = (-1.5 * center_weight - (upper_edge + lower_edge) / 2.0) * scale
    results = []
    for at, rows in enumerate((even + odd, even - odd)):
        result = (pot[:, at] * scale + diag) * mid[:, at]
        result = result + (-0.5 * scale) * (total[:, at] + rows)
        if before is not None:
            result = result - weight * before[:, at]
        results.append(result)
    return results


def filter_kernel(
    bands, doms, orb, pot, sub, recv, rows, p0, p1, p2, out, pot_v,
    near_send, near_recv, far_send, far_recv, pot_send, pot_recv,
    move_sem, all_send, all_recv, row_send, row_recv,
):
    orbs, planes = orb.shape[0], orb.shape[1]
    band, dom = lax.axis_index("band"), lax.axis_index("dom")
    core, half = lax.rem(dom, 2), lax.div(dom, 2)
    side = 4
    zl, y, x = lax.div(band, side * side), lax.rem(lax.div(band, side), side), lax.rem(band, side)
    sibling = {"dom": dom + 1 - 2 * core}
    across = {"dom": 2 * (1 - half) + 1 - core}
    scalars = filter_scalars(DEG)
    buffers = (p0, p1, p2, out)
    rims = tuple(REACH * (DEG - level) for level in range(DEG + 1))
    deep, pot_rim = rims[0], rims[1]
    step = 4

    load = pltpu.make_async_copy(orb, p0.at[:, pl.ds(deep, planes)], move_sem.at[0])
    load.start()
    load_pot = pltpu.make_async_copy(pot, pot_v.at[pl.ds(pot_rim, planes)], move_sem.at[1])
    load_pot.start()

    def neighbour(i):
        dz, dy, dx = lax.rem(i, side), lax.rem(lax.div(i, side), side), lax.div(i, side * side)
        return (
            lax.rem(zl + dz, side) * side * side + lax.rem(y + dy, side) * side + lax.rem(x + dx, side)
        )

    barrier = pltpu.get_barrier_semaphore()
    for peer in (sibling, across):
        pl.semaphore_signal(barrier, inc=1, device_id=peer, device_id_type=MESH)

    def greet(i, c):
        pl.semaphore_signal(
            barrier, inc=1, device_id={"band": neighbour(i)}, device_id_type=MESH
        )
        return c

    lax.fori_loop(1, bands, greet, 0)
    lanes = lane_matrix()
    cyclic, negacyclic = row_weights()
    pl.semaphore_wait(barrier, bands + 1)

    def remote(src, dst, send_sem, recv_sem, peer):
        return pltpu.make_async_remote_copy(
            src_ref=src, dst_ref=dst, send_sem=send_sem, recv_sem=recv_sem,
            device_id=peer, device_id_type=MESH,
        )

    def rim_copies(src, dst, width, sems_near, sems_far):
        inner = planes - width
        near = remote(
            src.at[pl.ds((1 - core) * inner, width)],
            dst.at[pl.ds(core * (planes + width), width)], *sems_near, sibling,
        )
        far = remote(
            src.at[pl.ds(core * inner, width)],
            dst.at[pl.ds((1 - core) * (planes + width), width)], *sems_far, across,
        )
        return near, far

    part = pot_rim // side
    pot_far = remote(
        pot.at[pl.ds(core * (planes - pot_rim) + x * part, part)],
        pot_v.at[pl.ds((1 - core) * (planes + pot_rim) + x * part, part)],
        pot_send.at[0], pot_recv.at[0], across,
    )
    pot_near = remote(
        pot.at[pl.ds((1 - core) * (planes - pot_rim), pot_rim)],
        pot_v.at[pl.ds(core * (planes + pot_rim), pot_rim)],
        pot_send.at[1], pot_recv.at[1], sibling,
    )
    pot_far.start()
    pot_near.start()
    nears, fars = [], []
    for o in range(orbs):
        near, far = rim_copies(
            orb.at[o], p0.at[o], deep,
            (near_send.at[o], near_recv.at[o]), (far_send.at[o], far_recv.at[o]),
        )
        far.start()
        near.start()
        nears.append(near)
        fars.append(far)

    own_rows = pltpu.make_async_copy(sub, rows.at[band], move_sem.at[2])
    own_rows.start()

    def send_rows(i, c):
        remote(sub, rows.at[band], row_send, row_recv, {"band": neighbour(i)}).start()
        return c

    lax.fori_loop(1, bands, send_rows, 0)

    def apply(level, o, begin, blocks):
        scale, weight = scalars[level]

        def body(i, c):
            at = begin + i * step
            before = None
            if level > 0:
                before = buffers[level - 1][o, pl.ds(at + rims[level - 1], step)]
            window = buffers[level][o, pl.ds(at + rims[level] - REACH, step + 2 * REACH)]
            low, high = filtered_block(
                window, pot_v[pl.ds(at + pot_rim, step)], before, scale, weight,
                lanes, cyclic, negacyclic,
            )
            target = buffers[level + 1]
            target[o, pl.ds(at + rims[level + 1], step), 0] = low
            target[o, pl.ds(at + rims[level + 1], step), 1] = high
            return c

        lax.fori_loop(0, blocks, body, 0)

    early = [(planes + 2 * rims[level + 1] - 20) // step for level in range(DEG)]
    load.wait()
    load_pot.wait()
    pot_near.wait_recv()
    for o in range(orbs):
        nears[o].wait_recv()
        for level in range(DEG):
            rim = rims[level + 1]
            apply(level, o, core * -rim + (1 - core) * (20 - rim), early[level])

    pot_far.wait_recv()
    at_far = (planes + pot_rim) * core + x * part
    passed = []
    for d in range(1, side):
        mine = pot_v.at[pl.ds(at_far, part)]
        peer = {"band": band - x + lax.rem(x + d, side)}
        copy = remote(mine, mine, pot_send.at[1 + d], pot_recv.at[1 + d], peer)
        copy.start()
        passed.append(copy)
    for copy in passed:
        copy.wait_recv()

    def spread(o):
        own = pltpu.make_async_copy(
            out.at[o, lax.div(band, 2), lax.rem(band, 2)], recv.at[band, o], move_sem.at[3 + o]
        )
        own.start()

        def send(i, c):
            peer = neighbour(i)
            remote(
                out.at[o, lax.div(peer, 2), lax.rem(peer, 2)], recv.at[band, o],
                all_send, all_recv, {"band": peer},
            ).start()
            return c

        lax.fori_loop(1, bands, send, 0)
        return own

    owns = []
    for o in range(orbs):
        fars[o].wait_recv()
        for level in range(DEG):
            rim = rims[level + 1]
            apply(level, o, core * (planes + rim - 20) - (1 - core) * rim, 20 // step)
        owns.append(spread(o))

    for copy in (*nears, *fars, pot_far, pot_near, *passed):
        copy.wait_send()
    own_rows.wait()
    for own in owns:
        own.wait()
    for ref, sem_a, sem_b in ((rows, row_send, row_recv), (recv, all_send, all_recv)):
        whole = ref.at[pl.ds(0, bands - 1)]
        pltpu.make_async_copy(whole, whole, sem_a).wait()
        pltpu.make_async_copy(whole, whole, sem_b).wait()


def rotate_kernel(recv, rows, out, recv_v, rows_v, out_v, sems):
    load = pltpu.make_async_copy(recv, recv_v, sems.at[0])
    load_rows = pltpu.make_async_copy(rows, rows_v, sems.at[1])
    load.start()
    load_rows.start()
    load_rows.wait()
    high, low = two_parts(jnp.concatenate([rows_v[:, 0], rows_v[:, 1]], axis=0).T)
    matrix = jnp.concatenate([high, high, low], axis=1)
    load.wait()
    width = 256
    stores = []
    for at in range(0, 8 * 128, width):
        columns = []
        for r in range(at // 128, (at + width) // 128):
            values = jnp.concatenate([recv_v[:, 0, r], recv_v[:, 1, r]], axis=0)
            high, low = two_parts(values)
            columns.append(jnp.concatenate([high, low, high], axis=0))
        out_v[:, pl.ds(at, width)] = jnp.dot(
            matrix, jnp.concatenate(columns, axis=1), preferred_element_type=jnp.float32
        )
        store = pltpu.make_async_copy(
            out_v.at[:, pl.ds(at, width)], out.at[:, pl.ds(at, width)], sems.at[2 + at // width]
        )
        store.start()
        stores.append(store)
    for store in stores:
        store.wait()


def per_device(bands, doms, orbitals, potential, subspace):
    orbs, planes = orbitals.shape[0], orbitals.shape[1]
    orb = orbitals.reshape(orbs, planes, 2, 8, 128)
    pot = potential.reshape(planes, 2, 8, 128)
    f32 = jnp.float32
    dma = pltpu.SemaphoreType.DMA
    anywhere = pl.BlockSpec(memory_space=pl.ANY)
    recv, rows = pl.pallas_call(
        functools.partial(filter_kernel, bands, doms),
        out_shape=(
            jax.ShapeDtypeStruct((bands, orbs, 8, 128), f32),
            jax.ShapeDtypeStruct((bands, orbs, 128), f32),
        ),
        in_specs=[anywhere] * 3,
        out_specs=(anywhere,) * 2,
        scratch_shapes=[
            *[
                pltpu.VMEM((orbs, planes + 2 * REACH * (DEG - level), 2, 8, 128), f32)
                for level in range(DEG + 1)
            ],
            pltpu.VMEM((planes + 2 * REACH * (DEG - 1), 2, 8, 128), f32),
            dma((orbs,)),
            dma((orbs,)),
            dma((orbs,)),
            dma((orbs,)),
            dma((5,)),
            dma((5,)),
            dma((3 + orbs,)),
            dma,
            dma,
            dma,
            dma,
        ],
        compiler_params=pltpu.CompilerParams(
            collective_id=0, has_side_effects=True, vmem_limit_bytes=60 * 2**20
        ),
        name="filter",
    )(orb, pot, subspace)
    return pl.pallas_call(
        rotate_kernel,
        out_shape=jax.ShapeDtypeStruct((bands * orbs, 1024), f32),
        in_specs=[anywhere] * 2,
        out_specs=anywhere,
        scratch_shapes=[
            pltpu.VMEM((bands, orbs, 8, 128), f32),
            pltpu.VMEM((bands, orbs, 128), f32),
            pltpu.VMEM((bands * orbs, 1024), f32),
            dma((6,)),
        ],
        compiler_params=pltpu.CompilerParams(vmem_limit_bytes=60 * 2**20),
        name="rotate",
    )(recv, rows)


def solution(mesh):
    in_specs = (P("band", "dom", None, None), P("dom", None, None), P("band", None))
    out_specs = P(None, ("dom", "band"))
    return jax.shard_map(
        functools.partial(per_device, mesh.shape["band"], mesh.shape["dom"]),
        mesh=mesh,
        in_specs=in_specs,
        out_specs=out_specs,
        check_vma=False,
    )
```

```python
import functools
import math

import jax
import jax.numpy as jnp
from jax import lax
from jax.experimental import pallas as pl
from jax.experimental.pallas import tpu as pltpu
from jax.sharding import PartitionSpec as P

DEG = 3
REACH = 6
MESH = pl.DeviceIdType.MESH

upper_edge = 10.7
lower_edge = 1.5
bottom_edge = -1.0


def stencil_weights():
    factor_square = math.factorial(6) ** 2
    side_weights = []
    for offset in range(1, 7):
        side_weights.append(
            2.0
            * (-1.0) ** (offset + 1)
            * factor_square
            / (offset * offset * math.factorial(6 - offset) * math.factorial(6 + offset))
        )
    center_weight = -2.0 * sum(side_weights)
    return (center_weight, side_weights)


def filter_scalars(pass_count):
    half_width = (upper_edge - lower_edge) / 2.0
    sigma_now = half_width / (bottom_edge - (upper_edge + lower_edge) / 2.0)
    gamma_value = 2.0 / sigma_now
    scalars = [(sigma_now / half_width, 0.0)]
    for pass_index in range(pass_count - 1):
        sigma_next = 1.0 / (gamma_value - sigma_now)
        scalars.append((2.0 * sigma_next / half_width, sigma_now * sigma_next))
        sigma_now = sigma_next
    return scalars


def two_parts(values):
    high = values.astype(jnp.bfloat16)
    return high, (values - high.astype(jnp.float32)).astype(jnp.bfloat16)


def lane_matrix():
    rows = lax.broadcasted_iota(jnp.int32, (128, 128), 0)
    columns = lax.broadcasted_iota(jnp.int32, (128, 128), 1)
    apart = jnp.abs(rows - columns)
    apart = jnp.minimum(apart, 128 - apart)
    matrix = jnp.zeros((128, 128), jnp.float32)
    for k, w in enumerate(stencil_weights()[1], 1):
        matrix = jnp.where(apart == k, jnp.float32(w), matrix)
    high, low = two_parts(matrix)
    return jnp.concatenate([high, high, low], axis=0)


def row_weights():
    side = stencil_weights()[1]
    weight = lambda k: side[k - 1] if 1 <= k <= REACH else 0.0
    rows = lax.broadcasted_iota(jnp.int32, (8, 128), 0)
    cyclic, negacyclic = {}, {}
    for r in range(1, 8):
        cyclic[r] = 0.5 * (weight(r) + weight(8 - r))
        if r != 4:
            w = 0.5 * (weight(r) - weight(8 - r))
            negacyclic[r] = jnp.where(rows >= r, jnp.float32(w), jnp.float32(-w))
    return cyclic, negacyclic


def filtered_block(window, pot, before, scale, weight, lanes, cyclic, negacyclic):
    center_weight, side = stencil_weights()
    n = window.shape[0] - 2 * REACH
    mid = window[REACH : REACH + n]
    high, low = two_parts(mid.reshape(n * 16, 128))
    total = jnp.dot(
        jnp.concatenate([high, low, high], axis=1), lanes, preferred_element_type=jnp.float32
    ).reshape(n, 2, 8, 128)
    for k in range(1, REACH + 1):
        beside = window[REACH + k : REACH + k + n] + window[REACH - k : REACH - k + n]
        total = total + side[k - 1] * beside
    both, apart = mid[:, 0] + mid[:, 1], mid[:, 0] - mid[:, 1]
    even = cyclic[4] * pltpu.roll(both, 4, 1)
    for r in range(1, 4):
        even = even + cyclic[r] * (pltpu.roll(both, r, 1) + pltpu.roll(both, 8 - r, 1))
    odd = None
    for r, w in negacyclic.items():
        term = w * pltpu.roll(apart, r, 1)
        odd = term if odd is None else odd + term
    diag = (-1.5 * center_weight - (upper_edge + lower_edge) / 2.0) * scale
    results = []
    for at, rows in enumerate((even + odd, even - odd)):
        result = (pot[:, at] * scale + diag) * mid[:, at]
        result = result + (-0.5 * scale) * (total[:, at] + rows)
        if before is not None:
            result = result - weight * before[:, at]
        results.append(result)
    return results


def filter_kernel(
    bands, doms, orb, pot, sub, recv, rows, p0, p1, p2, out, pot_v,
    near_send, near_recv, far_send, far_recv, pot_send, pot_recv,
    move_sem, all_send, all_recv, row_send, row_recv,
):
    orbs, planes = orb.shape[0], orb.shape[1]
    band, dom = lax.axis_index("band"), lax.axis_index("dom")
    core, half = lax.rem(dom, 2), lax.div(dom, 2)
    side = 4
    zl, y, x = lax.div(band, side * side), lax.rem(lax.div(band, side), side), lax.rem(band, side)
    sibling = {"dom": dom + 1 - 2 * core}
    across = {"dom": 2 * (1 - half) + 1 - core}
    scalars = filter_scalars(DEG)
    buffers = (p0, p1, p2)
    rims = tuple(REACH * (DEG - level) for level in range(DEG + 1))
    deep, pot_rim = rims[0], rims[1]
    step = 4

    load = pltpu.make_async_copy(orb, p0.at[:, pl.ds(deep, planes)], move_sem.at[0])
    load.start()
    load_pot = pltpu.make_async_copy(pot, pot_v.at[pl.ds(pot_rim, planes)], move_sem.at[1])
    load_pot.start()

    along_z = [lax.rem(zl + d, side) * side * side for d in range(side)]
    along_y = [lax.rem(y + d, side) * side for d in range(side)]
    along_x = [lax.rem(x + d, side) for d in range(side)]
    others = [
        along_z[dz] + along_y[dy] + along_x[dx]
        for dx in range(side)
        for dy in range(side)
        for dz in range(side)
    ][1:]

    barrier = pltpu.get_barrier_semaphore()
    for peer in (sibling, across):
        pl.semaphore_signal(barrier, inc=1, device_id=peer, device_id_type=MESH)

    for peer in others:
        pl.semaphore_signal(barrier, inc=1, device_id={"band": peer}, device_id_type=MESH)
    lanes = lane_matrix()
    cyclic, negacyclic = row_weights()
    pl.semaphore_wait(barrier, bands + 1)

    def remote(src, dst, send_sem, recv_sem, peer):
        return pltpu.make_async_remote_copy(
            src_ref=src, dst_ref=dst, send_sem=send_sem, recv_sem=recv_sem,
            device_id=peer, device_id_type=MESH,
        )

    def rim_copies(src, dst, width, sems_near, sems_far):
        inner = planes - width
        near = remote(
            src.at[pl.ds((1 - core) * inner, width)],
            dst.at[pl.ds(core * (planes + width), width)], *sems_near, sibling,
        )
        far = remote(
            src.at[pl.ds(core * inner, width)],
            dst.at[pl.ds((1 - core) * (planes + width), width)], *sems_far, across,
        )
        return near, far

    part = pot_rim // side
    pot_far = remote(
        pot.at[pl.ds(core * (planes - pot_rim) + x * part, part)],
        pot_v.at[pl.ds((1 - core) * (planes + pot_rim) + x * part, part)],
        pot_send.at[0], pot_recv.at[0], across,
    )
    pot_near = remote(
        pot.at[pl.ds((1 - core) * (planes - pot_rim), pot_rim)],
        pot_v.at[pl.ds(core * (planes + pot_rim), pot_rim)],
        pot_send.at[1], pot_recv.at[1], sibling,
    )
    pot_far.start()
    pot_near.start()
    nears, fars = [], []
    for o in range(orbs):
        near, far = rim_copies(
            orb.at[o], p0.at[o], deep,
            (near_send.at[o], near_recv.at[o]), (far_send.at[o], far_recv.at[o]),
        )
        far.start()
        near.start()
        nears.append(near)
        fars.append(far)

    own_rows = pltpu.make_async_copy(sub, rows.at[band], move_sem.at[2])
    own_rows.start()

    for peer in others:
        remote(sub, rows.at[band], row_send, row_recv, {"band": peer}).start()

    def apply(level, o, begin, blocks):
        scale, weight = scalars[level]

        def body(i, c):
            at = begin + i * step
            before = None
            if level > 0:
                before = buffers[level - 1][o, pl.ds(at + rims[level - 1], step)]
            window = buffers[level][o, pl.ds(at + rims[level] - REACH, step + 2 * REACH)]
            low, high = filtered_block(
                window, pot_v[pl.ds(at + pot_rim, step)], before, scale, weight,
                lanes, cyclic, negacyclic,
            )
            if level < DEG - 1:
                buffers[level + 1][o, pl.ds(at + rims[level + 1], step), 0] = low
                buffers[level + 1][o, pl.ds(at + rims[level + 1], step), 1] = high
            else:
                pairs = jnp.stack([low, high], axis=1)
                out[o, pl.ds(2 * at, 2 * step)] = pairs.reshape(2 * step, 8, 128)
            return c

        lax.fori_loop(0, blocks, body, 0)

    early = [(planes + 2 * rims[level + 1] - 20) // step for level in range(DEG)]
    load.wait()
    load_pot.wait()
    pot_near.wait_recv()
    for o in range(orbs):
        nears[o].wait_recv()
        for level in range(DEG):
            rim = rims[level + 1]
            apply(level, o, core * -rim + (1 - core) * (20 - rim), early[level])

    pot_far.wait_recv()
    at_far = (planes + pot_rim) * core + x * part
    passed = []
    for d in range(1, side):
        mine = pot_v.at[pl.ds(at_far, part)]
        peer = {"band": band - x + lax.rem(x + d, side)}
        copy = remote(mine, mine, pot_send.at[1 + d], pot_recv.at[1 + d], peer)
        copy.start()
        passed.append(copy)
    for copy in passed:
        copy.wait_recv()

    def spread(o):
        own = pltpu.make_async_copy(
            out.at[o, band], recv.at[band, o], move_sem.at[3 + o]
        )
        own.start()

        for peer in others:
            remote(
                out.at[o, peer], recv.at[band, o], all_send, all_recv, {"band": peer}
            ).start()
        return own

    owns = []
    for o in range(orbs):
        fars[o].wait_recv()
        for level in range(DEG):
            rim = rims[level + 1]
            apply(level, o, core * (planes + rim - 20) - (1 - core) * rim, 20 // step)
        owns.append(spread(o))

    for copy in (*nears, *fars, pot_far, pot_near, *passed):
        copy.wait_send()
    own_rows.wait()
    for own in owns:
        own.wait()
    for ref, sem_a, sem_b in ((rows, row_send, row_recv), (recv, all_send, all_recv)):
        whole = ref.at[pl.ds(0, bands - 1)]
        pltpu.make_async_copy(whole, whole, sem_a).wait()
        pltpu.make_async_copy(whole, whole, sem_b).wait()


def rotate_kernel(recv_v, rows_v, out, out_v, sems):
    high, low = two_parts(jnp.concatenate([rows_v[:, 0], rows_v[:, 1]], axis=0).T)
    matrix = jnp.concatenate([high, high, low], axis=1)
    width = 256
    stores = []
    for at in range(0, 8 * 128, width):
        columns = []
        for r in range(at // 128, (at + width) // 128):
            values = jnp.concatenate([recv_v[:, 0, r], recv_v[:, 1, r]], axis=0)
            high, low = two_parts(values)
            columns.append(jnp.concatenate([high, low, high], axis=0))
        out_v[:, pl.ds(at, width)] = jnp.dot(
            matrix, jnp.concatenate(columns, axis=1), preferred_element_type=jnp.float32
        )
        store = pltpu.make_async_copy(
            out_v.at[:, pl.ds(at, width)], out.at[:, pl.ds(at, width)], sems.at[at // width]
        )
        store.start()
        stores.append(store)
    for store in stores:
        store.wait()


def per_device(bands, doms, orbitals, potential, subspace):
    orbs, planes = orbitals.shape[0], orbitals.shape[1]
    orb = orbitals.reshape(orbs, planes, 2, 8, 128)
    pot = potential.reshape(planes, 2, 8, 128)
    f32 = jnp.float32
    dma = pltpu.SemaphoreType.DMA
    anywhere = pl.BlockSpec(memory_space=pl.ANY)
    recv, rows = pl.pallas_call(
        functools.partial(filter_kernel, bands, doms),
        out_shape=(
            pltpu.VMEM((bands, orbs, 8, 128), f32),
            pltpu.VMEM((bands, orbs, 128), f32),
        ),
        in_specs=[anywhere] * 3,
        out_specs=(anywhere,) * 2,
        scratch_shapes=[
            *[
                pltpu.VMEM((orbs, planes + 2 * REACH * (DEG - level), 2, 8, 128), f32)
                for level in range(DEG)
            ],
            pltpu.VMEM((orbs, bands, 8, 128), f32),
            pltpu.VMEM((planes + 2 * REACH * (DEG - 1), 2, 8, 128), f32),
            dma((orbs,)),
            dma((orbs,)),
            dma((orbs,)),
            dma((orbs,)),
            dma((5,)),
            dma((5,)),
            dma((3 + orbs,)),
            dma,
            dma,
            dma,
            dma,
        ],
        compiler_params=pltpu.CompilerParams(
            collective_id=0, has_side_effects=True, vmem_limit_bytes=32 * 2**20
        ),
        name="filter",
    )(*(pltpu.with_memory_space_constraint(a, pltpu.HBM) for a in (orb, pot, subspace)))
    return pl.pallas_call(
        rotate_kernel,
        out_shape=jax.ShapeDtypeStruct((bands * orbs, 1024), f32),
        in_specs=[pl.BlockSpec(memory_space=pltpu.VMEM)] * 2,
        out_specs=anywhere,
        scratch_shapes=[pltpu.VMEM((bands * orbs, 1024), f32), dma((4,))],
        compiler_params=pltpu.CompilerParams(vmem_limit_bytes=32 * 2**20),
        name="rotate",
    )(*(pltpu.with_memory_space_constraint(a, pltpu.VMEM) for a in (recv, rows)))


def solution(mesh):
    in_specs = (P("band", "dom", None, None), P("dom", None, None), P("band", None))
    out_specs = P(None, ("dom", "band"))
    return jax.shard_map(
        functools.partial(per_device, mesh.shape["band"], mesh.shape["dom"]),
        mesh=mesh,
        in_specs=in_specs,
        out_specs=out_specs,
        check_vma=False,
    )
```

```python
import functools
import math

import jax
import jax.numpy as jnp
from jax import lax
from jax.experimental import pallas as pl
from jax.experimental.pallas import tpu as pltpu
from jax.sharding import PartitionSpec as P

DEG = 3
REACH = 6
MESH = pl.DeviceIdType.MESH

upper_edge = 10.7
lower_edge = 1.5
bottom_edge = -1.0


def stencil_weights():
    factor_square = math.factorial(6) ** 2
    side_weights = []
    for offset in range(1, 7):
        side_weights.append(
            2.0
            * (-1.0) ** (offset + 1)
            * factor_square
            / (offset * offset * math.factorial(6 - offset) * math.factorial(6 + offset))
        )
    center_weight = -2.0 * sum(side_weights)
    return (center_weight, side_weights)


def filter_scalars(pass_count):
    half_width = (upper_edge - lower_edge) / 2.0
    sigma_now = half_width / (bottom_edge - (upper_edge + lower_edge) / 2.0)
    gamma_value = 2.0 / sigma_now
    scalars = [(sigma_now / half_width, 0.0)]
    for pass_index in range(pass_count - 1):
        sigma_next = 1.0 / (gamma_value - sigma_now)
        scalars.append((2.0 * sigma_next / half_width, sigma_now * sigma_next))
        sigma_now = sigma_next
    return scalars


def two_parts(values):
    high = values.astype(jnp.bfloat16)
    return high, (values - high.astype(jnp.float32)).astype(jnp.bfloat16)


def lane_matrix():
    rows = lax.broadcasted_iota(jnp.int32, (128, 128), 0)
    columns = lax.broadcasted_iota(jnp.int32, (128, 128), 1)
    apart = jnp.abs(rows - columns)
    apart = jnp.minimum(apart, 128 - apart)
    matrix = jnp.zeros((128, 128), jnp.float32)
    for k, w in enumerate(stencil_weights()[1], 1):
        matrix = jnp.where(apart == k, jnp.float32(w), matrix)
    high, low = two_parts(matrix)
    return jnp.concatenate([high, high, low], axis=0)


def row_weights():
    side = stencil_weights()[1]
    weight = lambda k: side[k - 1] if 1 <= k <= REACH else 0.0
    rows = lax.broadcasted_iota(jnp.int32, (8, 128), 0)
    cyclic, negacyclic = {}, {}
    for r in range(1, 8):
        cyclic[r] = 0.5 * (weight(r) + weight(8 - r))
        if r != 4:
            w = 0.5 * (weight(r) - weight(8 - r))
            negacyclic[r] = jnp.where(rows >= r, jnp.float32(w), jnp.float32(-w))
    return cyclic, negacyclic


def filtered_block(window, pot, before, scale, weight, lanes, cyclic, negacyclic):
    center_weight, side = stencil_weights()
    n = window.shape[0] - 2 * REACH
    mid = window[REACH : REACH + n]
    high, low = two_parts(mid.reshape(n * 16, 128))
    total = jnp.dot(
        jnp.concatenate([high, low, high], axis=1), lanes, preferred_element_type=jnp.float32
    ).reshape(n, 2, 8, 128)
    for k in range(1, REACH + 1):
        beside = window[REACH + k : REACH + k + n] + window[REACH - k : REACH - k + n]
        total = total + side[k - 1] * beside
    both, apart = mid[:, 0] + mid[:, 1], mid[:, 0] - mid[:, 1]
    even = cyclic[4] * pltpu.roll(both, 4, 1)
    for r in range(1, 4):
        even = even + cyclic[r] * (pltpu.roll(both, r, 1) + pltpu.roll(both, 8 - r, 1))
    odd = None
    for r, w in negacyclic.items():
        term = w * pltpu.roll(apart, r, 1)
        odd = term if odd is None else odd + term
    diag = (-1.5 * center_weight - (upper_edge + lower_edge) / 2.0) * scale
    results = []
    for at, rows in enumerate((even + odd, even - odd)):
        result = (pot[:, at] * scale + diag) * mid[:, at]
        result = result + (-0.5 * scale) * (total[:, at] + rows)
        if before is not None:
            result = result - weight * before[:, at]
        results.append(result)
    return results


def filter_kernel(
    bands, doms, orb, pot, sub, recv, rows, p0, p1, p2, out, pot_v,
    near_send, near_recv, far_send, far_recv, pot_send, pot_recv,
    move_sem, all_send, all_recv, row_send, row_recv,
):
    orbs, planes = orb.shape[0], orb.shape[1]
    band, dom = lax.axis_index("band"), lax.axis_index("dom")
    core, half = lax.rem(dom, 2), lax.div(dom, 2)
    side = 4
    zl, y, x = lax.div(band, side * side), lax.rem(lax.div(band, side), side), lax.rem(band, side)
    sibling = {"dom": dom + 1 - 2 * core}
    across = {"dom": 2 * (1 - half) + 1 - core}
    scalars = filter_scalars(DEG)
    buffers = (p0, p1, p2)
    rims = tuple(REACH * (DEG - level) for level in range(DEG + 1))
    deep, pot_rim = rims[0], rims[1]
    step = 4

    load = pltpu.make_async_copy(orb, p0.at[:, pl.ds(deep, planes)], move_sem.at[0])
    load.start()
    load_pot = pltpu.make_async_copy(pot, pot_v.at[pl.ds(pot_rim, planes)], move_sem.at[1])
    load_pot.start()

    along_z = [lax.rem(zl + d, side) * side * side for d in range(side)]
    along_y = [lax.rem(y + d, side) * side for d in range(side)]
    along_x = [lax.rem(x + d, side) for d in range(side)]
    others = [
        along_z[dz] + along_y[dy] + along_x[dx]
        for dx in range(side)
        for dy in range(side)
        for dz in range(side)
    ][1:]

    barrier = pltpu.get_barrier_semaphore()
    for peer in (sibling, across):
        pl.semaphore_signal(barrier, inc=1, device_id=peer, device_id_type=MESH)

    for peer in others:
        pl.semaphore_signal(barrier, inc=1, device_id={"band": peer}, device_id_type=MESH)
    lanes = lane_matrix()
    cyclic, negacyclic = row_weights()
    pl.semaphore_wait(barrier, bands + 1)

    def remote(src, dst, send_sem, recv_sem, peer):
        return pltpu.make_async_remote_copy(
            src_ref=src, dst_ref=dst, send_sem=send_sem, recv_sem=recv_sem,
            device_id=peer, device_id_type=MESH,
        )

    def rim_copies(src, dst, width, sems_near, sems_far):
        inner = planes - width
        near = remote(
            src.at[pl.ds((1 - core) * inner, width)],
            dst.at[pl.ds(core * (planes + width), width)], *sems_near, sibling,
        )
        far = remote(
            src.at[pl.ds(core * inner, width)],
            dst.at[pl.ds((1 - core) * (planes + width), width)], *sems_far, across,
        )
        return near, far

    part = pot_rim // side
    pot_far = remote(
        pot.at[pl.ds(core * (planes - pot_rim) + x * part, part)],
        pot_v.at[pl.ds((1 - core) * (planes + pot_rim) + x * part, part)],
        pot_send.at[0], pot_recv.at[0], across,
    )
    pot_near = remote(
        pot.at[pl.ds((1 - core) * (planes - pot_rim), pot_rim)],
        pot_v.at[pl.ds(core * (planes + pot_rim), pot_rim)],
        pot_send.at[1], pot_recv.at[1], sibling,
    )
    pot_far.start()
    pot_near.start()
    nears, fars = [], []
    for o in range(orbs):
        near, far = rim_copies(
            orb.at[o], p0.at[o], deep,
            (near_send.at[o], near_recv.at[o]), (far_send.at[o], far_recv.at[o]),
        )
        far.start()
        near.start()
        nears.append(near)
        fars.append(far)

    own_rows = pltpu.make_async_copy(sub, rows.at[zl, y, x], move_sem.at[2])
    own_rows.start()
    lines = [
        (rows.at[zl, y, x], [along_z[d] + along_y[0] + along_x[0] for d in range(1, side)]),
        (rows.at[:, y, x], [along_z[0] + along_y[d] + along_x[0] for d in range(1, side)]),
        (rows.at[:, :, x], [along_z[0] + along_y[0] + along_x[d] for d in range(1, side)]),
    ]

    def send_rows(stage):
        mine, peers = lines[stage]
        copies = [
            remote(mine, mine, row_send.at[stage, at], row_recv.at[stage, at], {"band": peer})
            for at, peer in enumerate(peers)
        ]
        for copy in copies:
            copy.start()
        return copies

    own_rows.wait()
    row_copies = [send_rows(0)]


    def apply(level, o, begin, blocks):
        scale, weight = scalars[level]

        def body(i, c):
            at = begin + i * step
            before = None
            if level > 0:
                before = buffers[level - 1][o, pl.ds(at + rims[level - 1], step)]
            window = buffers[level][o, pl.ds(at + rims[level] - REACH, step + 2 * REACH)]
            low, high = filtered_block(
                window, pot_v[pl.ds(at + pot_rim, step)], before, scale, weight,
                lanes, cyclic, negacyclic,
            )
            if level < DEG - 1:
                buffers[level + 1][o, pl.ds(at + rims[level + 1], step), 0] = low
                buffers[level + 1][o, pl.ds(at + rims[level + 1], step), 1] = high
            else:
                pairs = jnp.stack([low, high], axis=1)
                out[pl.ds(2 * at, 2 * step), o] = pairs.reshape(2 * step, 8, 128)
            return c

        lax.fori_loop(0, blocks, body, 0)

    early = [(planes + 2 * rims[level + 1] - 20) // step for level in range(DEG)]
    load.wait()
    load_pot.wait()
    pot_near.wait_recv()
    for o in range(orbs):
        nears[o].wait_recv()
        for level in range(DEG):
            rim = rims[level + 1]
            apply(level, o, core * -rim + (1 - core) * (20 - rim), early[level])

    for copy in row_copies[0]:
        copy.wait_recv()
    row_copies.append(send_rows(1))
    pot_far.wait_recv()
    at_far = (planes + pot_rim) * core + x * part
    passed = []
    for d in range(1, side):
        mine = pot_v.at[pl.ds(at_far, part)]
        peer = {"band": band - x + lax.rem(x + d, side)}
        copy = remote(mine, mine, pot_send.at[1 + d], pot_recv.at[1 + d], peer)
        copy.start()
        passed.append(copy)
    for copy in row_copies[1]:
        copy.wait_recv()
    row_copies.append(send_rows(2))
    for copy in passed:
        copy.wait_recv()

    for o in range(orbs):
        fars[o].wait_recv()
        for level in range(DEG):
            rim = rims[level + 1]
            apply(level, o, core * (planes + rim - 20) - (1 - core) * rim, 20 // step)

    for peer in others:
        remote(out.at[peer], recv.at[band], all_send, all_recv, {"band": peer}).start()
    own = pltpu.make_async_copy(out.at[band], recv.at[band], move_sem.at[3])
    own.start()

    for copy in (*nears, *fars, pot_far, pot_near, *passed):
        copy.wait_send()
    for stage in row_copies:
        for copy in stage:
            copy.wait_send()
    for copy in row_copies[2]:
        copy.wait_recv()
    own.wait()
    whole = recv.at[pl.ds(0, bands - 1)]
    pltpu.make_async_copy(whole, whole, all_send).wait()
    pltpu.make_async_copy(whole, whole, all_recv).wait()


def rotate_kernel(recv_v, rows_v, out, out_v, sems):
    high, low = two_parts(jnp.concatenate([rows_v[:, 0], rows_v[:, 1]], axis=0).T)
    matrix = jnp.concatenate([high, high, low], axis=1)
    width = 256
    stores = []
    for at in range(0, 8 * 128, width):
        columns = []
        for r in range(at // 128, (at + width) // 128):
            values = jnp.concatenate([recv_v[:, 0, r], recv_v[:, 1, r]], axis=0)
            high, low = two_parts(values)
            columns.append(jnp.concatenate([high, low, high], axis=0))
        out_v[:, pl.ds(at, width)] = jnp.dot(
            matrix, jnp.concatenate(columns, axis=1), preferred_element_type=jnp.float32
        )
        store = pltpu.make_async_copy(
            out_v.at[:, pl.ds(at, width)], out.at[:, pl.ds(at, width)], sems.at[at // width]
        )
        store.start()
        stores.append(store)
    for store in stores:
        store.wait()


def per_device(bands, doms, orbitals, potential, subspace):
    orbs, planes = orbitals.shape[0], orbitals.shape[1]
    orb = orbitals.reshape(orbs, planes, 2, 8, 128)
    pot = potential.reshape(planes, 2, 8, 128)
    f32 = jnp.float32
    dma = pltpu.SemaphoreType.DMA
    anywhere = pl.BlockSpec(memory_space=pl.ANY)
    recv, rows = pl.pallas_call(
        functools.partial(filter_kernel, bands, doms),
        out_shape=(
            pltpu.VMEM((bands, orbs, 8, 128), f32),
            pltpu.VMEM((4, 4, 4, orbs, 128), f32),
        ),
        in_specs=[anywhere] * 3,
        out_specs=(anywhere,) * 2,
        scratch_shapes=[
            *[
                pltpu.VMEM((orbs, planes + 2 * REACH * (DEG - level), 2, 8, 128), f32)
                for level in range(DEG)
            ],
            pltpu.VMEM((bands, orbs, 8, 128), f32),
            pltpu.VMEM((planes + 2 * REACH * (DEG - 1), 2, 8, 128), f32),
            dma((orbs,)),
            dma((orbs,)),
            dma((orbs,)),
            dma((orbs,)),
            dma((5,)),
            dma((5,)),
            dma((4,)),
            dma,
            dma,
            dma((3, 3)),
            dma((3, 3)),
        ],
        compiler_params=pltpu.CompilerParams(
            collective_id=0, has_side_effects=True, vmem_limit_bytes=32 * 2**20
        ),
        name="filter",
    )(*(pltpu.with_memory_space_constraint(a, pltpu.HBM) for a in (orb, pot, subspace)))
    return pl.pallas_call(
        rotate_kernel,
        out_shape=jax.ShapeDtypeStruct((bands * orbs, 1024), f32),
        in_specs=[pl.BlockSpec(memory_space=pltpu.VMEM)] * 2,
        out_specs=anywhere,
        scratch_shapes=[pltpu.VMEM((bands * orbs, 1024), f32), dma((4,))],
        compiler_params=pltpu.CompilerParams(vmem_limit_bytes=32 * 2**20),
        name="rotate",
    )(*(pltpu.with_memory_space_constraint(a, pltpu.VMEM) for a in (recv, rows.reshape(bands, orbs, 128))))


def solution(mesh):
    in_specs = (P("band", "dom", None, None), P("dom", None, None), P("band", None))
    out_specs = P(None, ("dom", "band"))
    return jax.shard_map(
        functools.partial(per_device, mesh.shape["band"], mesh.shape["dom"]),
        mesh=mesh,
        in_specs=in_specs,
        out_specs=out_specs,
        check_vma=False,
    )
```

```python
import functools
import math

import jax
import jax.numpy as jnp
from jax import lax
from jax.experimental import pallas as pl
from jax.experimental.pallas import tpu as pltpu
from jax.sharding import PartitionSpec as P

DEG = 3
REACH = 6
MESH = pl.DeviceIdType.MESH

upper_edge = 10.7
lower_edge = 1.5
bottom_edge = -1.0


def stencil_weights():
    factor_square = math.factorial(6) ** 2
    side_weights = []
    for offset in range(1, 7):
        side_weights.append(
            2.0
            * (-1.0) ** (offset + 1)
            * factor_square
            / (offset * offset * math.factorial(6 - offset) * math.factorial(6 + offset))
        )
    center_weight = -2.0 * sum(side_weights)
    return (center_weight, side_weights)


def filter_scalars(pass_count):
    half_width = (upper_edge - lower_edge) / 2.0
    sigma_now = half_width / (bottom_edge - (upper_edge + lower_edge) / 2.0)
    gamma_value = 2.0 / sigma_now
    scalars = [(sigma_now / half_width, 0.0)]
    for pass_index in range(pass_count - 1):
        sigma_next = 1.0 / (gamma_value - sigma_now)
        scalars.append((2.0 * sigma_next / half_width, sigma_now * sigma_next))
        sigma_now = sigma_next
    return scalars


def two_parts(values):
    high = values.astype(jnp.bfloat16)
    return high, (values - high.astype(jnp.float32)).astype(jnp.bfloat16)


def lane_matrix():
    rows = lax.broadcasted_iota(jnp.int32, (128, 128), 0)
    columns = lax.broadcasted_iota(jnp.int32, (128, 128), 1)
    apart = jnp.abs(rows - columns)
    apart = jnp.minimum(apart, 128 - apart)
    matrix = jnp.zeros((128, 128), jnp.float32)
    for k, w in enumerate(stencil_weights()[1], 1):
        matrix = jnp.where(apart == k, jnp.float32(w), matrix)
    high, low = two_parts(matrix)
    return jnp.concatenate([high, high, low], axis=0)


def row_weights():
    side = stencil_weights()[1]
    weight = lambda k: side[k - 1] if 1 <= k <= REACH else 0.0
    rows = lax.broadcasted_iota(jnp.int32, (8, 128), 0)
    cyclic, negacyclic = {}, {}
    for r in range(1, 8):
        cyclic[r] = 0.5 * (weight(r) + weight(8 - r))
        if r != 4:
            w = 0.5 * (weight(r) - weight(8 - r))
            negacyclic[r] = jnp.where(rows >= r, jnp.float32(w), jnp.float32(-w))
    return cyclic, negacyclic


def filtered_block(window, pot, before, scale, weight, lanes, cyclic, negacyclic):
    center_weight, side = stencil_weights()
    n = window.shape[0] - 2 * REACH
    mid = window[REACH : REACH + n]
    high, low = two_parts(mid.reshape(n * 16, 128))
    total = jnp.dot(
        jnp.concatenate([high, low, high], axis=1), lanes, preferred_element_type=jnp.float32
    ).reshape(n, 2, 8, 128)
    for k in range(1, REACH + 1):
        beside = window[REACH + k : REACH + k + n] + window[REACH - k : REACH - k + n]
        total = total + side[k - 1] * beside
    both, apart = mid[:, 0] + mid[:, 1], mid[:, 0] - mid[:, 1]
    even = cyclic[4] * pltpu.roll(both, 4, 1)
    for r in range(1, 4):
        even = even + cyclic[r] * (pltpu.roll(both, r, 1) + pltpu.roll(both, 8 - r, 1))
    odd = None
    for r, w in negacyclic.items():
        term = w * pltpu.roll(apart, r, 1)
        odd = term if odd is None else odd + term
    diag = (-1.5 * center_weight - (upper_edge + lower_edge) / 2.0) * scale
    results = []
    for at, rows in enumerate((even + odd, even - odd)):
        result = (pot[:, at] * scale + diag) * mid[:, at]
        result = result + (-0.5 * scale) * (total[:, at] + rows)
        if before is not None:
            result = result - weight * before[:, at]
        results.append(result)
    return results


def filter_kernel(
    bands, doms, orb, pot, sub, recv, rows, p0, p1, p2, out, pot_v, held,
    near_send, near_recv, pass_send, pass_recv, far_send, far_recv, pot_send, pot_recv,
    move_sem, all_send, all_recv, row_send, row_recv,
):
    orbs, planes = orb.shape[0], orb.shape[1]
    band, dom = lax.axis_index("band"), lax.axis_index("dom")
    core, half = lax.rem(dom, 2), lax.div(dom, 2)
    side = 4
    zl, y, x = lax.div(band, side * side), lax.rem(lax.div(band, side), side), lax.rem(band, side)
    sibling = {"dom": dom + 1 - 2 * core}
    across = {"dom": 2 * (1 - half) + 1 - core}
    z = half * side + zl

    def chip_along(shift, core_there):
        there = lax.rem(z + shift + 2 * side, 2 * side)
        return {
            "band": lax.rem(there, side) * side * side + lax.rem(band, side * side),
            "dom": lax.div(there, side) * 2 + core_there,
        }

    hop = (2 * core - 1) * (side // 2)
    relay_to, relay_from = chip_along(hop, core), chip_along(-hop, core)
    onward_to = chip_along(hop, 1 - core)
    scalars = filter_scalars(DEG)
    buffers = (p0, p1, p2)
    rims = tuple(REACH * (DEG - level) for level in range(DEG + 1))
    deep, pot_rim = rims[0], rims[1]
    step = 4

    load = pltpu.make_async_copy(orb, p0.at[:, pl.ds(deep, planes)], move_sem.at[0])
    load.start()
    load_pot = pltpu.make_async_copy(pot, pot_v.at[pl.ds(pot_rim, planes)], move_sem.at[1])
    load_pot.start()

    along_z = [lax.rem(zl + d, side) * side * side for d in range(side)]
    along_y = [lax.rem(y + d, side) * side for d in range(side)]
    along_x = [lax.rem(x + d, side) for d in range(side)]
    others = [
        along_z[dz] + along_y[dy] + along_x[dx]
        for dx in range(side)
        for dy in range(side)
        for dz in range(side)
    ][1:]

    barrier = pltpu.get_barrier_semaphore()
    for peer in (sibling, across, relay_from, onward_to):
        pl.semaphore_signal(barrier, inc=1, device_id=peer, device_id_type=MESH)

    for peer in others:
        pl.semaphore_signal(barrier, inc=1, device_id={"band": peer}, device_id_type=MESH)
    lanes = lane_matrix()
    cyclic, negacyclic = row_weights()
    pl.semaphore_wait(barrier, bands + 3)

    def remote(src, dst, send_sem, recv_sem, peer):
        return pltpu.make_async_remote_copy(
            src_ref=src, dst_ref=dst, send_sem=send_sem, recv_sem=recv_sem,
            device_id=peer, device_id_type=MESH,
        )

    part = pot_rim // side
    pot_far = remote(
        pot.at[pl.ds(core * (planes - pot_rim) + x * part, part)],
        pot_v.at[pl.ds((1 - core) * (planes + pot_rim) + x * part, part)],
        pot_send.at[0], pot_recv.at[0], across,
    )
    pot_near = remote(
        pot.at[pl.ds((1 - core) * (planes - pot_rim), pot_rim)],
        pot_v.at[pl.ds(core * (planes + pot_rim), pot_rim)],
        pot_send.at[1], pot_recv.at[1], sibling,
    )
    pot_far.start()
    pot_near.start()
    inner = planes - deep
    nears, firsts, seconds = [], [], []
    for o in range(orbs):
        near = remote(
            orb.at[o, pl.ds((1 - core) * inner, deep)],
            p0.at[o, pl.ds(core * (planes + deep), deep)],
            near_send.at[o], near_recv.at[o], sibling,
        )
        for piece in range(DEG):
            at = piece * REACH
            first = remote(
                orb.at[o, pl.ds(core * inner + at, REACH)], held.at[o, piece],
                pass_send.at[o, piece], pass_recv.at[o, piece], relay_to,
            )
            second = remote(
                held.at[o, piece],
                p0.at[o, pl.ds((1 - core) * (planes + deep) + at, REACH)],
                far_send.at[o, piece], far_recv.at[o, piece], onward_to,
            )
            first.start()
            firsts.append(first)
            seconds.append(second)
        near.start()
        nears.append(near)

    own_rows = pltpu.make_async_copy(sub, rows.at[band], move_sem.at[2])
    own_rows.start()

    for peer in others:
        remote(sub, rows.at[band], row_send, row_recv, {"band": peer}).start()

    def apply(level, o, begin, blocks):
        scale, weight = scalars[level]

        def body(i, c):
            at = begin + i * step
            before = None
            if level > 0:
                before = buffers[level - 1][o, pl.ds(at + rims[level - 1], step)]
            window = buffers[level][o, pl.ds(at + rims[level] - REACH, step + 2 * REACH)]
            low, high = filtered_block(
                window, pot_v[pl.ds(at + pot_rim, step)], before, scale, weight,
                lanes, cyclic, negacyclic,
            )
            if level < DEG - 1:
                buffers[level + 1][o, pl.ds(at + rims[level + 1], step), 0] = low
                buffers[level + 1][o, pl.ds(at + rims[level + 1], step), 1] = high
            else:
                pairs = jnp.stack([low, high], axis=1)
                out[o, pl.ds(2 * at, 2 * step)] = pairs.reshape(2 * step, 8, 128)
            return c

        lax.fori_loop(0, blocks, body, 0)

    early = [(planes + 2 * rims[level + 1] - 20) // step for level in range(DEG)]
    load.wait()
    load_pot.wait()
    pot_near.wait_recv()
    for o in range(orbs):
        nears[o].wait_recv()
        for level in range(DEG):
            firsts[o * DEG + level].wait_recv()
            seconds[o * DEG + level].start()
            rim = rims[level + 1]
            apply(level, o, core * -rim + (1 - core) * (20 - rim), early[level])

    pot_far.wait_recv()
    at_far = (planes + pot_rim) * core + x * part
    passed = []
    for d in range(1, side):
        mine = pot_v.at[pl.ds(at_far, part)]
        peer = {"band": band - x + lax.rem(x + d, side)}
        copy = remote(mine, mine, pot_send.at[1 + d], pot_recv.at[1 + d], peer)
        copy.start()
        passed.append(copy)
    for copy in passed:
        copy.wait_recv()

    def spread(o):
        own = pltpu.make_async_copy(
            out.at[o, band], recv.at[band, o], move_sem.at[3 + o]
        )
        own.start()

        for peer in others:
            remote(
                out.at[o, peer], recv.at[band, o], all_send, all_recv, {"band": peer}
            ).start()
        return own

    owns = []
    for o in range(orbs):
        for second in seconds[o * DEG : (o + 1) * DEG]:
            second.wait_recv()
        for level in range(DEG):
            rim = rims[level + 1]
            apply(level, o, core * (planes + rim - 20) - (1 - core) * rim, 20 // step)
        owns.append(spread(o))

    for copy in (*nears, *firsts, *seconds, pot_far, pot_near, *passed):
        copy.wait_send()
    own_rows.wait()
    for own in owns:
        own.wait()
    for ref, sem_a, sem_b in ((rows, row_send, row_recv), (recv, all_send, all_recv)):
        whole = ref.at[pl.ds(0, bands - 1)]
        pltpu.make_async_copy(whole, whole, sem_a).wait()
        pltpu.make_async_copy(whole, whole, sem_b).wait()


def rotate_kernel(recv_v, rows_v, out, out_v, sems):
    high, low = two_parts(jnp.concatenate([rows_v[:, 0], rows_v[:, 1]], axis=0).T)
    matrix = jnp.concatenate([high, high, low], axis=1)
    width = 256
    stores = []
    for at in range(0, 8 * 128, width):
        columns = []
        for r in range(at // 128, (at + width) // 128):
            values = jnp.concatenate([recv_v[:, 0, r], recv_v[:, 1, r]], axis=0)
            high, low = two_parts(values)
            columns.append(jnp.concatenate([high, low, high], axis=0))
        out_v[:, pl.ds(at, width)] = jnp.dot(
            matrix, jnp.concatenate(columns, axis=1), preferred_element_type=jnp.float32
        )
        store = pltpu.make_async_copy(
            out_v.at[:, pl.ds(at, width)], out.at[:, pl.ds(at, width)], sems.at[at // width]
        )
        store.start()
        stores.append(store)
    for store in stores:
        store.wait()


def per_device(bands, doms, orbitals, potential, subspace):
    orbs, planes = orbitals.shape[0], orbitals.shape[1]
    orb = orbitals.reshape(orbs, planes, 2, 8, 128)
    pot = potential.reshape(planes, 2, 8, 128)
    f32 = jnp.float32
    dma = pltpu.SemaphoreType.DMA
    anywhere = pl.BlockSpec(memory_space=pl.ANY)
    recv, rows = pl.pallas_call(
        functools.partial(filter_kernel, bands, doms),
        out_shape=(
            pltpu.VMEM((bands, orbs, 8, 128), f32),
            pltpu.VMEM((bands, orbs, 128), f32),
        ),
        in_specs=[anywhere] * 3,
        out_specs=(anywhere,) * 2,
        scratch_shapes=[
            *[
                pltpu.VMEM((orbs, planes + 2 * REACH * (DEG - level), 2, 8, 128), f32)
                for level in range(DEG)
            ],
            pltpu.VMEM((orbs, bands, 8, 128), f32),
            pltpu.VMEM((planes + 2 * REACH * (DEG - 1), 2, 8, 128), f32),
            pltpu.VMEM((orbs, DEG, REACH, 2, 8, 128), f32),
            dma((orbs,)),
            dma((orbs,)),
            dma((orbs, DEG)),
            dma((orbs, DEG)),
            dma((orbs, DEG)),
            dma((orbs, DEG)),
            dma((5,)),
            dma((5,)),
            dma((3 + orbs,)),
            dma,
            dma,
            dma,
            dma,
        ],
        compiler_params=pltpu.CompilerParams(
            collective_id=0, has_side_effects=True, vmem_limit_bytes=32 * 2**20
        ),
        name="filter",
    )(*(pltpu.with_memory_space_constraint(a, pltpu.HBM) for a in (orb, pot, subspace)))
    return pl.pallas_call(
        rotate_kernel,
        out_shape=jax.ShapeDtypeStruct((bands * orbs, 1024), f32),
        in_specs=[pl.BlockSpec(memory_space=pltpu.VMEM)] * 2,
        out_specs=anywhere,
        scratch_shapes=[pltpu.VMEM((bands * orbs, 1024), f32), dma((4,))],
        compiler_params=pltpu.CompilerParams(vmem_limit_bytes=32 * 2**20),
        name="rotate",
    )(*(pltpu.with_memory_space_constraint(a, pltpu.VMEM) for a in (recv, rows)))


def solution(mesh):
    in_specs = (P("band", "dom", None, None), P("dom", None, None), P("band", None))
    out_specs = P(None, ("dom", "band"))
    return jax.shard_map(
        functools.partial(per_device, mesh.shape["band"], mesh.shape["dom"]),
        mesh=mesh,
        in_specs=in_specs,
        out_specs=out_specs,
        check_vma=False,
    )
```

```python
import functools
import math

import jax
import jax.numpy as jnp
from jax import lax
from jax.experimental import pallas as pl
from jax.experimental.pallas import tpu as pltpu
from jax.sharding import PartitionSpec as P

DEG = 3
REACH = 6
MESH = pl.DeviceIdType.MESH

upper_edge = 10.7
lower_edge = 1.5
bottom_edge = -1.0


def stencil_weights():
    factor_square = math.factorial(6) ** 2
    side_weights = []
    for offset in range(1, 7):
        side_weights.append(
            2.0
            * (-1.0) ** (offset + 1)
            * factor_square
            / (offset * offset * math.factorial(6 - offset) * math.factorial(6 + offset))
        )
    center_weight = -2.0 * sum(side_weights)
    return (center_weight, side_weights)


def filter_scalars(pass_count):
    half_width = (upper_edge - lower_edge) / 2.0
    sigma_now = half_width / (bottom_edge - (upper_edge + lower_edge) / 2.0)
    gamma_value = 2.0 / sigma_now
    scalars = [(sigma_now / half_width, 0.0)]
    for pass_index in range(pass_count - 1):
        sigma_next = 1.0 / (gamma_value - sigma_now)
        scalars.append((2.0 * sigma_next / half_width, sigma_now * sigma_next))
        sigma_now = sigma_next
    return scalars


def two_parts(values):
    high = values.astype(jnp.bfloat16)
    return high, (values - high.astype(jnp.float32)).astype(jnp.bfloat16)


def lane_matrix():
    rows = lax.broadcasted_iota(jnp.int32, (128, 128), 0)
    columns = lax.broadcasted_iota(jnp.int32, (128, 128), 1)
    apart = jnp.abs(rows - columns)
    apart = jnp.minimum(apart, 128 - apart)
    matrix = jnp.zeros((128, 128), jnp.float32)
    for k, w in enumerate(stencil_weights()[1], 1):
        matrix = jnp.where(apart == k, jnp.float32(w), matrix)
    high, low = two_parts(matrix)
    return jnp.concatenate([high, high, low], axis=0)


def row_weights():
    side = stencil_weights()[1]
    weight = lambda k: side[k - 1] if 1 <= k <= REACH else 0.0
    rows = lax.broadcasted_iota(jnp.int32, (8, 128), 0)
    cyclic, negacyclic = {}, {}
    for r in range(1, 8):
        cyclic[r] = 0.5 * (weight(r) + weight(8 - r))
        if r != 4:
            w = 0.5 * (weight(r) - weight(8 - r))
            negacyclic[r] = jnp.where(rows >= r, jnp.float32(w), jnp.float32(-w))
    return cyclic, negacyclic


def filtered_block(window, pot, before, scale, weight, lanes, cyclic, negacyclic):
    center_weight, side = stencil_weights()
    n = window.shape[0] - 2 * REACH
    mid = window[REACH : REACH + n]
    high, low = two_parts(mid.reshape(n * 16, 128))
    total = jnp.dot(
        jnp.concatenate([high, low, high], axis=1), lanes, preferred_element_type=jnp.float32
    ).reshape(n, 2, 8, 128)
    for k in range(1, REACH + 1):
        beside = window[REACH + k : REACH + k + n] + window[REACH - k : REACH - k + n]
        total = total + side[k - 1] * beside
    both, apart = mid[:, 0] + mid[:, 1], mid[:, 0] - mid[:, 1]
    even = cyclic[4] * pltpu.roll(both, 4, 1)
    for r in range(1, 4):
        even = even + cyclic[r] * (pltpu.roll(both, r, 1) + pltpu.roll(both, 8 - r, 1))
    odd = None
    for r, w in negacyclic.items():
        term = w * pltpu.roll(apart, r, 1)
        odd = term if odd is None else odd + term
    diag = (-1.5 * center_weight - (upper_edge + lower_edge) / 2.0) * scale
    results = []
    for at, rows in enumerate((even + odd, even - odd)):
        result = (pot[:, at] * scale + diag) * mid[:, at]
        result = result + (-0.5 * scale) * (total[:, at] + rows)
        if before is not None:
            result = result - weight * before[:, at]
        results.append(result)
    return results


def filter_kernel(
    bands, orb, pot, sub, recv, rows, p0, p1, p2, out, pot_v,
    near_send, near_recv, far_send, far_recv, pot_send, pot_recv, pass_send, pass_recv,
    move_sem, all_send, all_recv, row_send, row_recv,
):
    quarter = orb.shape[1]
    slab, whole = 2 * quarter, 4 * quarter
    band, dom = lax.axis_index("band"), lax.axis_index("dom")
    core, half = lax.rem(dom, 2), lax.div(dom, 2)
    side = 4
    floor = side * side
    zl, x, yx = lax.div(band, floor), lax.rem(band, side), lax.rem(band, floor)
    shift = 2 * REACH
    left = jnp.where(zl < side // 2, 1, 0)
    long = core == left
    base = half * slab
    own_tile = dom * bands + band
    own_plane = lax.div(own_tile, 2)
    scalars = filter_scalars(DEG)
    buffers = (p0, p1, p2)
    rims = tuple(shift + REACH * (DEG - level) for level in range(DEG + 1))
    pot_rim = rims[1]
    step = 4

    def placed(u, count):
        return jnp.where(left == 1, u, slab - count - u)

    load = pltpu.make_async_copy(
        orb.at[core], p0.at[pl.ds(core * quarter + rims[0], quarter)], move_sem.at[0]
    )
    load.start()
    load_pot = pltpu.make_async_copy(
        pot, pot_v.at[pl.ds(core * quarter + pot_rim, quarter)], move_sem.at[1]
    )
    load_pot.start()

    sibling = {"dom": dom + 1 - 2 * core}
    partners = [{"dom": 2 * (1 - half) + k} for k in range(2)]

    barrier = pltpu.get_barrier_semaphore()
    for peer in partners:
        pl.semaphore_signal(barrier, inc=1, device_id=peer, device_id_type=MESH)
    in_left = (own_plane >= slab - shift) & (own_plane < whole - shift)
    in_right = (own_plane >= slab + shift) | (own_plane < shift)
    for line in range(side):
        there = jnp.where(in_left if line < side // 2 else in_right, 2, 0)
        for k in range(2):

            def greet(i, c, line=line, k=k, there=there):
                peer = line * floor + lax.rem(yx + i, floor)

                @pl.when((peer != band) | (there + k != dom))
                def _():
                    pl.semaphore_signal(
                        barrier, inc=1, device_id={"band": peer, "dom": there + k},
                        device_id_type=MESH,
                    )

                return c

            lax.fori_loop(0, floor, greet, 0)
    lanes = lane_matrix()
    cyclic, negacyclic = row_weights()
    pl.semaphore_wait(barrier, 2 * bands + 1)

    def remote(src, dst, send_sem, recv_sem, peer):
        return pltpu.make_async_remote_copy(
            src_ref=src, dst_ref=dst, send_sem=send_sem, recv_sem=recv_sem,
            device_id=peer, device_id_type=MESH,
        )

    pieces = [(0, REACH)] + [(REACH + 8 * i, 8) for i in range(3)]
    assert sum(n for _, n in pieces) == rims[0]
    far = []
    for o in range(2):
        group = []
        for at, (a, n) in enumerate(pieces):
            group.append(
                remote(
                    orb.at[o, pl.ds(jnp.where(left == 1, quarter - a - n, a), n)],
                    p0.at[pl.ds(placed(-a - n, n) + rims[0], n)],
                    far_send.at[o, at], far_recv.at[at], partners[o],
                )
            )
        n = REACH
        group.append(
            remote(
                orb.at[o, pl.ds(jnp.where(left == 1, 0, quarter - n), n)],
                p0.at[pl.ds(placed(slab, n) + rims[0], n)],
                far_send.at[o, 4], far_recv.at[4], partners[o],
            )
        )
        far.append(group)
    part = pot_rim // 8
    pot_far = [
        remote(
            pot.at[pl.ds(jnp.where(left == 1, quarter - pot_rim, 0) + (2 * x + o) * part, part)],
            pot_v.at[pl.ds(placed(-pot_rim, pot_rim) + pot_rim + (2 * x + o) * part, part)],
            pot_send.at[o], pot_recv, partners[o],
        )
        for o in range(2)
    ]
    mine = pot_v.at[pl.ds(placed(-pot_rim, pot_rim) + pot_rim + (2 * x + core) * part, part)]

    @pl.when(long)
    def _():
        for o in range(2):
            pot_far[o].start()
        for o in range(2):
            far[o][0].start()

    @pl.when(jnp.logical_not(long))
    def _():
        for o in range(2):
            far[o][4].start()

    near = remote(
        orb.at[1 - core], p0.at[pl.ds(core * quarter + rims[0], quarter)],
        near_send.at[0], near_recv.at[0], sibling,
    )
    near_pot = remote(
        pot, pot_v.at[pl.ds(core * quarter + pot_rim, quarter)],
        near_send.at[1], near_recv.at[1], sibling,
    )
    near.start()
    near_pot.start()

    @pl.when(long)
    def _():
        for at in range(1, 4):
            for o in range(2):
                far[o][at].start()

    def send_rows(i, c):
        at = lax.rem(i + band, bands)
        plane = core * quarter + lax.div(at, 2)
        plane = jnp.where(
            left == 1,
            jnp.where(plane >= slab - shift, plane - slab, plane),
            jnp.where(plane < shift, plane + slab, plane),
        )
        tile = lax.rem(2 * (base + plane) + lax.rem(at, 2) + 2 * whole, 2 * whole)

        @pl.when(tile != own_tile)
        def _():
            peer = {"band": lax.rem(tile, bands), "dom": lax.div(tile, bands)}
            remote(sub, rows.at[band], row_send, row_recv, peer).start()

        return c

    lax.fori_loop(0, bands, send_rows, 0)
    own_rows = pltpu.make_async_copy(sub, rows.at[band], move_sem.at[2])
    own_rows.start()

    def apply(level, u, blocks):
        scale, weight = scalars[level]

        def body(i, c):
            at = placed(u + i * step, step)
            before = None
            if level > 0:
                before = buffers[level - 1][pl.ds(at + rims[level - 1], step)]
            window = buffers[level][pl.ds(at + rims[level] - REACH, step + 2 * REACH)]
            low, high = filtered_block(
                window, pot_v[pl.ds(at + pot_rim, step)], before, scale, weight,
                lanes, cyclic, negacyclic,
            )
            pairs = jnp.stack([low, high], axis=1)
            if level < DEG - 1:
                buffers[level + 1][pl.ds(at + rims[level + 1], step)] = pairs
            else:
                out[pl.ds(2 * (at + rims[DEG]), 2 * step)] = pairs.reshape(2 * step, 8, 128)
            return c

        lax.fori_loop(0, blocks, body, 0)

    row = 2 * band + core

    def spread(u, count):
        start = placed(u, count)
        tiles = 2 * count

        def send(i, c):
            at = lax.rem(i + yx * (tiles // floor), tiles)
            tile = lax.rem(2 * (base + start) + at + 2 * whole, 2 * whole)
            src = out.at[2 * (start + rims[DEG]) + at]

            @pl.when(tile != own_tile)
            def _():
                peer = {"band": lax.rem(tile, bands), "dom": lax.div(tile, bands)}
                remote(src, recv.at[row], all_send, all_recv, peer).start()

            @pl.when(tile == own_tile)
            def _():
                pltpu.make_async_copy(src, recv.at[row], move_sem.at[3]).start()

            return c

        lax.fori_loop(0, tiles, send, 0)

    def advance(u, blocks):
        for level in range(DEG):
            apply(level, u + level * REACH, blocks)
        spread(u + (DEG - 1) * REACH, blocks * step)

    load.wait()
    load_pot.wait()
    near.wait_recv()
    near_pot.wait_recv()
    apply(0, 8, 12)
    apply(1, 14, 9)
    apply(2, 20, 6)
    spread(20, 24)

    pot_far[0].wait_recv()
    passed = []
    for dx in range(side):
        for dk in range(2):
            if dx or dk:
                peer = {
                    "band": band - x + lax.rem(x + dx, side),
                    "dom": dom if dk == 0 else dom + 1 - 2 * core,
                }
                at = 2 * dx + dk - 1
                passed.append(remote(mine, mine, pass_send.at[at], pass_recv.at[at], peer))
    for copy in passed:
        copy.start()

    far[0][4].wait_recv()
    apply(0, slab - 8, 2)
    apply(1, slab - 14, 2)
    apply(2, slab - 20, 2)
    spread(slab - 20, 8)
    for at in range(4):
        if at == 1:
            for copy in passed:
                copy.wait_recv()
        far[0][at].wait_recv()
        advance(-8 * at, 2)

    @pl.when(long)
    def _():
        for o in range(2):
            pot_far[o].wait_send()
            for at in range(4):
                far[o][at].wait_send()

    @pl.when(jnp.logical_not(long))
    def _():
        for o in range(2):
            far[o][4].wait_send()

    for copy in (near, near_pot, *passed):
        copy.wait_send()
    own_rows.wait()
    pltpu.make_async_copy(out.at[0], recv.at[row], move_sem.at[3]).wait()
    for ref, sem_a, sem_b in ((rows, row_send, row_recv), (recv, all_send, all_recv)):
        all_but_own = ref.at[pl.ds(0, ref.shape[0] - 1)]
        pltpu.make_async_copy(all_but_own, all_but_own, sem_a).wait()
        pltpu.make_async_copy(all_but_own, all_but_own, sem_b).wait()


def rotate_kernel(recv_v, rows_v, out, out_v, sems):
    high, low = two_parts(jnp.concatenate([rows_v[:, 0], rows_v[:, 1]], axis=0).T)
    matrix = jnp.concatenate([high, high, low], axis=1)
    width = 256
    stores = []
    for at in range(0, 8 * 128, width):
        columns = []
        for r in range(at // 128, (at + width) // 128):
            values = jnp.concatenate([recv_v[:, 0, r], recv_v[:, 1, r]], axis=0)
            high, low = two_parts(values)
            columns.append(jnp.concatenate([high, low, high], axis=0))
        out_v[:, pl.ds(at, width)] = jnp.dot(
            matrix, jnp.concatenate(columns, axis=1), preferred_element_type=jnp.float32
        )
        store = pltpu.make_async_copy(
            out_v.at[:, pl.ds(at, width)], out.at[:, pl.ds(at, width)], sems.at[at // width]
        )
        store.start()
        stores.append(store)
    for store in stores:
        store.wait()


def per_device(bands, orbitals, potential, subspace):
    orbs, planes = orbitals.shape[0], orbitals.shape[1]
    orb = orbitals.reshape(orbs, planes, 2, 8, 128)
    pot = potential.reshape(planes, 2, 8, 128)
    f32 = jnp.float32
    dma = pltpu.SemaphoreType.DMA
    anywhere = pl.BlockSpec(memory_space=pl.ANY)
    slab, shift = 2 * planes, 2 * REACH
    recv, rows = pl.pallas_call(
        functools.partial(filter_kernel, bands),
        out_shape=(
            pltpu.VMEM((bands * orbs, 8, 128), f32),
            pltpu.VMEM((bands, orbs, 128), f32),
        ),
        in_specs=[anywhere] * 3,
        out_specs=(anywhere,) * 2,
        scratch_shapes=[
            *[
                pltpu.VMEM((slab + 2 * (shift + REACH * (DEG - level)), 2, 8, 128), f32)
                for level in range(DEG)
            ],
            pltpu.VMEM((2 * (slab + 2 * shift), 8, 128), f32),
            pltpu.VMEM((slab + 2 * (shift + REACH * (DEG - 1)), 2, 8, 128), f32),
            dma((2,)),
            dma((2,)),
            dma((2, 5)),
            dma((5,)),
            dma((2,)),
            dma,
            dma((7,)),
            dma((7,)),
            dma((4,)),
            dma,
            dma,
            dma,
            dma,
        ],
        compiler_params=pltpu.CompilerParams(
            collective_id=0, has_side_effects=True, vmem_limit_bytes=32 * 2**20
        ),
        name="filter",
    )(*(pltpu.with_memory_space_constraint(a, pltpu.HBM) for a in (orb, pot, subspace)))
    recv = recv.reshape(bands, orbs, 8, 128)
    return pl.pallas_call(
        rotate_kernel,
        out_shape=jax.ShapeDtypeStruct((bands * orbs, 1024), f32),
        in_specs=[pl.BlockSpec(memory_space=pltpu.VMEM)] * 2,
        out_specs=anywhere,
        scratch_shapes=[pltpu.VMEM((bands * orbs, 1024), f32), dma((4,))],
        compiler_params=pltpu.CompilerParams(vmem_limit_bytes=32 * 2**20),
        name="rotate",
    )(*(pltpu.with_memory_space_constraint(a, pltpu.VMEM) for a in (recv, rows)))


def solution(mesh):
    in_specs = (P("band", "dom", None, None), P("dom", None, None), P("band", None))
    out_specs = P(None, ("dom", "band"))
    return jax.shard_map(
        functools.partial(per_device, mesh.shape["band"]),
        mesh=mesh,
        in_specs=in_specs,
        out_specs=out_specs,
        check_vma=False,
    )
```

```python
import functools
import math

import jax
import jax.numpy as jnp
from jax import lax
from jax.experimental import pallas as pl
from jax.experimental.pallas import tpu as pltpu
from jax.sharding import PartitionSpec as P

DEG = 3
REACH = 6
MESH = pl.DeviceIdType.MESH

upper_edge = 10.7
lower_edge = 1.5
bottom_edge = -1.0


def stencil_weights():
    factor_square = math.factorial(6) ** 2
    side_weights = []
    for offset in range(1, 7):
        side_weights.append(
            2.0
            * (-1.0) ** (offset + 1)
            * factor_square
            / (offset * offset * math.factorial(6 - offset) * math.factorial(6 + offset))
        )
    center_weight = -2.0 * sum(side_weights)
    return (center_weight, side_weights)


def filter_scalars(pass_count):
    half_width = (upper_edge - lower_edge) / 2.0
    sigma_now = half_width / (bottom_edge - (upper_edge + lower_edge) / 2.0)
    gamma_value = 2.0 / sigma_now
    scalars = [(sigma_now / half_width, 0.0)]
    for pass_index in range(pass_count - 1):
        sigma_next = 1.0 / (gamma_value - sigma_now)
        scalars.append((2.0 * sigma_next / half_width, sigma_now * sigma_next))
        sigma_now = sigma_next
    return scalars


def two_parts(values):
    high = values.astype(jnp.bfloat16)
    return high, (values - high.astype(jnp.float32)).astype(jnp.bfloat16)


def lane_matrix():
    rows = lax.broadcasted_iota(jnp.int32, (128, 128), 0)
    columns = lax.broadcasted_iota(jnp.int32, (128, 128), 1)
    apart = jnp.abs(rows - columns)
    apart = jnp.minimum(apart, 128 - apart)
    matrix = jnp.zeros((128, 128), jnp.float32)
    for k, w in enumerate(stencil_weights()[1], 1):
        matrix = jnp.where(apart == k, jnp.float32(w), matrix)
    high, low = two_parts(matrix)
    return jnp.concatenate([high, high, low], axis=0)


def row_weights():
    side = stencil_weights()[1]
    weight = lambda k: side[k - 1] if 1 <= k <= REACH else 0.0
    rows = lax.broadcasted_iota(jnp.int32, (8, 128), 0)
    cyclic, negacyclic = {}, {}
    for r in range(1, 8):
        cyclic[r] = 0.5 * (weight(r) + weight(8 - r))
        if r != 4:
            w = 0.5 * (weight(r) - weight(8 - r))
            negacyclic[r] = jnp.where(rows >= r, jnp.float32(w), jnp.float32(-w))
    return cyclic, negacyclic


def filtered_block(window, pot, before, scale, weight, lanes, cyclic, negacyclic):
    center_weight, side = stencil_weights()
    n = window.shape[0] - 2 * REACH
    mid = window[REACH : REACH + n]
    high, low = two_parts(mid.reshape(n * 16, 128))
    total = jnp.dot(
        jnp.concatenate([high, low, high], axis=1), lanes, preferred_element_type=jnp.float32
    ).reshape(n, 2, 8, 128)
    for k in range(1, REACH + 1):
        beside = window[REACH + k : REACH + k + n] + window[REACH - k : REACH - k + n]
        total = total + side[k - 1] * beside
    both, apart = mid[:, 0] + mid[:, 1], mid[:, 0] - mid[:, 1]
    even = cyclic[4] * pltpu.roll(both, 4, 1)
    for r in range(1, 4):
        even = even + cyclic[r] * (pltpu.roll(both, r, 1) + pltpu.roll(both, 8 - r, 1))
    odd = None
    for r, w in negacyclic.items():
        term = w * pltpu.roll(apart, r, 1)
        odd = term if odd is None else odd + term
    diag = (-1.5 * center_weight - (upper_edge + lower_edge) / 2.0) * scale
    results = []
    for at, rows in enumerate((even + odd, even - odd)):
        result = (pot[:, at] * scale + diag) * mid[:, at]
        result = result + (-0.5 * scale) * (total[:, at] + rows)
        if before is not None:
            result = result - weight * before[:, at]
        results.append(result)
    return results


def filter_kernel(
    bands, orb, pot, sub, recv, rows, p0, p1, p2, out, pot_v,
    near_send, near_recv, far_send, far_recv, pot_send, pot_recv, pass_send, pass_recv,
    move_sem, all_send, all_recv, row_send, row_recv,
):
    quarter = orb.shape[1]
    slab, whole = 2 * quarter, 4 * quarter
    band, dom = lax.axis_index("band"), lax.axis_index("dom")
    core, half = lax.rem(dom, 2), lax.div(dom, 2)
    side = 4
    floor = side * side
    zl, x, yx = lax.div(band, floor), lax.rem(band, side), lax.rem(band, floor)
    shift = 2 * REACH
    left = jnp.where(zl < side // 2, 1, 0)
    long = core == left
    base = half * slab
    own_tile = dom * bands + band
    own_plane = lax.div(own_tile, 2)
    scalars = filter_scalars(DEG)
    buffers = (p0, p1, p2)
    rims = tuple(shift + REACH * (DEG - level) for level in range(DEG + 1))
    pot_rim = rims[1]

    def placed(u, count):
        return jnp.where(left == 1, u, slab - count - u)

    load = pltpu.make_async_copy(
        orb.at[core], p0.at[pl.ds(core * quarter + rims[0], quarter)], move_sem.at[0]
    )
    load.start()
    load_pot = pltpu.make_async_copy(
        pot, pot_v.at[pl.ds(core * quarter + pot_rim, quarter)], move_sem.at[1]
    )
    load_pot.start()

    sibling = {"dom": dom + 1 - 2 * core}
    partners = [{"dom": 2 * (1 - half) + k} for k in range(2)]

    barrier = pltpu.get_barrier_semaphore()
    for peer in partners:
        pl.semaphore_signal(barrier, inc=1, device_id=peer, device_id_type=MESH)
    in_left = (own_plane >= slab - shift) & (own_plane < whole - shift)
    in_right = (own_plane >= slab + shift) | (own_plane < shift)
    for line in range(side):
        there = jnp.where(in_left if line < side // 2 else in_right, 2, 0)
        for k in range(2):

            def greet(i, c, line=line, k=k, there=there):
                peer = line * floor + lax.rem(yx + i, floor)

                @pl.when((peer != band) | (there + k != dom))
                def _():
                    pl.semaphore_signal(
                        barrier, inc=1, device_id={"band": peer, "dom": there + k},
                        device_id_type=MESH,
                    )

                return c

            lax.fori_loop(0, floor, greet, 0)
    lanes = lane_matrix()
    cyclic, negacyclic = row_weights()
    pl.semaphore_wait(barrier, 2 * bands + 1)

    def remote(src, dst, send_sem, recv_sem, peer):
        return pltpu.make_async_remote_copy(
            src_ref=src, dst_ref=dst, send_sem=send_sem, recv_sem=recv_sem,
            device_id=peer, device_id_type=MESH,
        )

    pieces = [(0, REACH)] + [(REACH + 8 * i, 8) for i in range(3)]
    assert sum(n for _, n in pieces) == rims[0]
    far = []
    for o in range(2):
        group = []
        for at, (a, n) in enumerate(pieces):
            group.append(
                remote(
                    orb.at[o, pl.ds(jnp.where(left == 1, quarter - a - n, a), n)],
                    p0.at[pl.ds(placed(-a - n, n) + rims[0], n)],
                    far_send.at[o, at], far_recv.at[at], partners[o],
                )
            )
        n = REACH
        group.append(
            remote(
                orb.at[o, pl.ds(jnp.where(left == 1, 0, quarter - n), n)],
                p0.at[pl.ds(placed(slab, n) + rims[0], n)],
                far_send.at[o, 4], far_recv.at[4], partners[o],
            )
        )
        far.append(group)
    part = pot_rim // 8
    pot_far = [
        remote(
            pot.at[pl.ds(jnp.where(left == 1, quarter - pot_rim, 0) + (2 * x + o) * part, part)],
            pot_v.at[pl.ds(placed(-pot_rim, pot_rim) + pot_rim + (2 * x + o) * part, part)],
            pot_send.at[o], pot_recv, partners[o],
        )
        for o in range(2)
    ]
    mine = pot_v.at[pl.ds(placed(-pot_rim, pot_rim) + pot_rim + (2 * x + core) * part, part)]

    @pl.when(long)
    def _():
        for o in range(2):
            pot_far[o].start()
        for o in range(2):
            far[o][0].start()

    @pl.when(jnp.logical_not(long))
    def _():
        for o in range(2):
            far[o][4].start()

    near = remote(
        orb.at[1 - core], p0.at[pl.ds(core * quarter + rims[0], quarter)],
        near_send.at[0], near_recv.at[0], sibling,
    )
    near_pot = remote(
        pot, pot_v.at[pl.ds(core * quarter + pot_rim, quarter)],
        near_send.at[1], near_recv.at[1], sibling,
    )
    near.start()
    near_pot.start()

    @pl.when(long)
    def _():
        for at in range(1, 4):
            for o in range(2):
                far[o][at].start()

    def send_rows(i, c):
        at = lax.rem(i + band, bands)
        plane = core * quarter + lax.div(at, 2)
        plane = jnp.where(
            left == 1,
            jnp.where(plane >= slab - shift, plane - slab, plane),
            jnp.where(plane < shift, plane + slab, plane),
        )
        tile = lax.rem(2 * (base + plane) + lax.rem(at, 2) + 2 * whole, 2 * whole)

        @pl.when(tile != own_tile)
        def _():
            peer = {"band": lax.rem(tile, bands), "dom": lax.div(tile, bands)}
            remote(sub, rows.at[band], row_send, row_recv, peer).start()

        return c

    lax.fori_loop(0, bands, send_rows, 0)
    own_rows = pltpu.make_async_copy(sub, rows.at[band], move_sem.at[2])
    own_rows.start()

    def apply(level, u, blocks, step):
        scale, weight = scalars[level]

        def body(i, c):
            at = placed(u + i * step, step)
            before = None
            if level > 0:
                before = buffers[level - 1][pl.ds(at + rims[level - 1], step)]
            window = buffers[level][pl.ds(at + rims[level] - REACH, step + 2 * REACH)]
            low, high = filtered_block(
                window, pot_v[pl.ds(at + pot_rim, step)], before, scale, weight,
                lanes, cyclic, negacyclic,
            )
            pairs = jnp.stack([low, high], axis=1)
            if level < DEG - 1:
                buffers[level + 1][pl.ds(at + rims[level + 1], step)] = pairs
            else:
                out[pl.ds(2 * (at + rims[DEG]), 2 * step)] = pairs.reshape(2 * step, 8, 128)
            return c

        lax.fori_loop(0, blocks, body, 0)

    row = 2 * band + core

    def spread(u, count):
        start = placed(u, count)
        tiles = 2 * count

        def send(i, c):
            at = lax.rem(i + yx * (tiles // floor), tiles)
            tile = lax.rem(2 * (base + start) + at + 2 * whole, 2 * whole)
            src = out.at[2 * (start + rims[DEG]) + at]

            @pl.when(tile != own_tile)
            def _():
                peer = {"band": lax.rem(tile, bands), "dom": lax.div(tile, bands)}
                remote(src, recv.at[row], all_send, all_recv, peer).start()

            @pl.when(tile == own_tile)
            def _():
                pltpu.make_async_copy(src, recv.at[row], move_sem.at[3]).start()

            return c

        lax.fori_loop(0, tiles, send, 0)

    def advance(u):
        for level in range(DEG):
            apply(level, u + level * REACH, 1, 8)
        spread(u + (DEG - 1) * REACH, 8)

    load.wait()
    load_pot.wait()
    near.wait_recv()
    near_pot.wait_recv()
    apply(0, 8, 4, 12)
    apply(1, 14, 3, 12)
    apply(2, 20, 2, 12)
    spread(20, 24)

    pot_far[0].wait_recv()
    passed = []
    for dx in range(side):
        for dk in range(2):
            if dx or dk:
                peer = {
                    "band": band - x + lax.rem(x + dx, side),
                    "dom": dom if dk == 0 else dom + 1 - 2 * core,
                }
                at = 2 * dx + dk - 1
                passed.append(remote(mine, mine, pass_send.at[at], pass_recv.at[at], peer))
    for copy in passed:
        copy.start()

    far[0][4].wait_recv()
    apply(0, slab - 8, 1, 8)
    apply(1, slab - 14, 1, 8)
    apply(2, slab - 20, 1, 8)
    spread(slab - 20, 8)
    for at in range(4):
        if at == 1:
            for copy in passed:
                copy.wait_recv()
        far[0][at].wait_recv()
        advance(-8 * at)

    @pl.when(long)
    def _():
        for o in range(2):
            pot_far[o].wait_send()
            for at in range(4):
                far[o][at].wait_send()

    @pl.when(jnp.logical_not(long))
    def _():
        for o in range(2):
            far[o][4].wait_send()

    for copy in (near, near_pot, *passed):
        copy.wait_send()
    own_rows.wait()
    pltpu.make_async_copy(out.at[0], recv.at[row], move_sem.at[3]).wait()
    for ref, sem_a, sem_b in ((rows, row_send, row_recv), (recv, all_send, all_recv)):
        all_but_own = ref.at[pl.ds(0, ref.shape[0] - 1)]
        pltpu.make_async_copy(all_but_own, all_but_own, sem_a).wait()
        pltpu.make_async_copy(all_but_own, all_but_own, sem_b).wait()


def rotate_kernel(recv_v, rows_v, out, out_v, sems):
    high, low = two_parts(jnp.concatenate([rows_v[:, 0], rows_v[:, 1]], axis=0).T)
    matrix = jnp.concatenate([high, high, low], axis=1)
    width = 256
    stores = []
    for at in range(0, 8 * 128, width):
        columns = []
        for r in range(at // 128, (at + width) // 128):
            values = jnp.concatenate([recv_v[:, 0, r], recv_v[:, 1, r]], axis=0)
            high, low = two_parts(values)
            columns.append(jnp.concatenate([high, low, high], axis=0))
        out_v[:, pl.ds(at, width)] = jnp.dot(
            matrix, jnp.concatenate(columns, axis=1), preferred_element_type=jnp.float32
        )
        store = pltpu.make_async_copy(
            out_v.at[:, pl.ds(at, width)], out.at[:, pl.ds(at, width)], sems.at[at // width]
        )
        store.start()
        stores.append(store)
    for store in stores:
        store.wait()


def per_device(bands, orbitals, potential, subspace):
    orbs, planes = orbitals.shape[0], orbitals.shape[1]
    orb = orbitals.reshape(orbs, planes, 2, 8, 128)
    pot = potential.reshape(planes, 2, 8, 128)
    f32 = jnp.float32
    dma = pltpu.SemaphoreType.DMA
    anywhere = pl.BlockSpec(memory_space=pl.ANY)
    slab, shift = 2 * planes, 2 * REACH
    recv, rows = pl.pallas_call(
        functools.partial(filter_kernel, bands),
        out_shape=(
            pltpu.VMEM((bands * orbs, 8, 128), f32),
            pltpu.VMEM((bands, orbs, 128), f32),
        ),
        in_specs=[anywhere] * 3,
        out_specs=(anywhere,) * 2,
        scratch_shapes=[
            *[
                pltpu.VMEM((slab + 2 * (shift + REACH * (DEG - level)), 2, 8, 128), f32)
                for level in range(DEG)
            ],
            pltpu.VMEM((2 * (slab + 2 * shift), 8, 128), f32),
            pltpu.VMEM((slab + 2 * (shift + REACH * (DEG - 1)), 2, 8, 128), f32),
            dma((2,)),
            dma((2,)),
            dma((2, 5)),
            dma((5,)),
            dma((2,)),
            dma,
            dma((7,)),
            dma((7,)),
            dma((4,)),
            dma,
            dma,
            dma,
            dma,
        ],
        compiler_params=pltpu.CompilerParams(
            collective_id=0, has_side_effects=True, vmem_limit_bytes=32 * 2**20
        ),
        name="filter",
    )(*(pltpu.with_memory_space_constraint(a, pltpu.HBM) for a in (orb, pot, subspace)))
    recv = recv.reshape(bands, orbs, 8, 128)
    return pl.pallas_call(
        rotate_kernel,
        out_shape=jax.ShapeDtypeStruct((bands * orbs, 1024), f32),
        in_specs=[pl.BlockSpec(memory_space=pltpu.VMEM)] * 2,
        out_specs=anywhere,
        scratch_shapes=[pltpu.VMEM((bands * orbs, 1024), f32), dma((4,))],
        compiler_params=pltpu.CompilerParams(vmem_limit_bytes=32 * 2**20),
        name="rotate",
    )(*(pltpu.with_memory_space_constraint(a, pltpu.VMEM) for a in (recv, rows)))


def solution(mesh):
    in_specs = (P("band", "dom", None, None), P("dom", None, None), P("band", None))
    out_specs = P(None, ("dom", "band"))
    return jax.shard_map(
        functools.partial(per_device, mesh.shape["band"]),
        mesh=mesh,
        in_specs=in_specs,
        out_specs=out_specs,
        check_vma=False,
    )
```

```python
import functools
import math

import jax
import jax.numpy as jnp
from jax import lax
from jax.experimental import pallas as pl
from jax.experimental.pallas import tpu as pltpu
from jax.sharding import PartitionSpec as P

DEG = 3
REACH = 6
MESH = pl.DeviceIdType.MESH

upper_edge = 10.7
lower_edge = 1.5
bottom_edge = -1.0


def stencil_weights():
    factor_square = math.factorial(6) ** 2
    side_weights = []
    for offset in range(1, 7):
        side_weights.append(
            2.0
            * (-1.0) ** (offset + 1)
            * factor_square
            / (offset * offset * math.factorial(6 - offset) * math.factorial(6 + offset))
        )
    center_weight = -2.0 * sum(side_weights)
    return (center_weight, side_weights)


def filter_scalars(pass_count):
    half_width = (upper_edge - lower_edge) / 2.0
    sigma_now = half_width / (bottom_edge - (upper_edge + lower_edge) / 2.0)
    gamma_value = 2.0 / sigma_now
    scalars = [(sigma_now / half_width, 0.0)]
    for pass_index in range(pass_count - 1):
        sigma_next = 1.0 / (gamma_value - sigma_now)
        scalars.append((2.0 * sigma_next / half_width, sigma_now * sigma_next))
        sigma_now = sigma_next
    return scalars


def two_parts(values):
    high = values.astype(jnp.bfloat16)
    return high, (values - high.astype(jnp.float32)).astype(jnp.bfloat16)


def lane_matrix():
    rows = lax.broadcasted_iota(jnp.int32, (128, 128), 0)
    columns = lax.broadcasted_iota(jnp.int32, (128, 128), 1)
    apart = jnp.abs(rows - columns)
    apart = jnp.minimum(apart, 128 - apart)
    matrix = jnp.zeros((128, 128), jnp.float32)
    for k, w in enumerate(stencil_weights()[1], 1):
        matrix = jnp.where(apart == k, jnp.float32(w), matrix)
    high, low = two_parts(matrix)
    return jnp.concatenate([high, high, low], axis=0)


def row_weights():
    side = stencil_weights()[1]
    weight = lambda k: side[k - 1] if 1 <= k <= REACH else 0.0
    rows = lax.broadcasted_iota(jnp.int32, (8, 128), 0)
    cyclic, negacyclic = {}, {}
    for r in range(1, 8):
        cyclic[r] = 0.5 * (weight(r) + weight(8 - r))
        if r != 4:
            w = 0.5 * (weight(r) - weight(8 - r))
            negacyclic[r] = jnp.where(rows >= r, jnp.float32(w), jnp.float32(-w))
    return cyclic, negacyclic


def filtered_block(window, pot, before, scale, weight, lanes, cyclic, negacyclic):
    center_weight, side = stencil_weights()
    n = window.shape[0] - 2 * REACH
    mid = window[REACH : REACH + n]
    high, low = two_parts(mid.reshape(n * 16, 128))
    total = jnp.dot(
        jnp.concatenate([high, low, high], axis=1), lanes, preferred_element_type=jnp.float32
    ).reshape(n, 2, 8, 128)
    for k in range(1, REACH + 1):
        beside = window[REACH + k : REACH + k + n] + window[REACH - k : REACH - k + n]
        total = total + side[k - 1] * beside
    both, apart = mid[:, 0] + mid[:, 1], mid[:, 0] - mid[:, 1]
    even = cyclic[4] * pltpu.roll(both, 4, 1)
    for r in range(1, 4):
        even = even + cyclic[r] * (pltpu.roll(both, r, 1) + pltpu.roll(both, 8 - r, 1))
    odd = None
    for r, w in negacyclic.items():
        term = w * pltpu.roll(apart, r, 1)
        odd = term if odd is None else odd + term
    diag = (-1.5 * center_weight - (upper_edge + lower_edge) / 2.0) * scale
    results = []
    for at, rows in enumerate((even + odd, even - odd)):
        result = (pot[:, at] * scale + diag) * mid[:, at]
        result = result + (-0.5 * scale) * (total[:, at] + rows)
        if before is not None:
            result = result - weight * before[:, at]
        results.append(result)
    return results


def filter_kernel(
    bands, orb, pot, sub, recv, rows, p0, p1, p2, out, pot_v, held,
    near_send, near_recv, far_send, far_recv, onward_send, onward_recv, pot_send, pot_recv, pass_send, pass_recv,
    move_sem, all_send, all_recv, row_send, row_recv,
):
    quarter = orb.shape[1]
    slab, whole = 2 * quarter, 4 * quarter
    band, dom = lax.axis_index("band"), lax.axis_index("dom")
    core, half = lax.rem(dom, 2), lax.div(dom, 2)
    side = 4
    floor = side * side
    zl, x, yx = lax.div(band, floor), lax.rem(band, side), lax.rem(band, floor)
    shift = 2 * REACH
    left = jnp.where(zl < side // 2, 1, 0)
    long = core == left
    base = half * slab
    own_tile = dom * bands + band
    own_plane = lax.div(own_tile, 2)
    scalars = filter_scalars(DEG)
    buffers = (p0, p1, p2)
    rims = tuple(shift + REACH * (DEG - level) for level in range(DEG + 1))
    pot_rim = rims[1]

    def placed(u, count):
        return jnp.where(left == 1, u, slab - count - u)

    load = pltpu.make_async_copy(
        orb.at[core], p0.at[pl.ds(core * quarter + rims[0], quarter)], move_sem.at[0]
    )
    load.start()
    load_pot = pltpu.make_async_copy(
        pot, pot_v.at[pl.ds(core * quarter + pot_rim, quarter)], move_sem.at[1]
    )
    load_pot.start()

    sibling = {"dom": dom + 1 - 2 * core}
    partners = [{"dom": 2 * (1 - half) + k} for k in range(2)]

    def chip_along(shift, core_there):
        there = lax.rem(half * side + zl + shift + 2 * side, 2 * side)
        return {
            "band": lax.rem(there, side) * floor + yx,
            "dom": lax.div(there, side) * 2 + core_there,
        }

    relays = [chip_along(2 - 4 * o, o) for o in range(2)]
    onward_to = chip_along(2 - 4 * core, core)
    relay_from = [chip_along(4 * core - 2, k) for k in range(2)]

    barrier = pltpu.get_barrier_semaphore()
    for peer in (*partners, *relay_from):
        pl.semaphore_signal(barrier, inc=1, device_id=peer, device_id_type=MESH)
    in_left = (own_plane >= slab - shift) & (own_plane < whole - shift)
    in_right = (own_plane >= slab + shift) | (own_plane < shift)
    for line in range(side):
        there = jnp.where(in_left if line < side // 2 else in_right, 2, 0)
        for k in range(2):

            def greet(i, c, line=line, k=k, there=there):
                peer = line * floor + lax.rem(yx + i, floor)

                @pl.when((peer != band) | (there + k != dom))
                def _():
                    pl.semaphore_signal(
                        barrier, inc=1, device_id={"band": peer, "dom": there + k},
                        device_id_type=MESH,
                    )

                return c

            lax.fori_loop(0, floor, greet, 0)
    lanes = lane_matrix()
    cyclic, negacyclic = row_weights()
    pl.semaphore_wait(barrier, 2 * bands + 3)

    def remote(src, dst, send_sem, recv_sem, peer):
        return pltpu.make_async_remote_copy(
            src_ref=src, dst_ref=dst, send_sem=send_sem, recv_sem=recv_sem,
            device_id=peer, device_id_type=MESH,
        )

    pieces = [(0, REACH)] + [(REACH + 8 * i, 8) for i in range(3)]
    assert sum(n for _, n in pieces) == rims[0]
    pieces.append((slab, REACH))
    far = [
        [
            remote(
                orb.at[
                    o,
                    pl.ds(
                        jnp.where(left == 1, 0, quarter - n)
                        if a == slab
                        else jnp.where(left == 1, quarter - a - n, a),
                        n,
                    ),
                ],
                held.at[at, pl.ds(0, n)], far_send.at[o, at], far_recv.at[at], relays[o],
            )
            for at, (a, n) in enumerate(pieces)
        ]
        for o in range(2)
    ]
    onward = []
    for at, (a, n) in enumerate(pieces):
        u = slab if a == slab else -a - n
        onward.append(
            remote(
                held.at[at, pl.ds(0, n)],
                p0.at[pl.ds(jnp.where(left == 1, slab - n - u, u) + rims[0], n)],
                onward_send.at[at], onward_recv.at[at], onward_to,
            )
        )

    def pass_on(*numbers):
        for at in numbers:
            far[0][at].wait_recv()
            onward[at].start()

    part = pot_rim // 8
    pot_far = [
        remote(
            pot.at[pl.ds(jnp.where(left == 1, quarter - pot_rim, 0) + (2 * x + o) * part, part)],
            pot_v.at[pl.ds(placed(-pot_rim, pot_rim) + pot_rim + (2 * x + o) * part, part)],
            pot_send.at[o], pot_recv, partners[o],
        )
        for o in range(2)
    ]
    mine = pot_v.at[pl.ds(placed(-pot_rim, pot_rim) + pot_rim + (2 * x + core) * part, part)]

    @pl.when(long)
    def _():
        for o in range(2):
            pot_far[o].start()
        for o in range(2):
            far[o][0].start()

    @pl.when(jnp.logical_not(long))
    def _():
        for o in range(2):
            far[o][4].start()

    near = remote(
        orb.at[1 - core], p0.at[pl.ds(core * quarter + rims[0], quarter)],
        near_send.at[0], near_recv.at[0], sibling,
    )
    near_pot = remote(
        pot, pot_v.at[pl.ds(core * quarter + pot_rim, quarter)],
        near_send.at[1], near_recv.at[1], sibling,
    )
    near.start()
    near_pot.start()

    @pl.when(long)
    def _():
        for at in range(1, 4):
            for o in range(2):
                far[o][at].start()

    def send_rows(i, c):
        at = lax.rem(i + band, bands)
        plane = core * quarter + lax.div(at, 2)
        plane = jnp.where(
            left == 1,
            jnp.where(plane >= slab - shift, plane - slab, plane),
            jnp.where(plane < shift, plane + slab, plane),
        )
        tile = lax.rem(2 * (base + plane) + lax.rem(at, 2) + 2 * whole, 2 * whole)

        @pl.when(tile != own_tile)
        def _():
            peer = {"band": lax.rem(tile, bands), "dom": lax.div(tile, bands)}
            remote(sub, rows.at[band], row_send, row_recv, peer).start()

        return c

    lax.fori_loop(0, bands, send_rows, 0)
    own_rows = pltpu.make_async_copy(sub, rows.at[band], move_sem.at[2])
    own_rows.start()

    def apply(level, u, blocks, step):
        scale, weight = scalars[level]

        def body(i, c):
            at = placed(u + i * step, step)
            before = None
            if level > 0:
                before = buffers[level - 1][pl.ds(at + rims[level - 1], step)]
            window = buffers[level][pl.ds(at + rims[level] - REACH, step + 2 * REACH)]
            low, high = filtered_block(
                window, pot_v[pl.ds(at + pot_rim, step)], before, scale, weight,
                lanes, cyclic, negacyclic,
            )
            pairs = jnp.stack([low, high], axis=1)
            if level < DEG - 1:
                buffers[level + 1][pl.ds(at + rims[level + 1], step)] = pairs
            else:
                out[pl.ds(2 * (at + rims[DEG]), 2 * step)] = pairs.reshape(2 * step, 8, 128)
            return c

        lax.fori_loop(0, blocks, body, 0)

    row = 2 * band + core

    def spread(u, count):
        start = placed(u, count)
        tiles = 2 * count

        def send(i, c):
            at = lax.rem(i + yx * (tiles // floor), tiles)
            tile = lax.rem(2 * (base + start) + at + 2 * whole, 2 * whole)
            src = out.at[2 * (start + rims[DEG]) + at]

            @pl.when(tile != own_tile)
            def _():
                peer = {"band": lax.rem(tile, bands), "dom": lax.div(tile, bands)}
                remote(src, recv.at[row], all_send, all_recv, peer).start()

            @pl.when(tile == own_tile)
            def _():
                pltpu.make_async_copy(src, recv.at[row], move_sem.at[3]).start()

            return c

        lax.fori_loop(0, tiles, send, 0)

    def advance(u):
        for level in range(DEG):
            apply(level, u + level * REACH, 1, 8)
        spread(u + (DEG - 1) * REACH, 8)

    load.wait()
    load_pot.wait()
    near.wait_recv()
    near_pot.wait_recv()
    apply(0, 8, 4, 12)
    pass_on(4, 0)
    apply(1, 14, 3, 12)
    pass_on(1)
    apply(2, 20, 2, 12)
    pass_on(2)
    spread(20, 24)

    pot_far[0].wait_recv()
    passed = []
    for dx in range(side):
        for dk in range(2):
            if dx or dk:
                peer = {
                    "band": band - x + lax.rem(x + dx, side),
                    "dom": dom if dk == 0 else dom + 1 - 2 * core,
                }
                at = 2 * dx + dk - 1
                passed.append(remote(mine, mine, pass_send.at[at], pass_recv.at[at], peer))
    for copy in passed:
        copy.start()

    pass_on(3)
    onward[4].wait_recv()
    apply(0, slab - 8, 1, 8)
    apply(1, slab - 14, 1, 8)
    apply(2, slab - 20, 1, 8)
    spread(slab - 20, 8)
    for at in range(4):
        if at == 1:
            for copy in passed:
                copy.wait_recv()
        onward[at].wait_recv()
        advance(-8 * at)

    @pl.when(long)
    def _():
        for o in range(2):
            pot_far[o].wait_send()
            for at in range(4):
                far[o][at].wait_send()

    @pl.when(jnp.logical_not(long))
    def _():
        for o in range(2):
            far[o][4].wait_send()

    for copy in (near, near_pot, *passed, *onward):
        copy.wait_send()
    own_rows.wait()
    pltpu.make_async_copy(out.at[0], recv.at[row], move_sem.at[3]).wait()
    for ref, sem_a, sem_b in ((rows, row_send, row_recv), (recv, all_send, all_recv)):
        all_but_own = ref.at[pl.ds(0, ref.shape[0] - 1)]
        pltpu.make_async_copy(all_but_own, all_but_own, sem_a).wait()
        pltpu.make_async_copy(all_but_own, all_but_own, sem_b).wait()


def rotate_kernel(recv_v, rows_v, out, out_v, sems):
    high, low = two_parts(jnp.concatenate([rows_v[:, 0], rows_v[:, 1]], axis=0).T)
    matrix = jnp.concatenate([high, high, low], axis=1)
    width = 256
    stores = []
    for at in range(0, 8 * 128, width):
        columns = []
        for r in range(at // 128, (at + width) // 128):
            values = jnp.concatenate([recv_v[:, 0, r], recv_v[:, 1, r]], axis=0)
            high, low = two_parts(values)
            columns.append(jnp.concatenate([high, low, high], axis=0))
        out_v[:, pl.ds(at, width)] = jnp.dot(
            matrix, jnp.concatenate(columns, axis=1), preferred_element_type=jnp.float32
        )
        store = pltpu.make_async_copy(
            out_v.at[:, pl.ds(at, width)], out.at[:, pl.ds(at, width)], sems.at[at // width]
        )
        store.start()
        stores.append(store)
    for store in stores:
        store.wait()


def per_device(bands, orbitals, potential, subspace):
    orbs, planes = orbitals.shape[0], orbitals.shape[1]
    orb = orbitals.reshape(orbs, planes, 2, 8, 128)
    pot = potential.reshape(planes, 2, 8, 128)
    f32 = jnp.float32
    dma = pltpu.SemaphoreType.DMA
    anywhere = pl.BlockSpec(memory_space=pl.ANY)
    slab, shift = 2 * planes, 2 * REACH
    recv, rows = pl.pallas_call(
        functools.partial(filter_kernel, bands),
        out_shape=(
            pltpu.VMEM((bands * orbs, 8, 128), f32),
            pltpu.VMEM((bands, orbs, 128), f32),
        ),
        in_specs=[anywhere] * 3,
        out_specs=(anywhere,) * 2,
        scratch_shapes=[
            *[
                pltpu.VMEM((slab + 2 * (shift + REACH * (DEG - level)), 2, 8, 128), f32)
                for level in range(DEG)
            ],
            pltpu.VMEM((2 * (slab + 2 * shift), 8, 128), f32),
            pltpu.VMEM((slab + 2 * (shift + REACH * (DEG - 1)), 2, 8, 128), f32),
            pltpu.VMEM((5, 8, 2, 8, 128), f32),
            dma((2,)),
            dma((2,)),
            dma((2, 5)),
            dma((5,)),
            dma((5,)),
            dma((5,)),
            dma((2,)),
            dma,
            dma((7,)),
            dma((7,)),
            dma((4,)),
            dma,
            dma,
            dma,
            dma,
        ],
        compiler_params=pltpu.CompilerParams(
            collective_id=0, has_side_effects=True, vmem_limit_bytes=32 * 2**20
        ),
        name="filter",
    )(*(pltpu.with_memory_space_constraint(a, pltpu.HBM) for a in (orb, pot, subspace)))
    recv = recv.reshape(bands, orbs, 8, 128)
    return pl.pallas_call(
        rotate_kernel,
        out_shape=jax.ShapeDtypeStruct((bands * orbs, 1024), f32),
        in_specs=[pl.BlockSpec(memory_space=pltpu.VMEM)] * 2,
        out_specs=anywhere,
        scratch_shapes=[pltpu.VMEM((bands * orbs, 1024), f32), dma((4,))],
        compiler_params=pltpu.CompilerParams(vmem_limit_bytes=32 * 2**20),
        name="rotate",
    )(*(pltpu.with_memory_space_constraint(a, pltpu.VMEM) for a in (recv, rows)))


def solution(mesh):
    in_specs = (P("band", "dom", None, None), P("dom", None, None), P("band", None))
    out_specs = P(None, ("dom", "band"))
    return jax.shard_map(
        functools.partial(per_device, mesh.shape["band"]),
        mesh=mesh,
        in_specs=in_specs,
        out_specs=out_specs,
        check_vma=False,
    )
```

```python
import functools
import math

import jax
import jax.numpy as jnp
from jax import lax
from jax.experimental import pallas as pl
from jax.experimental.pallas import tpu as pltpu
from jax.sharding import PartitionSpec as P

DEG = 3
REACH = 6
MESH = pl.DeviceIdType.MESH

upper_edge = 10.7
lower_edge = 1.5
bottom_edge = -1.0


def stencil_weights():
    factor_square = math.factorial(6) ** 2
    side_weights = []
    for offset in range(1, 7):
        side_weights.append(
            2.0
            * (-1.0) ** (offset + 1)
            * factor_square
            / (offset * offset * math.factorial(6 - offset) * math.factorial(6 + offset))
        )
    center_weight = -2.0 * sum(side_weights)
    return (center_weight, side_weights)


def filter_scalars(pass_count):
    half_width = (upper_edge - lower_edge) / 2.0
    sigma_now = half_width / (bottom_edge - (upper_edge + lower_edge) / 2.0)
    gamma_value = 2.0 / sigma_now
    scalars = [(sigma_now / half_width, 0.0)]
    for pass_index in range(pass_count - 1):
        sigma_next = 1.0 / (gamma_value - sigma_now)
        scalars.append((2.0 * sigma_next / half_width, sigma_now * sigma_next))
        sigma_now = sigma_next
    return scalars


def two_parts(values):
    high = values.astype(jnp.bfloat16)
    return high, (values - high.astype(jnp.float32)).astype(jnp.bfloat16)


def stencil_matrix(period, axis):
    rows = lax.broadcasted_iota(jnp.int32, (128, 128), 0)
    columns = lax.broadcasted_iota(jnp.int32, (128, 128), 1)
    apart = jnp.abs(rows - columns)
    if period < 128:
        same = jnp.bitwise_or(rows, period - 1) == jnp.bitwise_or(columns, period - 1)
        apart = jnp.where(same, apart, 0)
    apart = jnp.minimum(apart, period - apart)
    matrix = jnp.zeros((128, 128), jnp.float32)
    for k, w in enumerate(stencil_weights()[1], 1):
        matrix = jnp.where(apart == k, jnp.float32(w), matrix)
    high, low = two_parts(matrix)
    return jnp.concatenate([high, high, low], axis=axis)


def filtered_block(window, pot, before, scale, weight, lanes, rows):
    center_weight, side = stencil_weights()
    n = window.shape[0] - 2 * REACH
    mid = window[REACH : REACH + n]
    high, low = two_parts(mid.reshape(n * 16, 128))
    total = jnp.dot(
        jnp.concatenate([high, low, high], axis=1), lanes, preferred_element_type=jnp.float32
    ) + jnp.dot(
        rows, jnp.concatenate([high, low, high], axis=0), preferred_element_type=jnp.float32
    )
    total = total.reshape(n, 2, 8, 128)
    for k in range(1, REACH + 1):
        beside = window[REACH + k : REACH + k + n] + window[REACH - k : REACH - k + n]
        total = total + side[k - 1] * beside
    diag = (-1.5 * center_weight - (upper_edge + lower_edge) / 2.0) * scale
    result = (pot * scale + diag) * mid + (-0.5 * scale) * total
    if before is not None:
        result = result - weight * before
    return result


def filter_kernel(
    bands, orb, pot, sub, recv, rows, p0, p1, p2, out, pot_v,
    near_send, near_recv, far_send, far_recv, pot_send, pot_recv, pass_send, pass_recv,
    move_sem, all_send, all_recv, row_send, row_recv,
):
    quarter = orb.shape[1]
    slab, whole = 2 * quarter, 4 * quarter
    band, dom = lax.axis_index("band"), lax.axis_index("dom")
    core, half = lax.rem(dom, 2), lax.div(dom, 2)
    side = 4
    floor = side * side
    zl, x, yx = lax.div(band, floor), lax.rem(band, side), lax.rem(band, floor)
    shift = 2 * REACH
    left = jnp.where(zl < side // 2, 1, 0)
    long = core == left
    base = half * slab
    own_tile = dom * bands + band
    own_plane = lax.div(own_tile, 2)
    scalars = filter_scalars(DEG)
    buffers = (p0, p1, p2)
    rims = tuple(shift + REACH * (DEG - level) for level in range(DEG + 1))
    pot_rim = rims[1]

    def placed(u, count):
        return jnp.where(left == 1, u, slab - count - u)

    load = pltpu.make_async_copy(
        orb.at[core], p0.at[pl.ds(core * quarter + rims[0], quarter)], move_sem.at[0]
    )
    load.start()
    load_pot = pltpu.make_async_copy(
        pot, pot_v.at[pl.ds(core * quarter + pot_rim, quarter)], move_sem.at[1]
    )
    load_pot.start()

    sibling = {"dom": dom + 1 - 2 * core}
    partners = [{"dom": 2 * (1 - half) + k} for k in range(2)]

    barrier = pltpu.get_barrier_semaphore()
    for peer in partners:
        pl.semaphore_signal(barrier, inc=1, device_id=peer, device_id_type=MESH)
    in_left = (own_plane >= slab - shift) & (own_plane < whole - shift)
    in_right = (own_plane >= slab + shift) | (own_plane < shift)
    for line in range(side):
        there = jnp.where(in_left if line < side // 2 else in_right, 2, 0)
        for k in range(2):

            def greet(i, c, line=line, k=k, there=there):
                peer = line * floor + lax.rem(yx + i, floor)

                @pl.when((peer != band) | (there + k != dom))
                def _():
                    pl.semaphore_signal(
                        barrier, inc=1, device_id={"band": peer, "dom": there + k},
                        device_id_type=MESH,
                    )

                return c

            lax.fori_loop(0, floor, greet, 0)
    lanes, lines = stencil_matrix(128, 0), stencil_matrix(16, 1)
    pl.semaphore_wait(barrier, 2 * bands + 1)

    def remote(src, dst, send_sem, recv_sem, peer):
        return pltpu.make_async_remote_copy(
            src_ref=src, dst_ref=dst, send_sem=send_sem, recv_sem=recv_sem,
            device_id=peer, device_id_type=MESH,
        )

    pieces = [(0, REACH)] + [(REACH + 8 * i, 8) for i in range(3)]
    assert sum(n for _, n in pieces) == rims[0]
    far = []
    for o in range(2):
        group = []
        for at, (a, n) in enumerate(pieces):
            group.append(
                remote(
                    orb.at[o, pl.ds(jnp.where(left == 1, quarter - a - n, a), n)],
                    p0.at[pl.ds(placed(-a - n, n) + rims[0], n)],
                    far_send.at[o, at], far_recv.at[at], partners[o],
                )
            )
        n = REACH
        group.append(
            remote(
                orb.at[o, pl.ds(jnp.where(left == 1, 0, quarter - n), n)],
                p0.at[pl.ds(placed(slab, n) + rims[0], n)],
                far_send.at[o, 4], far_recv.at[4], partners[o],
            )
        )
        far.append(group)
    part = pot_rim // 8
    pot_far = [
        remote(
            pot.at[pl.ds(jnp.where(left == 1, quarter - pot_rim, 0) + (2 * x + o) * part, part)],
            pot_v.at[pl.ds(placed(-pot_rim, pot_rim) + pot_rim + (2 * x + o) * part, part)],
            pot_send.at[o], pot_recv, partners[o],
        )
        for o in range(2)
    ]
    mine = pot_v.at[pl.ds(placed(-pot_rim, pot_rim) + pot_rim + (2 * x + core) * part, part)]

    @pl.when(long)
    def _():
        for o in range(2):
            pot_far[o].start()
        for o in range(2):
            far[o][0].start()

    @pl.when(jnp.logical_not(long))
    def _():
        for o in range(2):
            far[o][4].start()

    near = remote(
        orb.at[1 - core], p0.at[pl.ds(core * quarter + rims[0], quarter)],
        near_send.at[0], near_recv.at[0], sibling,
    )
    near_pot = remote(
        pot, pot_v.at[pl.ds(core * quarter + pot_rim, quarter)],
        near_send.at[1], near_recv.at[1], sibling,
    )
    near.start()
    near_pot.start()

    @pl.when(long)
    def _():
        for at in range(1, 4):
            for o in range(2):
                far[o][at].start()

    def send_rows(i, c):
        at = lax.rem(i + band, bands)
        plane = core * quarter + lax.div(at, 2)
        plane = jnp.where(
            left == 1,
            jnp.where(plane >= slab - shift, plane - slab, plane),
            jnp.where(plane < shift, plane + slab, plane),
        )
        tile = lax.rem(2 * (base + plane) + lax.rem(at, 2) + 2 * whole, 2 * whole)

        @pl.when(tile != own_tile)
        def _():
            peer = {"band": lax.rem(tile, bands), "dom": lax.div(tile, bands)}
            remote(sub, rows.at[band], row_send, row_recv, peer).start()

        return c

    lax.fori_loop(0, bands, send_rows, 0)
    own_rows = pltpu.make_async_copy(sub, rows.at[band], move_sem.at[2])
    own_rows.start()

    step = 8

    def apply(level, u, blocks):
        scale, weight = scalars[level]

        def body(i, c):
            at = placed(u + i * step, step)
            before = None
            if level > 0:
                before = buffers[level - 1][pl.ds(at + rims[level - 1], step)]
            window = buffers[level][pl.ds(at + rims[level] - REACH, step + 2 * REACH)]
            pairs = filtered_block(
                window, pot_v[pl.ds(at + pot_rim, step)], before, scale, weight, lanes, lines
            )
            if level < DEG - 1:
                buffers[level + 1][pl.ds(at + rims[level + 1], step)] = pairs
            else:
                out[pl.ds(2 * (at + rims[DEG]), 2 * step)] = pairs.reshape(2 * step, 8, 128)
            return c

        lax.fori_loop(0, blocks, body, 0)

    row = 2 * band + core

    def spread(u, count):
        start = placed(u, count)
        tiles = 2 * count

        def send(i, c):
            at = lax.rem(i + yx * (tiles // floor), tiles)
            tile = lax.rem(2 * (base + start) + at + 2 * whole, 2 * whole)
            src = out.at[2 * (start + rims[DEG]) + at]

            @pl.when(tile != own_tile)
            def _():
                peer = {"band": lax.rem(tile, bands), "dom": lax.div(tile, bands)}
                remote(src, recv.at[row], all_send, all_recv, peer).start()

            @pl.when(tile == own_tile)
            def _():
                pltpu.make_async_copy(src, recv.at[row], move_sem.at[3]).start()

            return c

        lax.fori_loop(0, tiles, send, 0)

    def advance(u):
        for level in range(DEG):
            apply(level, u + level * REACH, 1)
        spread(u + (DEG - 1) * REACH, 8)

    load.wait()
    load_pot.wait()
    near.wait_recv()
    near_pot.wait_recv()
    apply(0, 8, 6)
    apply(1, 14, 4)
    apply(1, 42, 1)
    apply(2, 20, 3)
    spread(20, 24)

    pot_far[0].wait_recv()
    passed = []
    for dx in range(side):
        for dk in range(2):
            if dx or dk:
                peer = {
                    "band": band - x + lax.rem(x + dx, side),
                    "dom": dom if dk == 0 else dom + 1 - 2 * core,
                }
                at = 2 * dx + dk - 1
                passed.append(remote(mine, mine, pass_send.at[at], pass_recv.at[at], peer))
    for copy in passed:
        copy.start()

    far[0][4].wait_recv()
    apply(0, slab - 8, 1)
    apply(1, slab - 14, 1)
    apply(2, slab - 20, 1)
    spread(slab - 20, 8)
    for at in range(4):
        if at == 1:
            for copy in passed:
                copy.wait_recv()
        far[0][at].wait_recv()
        advance(-8 * at)

    @pl.when(long)
    def _():
        for o in range(2):
            pot_far[o].wait_send()
            for at in range(4):
                far[o][at].wait_send()

    @pl.when(jnp.logical_not(long))
    def _():
        for o in range(2):
            far[o][4].wait_send()

    for copy in (near, near_pot, *passed):
        copy.wait_send()
    own_rows.wait()
    pltpu.make_async_copy(out.at[0], recv.at[row], move_sem.at[3]).wait()
    for ref, sem_a, sem_b in ((rows, row_send, row_recv), (recv, all_send, all_recv)):
        all_but_own = ref.at[pl.ds(0, ref.shape[0] - 1)]
        pltpu.make_async_copy(all_but_own, all_but_own, sem_a).wait()
        pltpu.make_async_copy(all_but_own, all_but_own, sem_b).wait()


def rotate_kernel(recv_v, rows_v, out, out_v, sems):
    high, low = two_parts(jnp.concatenate([rows_v[:, 0], rows_v[:, 1]], axis=0).T)
    matrix = jnp.concatenate([high, high, low], axis=1)
    width = 256
    stores = []
    for at in range(0, 8 * 128, width):
        columns = []
        for r in range(at // 128, (at + width) // 128):
            values = jnp.concatenate([recv_v[:, 0, r], recv_v[:, 1, r]], axis=0)
            high, low = two_parts(values)
            columns.append(jnp.concatenate([high, low, high], axis=0))
        out_v[:, pl.ds(at, width)] = jnp.dot(
            matrix, jnp.concatenate(columns, axis=1), preferred_element_type=jnp.float32
        )
        store = pltpu.make_async_copy(
            out_v.at[:, pl.ds(at, width)], out.at[:, pl.ds(at, width)], sems.at[at // width]
        )
        store.start()
        stores.append(store)
    for store in stores:
        store.wait()


def per_device(bands, orbitals, potential, subspace):
    orbs, planes = orbitals.shape[0], orbitals.shape[1]
    orb = orbitals.reshape(orbs, planes, 2, 8, 128)
    pot = potential.reshape(planes, 2, 8, 128)
    f32 = jnp.float32
    dma = pltpu.SemaphoreType.DMA
    anywhere = pl.BlockSpec(memory_space=pl.ANY)
    slab, shift = 2 * planes, 2 * REACH
    recv, rows = pl.pallas_call(
        functools.partial(filter_kernel, bands),
        out_shape=(
            pltpu.VMEM((bands * orbs, 8, 128), f32),
            pltpu.VMEM((bands, orbs, 128), f32),
        ),
        in_specs=[anywhere] * 3,
        out_specs=(anywhere,) * 2,
        scratch_shapes=[
            *[
                pltpu.VMEM((slab + 2 * (shift + REACH * (DEG - level)), 2, 8, 128), f32)
                for level in range(DEG)
            ],
            pltpu.VMEM((2 * (slab + 2 * shift), 8, 128), f32),
            pltpu.VMEM((slab + 2 * (shift + REACH * (DEG - 1)), 2, 8, 128), f32),
            dma((2,)),
            dma((2,)),
            dma((2, 5)),
            dma((5,)),
            dma((2,)),
            dma,
            dma((7,)),
            dma((7,)),
            dma((4,)),
            dma,
            dma,
            dma,
            dma,
        ],
        compiler_params=pltpu.CompilerParams(
            collective_id=0, has_side_effects=True, vmem_limit_bytes=32 * 2**20
        ),
        name="filter",
    )(*(pltpu.with_memory_space_constraint(a, pltpu.HBM) for a in (orb, pot, subspace)))
    recv = recv.reshape(bands, orbs, 8, 128)
    return pl.pallas_call(
        rotate_kernel,
        out_shape=jax.ShapeDtypeStruct((bands * orbs, 1024), f32),
        in_specs=[pl.BlockSpec(memory_space=pltpu.VMEM)] * 2,
        out_specs=anywhere,
        scratch_shapes=[pltpu.VMEM((bands * orbs, 1024), f32), dma((4,))],
        compiler_params=pltpu.CompilerParams(vmem_limit_bytes=32 * 2**20),
        name="rotate",
    )(*(pltpu.with_memory_space_constraint(a, pltpu.VMEM) for a in (recv, rows)))


def solution(mesh):
    in_specs = (P("band", "dom", None, None), P("dom", None, None), P("band", None))
    out_specs = P(None, ("dom", "band"))
    return jax.shard_map(
        functools.partial(per_device, mesh.shape["band"]),
        mesh=mesh,
        in_specs=in_specs,
        out_specs=out_specs,
        check_vma=False,
    )
```

```python
import functools
import math

import jax
import jax.numpy as jnp
from jax import lax
from jax.experimental import pallas as pl
from jax.experimental.pallas import tpu as pltpu
from jax.sharding import PartitionSpec as P

DEG = 3
REACH = 6
MESH = pl.DeviceIdType.MESH

upper_edge = 10.7
lower_edge = 1.5
bottom_edge = -1.0


def stencil_weights():
    factor_square = math.factorial(6) ** 2
    side_weights = []
    for offset in range(1, 7):
        side_weights.append(
            2.0
            * (-1.0) ** (offset + 1)
            * factor_square
            / (offset * offset * math.factorial(6 - offset) * math.factorial(6 + offset))
        )
    center_weight = -2.0 * sum(side_weights)
    return (center_weight, side_weights)


def filter_scalars(pass_count):
    half_width = (upper_edge - lower_edge) / 2.0
    sigma_now = half_width / (bottom_edge - (upper_edge + lower_edge) / 2.0)
    gamma_value = 2.0 / sigma_now
    scalars = [(sigma_now / half_width, 0.0)]
    for pass_index in range(pass_count - 1):
        sigma_next = 1.0 / (gamma_value - sigma_now)
        scalars.append((2.0 * sigma_next / half_width, sigma_now * sigma_next))
        sigma_now = sigma_next
    return scalars


def two_parts(values):
    high = values.astype(jnp.bfloat16)
    return high, (values - high.astype(jnp.float32)).astype(jnp.bfloat16)


def stencil_matrix(period, axis):
    rows = lax.broadcasted_iota(jnp.int32, (128, 128), 0)
    columns = lax.broadcasted_iota(jnp.int32, (128, 128), 1)
    apart = jnp.abs(rows - columns)
    if period < 128:
        same = jnp.bitwise_or(rows, period - 1) == jnp.bitwise_or(columns, period - 1)
        apart = jnp.where(same, apart, 0)
    apart = jnp.minimum(apart, period - apart)
    matrix = jnp.zeros((128, 128), jnp.float32)
    for k, w in enumerate(stencil_weights()[1], 1):
        matrix = jnp.where(apart == k, jnp.float32(w), matrix)
    high, low = two_parts(matrix)
    return jnp.concatenate([high, high, low], axis=axis)


def filtered_block(window, pot, before, scale, weight, lanes, rows):
    center_weight, side = stencil_weights()
    n = window.shape[0] - 2 * REACH
    mid = window[REACH : REACH + n]
    high, low = two_parts(mid.reshape(n * 16, 128))
    total = jnp.dot(
        jnp.concatenate([high, low, high], axis=1), lanes, preferred_element_type=jnp.float32
    ) + jnp.dot(
        rows, jnp.concatenate([high, low, high], axis=0), preferred_element_type=jnp.float32
    )
    total = total.reshape(n, 2, 8, 128)
    for k in range(1, REACH + 1):
        beside = window[REACH + k : REACH + k + n] + window[REACH - k : REACH - k + n]
        total = total + side[k - 1] * beside
    diag = (-1.5 * center_weight - (upper_edge + lower_edge) / 2.0) * scale
    result = (pot * scale + diag) * mid + (-0.5 * scale) * total
    if before is not None:
        result = result - weight * before
    return result


def filter_kernel(
    bands, orb, pot, sub, recv, rows, p0, p1, p2, out, pot_v,
    near_send, near_recv, far_send, far_recv, pot_send, pot_recv, pass_send, pass_recv,
    move_sem, all_send, all_recv, row_send, row_recv, plane_sem, all_sem,
):
    quarter = orb.shape[1]
    slab, whole = 2 * quarter, 4 * quarter
    band, dom = lax.axis_index("band"), lax.axis_index("dom")
    core, half = lax.rem(dom, 2), lax.div(dom, 2)
    side = 4
    floor = side * side
    zl, x, yx = lax.div(band, floor), lax.rem(band, side), lax.rem(band, floor)
    shift = 2 * REACH
    left = jnp.where(zl < side // 2, 1, 0)
    long = core == left
    base = half * slab
    own_tile = dom * bands + band
    own_plane = lax.div(own_tile, 2)
    scalars = filter_scalars(DEG)
    buffers = (p0, p1, p2)
    rims = tuple(shift + REACH * (DEG - level) for level in range(DEG + 1))
    pot_rim = rims[1]

    def placed(u, count):
        return jnp.where(left == 1, u, slab - count - u)

    load = pltpu.make_async_copy(
        orb.at[core], p0.at[pl.ds(core * quarter + rims[0], quarter)], move_sem.at[0]
    )
    load.start()
    load_pot = pltpu.make_async_copy(
        pot, pot_v.at[pl.ds(core * quarter + pot_rim, quarter)], move_sem.at[1]
    )
    load_pot.start()

    sibling = {"dom": dom + 1 - 2 * core}
    partners = [{"dom": 2 * (1 - half) + k} for k in range(2)]

    def chip_along(shift):
        there = lax.rem(half * side + zl + shift, 2 * side)
        return {
            "band": lax.rem(there, side) * floor + yx,
            "dom": lax.div(there, side) * 2 + core,
        }

    x_line = [
        {"band": band - x + lax.rem(x + dx, side), "dom": dom if dk == 0 else dom + 1 - 2 * core}
        for dx in range(side)
        for dk in range(2)
    ][1:]
    y = lax.div(yx, side)
    y_line = [{"band": band + side * (lax.rem(y + dy, side) - y)} for dy in range(1, side)]
    z_line = [chip_along(dz) for dz in range(1, 2 * side)]
    other_partner = {"dom": 2 * (1 - half) + 1 - core}
    barrier = pltpu.get_barrier_semaphore()
    entered = (*z_line, other_partner, *x_line, *y_line)

    def tell(peers, semaphore):
        for peer in peers:
            pl.semaphore_signal(semaphore, inc=1, device_id=peer, device_id_type=MESH)

    tell(entered, barrier)
    lanes, lines = stencil_matrix(128, 0), stencil_matrix(16, 1)
    pl.semaphore_wait(barrier, len(entered))

    def remote(src, dst, send_sem, recv_sem, peer):
        return pltpu.make_async_remote_copy(
            src_ref=src, dst_ref=dst, send_sem=send_sem, recv_sem=recv_sem,
            device_id=peer, device_id_type=MESH,
        )

    pieces = [(0, REACH)] + [(REACH + 8 * i, 8) for i in range(3)]
    assert sum(n for _, n in pieces) == rims[0]
    far = []
    for o in range(2):
        group = []
        for at, (a, n) in enumerate(pieces):
            group.append(
                remote(
                    orb.at[o, pl.ds(jnp.where(left == 1, quarter - a - n, a), n)],
                    p0.at[pl.ds(placed(-a - n, n) + rims[0], n)],
                    far_send.at[o, at], far_recv.at[at], partners[o],
                )
            )
        n = REACH
        group.append(
            remote(
                orb.at[o, pl.ds(jnp.where(left == 1, 0, quarter - n), n)],
                p0.at[pl.ds(placed(slab, n) + rims[0], n)],
                far_send.at[o, 4], far_recv.at[4], partners[o],
            )
        )
        far.append(group)
    part = pot_rim // 8
    pot_far = [
        remote(
            pot.at[pl.ds(jnp.where(left == 1, quarter - pot_rim, 0) + (2 * x + o) * part, part)],
            pot_v.at[pl.ds(placed(-pot_rim, pot_rim) + pot_rim + (2 * x + o) * part, part)],
            pot_send.at[o], pot_recv, partners[o],
        )
        for o in range(2)
    ]
    mine = pot_v.at[pl.ds(placed(-pot_rim, pot_rim) + pot_rim + (2 * x + core) * part, part)]

    @pl.when(long)
    def _():
        for o in range(2):
            pot_far[o].start()
        for o in range(2):
            far[o][0].start()

    @pl.when(jnp.logical_not(long))
    def _():
        for o in range(2):
            far[o][4].start()

    near = remote(
        orb.at[1 - core], p0.at[pl.ds(core * quarter + rims[0], quarter)],
        near_send.at[0], near_recv.at[0], sibling,
    )
    near_pot = remote(
        pot, pot_v.at[pl.ds(core * quarter + pot_rim, quarter)],
        near_send.at[1], near_recv.at[1], sibling,
    )
    near.start()
    near_pot.start()

    @pl.when(long)
    def _():
        for at in range(1, 4):
            for o in range(2):
                far[o][at].start()

    tell(y_line, plane_sem)

    step = 8

    def apply(level, u, blocks):
        scale, weight = scalars[level]

        def body(i, c):
            at = placed(u + i * step, step)
            before = None
            if level > 0:
                before = buffers[level - 1][pl.ds(at + rims[level - 1], step)]
            window = buffers[level][pl.ds(at + rims[level] - REACH, step + 2 * REACH)]
            pairs = filtered_block(
                window, pot_v[pl.ds(at + pot_rim, step)], before, scale, weight, lanes, lines
            )
            if level < DEG - 1:
                buffers[level + 1][pl.ds(at + rims[level + 1], step)] = pairs
            else:
                out[pl.ds(2 * (at + rims[DEG]), 2 * step)] = pairs.reshape(2 * step, 8, 128)
            return c

        lax.fori_loop(0, blocks, body, 0)

    row = 2 * band + core

    def spread(u, count):
        start = placed(u, count)
        tiles = 2 * count

        def send(i, c):
            at = lax.rem(i + yx * (tiles // floor), tiles)
            tile = lax.rem(2 * (base + start) + at + 2 * whole, 2 * whole)
            src = out.at[2 * (start + rims[DEG]) + at]

            @pl.when(tile != own_tile)
            def _():
                peer = {"band": lax.rem(tile, bands), "dom": lax.div(tile, bands)}
                remote(src, recv.at[row], all_send, all_recv, peer).start()

            @pl.when(tile == own_tile)
            def _():
                pltpu.make_async_copy(src, recv.at[row], move_sem.at[3]).start()

            return c

        lax.fori_loop(0, tiles, send, 0)

    def advance(u):
        for level in range(DEG):
            apply(level, u + level * REACH, 1)
        spread(u + (DEG - 1) * REACH, 8)

    load.wait()
    load_pot.wait()
    near.wait_recv()
    near_pot.wait_recv()
    pl.semaphore_wait(plane_sem, len(y_line))
    tell(z_line, all_sem)
    apply(0, 8, 6)
    apply(1, 14, 4)
    apply(1, 42, 1)
    apply(2, 20, 3)
    pl.semaphore_wait(all_sem, len(z_line))

    def send_rows(i, c):
        at = lax.rem(i + band, bands)
        plane = core * quarter + lax.div(at, 2)
        plane = jnp.where(
            left == 1,
            jnp.where(plane >= slab - shift, plane - slab, plane),
            jnp.where(plane < shift, plane + slab, plane),
        )
        tile = lax.rem(2 * (base + plane) + lax.rem(at, 2) + 2 * whole, 2 * whole)

        @pl.when(tile != own_tile)
        def _():
            peer = {"band": lax.rem(tile, bands), "dom": lax.div(tile, bands)}
            remote(sub, rows.at[band], row_send, row_recv, peer).start()

        return c

    lax.fori_loop(0, bands, send_rows, 0)
    own_rows = pltpu.make_async_copy(sub, rows.at[band], move_sem.at[2])
    own_rows.start()
    spread(20, 24)

    pot_far[0].wait_recv()
    passed = [
        remote(mine, mine, pass_send.at[at], pass_recv.at[at], peer)
        for at, peer in enumerate(x_line)
    ]
    for copy in passed:
        copy.start()

    far[0][4].wait_recv()
    apply(0, slab - 8, 1)
    apply(1, slab - 14, 1)
    apply(2, slab - 20, 1)
    spread(slab - 20, 8)
    for at in range(4):
        if at == 1:
            for copy in passed:
                copy.wait_recv()
        far[0][at].wait_recv()
        advance(-8 * at)

    @pl.when(long)
    def _():
        for o in range(2):
            pot_far[o].wait_send()
            for at in range(4):
                far[o][at].wait_send()

    @pl.when(jnp.logical_not(long))
    def _():
        for o in range(2):
            far[o][4].wait_send()

    for copy in (near, near_pot, *passed):
        copy.wait_send()
    own_rows.wait()
    pltpu.make_async_copy(out.at[0], recv.at[row], move_sem.at[3]).wait()
    for ref, sem_a, sem_b in ((rows, row_send, row_recv), (recv, all_send, all_recv)):
        all_but_own = ref.at[pl.ds(0, ref.shape[0] - 1)]
        pltpu.make_async_copy(all_but_own, all_but_own, sem_a).wait()
        pltpu.make_async_copy(all_but_own, all_but_own, sem_b).wait()


def rotate_kernel(recv_v, rows_v, out, out_v, sems):
    high, low = two_parts(jnp.concatenate([rows_v[:, 0], rows_v[:, 1]], axis=0).T)
    matrix = jnp.concatenate([high, high, low], axis=1)
    width = 256
    stores = []
    for at in range(0, 8 * 128, width):
        columns = []
        for r in range(at // 128, (at + width) // 128):
            values = jnp.concatenate([recv_v[:, 0, r], recv_v[:, 1, r]], axis=0)
            high, low = two_parts(values)
            columns.append(jnp.concatenate([high, low, high], axis=0))
        out_v[:, pl.ds(at, width)] = jnp.dot(
            matrix, jnp.concatenate(columns, axis=1), preferred_element_type=jnp.float32
        )
        store = pltpu.make_async_copy(
            out_v.at[:, pl.ds(at, width)], out.at[:, pl.ds(at, width)], sems.at[at // width]
        )
        store.start()
        stores.append(store)
    for store in stores:
        store.wait()


def per_device(bands, orbitals, potential, subspace):
    orbs, planes = orbitals.shape[0], orbitals.shape[1]
    orb = orbitals.reshape(orbs, planes, 2, 8, 128)
    pot = potential.reshape(planes, 2, 8, 128)
    f32 = jnp.float32
    dma = pltpu.SemaphoreType.DMA
    anywhere = pl.BlockSpec(memory_space=pl.ANY)
    slab, shift = 2 * planes, 2 * REACH
    recv, rows = pl.pallas_call(
        functools.partial(filter_kernel, bands),
        out_shape=(
            pltpu.VMEM((bands * orbs, 8, 128), f32),
            pltpu.VMEM((bands, orbs, 128), f32),
        ),
        in_specs=[anywhere] * 3,
        out_specs=(anywhere,) * 2,
        scratch_shapes=[
            *[
                pltpu.VMEM((slab + 2 * (shift + REACH * (DEG - level)), 2, 8, 128), f32)
                for level in range(DEG)
            ],
            pltpu.VMEM((2 * (slab + 2 * shift), 8, 128), f32),
            pltpu.VMEM((slab + 2 * (shift + REACH * (DEG - 1)), 2, 8, 128), f32),
            dma((2,)),
            dma((2,)),
            dma((2, 5)),
            dma((5,)),
            dma((2,)),
            dma,
            dma((7,)),
            dma((7,)),
            dma((4,)),
            dma,
            dma,
            dma,
            dma,
            pltpu.SemaphoreType.REGULAR,
            pltpu.SemaphoreType.REGULAR,
        ],
        compiler_params=pltpu.CompilerParams(
            collective_id=0, has_side_effects=True, vmem_limit_bytes=32 * 2**20
        ),
        name="filter",
    )(*(pltpu.with_memory_space_constraint(a, pltpu.HBM) for a in (orb, pot, subspace)))
    recv = recv.reshape(bands, orbs, 8, 128)
    return pl.pallas_call(
        rotate_kernel,
        out_shape=jax.ShapeDtypeStruct((bands * orbs, 1024), f32),
        in_specs=[pl.BlockSpec(memory_space=pltpu.VMEM)] * 2,
        out_specs=anywhere,
        scratch_shapes=[pltpu.VMEM((bands * orbs, 1024), f32), dma((4,))],
        compiler_params=pltpu.CompilerParams(vmem_limit_bytes=32 * 2**20),
        name="rotate",
    )(*(pltpu.with_memory_space_constraint(a, pltpu.VMEM) for a in (recv, rows)))


def solution(mesh):
    in_specs = (P("band", "dom", None, None), P("dom", None, None), P("band", None))
    out_specs = P(None, ("dom", "band"))
    return jax.shard_map(
        functools.partial(per_device, mesh.shape["band"]),
        mesh=mesh,
        in_specs=in_specs,
        out_specs=out_specs,
        check_vma=False,
    )
```

```python
import functools
import math

import jax
import jax.numpy as jnp
from jax import lax
from jax.experimental import pallas as pl
from jax.experimental.pallas import tpu as pltpu
from jax.sharding import PartitionSpec as P

DEG = 3
REACH = 6
MESH = pl.DeviceIdType.MESH

upper_edge = 10.7
lower_edge = 1.5
bottom_edge = -1.0


def stencil_weights():
    factor_square = math.factorial(6) ** 2
    side_weights = []
    for offset in range(1, 7):
        side_weights.append(
            2.0
            * (-1.0) ** (offset + 1)
            * factor_square
            / (offset * offset * math.factorial(6 - offset) * math.factorial(6 + offset))
        )
    center_weight = -2.0 * sum(side_weights)
    return (center_weight, side_weights)


def filter_scalars(pass_count):
    half_width = (upper_edge - lower_edge) / 2.0
    sigma_now = half_width / (bottom_edge - (upper_edge + lower_edge) / 2.0)
    gamma_value = 2.0 / sigma_now
    scalars = [(sigma_now / half_width, 0.0)]
    for pass_index in range(pass_count - 1):
        sigma_next = 1.0 / (gamma_value - sigma_now)
        scalars.append((2.0 * sigma_next / half_width, sigma_now * sigma_next))
        sigma_now = sigma_next
    return scalars


def two_parts(values):
    high = values.astype(jnp.bfloat16)
    return high, (values - high.astype(jnp.float32)).astype(jnp.bfloat16)


def stencil_matrix(period, axis):
    rows = lax.broadcasted_iota(jnp.int32, (128, 128), 0)
    columns = lax.broadcasted_iota(jnp.int32, (128, 128), 1)
    apart = jnp.abs(rows - columns)
    if period < 128:
        same = jnp.bitwise_or(rows, period - 1) == jnp.bitwise_or(columns, period - 1)
        apart = jnp.where(same, apart, 0)
    apart = jnp.minimum(apart, period - apart)
    matrix = jnp.zeros((128, 128), jnp.float32)
    for k, w in enumerate(stencil_weights()[1], 1):
        matrix = jnp.where(apart == k, jnp.float32(w), matrix)
    high, low = two_parts(matrix)
    return jnp.concatenate([high, high, low], axis=axis)


def filtered_block(window, pot, before, scale, weight, lanes, rows):
    center_weight, side = stencil_weights()
    n = window.shape[0] - 2 * REACH
    mid = window[REACH : REACH + n]
    high, low = two_parts(mid.reshape(n * 16, 128))
    total = jnp.dot(
        jnp.concatenate([high, low, high], axis=1), lanes, preferred_element_type=jnp.float32
    ) + jnp.dot(
        rows, jnp.concatenate([high, low, high], axis=0), preferred_element_type=jnp.float32
    )
    total = total.reshape(n, 2, 8, 128)
    for k in range(1, REACH + 1):
        beside = window[REACH + k : REACH + k + n] + window[REACH - k : REACH - k + n]
        total = total + side[k - 1] * beside
    diag = (-1.5 * center_weight - (upper_edge + lower_edge) / 2.0) * scale
    result = (pot * scale + diag) * mid + (-0.5 * scale) * total
    if before is not None:
        result = result - weight * before
    return result


def filter_kernel(
    bands, orb, pot, sub, recv, rows, p0, p1, p2, out, pot_v,
    near_send, near_recv, far_send, far_recv, pot_send, pot_recv, pass_send, pass_recv,
    move_sem, all_send, all_recv, row_send, row_recv, plane_sem, all_sem,
):
    quarter = orb.shape[1]
    slab, whole = 2 * quarter, 4 * quarter
    band, dom = lax.axis_index("band"), lax.axis_index("dom")
    core, half = lax.rem(dom, 2), lax.div(dom, 2)
    side = 4
    floor = side * side
    zl, x, yx = lax.div(band, floor), lax.rem(band, side), lax.rem(band, floor)
    shift = 2 * REACH
    left = jnp.where(zl < side // 2, 1, 0)
    long = core == left
    base = half * slab
    own_tile = dom * bands + band
    own_plane = lax.div(own_tile, 2)
    scalars = filter_scalars(DEG)
    buffers = (p0, p1, p2)
    rims = tuple(shift + REACH * (DEG - level) for level in range(DEG + 1))
    pot_rim = rims[1]

    def placed(u, count):
        return jnp.where(left == 1, u, slab - count - u)

    load = pltpu.make_async_copy(
        orb.at[core], p0.at[pl.ds(core * quarter + rims[0], quarter)], move_sem.at[0]
    )
    load.start()
    load_pot = pltpu.make_async_copy(
        pot, pot_v.at[pl.ds(core * quarter + pot_rim, quarter)], move_sem.at[1]
    )
    load_pot.start()

    sibling = {"dom": dom + 1 - 2 * core}
    partners = [{"dom": 2 * (1 - half) + k} for k in range(2)]

    def chip_along(shift):
        there = lax.rem(half * side + zl + shift, 2 * side)
        return {
            "band": lax.rem(there, side) * floor + yx,
            "dom": lax.div(there, side) * 2 + core,
        }

    x_line = [
        {"band": band - x + lax.rem(x + dx, side), "dom": dom if dk == 0 else dom + 1 - 2 * core}
        for dx in range(side)
        for dk in range(2)
    ][1:]
    y = lax.div(yx, side)
    y_line = [{"band": band + side * (lax.rem(y + dy, side) - y)} for dy in range(1, side)]
    z_line = [chip_along(dz) for dz in range(1, 2 * side)]
    other_partner = {"dom": 2 * (1 - half) + 1 - core}
    barrier = pltpu.get_barrier_semaphore()
    entered = (*z_line, other_partner, *x_line, *y_line)

    def tell(peers, semaphore):
        for peer in peers:
            pl.semaphore_signal(semaphore, inc=1, device_id=peer, device_id_type=MESH)

    tell(entered, barrier)
    lanes, lines = stencil_matrix(128, 0), stencil_matrix(16, 1)
    pl.semaphore_wait(barrier, len(entered))

    def remote(src, dst, send_sem, recv_sem, peer):
        return pltpu.make_async_remote_copy(
            src_ref=src, dst_ref=dst, send_sem=send_sem, recv_sem=recv_sem,
            device_id=peer, device_id_type=MESH,
        )

    own_rows = pltpu.make_async_copy(sub, rows.at[zl, y, x], move_sem.at[2])
    own_rows.start()
    row_lines = [
        (rows.at[zl, y, x], [{"band": lax.rem(band + d * floor, bands)} for d in range(1, side)]),
        (rows.at[:, y, x], y_line),
        (rows.at[:, :, x], [{"band": band - x + lax.rem(x + d, side)} for d in range(1, side)]),
    ]
    row_copies = [
        [
            remote(
                sub if stage == 0 else part_rows, part_rows,
                row_send.at[stage, at], row_recv.at[stage, at], peer,
            )
            for at, peer in enumerate(peers)
        ]
        for stage, (part_rows, peers) in enumerate(row_lines)
    ]

    def gather_rows(stage):
        if stage > 0:
            for copy in row_copies[stage - 1]:
                copy.wait_recv()
        for copy in row_copies[stage]:
            copy.start()

    gather_rows(0)
    pieces = [(0, REACH)] + [(REACH + 8 * i, 8) for i in range(3)]
    assert sum(n for _, n in pieces) == rims[0]
    far = []
    for o in range(2):
        group = []
        for at, (a, n) in enumerate(pieces):
            group.append(
                remote(
                    orb.at[o, pl.ds(jnp.where(left == 1, quarter - a - n, a), n)],
                    p0.at[pl.ds(placed(-a - n, n) + rims[0], n)],
                    far_send.at[o, at], far_recv.at[at], partners[o],
                )
            )
        n = REACH
        group.append(
            remote(
                orb.at[o, pl.ds(jnp.where(left == 1, 0, quarter - n), n)],
                p0.at[pl.ds(placed(slab, n) + rims[0], n)],
                far_send.at[o, 4], far_recv.at[4], partners[o],
            )
        )
        far.append(group)
    part = pot_rim // 8
    pot_far = [
        remote(
            pot.at[pl.ds(jnp.where(left == 1, quarter - pot_rim, 0) + (2 * x + o) * part, part)],
            pot_v.at[pl.ds(placed(-pot_rim, pot_rim) + pot_rim + (2 * x + o) * part, part)],
            pot_send.at[o], pot_recv, partners[o],
        )
        for o in range(2)
    ]
    mine = pot_v.at[pl.ds(placed(-pot_rim, pot_rim) + pot_rim + (2 * x + core) * part, part)]

    @pl.when(long)
    def _():
        for o in range(2):
            pot_far[o].start()
        for o in range(2):
            far[o][0].start()

    @pl.when(jnp.logical_not(long))
    def _():
        for o in range(2):
            far[o][4].start()

    near = remote(
        orb.at[1 - core], p0.at[pl.ds(core * quarter + rims[0], quarter)],
        near_send.at[0], near_recv.at[0], sibling,
    )
    near_pot = remote(
        pot, pot_v.at[pl.ds(core * quarter + pot_rim, quarter)],
        near_send.at[1], near_recv.at[1], sibling,
    )
    near.start()
    near_pot.start()

    @pl.when(long)
    def _():
        for at in range(1, 4):
            for o in range(2):
                far[o][at].start()

    tell(y_line, plane_sem)

    step = 8

    def apply(level, u, blocks):
        scale, weight = scalars[level]

        def body(i, c):
            at = placed(u + i * step, step)
            before = None
            if level > 0:
                before = buffers[level - 1][pl.ds(at + rims[level - 1], step)]
            window = buffers[level][pl.ds(at + rims[level] - REACH, step + 2 * REACH)]
            pairs = filtered_block(
                window, pot_v[pl.ds(at + pot_rim, step)], before, scale, weight, lanes, lines
            )
            if level < DEG - 1:
                buffers[level + 1][pl.ds(at + rims[level + 1], step)] = pairs
            else:
                out[pl.ds(2 * (at + rims[DEG]), 2 * step)] = pairs.reshape(2 * step, 8, 128)
            return c

        lax.fori_loop(0, blocks, body, 0)

    row = 2 * band + core

    def spread(u, count):
        start = placed(u, count)
        tiles = 2 * count

        def send(i, c):
            at = lax.rem(i + yx * (tiles // floor), tiles)
            tile = lax.rem(2 * (base + start) + at + 2 * whole, 2 * whole)
            src = out.at[2 * (start + rims[DEG]) + at]

            @pl.when(tile != own_tile)
            def _():
                peer = {"band": lax.rem(tile, bands), "dom": lax.div(tile, bands)}
                remote(src, recv.at[row], all_send, all_recv, peer).start()

            @pl.when(tile == own_tile)
            def _():
                pltpu.make_async_copy(src, recv.at[row], move_sem.at[3]).start()

            return c

        lax.fori_loop(0, tiles, send, 0)

    def advance(u):
        for level in range(DEG):
            apply(level, u + level * REACH, 1)
        spread(u + (DEG - 1) * REACH, 8)

    load.wait()
    load_pot.wait()
    near.wait_recv()
    near_pot.wait_recv()
    pl.semaphore_wait(plane_sem, len(y_line))
    tell(z_line, all_sem)
    apply(0, 8, 6)
    apply(1, 14, 4)
    apply(1, 42, 1)
    apply(2, 20, 3)
    pl.semaphore_wait(all_sem, len(z_line))

    pot_far[0].wait_recv()
    passed = [
        remote(mine, mine, pass_send.at[at], pass_recv.at[at], peer)
        for at, peer in enumerate(x_line)
    ]
    for copy in passed:
        copy.start()

    far[0][4].wait_recv()
    apply(0, slab - 8, 1)
    apply(1, slab - 14, 1)
    apply(2, slab - 20, 1)
    spread(slab - 20, 8)
    for at in range(4):
        if at == 1:
            own_rows.wait()
            gather_rows(1)
            for copy in passed:
                copy.wait_recv()
        if at == 3:
            gather_rows(2)
        far[0][at].wait_recv()
        advance(-8 * at)
    spread(20, 24)

    @pl.when(long)
    def _():
        for o in range(2):
            pot_far[o].wait_send()
            for at in range(4):
                far[o][at].wait_send()

    @pl.when(jnp.logical_not(long))
    def _():
        for o in range(2):
            far[o][4].wait_send()

    for copy in (near, near_pot, *passed):
        copy.wait_send()
    for copy in row_copies[2]:
        copy.wait_recv()
    for copies in row_copies:
        for copy in copies:
            copy.wait_send()
    pltpu.make_async_copy(out.at[0], recv.at[row], move_sem.at[3]).wait()
    all_but_own = recv.at[pl.ds(0, recv.shape[0] - 1)]
    pltpu.make_async_copy(all_but_own, all_but_own, all_send).wait()
    pltpu.make_async_copy(all_but_own, all_but_own, all_recv).wait()


def rotate_kernel(recv_v, rows_v, out, out_v, sems):
    high, low = two_parts(jnp.concatenate([rows_v[:, 0], rows_v[:, 1]], axis=0).T)
    matrix = jnp.concatenate([high, high, low], axis=1)
    width = 256
    stores = []
    for at in range(0, 8 * 128, width):
        columns = []
        for r in range(at // 128, (at + width) // 128):
            values = jnp.concatenate([recv_v[:, 0, r], recv_v[:, 1, r]], axis=0)
            high, low = two_parts(values)
            columns.append(jnp.concatenate([high, low, high], axis=0))
        out_v[:, pl.ds(at, width)] = jnp.dot(
            matrix, jnp.concatenate(columns, axis=1), preferred_element_type=jnp.float32
        )
        store = pltpu.make_async_copy(
            out_v.at[:, pl.ds(at, width)], out.at[:, pl.ds(at, width)], sems.at[at // width]
        )
        store.start()
        stores.append(store)
    for store in stores:
        store.wait()


def per_device(bands, orbitals, potential, subspace):
    orbs, planes = orbitals.shape[0], orbitals.shape[1]
    orb = orbitals.reshape(orbs, planes, 2, 8, 128)
    pot = potential.reshape(planes, 2, 8, 128)
    f32 = jnp.float32
    dma = pltpu.SemaphoreType.DMA
    anywhere = pl.BlockSpec(memory_space=pl.ANY)
    slab, shift = 2 * planes, 2 * REACH
    recv, rows = pl.pallas_call(
        functools.partial(filter_kernel, bands),
        out_shape=(
            pltpu.VMEM((bands * orbs, 8, 128), f32),
            pltpu.VMEM((4, 4, 4, orbs, 128), f32),
        ),
        in_specs=[anywhere] * 3,
        out_specs=(anywhere,) * 2,
        scratch_shapes=[
            *[
                pltpu.VMEM((slab + 2 * (shift + REACH * (DEG - level)), 2, 8, 128), f32)
                for level in range(DEG)
            ],
            pltpu.VMEM((2 * (slab + 2 * shift), 8, 128), f32),
            pltpu.VMEM((slab + 2 * (shift + REACH * (DEG - 1)), 2, 8, 128), f32),
            dma((2,)),
            dma((2,)),
            dma((2, 5)),
            dma((5,)),
            dma((2,)),
            dma,
            dma((7,)),
            dma((7,)),
            dma((4,)),
            dma,
            dma,
            dma((3, 3)),
            dma((3, 3)),
            pltpu.SemaphoreType.REGULAR,
            pltpu.SemaphoreType.REGULAR,
        ],
        compiler_params=pltpu.CompilerParams(
            collective_id=0, has_side_effects=True, vmem_limit_bytes=32 * 2**20
        ),
        name="filter",
    )(*(pltpu.with_memory_space_constraint(a, pltpu.HBM) for a in (orb, pot, subspace)))
    recv, rows = recv.reshape(bands, orbs, 8, 128), rows.reshape(bands, orbs, 128)
    return pl.pallas_call(
        rotate_kernel,
        out_shape=jax.ShapeDtypeStruct((bands * orbs, 1024), f32),
        in_specs=[pl.BlockSpec(memory_space=pltpu.VMEM)] * 2,
        out_specs=anywhere,
        scratch_shapes=[pltpu.VMEM((bands * orbs, 1024), f32), dma((4,))],
        compiler_params=pltpu.CompilerParams(vmem_limit_bytes=32 * 2**20),
        name="rotate",
    )(*(pltpu.with_memory_space_constraint(a, pltpu.VMEM) for a in (recv, rows)))


def solution(mesh):
    in_specs = (P("band", "dom", None, None), P("dom", None, None), P("band", None))
    out_specs = P(None, ("dom", "band"))
    return jax.shard_map(
        functools.partial(per_device, mesh.shape["band"]),
        mesh=mesh,
        in_specs=in_specs,
        out_specs=out_specs,
        check_vma=False,
    )
```

```python
import functools
import math

import jax
import jax.numpy as jnp
from jax import lax
from jax.experimental import pallas as pl
from jax.experimental.pallas import tpu as pltpu
from jax.sharding import PartitionSpec as P

DEG = 3
REACH = 6
MESH = pl.DeviceIdType.MESH

upper_edge = 10.7
lower_edge = 1.5
bottom_edge = -1.0


def stencil_weights():
    factor_square = math.factorial(6) ** 2
    side_weights = []
    for offset in range(1, 7):
        side_weights.append(
            2.0
            * (-1.0) ** (offset + 1)
            * factor_square
            / (offset * offset * math.factorial(6 - offset) * math.factorial(6 + offset))
        )
    center_weight = -2.0 * sum(side_weights)
    return (center_weight, side_weights)


def filter_scalars(pass_count):
    half_width = (upper_edge - lower_edge) / 2.0
    sigma_now = half_width / (bottom_edge - (upper_edge + lower_edge) / 2.0)
    gamma_value = 2.0 / sigma_now
    scalars = [(sigma_now / half_width, 0.0)]
    for pass_index in range(pass_count - 1):
        sigma_next = 1.0 / (gamma_value - sigma_now)
        scalars.append((2.0 * sigma_next / half_width, sigma_now * sigma_next))
        sigma_now = sigma_next
    return scalars


def two_parts(values):
    high = values.astype(jnp.bfloat16)
    return high, (values - high.astype(jnp.float32)).astype(jnp.bfloat16)


def stencil_matrix(period, axis):
    rows = lax.broadcasted_iota(jnp.int32, (128, 128), 0)
    columns = lax.broadcasted_iota(jnp.int32, (128, 128), 1)
    apart = jnp.abs(rows - columns)
    if period < 128:
        same = jnp.bitwise_or(rows, period - 1) == jnp.bitwise_or(columns, period - 1)
        apart = jnp.where(same, apart, 0)
    apart = jnp.minimum(apart, period - apart)
    matrix = jnp.zeros((128, 128), jnp.float32)
    for k, w in enumerate(stencil_weights()[1], 1):
        matrix = jnp.where(apart == k, jnp.float32(w), matrix)
    high, low = two_parts(matrix)
    return jnp.concatenate([high, high, low], axis=axis)


def filtered_block(window, pot, before, scale, weight, lanes, rows):
    center_weight, side = stencil_weights()
    n = window.shape[0] - 2 * REACH
    mid = window[REACH : REACH + n]
    high, low = two_parts(mid.reshape(n * 16, 128))
    total = jnp.dot(
        jnp.concatenate([high, low, high], axis=1), lanes, preferred_element_type=jnp.float32
    ) + jnp.dot(
        rows, jnp.concatenate([high, low, high], axis=0), preferred_element_type=jnp.float32
    )
    total = total.reshape(n, 2, 8, 128)
    for k in range(1, REACH + 1):
        beside = window[REACH + k : REACH + k + n] + window[REACH - k : REACH - k + n]
        total = total + side[k - 1] * beside
    diag = (-1.5 * center_weight - (upper_edge + lower_edge) / 2.0) * scale
    result = (pot * scale + diag) * mid + (-0.5 * scale) * total
    if before is not None:
        result = result - weight * before
    return result


def filter_kernel(
    bands, orb, pot, sub, recv, rows, p0, p1, p2, out, pot_v,
    near_send, near_recv, far_send, far_recv, pot_send, pot_recv, pass_send, pass_recv,
    move_sem, all_send, all_recv, row_send, row_recv, plane_sem, all_sem,
):
    quarter = orb.shape[1]
    slab, whole = 2 * quarter, 4 * quarter
    band, dom = lax.axis_index("band"), lax.axis_index("dom")
    core, half = lax.rem(dom, 2), lax.div(dom, 2)
    side = 4
    floor = side * side
    zl, x, yx = lax.div(band, floor), lax.rem(band, side), lax.rem(band, floor)
    shift = 2 * REACH
    left = jnp.where(zl < side // 2, 1, 0)
    long = core == left
    base = half * slab
    own_tile = dom * bands + band
    own_plane = lax.div(own_tile, 2)
    scalars = filter_scalars(DEG)
    buffers = (p0, p1, p2)
    rims = tuple(shift + REACH * (DEG - level) for level in range(DEG + 1))
    pot_rim = rims[1]

    def placed(u, count):
        return jnp.where(left == 1, u, slab - count - u)

    load = pltpu.make_async_copy(
        orb.at[core], p0.at[pl.ds(core * quarter + rims[0], quarter)], move_sem.at[0]
    )
    load.start()
    load_pot = pltpu.make_async_copy(
        pot, pot_v.at[pl.ds(core * quarter + pot_rim, quarter)], move_sem.at[1]
    )
    load_pot.start()

    sibling = {"dom": dom + 1 - 2 * core}
    partners = [{"dom": 2 * (1 - half) + k} for k in range(2)]

    def chip_along(shift):
        there = lax.rem(half * side + zl + shift, 2 * side)
        return {
            "band": lax.rem(there, side) * floor + yx,
            "dom": lax.div(there, side) * 2 + core,
        }

    x_line = [
        {"band": band - x + lax.rem(x + dx, side), "dom": dom if dk == 0 else dom + 1 - 2 * core}
        for dx in range(side)
        for dk in range(2)
    ][1:]
    y = lax.div(yx, side)
    y_line = [{"band": band + side * (lax.rem(y + dy, side) - y)} for dy in range(1, side)]
    z_line = [chip_along(dz) for dz in range(1, 2 * side)]
    other_partner = {"dom": 2 * (1 - half) + 1 - core}
    barrier = pltpu.get_barrier_semaphore()
    entered = (*z_line, other_partner, *x_line, *y_line)

    def tell(peers, semaphore):
        for peer in peers:
            pl.semaphore_signal(semaphore, inc=1, device_id=peer, device_id_type=MESH)

    tell(entered, barrier)
    lanes, lines = stencil_matrix(128, 0), stencil_matrix(16, 1)
    pl.semaphore_wait(barrier, len(entered))

    def remote(src, dst, send_sem, recv_sem, peer):
        return pltpu.make_async_remote_copy(
            src_ref=src, dst_ref=dst, send_sem=send_sem, recv_sem=recv_sem,
            device_id=peer, device_id_type=MESH,
        )

    own_rows = pltpu.make_async_copy(sub, rows.at[zl, y, x], move_sem.at[2])
    own_rows.start()
    row_lines = [
        (rows.at[zl, y, x], [{"band": lax.rem(band + d * floor, bands)} for d in range(1, side)]),
        (rows.at[:, y, x], y_line),
        (rows.at[:, :, x], [{"band": band - x + lax.rem(x + d, side)} for d in range(1, side)]),
    ]
    row_copies = [
        [
            remote(
                sub if stage == 0 else part_rows, part_rows,
                row_send.at[stage, at], row_recv.at[stage, at], peer,
            )
            for at, peer in enumerate(peers)
        ]
        for stage, (part_rows, peers) in enumerate(row_lines)
    ]

    def gather_rows(stage):
        if stage > 0:
            for copy in row_copies[stage - 1]:
                copy.wait_recv()
        for copy in row_copies[stage]:
            copy.start()

    gather_rows(0)
    pieces = [(0, REACH)] + [(REACH + 8 * i, 8) for i in range(3)]
    assert sum(n for _, n in pieces) == rims[0]
    far = []
    for o in range(2):
        group = []
        for at, (a, n) in enumerate(pieces):
            group.append(
                remote(
                    orb.at[o, pl.ds(jnp.where(left == 1, quarter - a - n, a), n)],
                    p0.at[pl.ds(placed(-a - n, n) + rims[0], n)],
                    far_send.at[o, at], far_recv.at[at], partners[o],
                )
            )
        n = REACH
        group.append(
            remote(
                orb.at[o, pl.ds(jnp.where(left == 1, 0, quarter - n), n)],
                p0.at[pl.ds(placed(slab, n) + rims[0], n)],
                far_send.at[o, 4], far_recv.at[4], partners[o],
            )
        )
        far.append(group)
    part = pot_rim // 8
    pot_far = [
        remote(
            pot.at[pl.ds(jnp.where(left == 1, quarter - pot_rim, 0) + (2 * x + o) * part, part)],
            pot_v.at[pl.ds(placed(-pot_rim, pot_rim) + pot_rim + (2 * x + o) * part, part)],
            pot_send.at[o], pot_recv, partners[o],
        )
        for o in range(2)
    ]
    mine = pot_v.at[pl.ds(placed(-pot_rim, pot_rim) + pot_rim + (2 * x + core) * part, part)]

    @pl.when(long)
    def _():
        for o in range(2):
            pot_far[o].start()
        for o in range(2):
            far[o][0].start()

    @pl.when(jnp.logical_not(long))
    def _():
        for o in range(2):
            far[o][4].start()

    near = remote(
        orb.at[1 - core], p0.at[pl.ds(core * quarter + rims[0], quarter)],
        near_send.at[0], near_recv.at[0], sibling,
    )
    near_pot = remote(
        pot, pot_v.at[pl.ds(core * quarter + pot_rim, quarter)],
        near_send.at[1], near_recv.at[1], sibling,
    )
    near.start()
    near_pot.start()

    @pl.when(long)
    def _():
        for at in range(1, 4):
            for o in range(2):
                far[o][at].start()

    tell(y_line, plane_sem)

    step = 8

    def apply(level, u, blocks):
        scale, weight = scalars[level]

        def body(i, c):
            at = placed(u + i * step, step)
            before = None
            if level > 0:
                before = buffers[level - 1][pl.ds(at + rims[level - 1], step)]
            window = buffers[level][pl.ds(at + rims[level] - REACH, step + 2 * REACH)]
            pairs = filtered_block(
                window, pot_v[pl.ds(at + pot_rim, step)], before, scale, weight, lanes, lines
            )
            if level < DEG - 1:
                buffers[level + 1][pl.ds(at + rims[level + 1], step)] = pairs
            else:
                out[pl.ds(2 * (at + rims[DEG]), 2 * step)] = pairs.reshape(2 * step, 8, 128)
            return c

        lax.fori_loop(0, blocks, body, 0)

    row = 2 * band + core

    def spread(u, count, first, number):
        start = placed(u, count)
        tiles = 2 * count

        def send(i, c):
            at = lax.rem(i + yx * (tiles // floor), tiles)
            tile = lax.rem(2 * (base + start) + at + 2 * whole, 2 * whole)
            src = out.at[2 * (start + rims[DEG]) + at]

            @pl.when(tile != own_tile)
            def _():
                peer = {"band": lax.rem(tile, bands), "dom": lax.div(tile, bands)}
                remote(src, recv.at[row], all_send, all_recv, peer).start()

            @pl.when(tile == own_tile)
            def _():
                pltpu.make_async_copy(src, recv.at[row], move_sem.at[3]).start()

            return c

        lax.fori_loop(first, first + number, send, 0)

    def advance(u):
        for level in range(DEG):
            apply(level, u + level * REACH, 1)

    load.wait()
    load_pot.wait()
    near.wait_recv()
    near_pot.wait_recv()
    pl.semaphore_wait(plane_sem, len(y_line))
    tell(z_line, all_sem)
    apply(0, 8, 6)
    apply(1, 14, 4)
    apply(1, 42, 1)
    apply(2, 20, 3)
    pl.semaphore_wait(all_sem, len(z_line))
    spread(20, 24, 0, 12)

    pot_far[0].wait_recv()
    passed = [
        remote(mine, mine, pass_send.at[at], pass_recv.at[at], peer)
        for at, peer in enumerate(x_line)
    ]
    for copy in passed:
        copy.start()

    far[0][4].wait_recv()
    apply(0, slab - 8, 1)
    apply(1, slab - 14, 1)
    apply(2, slab - 20, 1)
    spread(slab - 20, 8, 0, 12)
    for at in range(4):
        if at == 1:
            own_rows.wait()
            gather_rows(1)
            for copy in passed:
                copy.wait_recv()
        if at == 3:
            gather_rows(2)
        far[0][at].wait_recv()
        advance(-8 * at)
        if at < 3:
            spread(12 - 8 * at, 8, 0, 12)
        if at == 1:
            spread(20, 24, 12, 12)

    def rest(i, c):
        spread(-12, 8, 4 * i, 4)
        spread(20, 24, 24 + 6 * i, 6)
        for u in (slab - 20, 12, 4, -4):
            spread(u, 8, 12 + i, 1)
        return c

    lax.fori_loop(0, 4, rest, 0)

    @pl.when(long)
    def _():
        for o in range(2):
            pot_far[o].wait_send()
            for at in range(4):
                far[o][at].wait_send()

    @pl.when(jnp.logical_not(long))
    def _():
        for o in range(2):
            far[o][4].wait_send()

    for copy in (near, near_pot, *passed):
        copy.wait_send()
    for copy in row_copies[2]:
        copy.wait_recv()
    for copies in row_copies:
        for copy in copies:
            copy.wait_send()
    pltpu.make_async_copy(out.at[0], recv.at[row], move_sem.at[3]).wait()
    all_but_own = recv.at[pl.ds(0, recv.shape[0] - 1)]
    pltpu.make_async_copy(all_but_own, all_but_own, all_send).wait()
    pltpu.make_async_copy(all_but_own, all_but_own, all_recv).wait()


def rotate_kernel(recv_v, rows_v, out, out_v, sems):
    high, low = two_parts(jnp.concatenate([rows_v[:, 0], rows_v[:, 1]], axis=0).T)
    matrix = jnp.concatenate([high, high, low], axis=1)
    width = 256
    stores = []
    for at in range(0, 8 * 128, width):
        columns = []
        for r in range(at // 128, (at + width) // 128):
            values = jnp.concatenate([recv_v[:, 0, r], recv_v[:, 1, r]], axis=0)
            high, low = two_parts(values)
            columns.append(jnp.concatenate([high, low, high], axis=0))
        out_v[:, pl.ds(at, width)] = jnp.dot(
            matrix, jnp.concatenate(columns, axis=1), preferred_element_type=jnp.float32
        )
        store = pltpu.make_async_copy(
            out_v.at[:, pl.ds(at, width)], out.at[:, pl.ds(at, width)], sems.at[at // width]
        )
        store.start()
        stores.append(store)
    for store in stores:
        store.wait()


def per_device(bands, orbitals, potential, subspace):
    orbs, planes = orbitals.shape[0], orbitals.shape[1]
    orb = orbitals.reshape(orbs, planes, 2, 8, 128)
    pot = potential.reshape(planes, 2, 8, 128)
    f32 = jnp.float32
    dma = pltpu.SemaphoreType.DMA
    anywhere = pl.BlockSpec(memory_space=pl.ANY)
    slab, shift = 2 * planes, 2 * REACH
    recv, rows = pl.pallas_call(
        functools.partial(filter_kernel, bands),
        out_shape=(
            pltpu.VMEM((bands * orbs, 8, 128), f32),
            pltpu.VMEM((4, 4, 4, orbs, 128), f32),
        ),
        in_specs=[anywhere] * 3,
        out_specs=(anywhere,) * 2,
        scratch_shapes=[
            *[
                pltpu.VMEM((slab + 2 * (shift + REACH * (DEG - level)), 2, 8, 128), f32)
                for level in range(DEG)
            ],
            pltpu.VMEM((2 * (slab + 2 * shift), 8, 128), f32),
            pltpu.VMEM((slab + 2 * (shift + REACH * (DEG - 1)), 2, 8, 128), f32),
            dma((2,)),
            dma((2,)),
            dma((2, 5)),
            dma((5,)),
            dma((2,)),
            dma,
            dma((7,)),
            dma((7,)),
            dma((4,)),
            dma,
            dma,
            dma((3, 3)),
            dma((3, 3)),
            pltpu.SemaphoreType.REGULAR,
            pltpu.SemaphoreType.REGULAR,
        ],
        compiler_params=pltpu.CompilerParams(
            collective_id=0, has_side_effects=True, vmem_limit_bytes=32 * 2**20
        ),
        name="filter",
    )(*(pltpu.with_memory_space_constraint(a, pltpu.HBM) for a in (orb, pot, subspace)))
    recv, rows = recv.reshape(bands, orbs, 8, 128), rows.reshape(bands, orbs, 128)
    return pl.pallas_call(
        rotate_kernel,
        out_shape=jax.ShapeDtypeStruct((bands * orbs, 1024), f32),
        in_specs=[pl.BlockSpec(memory_space=pltpu.VMEM)] * 2,
        out_specs=anywhere,
        scratch_shapes=[pltpu.VMEM((bands * orbs, 1024), f32), dma((4,))],
        compiler_params=pltpu.CompilerParams(vmem_limit_bytes=32 * 2**20),
        name="rotate",
    )(*(pltpu.with_memory_space_constraint(a, pltpu.VMEM) for a in (recv, rows)))


def solution(mesh):
    in_specs = (P("band", "dom", None, None), P("dom", None, None), P("band", None))
    out_specs = P(None, ("dom", "band"))
    return jax.shard_map(
        functools.partial(per_device, mesh.shape["band"]),
        mesh=mesh,
        in_specs=in_specs,
        out_specs=out_specs,
        check_vma=False,
    )
```

```python
import functools
import math

import jax
import jax.numpy as jnp
from jax import lax
from jax.experimental import pallas as pl
from jax.experimental.pallas import tpu as pltpu
from jax.sharding import PartitionSpec as P

DEG = 3
REACH = 6
MESH = pl.DeviceIdType.MESH

upper_edge = 10.7
lower_edge = 1.5
bottom_edge = -1.0


def stencil_weights():
    factor_square = math.factorial(6) ** 2
    side_weights = []
    for offset in range(1, 7):
        side_weights.append(
            2.0
            * (-1.0) ** (offset + 1)
            * factor_square
            / (offset * offset * math.factorial(6 - offset) * math.factorial(6 + offset))
        )
    center_weight = -2.0 * sum(side_weights)
    return (center_weight, side_weights)


def filter_scalars(pass_count):
    half_width = (upper_edge - lower_edge) / 2.0
    sigma_now = half_width / (bottom_edge - (upper_edge + lower_edge) / 2.0)
    gamma_value = 2.0 / sigma_now
    scalars = [(sigma_now / half_width, 0.0)]
    for pass_index in range(pass_count - 1):
        sigma_next = 1.0 / (gamma_value - sigma_now)
        scalars.append((2.0 * sigma_next / half_width, sigma_now * sigma_next))
        sigma_now = sigma_next
    return scalars


def two_parts(values):
    high = values.astype(jnp.bfloat16)
    return high, (values - high.astype(jnp.float32)).astype(jnp.bfloat16)


def stencil_matrix(period, axis):
    rows = lax.broadcasted_iota(jnp.int32, (128, 128), 0)
    columns = lax.broadcasted_iota(jnp.int32, (128, 128), 1)
    apart = jnp.abs(rows - columns)
    if period < 128:
        same = jnp.bitwise_or(rows, period - 1) == jnp.bitwise_or(columns, period - 1)
        apart = jnp.where(same, apart, 0)
    apart = jnp.minimum(apart, period - apart)
    matrix = jnp.zeros((128, 128), jnp.float32)
    for k, w in enumerate(stencil_weights()[1], 1):
        matrix = jnp.where(apart == k, jnp.float32(w), matrix)
    high, low = two_parts(matrix)
    return jnp.concatenate([high, high, low], axis=axis)


def filtered_block(window, pot, before, scale, weight, lanes, rows):
    center_weight, side = stencil_weights()
    n = window.shape[0] - 2 * REACH
    mid = window[REACH : REACH + n]
    high, low = two_parts(mid.reshape(n * 16, 128))
    total = jnp.dot(
        jnp.concatenate([high, low, high], axis=1), lanes, preferred_element_type=jnp.float32
    ) + jnp.dot(
        rows, jnp.concatenate([high, low, high], axis=0), preferred_element_type=jnp.float32
    )
    total = total.reshape(n, 2, 8, 128)
    for k in range(1, REACH + 1):
        beside = window[REACH + k : REACH + k + n] + window[REACH - k : REACH - k + n]
        total = total + side[k - 1] * beside
    diag = (-1.5 * center_weight - (upper_edge + lower_edge) / 2.0) * scale
    result = (pot * scale + diag) * mid + (-0.5 * scale) * total
    if before is not None:
        result = result - weight * before
    return result


def filter_kernel(
    bands, orb, pot, sub, out, rows, p0, p1, p2, pot_v,
    near_send, near_recv, far_send, far_recv, pot_send, pot_recv, pass_send, pass_recv,
    move_sem, row_send, row_recv,
):
    quarter = orb.shape[1]
    slab, whole = 2 * quarter, 4 * quarter
    band, dom = lax.axis_index("band"), lax.axis_index("dom")
    core, half = lax.rem(dom, 2), lax.div(dom, 2)
    side = 4
    floor = side * side
    zl, x, yx = lax.div(band, floor), lax.rem(band, side), lax.rem(band, floor)
    shift = 2 * REACH
    left = jnp.where(zl < side // 2, 1, 0)
    long = core == left
    base = half * slab
    own_tile = dom * bands + band
    own_plane = lax.div(own_tile, 2)
    scalars = filter_scalars(DEG)
    buffers = (p0, p1, p2)
    rims = tuple(shift + REACH * (DEG - level) for level in range(DEG + 1))
    pot_rim = rims[1]

    def placed(u, count):
        return jnp.where(left == 1, u, slab - count - u)

    load = pltpu.make_async_copy(
        orb.at[core], p0.at[pl.ds(core * quarter + rims[0], quarter)], move_sem.at[0]
    )
    load.start()
    load_pot = pltpu.make_async_copy(
        pot, pot_v.at[pl.ds(core * quarter + pot_rim, quarter)], move_sem.at[1]
    )
    load_pot.start()

    sibling = {"dom": dom + 1 - 2 * core}
    partners = [{"dom": 2 * (1 - half) + k} for k in range(2)]

    def chip_along(shift):
        there = lax.rem(half * side + zl + shift, 2 * side)
        return {
            "band": lax.rem(there, side) * floor + yx,
            "dom": lax.div(there, side) * 2 + core,
        }

    x_line = [
        {"band": band - x + lax.rem(x + dx, side), "dom": dom if dk == 0 else dom + 1 - 2 * core}
        for dx in range(side)
        for dk in range(2)
    ][1:]
    y = lax.div(yx, side)
    y_line = [{"band": band + side * (lax.rem(y + dy, side) - y)} for dy in range(1, side)]
    z_line = [chip_along(dz) for dz in range(1, 2 * side)]
    other_partner = {"dom": 2 * (1 - half) + 1 - core}
    barrier = pltpu.get_barrier_semaphore()
    entered = (*z_line, other_partner, *x_line, *y_line)

    def tell(peers, semaphore):
        for peer in peers:
            pl.semaphore_signal(semaphore, inc=1, device_id=peer, device_id_type=MESH)

    tell(entered, barrier)
    lanes, lines = stencil_matrix(128, 0), stencil_matrix(16, 1)
    pl.semaphore_wait(barrier, len(entered))

    def remote(src, dst, send_sem, recv_sem, peer):
        return pltpu.make_async_remote_copy(
            src_ref=src, dst_ref=dst, send_sem=send_sem, recv_sem=recv_sem,
            device_id=peer, device_id_type=MESH,
        )

    own_rows = pltpu.make_async_copy(sub, rows.at[zl, y, x], move_sem.at[2])
    own_rows.start()
    row_lines = [
        (rows.at[zl, y, x], [{"band": lax.rem(band + d * floor, bands)} for d in range(1, side)]),
        (rows.at[:, y, x], y_line),
        (rows.at[:, :, x], [{"band": band - x + lax.rem(x + d, side)} for d in range(1, side)]),
    ]
    row_copies = [
        [
            remote(
                sub if stage == 0 else part_rows, part_rows,
                row_send.at[stage, at], row_recv.at[stage, at], peer,
            )
            for at, peer in enumerate(peers)
        ]
        for stage, (part_rows, peers) in enumerate(row_lines)
    ]

    def gather_rows(stage):
        if stage > 0:
            for copy in row_copies[stage - 1]:
                copy.wait_recv()
        for copy in row_copies[stage]:
            copy.start()

    gather_rows(0)
    pieces = [(0, REACH)] + [(REACH + 8 * i, 8) for i in range(3)]
    assert sum(n for _, n in pieces) == rims[0]
    far = []
    for o in range(2):
        group = []
        for at, (a, n) in enumerate(pieces):
            group.append(
                remote(
                    orb.at[o, pl.ds(jnp.where(left == 1, quarter - a - n, a), n)],
                    p0.at[pl.ds(placed(-a - n, n) + rims[0], n)],
                    far_send.at[o, at], far_recv.at[at], partners[o],
                )
            )
        n = REACH
        group.append(
            remote(
                orb.at[o, pl.ds(jnp.where(left == 1, 0, quarter - n), n)],
                p0.at[pl.ds(placed(slab, n) + rims[0], n)],
                far_send.at[o, 4], far_recv.at[4], partners[o],
            )
        )
        far.append(group)
    part = pot_rim // 8
    pot_far = [
        remote(
            pot.at[pl.ds(jnp.where(left == 1, quarter - pot_rim, 0) + (2 * x + o) * part, part)],
            pot_v.at[pl.ds(placed(-pot_rim, pot_rim) + pot_rim + (2 * x + o) * part, part)],
            pot_send.at[o], pot_recv, partners[o],
        )
        for o in range(2)
    ]
    mine = pot_v.at[pl.ds(placed(-pot_rim, pot_rim) + pot_rim + (2 * x + core) * part, part)]

    @pl.when(long)
    def _():
        for o in range(2):
            pot_far[o].start()
        for o in range(2):
            far[o][0].start()

    @pl.when(jnp.logical_not(long))
    def _():
        for o in range(2):
            far[o][4].start()

    near = remote(
        orb.at[1 - core], p0.at[pl.ds(core * quarter + rims[0], quarter)],
        near_send.at[0], near_recv.at[0], sibling,
    )
    near_pot = remote(
        pot, pot_v.at[pl.ds(core * quarter + pot_rim, quarter)],
        near_send.at[1], near_recv.at[1], sibling,
    )
    near.start()
    near_pot.start()

    @pl.when(long)
    def _():
        for at in range(1, 4):
            for o in range(2):
                far[o][at].start()


    step = 8

    def apply(level, u, blocks):
        scale, weight = scalars[level]

        def body(i, c):
            at = placed(u + i * step, step)
            before = None
            if level > 0:
                before = buffers[level - 1][pl.ds(at + rims[level - 1], step)]
            window = buffers[level][pl.ds(at + rims[level] - REACH, step + 2 * REACH)]
            pairs = filtered_block(
                window, pot_v[pl.ds(at + pot_rim, step)], before, scale, weight, lanes, lines
            )
            if level < DEG - 1:
                buffers[level + 1][pl.ds(at + rims[level + 1], step)] = pairs
            else:
                out[pl.ds(2 * (at + rims[DEG]), 2 * step)] = pairs.reshape(2 * step, 8, 128)
            return c

        lax.fori_loop(0, blocks, body, 0)

    def advance(u):
        for level in range(DEG):
            apply(level, u + level * REACH, 1)

    load.wait()
    load_pot.wait()
    near.wait_recv()
    near_pot.wait_recv()
    apply(0, 8, 6)
    apply(1, 14, 4)
    apply(1, 42, 1)
    apply(2, 20, 3)

    pot_far[0].wait_recv()
    passed = [
        remote(mine, mine, pass_send.at[at], pass_recv.at[at], peer)
        for at, peer in enumerate(x_line)
    ]
    for copy in passed:
        copy.start()

    far[0][4].wait_recv()
    apply(0, slab - 8, 1)
    apply(1, slab - 14, 1)
    apply(2, slab - 20, 1)
    for at in range(4):
        if at == 1:
            own_rows.wait()
            gather_rows(1)
            for copy in passed:
                copy.wait_recv()
        if at == 3:
            gather_rows(2)
        far[0][at].wait_recv()
        advance(-8 * at)

    @pl.when(long)
    def _():
        for o in range(2):
            pot_far[o].wait_send()
            for at in range(4):
                far[o][at].wait_send()

    @pl.when(jnp.logical_not(long))
    def _():
        for o in range(2):
            far[o][4].wait_send()

    for copy in (near, near_pot, *passed):
        copy.wait_send()
    for copy in row_copies[2]:
        copy.wait_recv()
    for copies in row_copies:
        for copy in copies:
            copy.wait_send()


def spread_kernel(bands, out, recv, move_sem, all_send, all_recv, plane_sem, all_sem):
    band, dom = lax.axis_index("band"), lax.axis_index("dom")
    core, half = lax.rem(dom, 2), lax.div(dom, 2)
    side = 4
    floor = side * side
    zl, x, yx = lax.div(band, floor), lax.rem(band, side), lax.rem(band, floor)
    tiles = 2 * bands
    rim = lax.div(out.shape[0] - tiles, 2)
    left = jnp.where(zl < side // 2, 1, 0)
    own_tile = dom * bands + band
    x_line = [
        {"band": band - x + lax.rem(x + dx, side), "dom": dom if dk == 0 else dom + 1 - 2 * core}
        for dx in range(side)
        for dk in range(2)
    ][1:]
    y = lax.div(yx, side)
    y_line = [{"band": band + side * (lax.rem(y + dy, side) - y)} for dy in range(1, side)]
    z_line = []
    for dz in range(1, 2 * side):
        there = lax.rem(half * side + zl + dz, 2 * side)
        z_line.append(
            {
                "band": lax.rem(there, side) * floor + yx,
                "dom": lax.div(there, side) * 2 + core,
            }
        )
    barrier = pltpu.get_barrier_semaphore()
    entered = (*x_line, *y_line, *z_line)

    def tell(peers, semaphore):
        for peer in peers:
            pl.semaphore_signal(semaphore, inc=1, device_id=peer, device_id_type=MESH)

    tell(entered, barrier)
    pl.semaphore_wait(barrier, len(entered))
    tell(y_line, plane_sem)
    pl.semaphore_wait(plane_sem, len(y_line))
    tell(z_line, all_sem)
    pl.semaphore_wait(all_sem, len(z_line))

    row = 2 * band + core
    first = (1 - left) * 2 * rim

    def send(i, c):
        at = lax.rem(37 * i + 8 * yx + 19 * zl, tiles)
        tile = lax.rem(half * tiles + first - rim + at + 2 * tiles, 2 * tiles)
        src = out.at[first + at]

        @pl.when(tile != own_tile)
        def _():
            peer = {"band": lax.rem(tile, bands), "dom": lax.div(tile, bands)}
            pltpu.make_async_remote_copy(
                src_ref=src, dst_ref=recv.at[row], send_sem=all_send, recv_sem=all_recv,
                device_id=peer, device_id_type=MESH,
            ).start()

        @pl.when(tile == own_tile)
        def _():
            pltpu.make_async_copy(src, recv.at[row], move_sem).start()

        return c

    lax.fori_loop(0, tiles, send, 0)
    pltpu.make_async_copy(out.at[0], recv.at[row], move_sem).wait()
    all_but_own = recv.at[pl.ds(0, recv.shape[0] - 1)]
    pltpu.make_async_copy(all_but_own, all_but_own, all_send).wait()
    pltpu.make_async_copy(all_but_own, all_but_own, all_recv).wait()


def rotate_kernel(recv_v, rows_v, out, out_v, sems):
    high, low = two_parts(jnp.concatenate([rows_v[:, 0], rows_v[:, 1]], axis=0).T)
    matrix = jnp.concatenate([high, high, low], axis=1)
    width = 256
    stores = []
    for at in range(0, 8 * 128, width):
        columns = []
        for r in range(at // 128, (at + width) // 128):
            values = jnp.concatenate([recv_v[:, 0, r], recv_v[:, 1, r]], axis=0)
            high, low = two_parts(values)
            columns.append(jnp.concatenate([high, low, high], axis=0))
        out_v[:, pl.ds(at, width)] = jnp.dot(
            matrix, jnp.concatenate(columns, axis=1), preferred_element_type=jnp.float32
        )
        store = pltpu.make_async_copy(
            out_v.at[:, pl.ds(at, width)], out.at[:, pl.ds(at, width)], sems.at[at // width]
        )
        store.start()
        stores.append(store)
    for store in stores:
        store.wait()


def per_device(bands, orbitals, potential, subspace):
    orbs, planes = orbitals.shape[0], orbitals.shape[1]
    orb = orbitals.reshape(orbs, planes, 2, 8, 128)
    pot = potential.reshape(planes, 2, 8, 128)
    f32 = jnp.float32
    dma = pltpu.SemaphoreType.DMA
    anywhere = pl.BlockSpec(memory_space=pl.ANY)
    slab, shift = 2 * planes, 2 * REACH
    finished, rows = pl.pallas_call(
        functools.partial(filter_kernel, bands),
        out_shape=(
            pltpu.VMEM((2 * (slab + 2 * shift), 8, 128), f32),
            pltpu.VMEM((4, 4, 4, orbs, 128), f32),
        ),
        in_specs=[anywhere] * 3,
        out_specs=(pl.BlockSpec(memory_space=pltpu.VMEM), anywhere),
        scratch_shapes=[
            *[
                pltpu.VMEM((slab + 2 * (shift + REACH * (DEG - level)), 2, 8, 128), f32)
                for level in range(DEG)
            ],
            pltpu.VMEM((slab + 2 * (shift + REACH * (DEG - 1)), 2, 8, 128), f32),
            dma((2,)),
            dma((2,)),
            dma((2, 5)),
            dma((5,)),
            dma((2,)),
            dma,
            dma((7,)),
            dma((7,)),
            dma((4,)),
            dma((3, 3)),
            dma((3, 3)),
        ],
        compiler_params=pltpu.CompilerParams(
            collective_id=0, has_side_effects=True, vmem_limit_bytes=32 * 2**20
        ),
        name="filter",
    )(*(pltpu.with_memory_space_constraint(a, pltpu.HBM) for a in (orb, pot, subspace)))
    recv = pl.pallas_call(
        functools.partial(spread_kernel, bands),
        out_shape=pltpu.VMEM((bands * orbs, 8, 128), f32),
        in_specs=[anywhere],
        out_specs=anywhere,
        scratch_shapes=[dma, dma, dma, pltpu.SemaphoreType.REGULAR, pltpu.SemaphoreType.REGULAR],
        compiler_params=pltpu.CompilerParams(
            collective_id=1, has_side_effects=True, vmem_limit_bytes=32 * 2**20
        ),
        name="spread",
    )(pltpu.with_memory_space_constraint(finished, pltpu.VMEM))
    recv, rows = recv.reshape(bands, orbs, 8, 128), rows.reshape(bands, orbs, 128)
    return pl.pallas_call(
        rotate_kernel,
        out_shape=jax.ShapeDtypeStruct((bands * orbs, 1024), f32),
        in_specs=[pl.BlockSpec(memory_space=pltpu.VMEM)] * 2,
        out_specs=anywhere,
        scratch_shapes=[pltpu.VMEM((bands * orbs, 1024), f32), dma((4,))],
        compiler_params=pltpu.CompilerParams(vmem_limit_bytes=32 * 2**20),
        name="rotate",
    )(*(pltpu.with_memory_space_constraint(a, pltpu.VMEM) for a in (recv, rows)))


def solution(mesh):
    in_specs = (P("band", "dom", None, None), P("dom", None, None), P("band", None))
    out_specs = P(None, ("dom", "band"))
    return jax.shard_map(
        functools.partial(per_device, mesh.shape["band"]),
        mesh=mesh,
        in_specs=in_specs,
        out_specs=out_specs,
        check_vma=False,
    )
```

```python
import functools
import math

import jax
import jax.numpy as jnp
from jax import lax
from jax.experimental import pallas as pl
from jax.experimental.pallas import tpu as pltpu
from jax.sharding import PartitionSpec as P

DEG = 3
REACH = 6
MESH = pl.DeviceIdType.MESH

upper_edge = 10.7
lower_edge = 1.5
bottom_edge = -1.0


def stencil_weights():
    factor_square = math.factorial(6) ** 2
    side_weights = []
    for offset in range(1, 7):
        side_weights.append(
            2.0
            * (-1.0) ** (offset + 1)
            * factor_square
            / (offset * offset * math.factorial(6 - offset) * math.factorial(6 + offset))
        )
    center_weight = -2.0 * sum(side_weights)
    return (center_weight, side_weights)


def filter_scalars(pass_count):
    half_width = (upper_edge - lower_edge) / 2.0
    sigma_now = half_width / (bottom_edge - (upper_edge + lower_edge) / 2.0)
    gamma_value = 2.0 / sigma_now
    scalars = [(sigma_now / half_width, 0.0)]
    for pass_index in range(pass_count - 1):
        sigma_next = 1.0 / (gamma_value - sigma_now)
        scalars.append((2.0 * sigma_next / half_width, sigma_now * sigma_next))
        sigma_now = sigma_next
    return scalars


def two_parts(values):
    high = values.astype(jnp.bfloat16)
    return high, (values - high.astype(jnp.float32)).astype(jnp.bfloat16)


def stencil_matrix(period, axis):
    rows = lax.broadcasted_iota(jnp.int32, (128, 128), 0)
    columns = lax.broadcasted_iota(jnp.int32, (128, 128), 1)
    apart = jnp.abs(rows - columns)
    if period < 128:
        same = jnp.bitwise_or(rows, period - 1) == jnp.bitwise_or(columns, period - 1)
        apart = jnp.where(same, apart, 0)
    apart = jnp.minimum(apart, period - apart)
    matrix = jnp.zeros((128, 128), jnp.float32)
    for k, w in enumerate(stencil_weights()[1], 1):
        matrix = jnp.where(apart == k, jnp.float32(w), matrix)
    high, low = two_parts(matrix)
    return jnp.concatenate([high, high, low], axis=axis)


def filtered_block(window, pot, before, scale, weight, lanes, rows):
    center_weight, side = stencil_weights()
    n = window.shape[0] - 2 * REACH
    mid = window[REACH : REACH + n]
    high, low = two_parts(mid.reshape(n * 16, 128))
    total = jnp.dot(
        jnp.concatenate([high, low, high], axis=1), lanes, preferred_element_type=jnp.float32
    ) + jnp.dot(
        rows, jnp.concatenate([high, low, high], axis=0), preferred_element_type=jnp.float32
    )
    total = total.reshape(n, 2, 8, 128)
    for k in range(1, REACH + 1):
        beside = window[REACH + k : REACH + k + n] + window[REACH - k : REACH - k + n]
        total = total + side[k - 1] * beside
    diag = (-1.5 * center_weight - (upper_edge + lower_edge) / 2.0) * scale
    result = (pot * scale + diag) * mid + (-0.5 * scale) * total
    if before is not None:
        result = result - weight * before
    return result


def filter_kernel(
    bands, orb, pot, sub, recv, rows, p0, p1, p2, out, given, pot_v,
    near_send, near_recv, far_send, far_recv, pot_send, pot_recv, pass_send, pass_recv,
    swap_send, swap_recv, move_sem, all_send, all_recv, row_send, row_recv, plane_sem, all_sem,
):
    quarter = orb.shape[1]
    slab, whole = 2 * quarter, 4 * quarter
    band, dom = lax.axis_index("band"), lax.axis_index("dom")
    core, half = lax.rem(dom, 2), lax.div(dom, 2)
    side = 4
    floor = side * side
    zl, x, yx = lax.div(band, floor), lax.rem(band, side), lax.rem(band, floor)
    shift = 2 * REACH
    left = jnp.where(zl < side // 2, 1, 0)
    long = core == left
    base = half * slab
    own_tile = dom * bands + band
    own_plane = lax.div(own_tile, 2)
    scalars = filter_scalars(DEG)
    buffers = (p0, p1, p2)
    rims = tuple(shift + REACH * (DEG - level) for level in range(DEG + 1))
    pot_rim = rims[1]

    def placed(u, count):
        return jnp.where(left == 1, u, slab - count - u)

    load = pltpu.make_async_copy(
        orb.at[core], p0.at[pl.ds(core * quarter + rims[0], quarter)], move_sem.at[0]
    )
    load.start()
    load_pot = pltpu.make_async_copy(
        pot, pot_v.at[pl.ds(core * quarter + pot_rim, quarter)], move_sem.at[1]
    )
    load_pot.start()

    sibling = {"dom": dom + 1 - 2 * core}
    partners = [{"dom": 2 * (1 - half) + k} for k in range(2)]

    def chip_along(shift):
        there = lax.rem(half * side + zl + shift, 2 * side)
        return {
            "band": lax.rem(there, side) * floor + yx,
            "dom": lax.div(there, side) * 2 + core,
        }

    x_line = [
        {"band": band - x + lax.rem(x + dx, side), "dom": dom if dk == 0 else dom + 1 - 2 * core}
        for dx in range(side)
        for dk in range(2)
    ][1:]
    y = lax.div(yx, side)
    y_line = [{"band": band + side * (lax.rem(y + dy, side) - y)} for dy in range(1, side)]
    z_line = [chip_along(dz) for dz in range(1, 2 * side)]
    other_partner = {"dom": 2 * (1 - half) + 1 - core}
    barrier = pltpu.get_barrier_semaphore()
    entered = (*z_line, other_partner, *x_line, *y_line)

    def tell(peers, semaphore):
        for peer in peers:
            pl.semaphore_signal(semaphore, inc=1, device_id=peer, device_id_type=MESH)

    tell(entered, barrier)
    lanes, lines = stencil_matrix(128, 0), stencil_matrix(16, 1)
    pl.semaphore_wait(barrier, len(entered))

    def remote(src, dst, send_sem, recv_sem, peer):
        return pltpu.make_async_remote_copy(
            src_ref=src, dst_ref=dst, send_sem=send_sem, recv_sem=recv_sem,
            device_id=peer, device_id_type=MESH,
        )

    own_rows = pltpu.make_async_copy(sub, rows.at[zl, y, x], move_sem.at[2])
    own_rows.start()
    row_lines = [
        (rows.at[zl, y, x], [{"band": lax.rem(band + d * floor, bands)} for d in range(1, side)]),
        (rows.at[:, y, x], y_line),
        (rows.at[:, :, x], [{"band": band - x + lax.rem(x + d, side)} for d in range(1, side)]),
    ]
    row_copies = [
        [
            remote(
                sub if stage == 0 else part_rows, part_rows,
                row_send.at[stage, at], row_recv.at[stage, at], peer,
            )
            for at, peer in enumerate(peers)
        ]
        for stage, (part_rows, peers) in enumerate(row_lines)
    ]

    def gather_rows(stage):
        if stage > 0:
            for copy in row_copies[stage - 1]:
                copy.wait_recv()
        for copy in row_copies[stage]:
            copy.start()

    gather_rows(0)
    pieces = [(0, REACH)] + [(REACH + 8 * i, 8) for i in range(3)]
    assert sum(n for _, n in pieces) == rims[0]
    far = []
    for o in range(2):
        group = []
        for at, (a, n) in enumerate(pieces):
            group.append(
                remote(
                    orb.at[o, pl.ds(jnp.where(left == 1, quarter - a - n, a), n)],
                    p0.at[pl.ds(placed(-a - n, n) + rims[0], n)],
                    far_send.at[o, at], far_recv.at[at], partners[o],
                )
            )
        n = REACH
        group.append(
            remote(
                orb.at[o, pl.ds(jnp.where(left == 1, 0, quarter - n), n)],
                p0.at[pl.ds(placed(slab, n) + rims[0], n)],
                far_send.at[o, 4], far_recv.at[4], partners[o],
            )
        )
        far.append(group)
    part = pot_rim // 8
    pot_far = [
        remote(
            pot.at[pl.ds(jnp.where(left == 1, quarter - pot_rim, 0) + (2 * x + o) * part, part)],
            pot_v.at[pl.ds(placed(-pot_rim, pot_rim) + pot_rim + (2 * x + o) * part, part)],
            pot_send.at[o], pot_recv, partners[o],
        )
        for o in range(2)
    ]
    mine = pot_v.at[pl.ds(placed(-pot_rim, pot_rim) + pot_rim + (2 * x + core) * part, part)]

    @pl.when(long)
    def _():
        for o in range(2):
            pot_far[o].start()
        for o in range(2):
            far[o][0].start()

    @pl.when(jnp.logical_not(long))
    def _():
        for o in range(2):
            far[o][4].start()

    near = remote(
        orb.at[1 - core], p0.at[pl.ds(core * quarter + rims[0], quarter)],
        near_send.at[0], near_recv.at[0], sibling,
    )
    near_pot = remote(
        pot, pot_v.at[pl.ds(core * quarter + pot_rim, quarter)],
        near_send.at[1], near_recv.at[1], sibling,
    )
    near.start()
    near_pot.start()

    @pl.when(long)
    def _():
        for at in range(1, 4):
            for o in range(2):
                far[o][at].start()

    tell(y_line, plane_sem)

    step = 8

    def apply(level, u, blocks):
        scale, weight = scalars[level]

        def body(i, c):
            at = placed(u + i * step, step)
            before = None
            if level > 0:
                before = buffers[level - 1][pl.ds(at + rims[level - 1], step)]
            window = buffers[level][pl.ds(at + rims[level] - REACH, step + 2 * REACH)]
            pairs = filtered_block(
                window, pot_v[pl.ds(at + pot_rim, step)], before, scale, weight, lanes, lines
            )
            if level < DEG - 1:
                buffers[level + 1][pl.ds(at + rims[level + 1], step)] = pairs
            else:
                keep = jnp.where(core == 0, pairs[:, 0], pairs[:, 1])
                give = jnp.where(core == 0, pairs[:, 1], pairs[:, 0])
                out[pl.ds(at + rims[DEG], step), core] = keep
                given[pl.ds(at + rims[DEG], step)] = give
            return c

        lax.fori_loop(0, blocks, body, 0)

    swaps = []

    def spread(u, count):
        start = placed(u, count)
        part = pl.ds(start + rims[DEG], count)
        number = len(swaps)
        swap = remote(
            given.at[part], out.at[part, core], swap_send.at[number], swap_recv.at[number], sibling
        )
        swap.start()
        swaps.append(swap)
        swap.wait_recv()

        def send(i, c):
            at = lax.rem(i + yx, count)
            tile = lax.rem(2 * (base + start + at) + core + 2 * whole, 2 * whole)
            src = out.at[start + rims[DEG] + at]

            @pl.when(tile != own_tile)
            def _():
                peer = {"band": lax.rem(tile, bands), "dom": lax.div(tile, bands)}
                remote(src, recv.at[band], all_send, all_recv, peer).start()

            @pl.when(tile == own_tile)
            def _():
                pltpu.make_async_copy(src, recv.at[band], move_sem.at[3]).start()

            return c

        lax.fori_loop(0, count, send, 0)

    def advance(u):
        for level in range(DEG):
            apply(level, u + level * REACH, 1)
        spread(u + (DEG - 1) * REACH, 8)

    load.wait()
    load_pot.wait()
    near.wait_recv()
    near_pot.wait_recv()
    pl.semaphore_wait(plane_sem, len(y_line))
    tell(z_line, all_sem)
    apply(0, 8, 6)
    apply(1, 14, 4)
    apply(1, 42, 1)
    apply(2, 20, 3)
    pl.semaphore_wait(all_sem, len(z_line))
    spread(20, 24)

    pot_far[0].wait_recv()
    passed = [
        remote(mine, mine, pass_send.at[at], pass_recv.at[at], peer)
        for at, peer in enumerate(x_line)
    ]
    for copy in passed:
        copy.start()

    far[0][4].wait_recv()
    apply(0, slab - 8, 1)
    apply(1, slab - 14, 1)
    apply(2, slab - 20, 1)
    spread(slab - 20, 8)
    for at in range(4):
        if at == 1:
            own_rows.wait()
            gather_rows(1)
            for copy in passed:
                copy.wait_recv()
        if at == 3:
            gather_rows(2)
        far[0][at].wait_recv()
        advance(-8 * at)

    @pl.when(long)
    def _():
        for o in range(2):
            pot_far[o].wait_send()
            for at in range(4):
                far[o][at].wait_send()

    @pl.when(jnp.logical_not(long))
    def _():
        for o in range(2):
            far[o][4].wait_send()

    for copy in (near, near_pot, *passed):
        copy.wait_send()
    for copy in row_copies[2]:
        copy.wait_recv()
    for copies in row_copies:
        for copy in copies:
            copy.wait_send()
    for swap in swaps:
        swap.wait_send()

    def finish(number):
        arrived = recv.at[pl.ds(0, number)]
        pltpu.make_async_copy(arrived, arrived, all_send).wait()
        pltpu.make_async_copy(arrived, arrived, all_recv).wait()

    @pl.when(lax.rem(x, 2) == core)
    def _():
        pltpu.make_async_copy(out.at[0], recv.at[0], move_sem.at[3]).wait()
        finish(bands - 1)

    @pl.when(lax.rem(x, 2) != core)
    def _():
        finish(bands)


def rotate_kernel(recv_v, rows_v, out, out_v, sems):
    high, low = two_parts(jnp.concatenate([rows_v[:, 0], rows_v[:, 1]], axis=0).T)
    matrix = jnp.concatenate([high, high, low], axis=1)
    width = 256
    stores = []
    for at in range(0, 8 * 128, width):
        columns = []
        for r in range(at // 128, (at + width) // 128):
            values = jnp.concatenate([recv_v[:, 0, r], recv_v[:, 1, r]], axis=0)
            high, low = two_parts(values)
            columns.append(jnp.concatenate([high, low, high], axis=0))
        out_v[:, pl.ds(at, width)] = jnp.dot(
            matrix, jnp.concatenate(columns, axis=1), preferred_element_type=jnp.float32
        )
        store = pltpu.make_async_copy(
            out_v.at[:, pl.ds(at, width)], out.at[:, pl.ds(at, width)], sems.at[at // width]
        )
        store.start()
        stores.append(store)
    for store in stores:
        store.wait()


def per_device(bands, orbitals, potential, subspace):
    orbs, planes = orbitals.shape[0], orbitals.shape[1]
    orb = orbitals.reshape(orbs, planes, 2, 8, 128)
    pot = potential.reshape(planes, 2, 8, 128)
    f32 = jnp.float32
    dma = pltpu.SemaphoreType.DMA
    anywhere = pl.BlockSpec(memory_space=pl.ANY)
    slab, shift = 2 * planes, 2 * REACH
    recv, rows = pl.pallas_call(
        functools.partial(filter_kernel, bands),
        out_shape=(
            pltpu.VMEM((bands, orbs, 8, 128), f32),
            pltpu.VMEM((4, 4, 4, orbs, 128), f32),
        ),
        in_specs=[anywhere] * 3,
        out_specs=(anywhere,) * 2,
        scratch_shapes=[
            *[
                pltpu.VMEM((slab + 2 * (shift + REACH * (DEG - level)), 2, 8, 128), f32)
                for level in range(DEG)
            ],
            pltpu.VMEM((slab + 2 * shift, orbs, 8, 128), f32),
            pltpu.VMEM((slab + 2 * shift, 8, 128), f32),
            pltpu.VMEM((slab + 2 * (shift + REACH * (DEG - 1)), 2, 8, 128), f32),
            dma((2,)),
            dma((2,)),
            dma((2, 5)),
            dma((5,)),
            dma((2,)),
            dma,
            dma((7,)),
            dma((7,)),
            dma((6,)),
            dma((6,)),
            dma((4,)),
            dma,
            dma,
            dma((3, 3)),
            dma((3, 3)),
            pltpu.SemaphoreType.REGULAR,
            pltpu.SemaphoreType.REGULAR,
        ],
        compiler_params=pltpu.CompilerParams(
            collective_id=0, has_side_effects=True, vmem_limit_bytes=32 * 2**20
        ),
        name="filter",
    )(*(pltpu.with_memory_space_constraint(a, pltpu.HBM) for a in (orb, pot, subspace)))
    rows = rows.reshape(bands, orbs, 128)
    return pl.pallas_call(
        rotate_kernel,
        out_shape=jax.ShapeDtypeStruct((bands * orbs, 1024), f32),
        in_specs=[pl.BlockSpec(memory_space=pltpu.VMEM)] * 2,
        out_specs=anywhere,
        scratch_shapes=[pltpu.VMEM((bands * orbs, 1024), f32), dma((4,))],
        compiler_params=pltpu.CompilerParams(vmem_limit_bytes=32 * 2**20),
        name="rotate",
    )(*(pltpu.with_memory_space_constraint(a, pltpu.VMEM) for a in (recv, rows)))


def solution(mesh):
    in_specs = (P("band", "dom", None, None), P("dom", None, None), P("band", None))
    out_specs = P(None, ("dom", "band"))
    return jax.shard_map(
        functools.partial(per_device, mesh.shape["band"]),
        mesh=mesh,
        in_specs=in_specs,
        out_specs=out_specs,
        check_vma=False,
    )
```

```python
import functools
import math

import jax
import jax.numpy as jnp
from jax import lax
from jax.experimental import pallas as pl
from jax.experimental.pallas import tpu as pltpu
from jax.sharding import PartitionSpec as P

DEG = 3
REACH = 6
MESH = pl.DeviceIdType.MESH

upper_edge = 10.7
lower_edge = 1.5
bottom_edge = -1.0


def stencil_weights():
    factor_square = math.factorial(6) ** 2
    side_weights = []
    for offset in range(1, 7):
        side_weights.append(
            2.0
            * (-1.0) ** (offset + 1)
            * factor_square
            / (offset * offset * math.factorial(6 - offset) * math.factorial(6 + offset))
        )
    center_weight = -2.0 * sum(side_weights)
    return (center_weight, side_weights)


def filter_scalars(pass_count):
    half_width = (upper_edge - lower_edge) / 2.0
    sigma_now = half_width / (bottom_edge - (upper_edge + lower_edge) / 2.0)
    gamma_value = 2.0 / sigma_now
    scalars = [(sigma_now / half_width, 0.0)]
    for pass_index in range(pass_count - 1):
        sigma_next = 1.0 / (gamma_value - sigma_now)
        scalars.append((2.0 * sigma_next / half_width, sigma_now * sigma_next))
        sigma_now = sigma_next
    return scalars


def two_parts(values):
    high = values.astype(jnp.bfloat16)
    return high, (values - high.astype(jnp.float32)).astype(jnp.bfloat16)


def stencil_matrix(period, axis):
    rows = lax.broadcasted_iota(jnp.int32, (128, 128), 0)
    columns = lax.broadcasted_iota(jnp.int32, (128, 128), 1)
    apart = jnp.abs(rows - columns)
    if period < 128:
        same = jnp.bitwise_or(rows, period - 1) == jnp.bitwise_or(columns, period - 1)
        apart = jnp.where(same, apart, 0)
    apart = jnp.minimum(apart, period - apart)
    matrix = jnp.zeros((128, 128), jnp.float32)
    for k, w in enumerate(stencil_weights()[1], 1):
        matrix = jnp.where(apart == k, jnp.float32(w), matrix)
    high, low = two_parts(matrix)
    return jnp.concatenate([high, high, low], axis=axis)


def filtered_block(window, pot, before, scale, weight, lanes, rows):
    center_weight, side = stencil_weights()
    n = window.shape[0] - 2 * REACH
    mid = window[REACH : REACH + n]
    high, low = two_parts(mid.reshape(n * 16, 128))
    total = jnp.dot(
        jnp.concatenate([high, low, high], axis=1), lanes, preferred_element_type=jnp.float32
    ) + jnp.dot(
        rows, jnp.concatenate([high, low, high], axis=0), preferred_element_type=jnp.float32
    )
    total = total.reshape(n, 2, 8, 128)
    for k in range(1, REACH + 1):
        beside = window[REACH + k : REACH + k + n] + window[REACH - k : REACH - k + n]
        total = total + side[k - 1] * beside
    diag = (-1.5 * center_weight - (upper_edge + lower_edge) / 2.0) * scale
    result = (pot * scale + diag) * mid + (-0.5 * scale) * total
    if before is not None:
        result = result - weight * before
    return result


def filter_kernel(
    bands, orb, pot, sub, recv, rows, p0, p1, p2, out, given, pot_v,
    near_send, near_recv, far_send, far_recv, pot_send, pot_recv, pass_send, pass_recv,
    swap_send, swap_recv, move_sem, all_send, all_recv, row_send, row_recv, plane_sem, all_sem,
):
    quarter = orb.shape[1]
    slab, whole = 2 * quarter, 4 * quarter
    band, dom = lax.axis_index("band"), lax.axis_index("dom")
    core, half = lax.rem(dom, 2), lax.div(dom, 2)
    side = 4
    floor = side * side
    zl, x, yx = lax.div(band, floor), lax.rem(band, side), lax.rem(band, floor)
    shift = 2 * REACH
    left = jnp.where(zl < side // 2, 1, 0)
    long = core == left
    base = half * slab
    own_tile = dom * bands + band
    own_plane = lax.div(own_tile, 2)
    scalars = filter_scalars(DEG)
    buffers = (p0, p1, p2)
    rims = tuple(shift + REACH * (DEG - level) for level in range(DEG + 1))
    pot_rim = rims[1]

    def placed(u, count):
        return jnp.where(left == 1, u, slab - count - u)

    load = pltpu.make_async_copy(
        orb.at[core], p0.at[pl.ds(core * quarter + rims[0], quarter)], move_sem.at[0]
    )
    load.start()
    load_pot = pltpu.make_async_copy(
        pot, pot_v.at[pl.ds(core * quarter + pot_rim, quarter)], move_sem.at[1]
    )
    load_pot.start()

    sibling = {"dom": dom + 1 - 2 * core}
    partners = [{"dom": 2 * (1 - half) + k} for k in range(2)]
    partner = {"dom": 2 * (1 - half) + core}

    def chip_along(shift):
        there = lax.rem(half * side + zl + shift, 2 * side)
        return {
            "band": lax.rem(there, side) * floor + yx,
            "dom": lax.div(there, side) * 2 + core,
        }

    x_line = [
        {"band": band - x + lax.rem(x + dx, side), "dom": dom if dk == 0 else dom + 1 - 2 * core}
        for dx in range(side)
        for dk in range(2)
    ][1:]
    y = lax.div(yx, side)
    y_line = [{"band": band + side * (lax.rem(y + dy, side) - y)} for dy in range(1, side)]
    z_line = [chip_along(dz) for dz in range(1, 2 * side)]
    other_partner = {"dom": 2 * (1 - half) + 1 - core}
    barrier = pltpu.get_barrier_semaphore()
    entered = (*z_line, other_partner, *x_line, *y_line)

    def tell(peers, semaphore):
        for peer in peers:
            pl.semaphore_signal(semaphore, inc=1, device_id=peer, device_id_type=MESH)

    tell(entered, barrier)
    lanes, lines = stencil_matrix(128, 0), stencil_matrix(16, 1)
    pl.semaphore_wait(barrier, len(entered))

    def remote(src, dst, send_sem, recv_sem, peer):
        return pltpu.make_async_remote_copy(
            src_ref=src, dst_ref=dst, send_sem=send_sem, recv_sem=recv_sem,
            device_id=peer, device_id_type=MESH,
        )

    own_rows = pltpu.make_async_copy(sub, rows.at[zl, y, x], move_sem.at[2])
    own_rows.start()
    row_lines = [
        (rows.at[zl, y, x], [{"band": lax.rem(band + d * floor, bands)} for d in range(1, side)]),
        (rows.at[:, y, x], y_line),
        (rows.at[:, :, x], [{"band": band - x + lax.rem(x + d, side)} for d in range(1, side)]),
    ]
    row_copies = [
        [
            remote(
                sub if stage == 0 else part_rows, part_rows,
                row_send.at[stage, at], row_recv.at[stage, at], peer,
            )
            for at, peer in enumerate(peers)
        ]
        for stage, (part_rows, peers) in enumerate(row_lines)
    ]

    def gather_rows(stage):
        if stage > 0:
            for copy in row_copies[stage - 1]:
                copy.wait_recv()
        for copy in row_copies[stage]:
            copy.start()

    gather_rows(0)
    pieces = [(0, REACH)] + [(REACH + 8 * i, 8) for i in range(3)]
    assert sum(n for _, n in pieces) == rims[0]
    far = []
    for at, (u, n) in enumerate([(-a - n, n) for a, n in pieces] + [(slab, REACH)]):
        here = placed(slab + u if u < 0 else u - slab, n)
        far.append(
            remote(
                p0.at[pl.ds(here + rims[0], n)], p0.at[pl.ds(placed(u, n) + rims[0], n)],
                far_send.at[at], far_recv.at[at], partner,
            )
        )
    part = pot_rim // 8
    pot_far = [
        remote(
            pot.at[pl.ds(jnp.where(left == 1, quarter - pot_rim, 0) + (2 * x + o) * part, part)],
            pot_v.at[pl.ds(placed(-pot_rim, pot_rim) + pot_rim + (2 * x + o) * part, part)],
            pot_send.at[o], pot_recv, partners[o],
        )
        for o in range(2)
    ]
    mine = pot_v.at[pl.ds(placed(-pot_rim, pot_rim) + pot_rim + (2 * x + core) * part, part)]

    @pl.when(long)
    def _():
        for o in range(2):
            pot_far[o].start()

    near = remote(
        orb.at[1 - core], p0.at[pl.ds(core * quarter + rims[0], quarter)],
        near_send.at[0], near_recv.at[0], sibling,
    )
    near_pot = remote(
        pot, pot_v.at[pl.ds(core * quarter + pot_rim, quarter)],
        near_send.at[1], near_recv.at[1], sibling,
    )
    near.start()
    near_pot.start()

    def send_far(numbers):
        for at in numbers:
            far[at].start()

    load.wait()
    pl.when(long)(functools.partial(send_far, (0, 1, 2, 3)))
    pl.when(jnp.logical_not(long))(functools.partial(send_far, (4,)))
    near.wait_recv()
    pl.when(long)(functools.partial(send_far, (4,)))
    pl.when(jnp.logical_not(long))(functools.partial(send_far, (0, 1, 2, 3)))

    tell(y_line, plane_sem)

    step = 8

    def apply(level, u, blocks):
        scale, weight = scalars[level]

        def body(i, c):
            at = placed(u + i * step, step)
            before = None
            if level > 0:
                before = buffers[level - 1][pl.ds(at + rims[level - 1], step)]
            window = buffers[level][pl.ds(at + rims[level] - REACH, step + 2 * REACH)]
            pairs = filtered_block(
                window, pot_v[pl.ds(at + pot_rim, step)], before, scale, weight, lanes, lines
            )
            if level < DEG - 1:
                buffers[level + 1][pl.ds(at + rims[level + 1], step)] = pairs
            else:
                keep = jnp.where(core == 0, pairs[:, 0], pairs[:, 1])
                give = jnp.where(core == 0, pairs[:, 1], pairs[:, 0])
                out[pl.ds(at + rims[DEG], step), core] = keep
                given[pl.ds(at + rims[DEG], step)] = give
            return c

        lax.fori_loop(0, blocks, body, 0)

    swaps = []

    def spread(u, count):
        start = placed(u, count)
        part = pl.ds(start + rims[DEG], count)
        number = len(swaps)
        swap = remote(
            given.at[part], out.at[part, core], swap_send.at[number], swap_recv.at[number], sibling
        )
        swap.start()
        swaps.append(swap)
        swap.wait_recv()

        def send(i, c):
            at = lax.rem(i + yx, count)
            tile = lax.rem(2 * (base + start + at) + core + 2 * whole, 2 * whole)
            src = out.at[start + rims[DEG] + at]

            @pl.when(tile != own_tile)
            def _():
                peer = {"band": lax.rem(tile, bands), "dom": lax.div(tile, bands)}
                remote(src, recv.at[band], all_send, all_recv, peer).start()

            @pl.when(tile == own_tile)
            def _():
                pltpu.make_async_copy(src, recv.at[band], move_sem.at[3]).start()

            return c

        lax.fori_loop(0, count, send, 0)

    def advance(u):
        for level in range(DEG):
            apply(level, u + level * REACH, 1)
        spread(u + (DEG - 1) * REACH, 8)

    load_pot.wait()
    near_pot.wait_recv()
    pl.semaphore_wait(plane_sem, len(y_line))
    tell(z_line, all_sem)
    apply(0, 8, 6)
    apply(1, 14, 4)
    apply(1, 42, 1)
    apply(2, 20, 3)
    pl.semaphore_wait(all_sem, len(z_line))
    spread(20, 24)

    pot_far[0].wait_recv()
    passed = [
        remote(mine, mine, pass_send.at[at], pass_recv.at[at], peer)
        for at, peer in enumerate(x_line)
    ]
    for copy in passed:
        copy.start()

    far[4].wait_recv()
    apply(0, slab - 8, 1)
    apply(1, slab - 14, 1)
    apply(2, slab - 20, 1)
    spread(slab - 20, 8)
    for at in range(4):
        if at == 1:
            own_rows.wait()
            gather_rows(1)
            for copy in passed:
                copy.wait_recv()
        if at == 3:
            gather_rows(2)
        far[at].wait_recv()
        advance(-8 * at)

    @pl.when(long)
    def _():
        for o in range(2):
            pot_far[o].wait_send()

    for copy in (near, *far, near_pot, *passed):
        copy.wait_send()
    for copy in row_copies[2]:
        copy.wait_recv()
    for copies in row_copies:
        for copy in copies:
            copy.wait_send()
    for swap in swaps:
        swap.wait_send()

    def finish(number):
        arrived = recv.at[pl.ds(0, number)]
        pltpu.make_async_copy(arrived, arrived, all_send).wait()
        pltpu.make_async_copy(arrived, arrived, all_recv).wait()

    @pl.when(lax.rem(x, 2) == core)
    def _():
        pltpu.make_async_copy(out.at[0], recv.at[0], move_sem.at[3]).wait()
        finish(bands - 1)

    @pl.when(lax.rem(x, 2) != core)
    def _():
        finish(bands)


def rotate_kernel(recv_v, rows_v, out, out_v, sems):
    high, low = two_parts(jnp.concatenate([rows_v[:, 0], rows_v[:, 1]], axis=0).T)
    matrix = jnp.concatenate([high, high, low], axis=1)
    width = 256
    stores = []
    for at in range(0, 8 * 128, width):
        columns = []
        for r in range(at // 128, (at + width) // 128):
            values = jnp.concatenate([recv_v[:, 0, r], recv_v[:, 1, r]], axis=0)
            high, low = two_parts(values)
            columns.append(jnp.concatenate([high, low, high], axis=0))
        out_v[:, pl.ds(at, width)] = jnp.dot(
            matrix, jnp.concatenate(columns, axis=1), preferred_element_type=jnp.float32
        )
        store = pltpu.make_async_copy(
            out_v.at[:, pl.ds(at, width)], out.at[:, pl.ds(at, width)], sems.at[at // width]
        )
        store.start()
        stores.append(store)
    for store in stores:
        store.wait()


def per_device(bands, orbitals, potential, subspace):
    orbs, planes = orbitals.shape[0], orbitals.shape[1]
    orb = orbitals.reshape(orbs, planes, 2, 8, 128)
    pot = potential.reshape(planes, 2, 8, 128)
    f32 = jnp.float32
    dma = pltpu.SemaphoreType.DMA
    anywhere = pl.BlockSpec(memory_space=pl.ANY)
    slab, shift = 2 * planes, 2 * REACH
    recv, rows = pl.pallas_call(
        functools.partial(filter_kernel, bands),
        out_shape=(
            pltpu.VMEM((bands, orbs, 8, 128), f32),
            pltpu.VMEM((4, 4, 4, orbs, 128), f32),
        ),
        in_specs=[anywhere] * 3,
        out_specs=(anywhere,) * 2,
        scratch_shapes=[
            *[
                pltpu.VMEM((slab + 2 * (shift + REACH * (DEG - level)), 2, 8, 128), f32)
                for level in range(DEG)
            ],
            pltpu.VMEM((slab + 2 * shift, orbs, 8, 128), f32),
            pltpu.VMEM((slab + 2 * shift, 8, 128), f32),
            pltpu.VMEM((slab + 2 * (shift + REACH * (DEG - 1)), 2, 8, 128), f32),
            dma((2,)),
            dma((2,)),
            dma((5,)),
            dma((5,)),
            dma((2,)),
            dma,
            dma((7,)),
            dma((7,)),
            dma((6,)),
            dma((6,)),
            dma((4,)),
            dma,
            dma,
            dma((3, 3)),
            dma((3, 3)),
            pltpu.SemaphoreType.REGULAR,
            pltpu.SemaphoreType.REGULAR,
        ],
        compiler_params=pltpu.CompilerParams(
            collective_id=0, has_side_effects=True, vmem_limit_bytes=32 * 2**20
        ),
        name="filter",
    )(*(pltpu.with_memory_space_constraint(a, pltpu.HBM) for a in (orb, pot, subspace)))
    rows = rows.reshape(bands, orbs, 128)
    return pl.pallas_call(
        rotate_kernel,
        out_shape=jax.ShapeDtypeStruct((bands * orbs, 1024), f32),
        in_specs=[pl.BlockSpec(memory_space=pltpu.VMEM)] * 2,
        out_specs=anywhere,
        scratch_shapes=[pltpu.VMEM((bands * orbs, 1024), f32), dma((4,))],
        compiler_params=pltpu.CompilerParams(vmem_limit_bytes=32 * 2**20),
        name="rotate",
    )(*(pltpu.with_memory_space_constraint(a, pltpu.VMEM) for a in (recv, rows)))


def solution(mesh):
    in_specs = (P("band", "dom", None, None), P("dom", None, None), P("band", None))
    out_specs = P(None, ("dom", "band"))
    return jax.shard_map(
        functools.partial(per_device, mesh.shape["band"]),
        mesh=mesh,
        in_specs=in_specs,
        out_specs=out_specs,
        check_vma=False,
    )
```

```python
import functools
import math

import jax
import jax.numpy as jnp
from jax import lax
from jax.experimental import pallas as pl
from jax.experimental.pallas import tpu as pltpu
from jax.sharding import PartitionSpec as P

DEG = 3
REACH = 6
MESH = pl.DeviceIdType.MESH

upper_edge = 10.7
lower_edge = 1.5
bottom_edge = -1.0


def stencil_weights():
    factor_square = math.factorial(6) ** 2
    side_weights = []
    for offset in range(1, 7):
        side_weights.append(
            2.0
            * (-1.0) ** (offset + 1)
            * factor_square
            / (offset * offset * math.factorial(6 - offset) * math.factorial(6 + offset))
        )
    center_weight = -2.0 * sum(side_weights)
    return (center_weight, side_weights)


def filter_scalars(pass_count):
    half_width = (upper_edge - lower_edge) / 2.0
    sigma_now = half_width / (bottom_edge - (upper_edge + lower_edge) / 2.0)
    gamma_value = 2.0 / sigma_now
    scalars = [(sigma_now / half_width, 0.0)]
    for pass_index in range(pass_count - 1):
        sigma_next = 1.0 / (gamma_value - sigma_now)
        scalars.append((2.0 * sigma_next / half_width, sigma_now * sigma_next))
        sigma_now = sigma_next
    return scalars


def two_parts(values):
    high = values.astype(jnp.bfloat16)
    return high, (values - high.astype(jnp.float32)).astype(jnp.bfloat16)


def stencil_matrix(period, axis):
    rows = lax.broadcasted_iota(jnp.int32, (128, 128), 0)
    columns = lax.broadcasted_iota(jnp.int32, (128, 128), 1)
    apart = jnp.abs(rows - columns)
    if period < 128:
        same = jnp.bitwise_or(rows, period - 1) == jnp.bitwise_or(columns, period - 1)
        apart = jnp.where(same, apart, 0)
    apart = jnp.minimum(apart, period - apart)
    matrix = jnp.zeros((128, 128), jnp.float32)
    for k, w in enumerate(stencil_weights()[1], 1):
        matrix = jnp.where(apart == k, jnp.float32(w), matrix)
    high, low = two_parts(matrix)
    return jnp.concatenate([high, high, low], axis=axis)


def filtered_block(window, pot, before, scale, weight, lanes, rows):
    center_weight, side = stencil_weights()
    n = window.shape[0] - 2 * REACH
    mid = window[REACH : REACH + n]
    high, low = two_parts(mid.reshape(n * 16, 128))
    total = jnp.dot(
        jnp.concatenate([high, low, high], axis=1), lanes, preferred_element_type=jnp.float32
    ) + jnp.dot(
        rows, jnp.concatenate([high, low, high], axis=0), preferred_element_type=jnp.float32
    )
    total = total.reshape(n, 2, 8, 128)
    for k in range(1, REACH + 1):
        beside = window[REACH + k : REACH + k + n] + window[REACH - k : REACH - k + n]
        total = total + side[k - 1] * beside
    diag = (-1.5 * center_weight - (upper_edge + lower_edge) / 2.0) * scale
    result = (pot * scale + diag) * mid + (-0.5 * scale) * total
    if before is not None:
        result = result - weight * before
    return result


def filter_kernel(
    bands, orb, pot, sub, recv, rows, p0, p1, p2, out, given, pot_v,
    near_send, near_recv, far_send, far_recv, pot_send, pot_recv, pass_send, pass_recv,
    swap_send, swap_recv, move_sem, all_send, all_recv, row_send, row_recv, plane_sem, all_sem,
):
    quarter = orb.shape[1]
    slab, whole = 2 * quarter, 4 * quarter
    band, dom = lax.axis_index("band"), lax.axis_index("dom")
    core, half = lax.rem(dom, 2), lax.div(dom, 2)
    side = 4
    floor = side * side
    zl, x, yx = lax.div(band, floor), lax.rem(band, side), lax.rem(band, floor)
    shift = 2 * REACH
    left = jnp.where(zl < side // 2, 1, 0)
    long = core == left
    base = half * slab
    own_tile = dom * bands + band
    own_plane = lax.div(own_tile, 2)
    scalars = filter_scalars(DEG)
    buffers = (p0, p1, p2)
    rims = tuple(shift + REACH * (DEG - level) for level in range(DEG + 1))
    pot_rim = rims[1]

    def placed(u, count):
        return jnp.where(left == 1, u, slab - count - u)

    load = pltpu.make_async_copy(
        orb.at[core], p0.at[pl.ds(core * quarter + rims[0], quarter)], move_sem.at[0]
    )
    load.start()
    load_pot = pltpu.make_async_copy(
        pot, pot_v.at[pl.ds(core * quarter + pot_rim, quarter)], move_sem.at[1]
    )
    load_pot.start()

    sibling = {"dom": dom + 1 - 2 * core}
    partners = [{"dom": 2 * (1 - half) + k} for k in range(2)]

    def chip_along(shift):
        there = lax.rem(half * side + zl + shift, 2 * side)
        return {
            "band": lax.rem(there, side) * floor + yx,
            "dom": lax.div(there, side) * 2 + core,
        }

    x_line = [
        {"band": band - x + lax.rem(x + dx, side), "dom": dom if dk == 0 else dom + 1 - 2 * core}
        for dx in range(side)
        for dk in range(2)
    ][1:]
    y = lax.div(yx, side)
    y_line = [{"band": band + side * (lax.rem(y + dy, side) - y)} for dy in range(1, side)]
    z_line = [chip_along(dz) for dz in range(1, 2 * side)]
    other_partner = {"dom": 2 * (1 - half) + 1 - core}
    barrier = pltpu.get_barrier_semaphore()
    entered = (*z_line, other_partner, *x_line, *y_line)

    def tell(peers, semaphore):
        for peer in peers:
            pl.semaphore_signal(semaphore, inc=1, device_id=peer, device_id_type=MESH)

    tell(entered, barrier)
    lanes, lines = stencil_matrix(128, 0), stencil_matrix(16, 1)
    pl.semaphore_wait(barrier, len(entered))

    def remote(src, dst, send_sem, recv_sem, peer):
        return pltpu.make_async_remote_copy(
            src_ref=src, dst_ref=dst, send_sem=send_sem, recv_sem=recv_sem,
            device_id=peer, device_id_type=MESH,
        )

    own_rows = pltpu.make_async_copy(sub, rows.at[zl, y, x], move_sem.at[2])
    own_rows.start()
    row_lines = [
        (rows.at[zl, y, x], [{"band": lax.rem(band + d * floor, bands)} for d in range(1, side)]),
        (rows.at[:, y, x], y_line),
        (rows.at[:, :, x], [{"band": band - x + lax.rem(x + d, side)} for d in range(1, side)]),
    ]
    row_copies = [
        [
            remote(
                sub if stage == 0 else part_rows, part_rows,
                row_send.at[stage, at], row_recv.at[stage, at], peer,
            )
            for at, peer in enumerate(peers)
        ]
        for stage, (part_rows, peers) in enumerate(row_lines)
    ]

    def gather_rows(stage):
        if stage > 0:
            for copy in row_copies[stage - 1]:
                copy.wait_recv()
        for copy in row_copies[stage]:
            copy.start()

    gather_rows(0)
    pieces = [(0, REACH)] + [(REACH + 8 * i, 8) for i in range(3)]
    assert sum(n for _, n in pieces) == rims[0]
    far = []
    for o in range(2):
        group = []
        for at, (a, n) in enumerate(pieces):
            group.append(
                remote(
                    orb.at[o, pl.ds(jnp.where(left == 1, quarter - a - n, a), n)],
                    p0.at[pl.ds(placed(-a - n, n) + rims[0], n)],
                    far_send.at[o, at], far_recv.at[at], partners[o],
                )
            )
        n = REACH
        group.append(
            remote(
                orb.at[o, pl.ds(jnp.where(left == 1, 0, quarter - n), n)],
                p0.at[pl.ds(placed(slab, n) + rims[0], n)],
                far_send.at[o, 4], far_recv.at[4], partners[o],
            )
        )
        far.append(group)
    part = pot_rim // 8
    pot_far = [
        remote(
            pot.at[pl.ds(jnp.where(left == 1, quarter - pot_rim, 0) + (2 * x + o) * part, part)],
            pot_v.at[pl.ds(placed(-pot_rim, pot_rim) + pot_rim + (2 * x + o) * part, part)],
            pot_send.at[o], pot_recv, partners[o],
        )
        for o in range(2)
    ]
    mine = pot_v.at[pl.ds(placed(-pot_rim, pot_rim) + pot_rim + (2 * x + core) * part, part)]

    @pl.when(long)
    def _():
        for o in range(2):
            pot_far[o].start()
        for at in range(4):
            for o in range(2):
                far[o][at].start()

    @pl.when(jnp.logical_not(long))
    def _():
        for o in range(2):
            far[o][4].start()

    near = remote(
        orb.at[1 - core], p0.at[pl.ds(core * quarter + rims[0], quarter)],
        near_send.at[0], near_recv.at[0], sibling,
    )
    near_pot = remote(
        pot, pot_v.at[pl.ds(core * quarter + pot_rim, quarter)],
        near_send.at[1], near_recv.at[1], sibling,
    )
    near.start()
    near_pot.start()

    tell(y_line, plane_sem)

    step = 8

    def apply(level, u, blocks):
        scale, weight = scalars[level]

        def body(i, c):
            at = placed(u + i * step, step)
            before = None
            if level > 0:
                before = buffers[level - 1][pl.ds(at + rims[level - 1], step)]
            window = buffers[level][pl.ds(at + rims[level] - REACH, step + 2 * REACH)]
            pairs = filtered_block(
                window, pot_v[pl.ds(at + pot_rim, step)], before, scale, weight, lanes, lines
            )
            if level < DEG - 1:
                buffers[level + 1][pl.ds(at + rims[level + 1], step)] = pairs
            else:
                keep = jnp.where(core == 0, pairs[:, 0], pairs[:, 1])
                give = jnp.where(core == 0, pairs[:, 1], pairs[:, 0])
                out[pl.ds(at + rims[DEG], step), core] = keep
                given[pl.ds(at + rims[DEG], step)] = give
            return c

        lax.fori_loop(0, blocks, body, 0)

    swaps = []

    def spread(u, count):
        start = placed(u, count)
        part = pl.ds(start + rims[DEG], count)
        number = len(swaps)
        swap = remote(
            given.at[part], out.at[part, core], swap_send.at[number], swap_recv.at[number], sibling
        )
        swap.start()
        swaps.append(swap)
        swap.wait_recv()

        def send(i, c):
            at = lax.rem(i + yx, count)
            tile = lax.rem(2 * (base + start + at) + core + 2 * whole, 2 * whole)
            src = out.at[start + rims[DEG] + at]

            @pl.when(tile != own_tile)
            def _():
                peer = {"band": lax.rem(tile, bands), "dom": lax.div(tile, bands)}
                remote(src, recv.at[band], all_send, all_recv, peer).start()

            @pl.when(tile == own_tile)
            def _():
                pltpu.make_async_copy(src, recv.at[band], move_sem.at[3]).start()

            return c

        lax.fori_loop(0, count, send, 0)

    def advance(u):
        for level in range(DEG):
            apply(level, u + level * REACH, 1)
        spread(u + (DEG - 1) * REACH, 8)

    load.wait()
    load_pot.wait()
    near.wait_recv()
    near_pot.wait_recv()
    pl.semaphore_wait(plane_sem, len(y_line))
    tell(z_line, all_sem)
    apply(0, 8, 6)
    apply(1, 14, 4)
    apply(1, 42, 1)
    apply(2, 20, 3)
    pl.semaphore_wait(all_sem, len(z_line))
    spread(20, 24)

    pot_far[0].wait_recv()
    passed = [
        remote(mine, mine, pass_send.at[at], pass_recv.at[at], peer)
        for at, peer in enumerate(x_line)
    ]
    for copy in passed:
        copy.start()

    far[0][4].wait_recv()
    apply(0, slab - 8, 1)
    apply(1, slab - 14, 1)
    apply(2, slab - 20, 1)
    spread(slab - 20, 8)
    for at in range(4):
        if at == 1:
            own_rows.wait()
            gather_rows(1)
            for copy in passed:
                copy.wait_recv()
        if at == 3:
            gather_rows(2)
        far[0][at].wait_recv()
        advance(-8 * at)

    @pl.when(long)
    def _():
        for o in range(2):
            pot_far[o].wait_send()
            for at in range(4):
                far[o][at].wait_send()

    @pl.when(jnp.logical_not(long))
    def _():
        for o in range(2):
            far[o][4].wait_send()

    for copy in (near, near_pot, *passed):
        copy.wait_send()
    for copy in row_copies[2]:
        copy.wait_recv()
    for copies in row_copies:
        for copy in copies:
            copy.wait_send()
    for swap in swaps:
        swap.wait_send()

    def finish(number):
        arrived = recv.at[pl.ds(0, number)]
        pltpu.make_async_copy(arrived, arrived, all_send).wait()
        pltpu.make_async_copy(arrived, arrived, all_recv).wait()

    @pl.when(lax.rem(x, 2) == core)
    def _():
        pltpu.make_async_copy(out.at[0], recv.at[0], move_sem.at[3]).wait()
        finish(bands - 1)

    @pl.when(lax.rem(x, 2) != core)
    def _():
        finish(bands)


def rotate_kernel(recv_v, rows_v, out, out_v, sems):
    high, low = two_parts(jnp.concatenate([rows_v[:, 0], rows_v[:, 1]], axis=0).T)
    matrix = jnp.concatenate([high, high, low], axis=1)
    width = 256
    stores = []
    for at in range(0, 8 * 128, width):
        columns = []
        for r in range(at // 128, (at + width) // 128):
            values = jnp.concatenate([recv_v[:, 0, r], recv_v[:, 1, r]], axis=0)
            high, low = two_parts(values)
            columns.append(jnp.concatenate([high, low, high], axis=0))
        out_v[:, pl.ds(at, width)] = jnp.dot(
            matrix, jnp.concatenate(columns, axis=1), preferred_element_type=jnp.float32
        )
        store = pltpu.make_async_copy(
            out_v.at[:, pl.ds(at, width)], out.at[:, pl.ds(at, width)], sems.at[at // width]
        )
        store.start()
        stores.append(store)
    for store in stores:
        store.wait()


def per_device(bands, orbitals, potential, subspace):
    orbs, planes = orbitals.shape[0], orbitals.shape[1]
    orb = orbitals.reshape(orbs, planes, 2, 8, 128)
    pot = potential.reshape(planes, 2, 8, 128)
    f32 = jnp.float32
    dma = pltpu.SemaphoreType.DMA
    anywhere = pl.BlockSpec(memory_space=pl.ANY)
    slab, shift = 2 * planes, 2 * REACH
    recv, rows = pl.pallas_call(
        functools.partial(filter_kernel, bands),
        out_shape=(
            pltpu.VMEM((bands, orbs, 8, 128), f32),
            pltpu.VMEM((4, 4, 4, orbs, 128), f32),
        ),
        in_specs=[anywhere] * 3,
        out_specs=(anywhere,) * 2,
        scratch_shapes=[
            *[
                pltpu.VMEM((slab + 2 * (shift + REACH * (DEG - level)), 2, 8, 128), f32)
                for level in range(DEG)
            ],
            pltpu.VMEM((slab + 2 * shift, orbs, 8, 128), f32),
            pltpu.VMEM((slab + 2 * shift, 8, 128), f32),
            pltpu.VMEM((slab + 2 * (shift + REACH * (DEG - 1)), 2, 8, 128), f32),
            dma((2,)),
            dma((2,)),
            dma((2, 5)),
            dma((5,)),
            dma((2,)),
            dma,
            dma((7,)),
            dma((7,)),
            dma((6,)),
            dma((6,)),
            dma((4,)),
            dma,
            dma,
            dma((3, 3)),
            dma((3, 3)),
            pltpu.SemaphoreType.REGULAR,
            pltpu.SemaphoreType.REGULAR,
        ],
        compiler_params=pltpu.CompilerParams(
            collective_id=0, has_side_effects=True, vmem_limit_bytes=32 * 2**20
        ),
        name="filter",
    )(*(pltpu.with_memory_space_constraint(a, pltpu.HBM) for a in (orb, pot, subspace)))
    rows = rows.reshape(bands, orbs, 128)
    return pl.pallas_call(
        rotate_kernel,
        out_shape=jax.ShapeDtypeStruct((bands * orbs, 1024), f32),
        in_specs=[pl.BlockSpec(memory_space=pltpu.VMEM)] * 2,
        out_specs=anywhere,
        scratch_shapes=[pltpu.VMEM((bands * orbs, 1024), f32), dma((4,))],
        compiler_params=pltpu.CompilerParams(vmem_limit_bytes=32 * 2**20),
        name="rotate",
    )(*(pltpu.with_memory_space_constraint(a, pltpu.VMEM) for a in (recv, rows)))


def solution(mesh):
    in_specs = (P("band", "dom", None, None), P("dom", None, None), P("band", None))
    out_specs = P(None, ("dom", "band"))
    return jax.shard_map(
        functools.partial(per_device, mesh.shape["band"]),
        mesh=mesh,
        in_specs=in_specs,
        out_specs=out_specs,
        check_vma=False,
    )
```

```python
import functools
import math

import jax
import jax.numpy as jnp
from jax import lax
from jax.experimental import pallas as pl
from jax.experimental.pallas import tpu as pltpu
from jax.sharding import PartitionSpec as P

DEG = 3
REACH = 6
MESH = pl.DeviceIdType.MESH

upper_edge = 10.7
lower_edge = 1.5
bottom_edge = -1.0


def stencil_weights():
    factor_square = math.factorial(6) ** 2
    side_weights = []
    for offset in range(1, 7):
        side_weights.append(
            2.0
            * (-1.0) ** (offset + 1)
            * factor_square
            / (offset * offset * math.factorial(6 - offset) * math.factorial(6 + offset))
        )
    center_weight = -2.0 * sum(side_weights)
    return (center_weight, side_weights)


def filter_scalars(pass_count):
    half_width = (upper_edge - lower_edge) / 2.0
    sigma_now = half_width / (bottom_edge - (upper_edge + lower_edge) / 2.0)
    gamma_value = 2.0 / sigma_now
    scalars = [(sigma_now / half_width, 0.0)]
    for pass_index in range(pass_count - 1):
        sigma_next = 1.0 / (gamma_value - sigma_now)
        scalars.append((2.0 * sigma_next / half_width, sigma_now * sigma_next))
        sigma_now = sigma_next
    return scalars


def two_parts(values):
    high = values.astype(jnp.bfloat16)
    return high, (values - high.astype(jnp.float32)).astype(jnp.bfloat16)


def stencil_matrix(period, axis):
    rows = lax.broadcasted_iota(jnp.int32, (128, 128), 0)
    columns = lax.broadcasted_iota(jnp.int32, (128, 128), 1)
    apart = jnp.abs(rows - columns)
    if period < 128:
        same = jnp.bitwise_or(rows, period - 1) == jnp.bitwise_or(columns, period - 1)
        apart = jnp.where(same, apart, 0)
    apart = jnp.minimum(apart, period - apart)
    matrix = jnp.zeros((128, 128), jnp.float32)
    for k, w in enumerate(stencil_weights()[1], 1):
        matrix = jnp.where(apart == k, jnp.float32(w), matrix)
    high, low = two_parts(matrix)
    return jnp.concatenate([high, high, low], axis=axis)


def filtered_block(window, pot, before, scale, weight, lanes, rows):
    center_weight, side = stencil_weights()
    n = window.shape[0] - 2 * REACH
    mid = window[REACH : REACH + n]
    high, low = two_parts(mid.reshape(n * 16, 128))
    total = jnp.dot(
        jnp.concatenate([high, low, high], axis=1), lanes, preferred_element_type=jnp.float32
    ) + jnp.dot(
        rows, jnp.concatenate([high, low, high], axis=0), preferred_element_type=jnp.float32
    )
    total = total.reshape(n, 2, 8, 128)
    for k in range(1, REACH + 1):
        beside = window[REACH + k : REACH + k + n] + window[REACH - k : REACH - k + n]
        total = total + side[k - 1] * beside
    diag = (-1.5 * center_weight - (upper_edge + lower_edge) / 2.0) * scale
    result = (pot * scale + diag) * mid + (-0.5 * scale) * total
    if before is not None:
        result = result - weight * before
    return result


def filter_kernel(
    bands, orb, pot, sub, recv, rows, p0, p1, p2, out, given, pot_v,
    near_send, near_recv, far_send, far_recv, pot_send, pot_recv, pass_send, pass_recv,
    swap_send, swap_recv, move_sem, all_send, all_recv, row_send, row_recv, plane_sem, all_sem,
):
    quarter = orb.shape[1]
    slab, whole = 2 * quarter, 4 * quarter
    band, dom = lax.axis_index("band"), lax.axis_index("dom")
    core, half = lax.rem(dom, 2), lax.div(dom, 2)
    side = 4
    floor = side * side
    zl, x, yx = lax.div(band, floor), lax.rem(band, side), lax.rem(band, floor)
    shift = 2 * REACH
    left = jnp.where(zl < side // 2, 1, 0)
    long = core == left
    base = half * slab
    own_tile = dom * bands + band
    own_plane = lax.div(own_tile, 2)
    scalars = filter_scalars(DEG)
    buffers = (p0, p1, p2)
    rims = tuple(shift + REACH * (DEG - level) for level in range(DEG + 1))
    pot_rim = rims[1]

    def placed(u, count):
        return jnp.where(left == 1, u, slab - count - u)

    load = pltpu.make_async_copy(
        orb.at[core], p0.at[pl.ds(core * quarter + rims[0], quarter)], move_sem.at[0]
    )
    load.start()
    load_pot = pltpu.make_async_copy(
        pot, pot_v.at[pl.ds(core * quarter + pot_rim, quarter)], move_sem.at[1]
    )
    load_pot.start()

    sibling = {"dom": dom + 1 - 2 * core}
    partners = [{"dom": 2 * (1 - half) + k} for k in range(2)]

    def chip_along(shift):
        there = lax.rem(half * side + zl + shift, 2 * side)
        return {
            "band": lax.rem(there, side) * floor + yx,
            "dom": lax.div(there, side) * 2 + core,
        }

    x_line = [
        {"band": band - x + lax.rem(x + dx, side), "dom": dom if dk == 0 else dom + 1 - 2 * core}
        for dx in range(side)
        for dk in range(2)
    ][1:]
    y = lax.div(yx, side)
    y_line = [{"band": band + side * (lax.rem(y + dy, side) - y)} for dy in range(1, side)]
    z_line = [chip_along(dz) for dz in range(1, 2 * side)]
    other_partner = {"dom": 2 * (1 - half) + 1 - core}
    barrier = pltpu.get_barrier_semaphore()
    entered = (*z_line, other_partner, *x_line, *y_line)

    def tell(peers, semaphore):
        for peer in peers:
            pl.semaphore_signal(semaphore, inc=1, device_id=peer, device_id_type=MESH)

    tell(entered, barrier)
    lanes, lines = stencil_matrix(128, 0), stencil_matrix(16, 1)
    pl.semaphore_wait(barrier, len(entered))

    def remote(src, dst, send_sem, recv_sem, peer):
        return pltpu.make_async_remote_copy(
            src_ref=src, dst_ref=dst, send_sem=send_sem, recv_sem=recv_sem,
            device_id=peer, device_id_type=MESH,
        )

    own_rows = pltpu.make_async_copy(sub, rows.at[zl, y, x], move_sem.at[2])
    own_rows.start()
    row_lines = [
        (rows.at[zl, y, x], [{"band": lax.rem(band + d * floor, bands)} for d in range(1, side)]),
        (rows.at[:, y, x], y_line),
        (rows.at[:, :, x], [{"band": band - x + lax.rem(x + d, side)} for d in range(1, side)]),
    ]
    row_copies = [
        [
            remote(
                sub if stage == 0 else part_rows, part_rows,
                row_send.at[stage, at], row_recv.at[stage, at], peer,
            )
            for at, peer in enumerate(peers)
        ]
        for stage, (part_rows, peers) in enumerate(row_lines)
    ]

    def gather_rows(stage):
        if stage > 0:
            for copy in row_copies[stage - 1]:
                copy.wait_recv()
        for copy in row_copies[stage]:
            copy.start()

    gather_rows(0)
    pieces = [(0, REACH)] + [(REACH + 8 * i, 8) for i in range(3)]
    assert sum(n for _, n in pieces) == rims[0]
    far = []
    for o in range(2):
        group = []
        for at, (a, n) in enumerate(pieces):
            group.append(
                remote(
                    orb.at[o, pl.ds(jnp.where(left == 1, quarter - a - n, a), n)],
                    p0.at[pl.ds(placed(-a - n, n) + rims[0], n)],
                    far_send.at[o, at], far_recv.at[at], partners[o],
                )
            )
        n = REACH
        group.append(
            remote(
                orb.at[o, pl.ds(jnp.where(left == 1, 0, quarter - n), n)],
                p0.at[pl.ds(placed(slab, n) + rims[0], n)],
                far_send.at[o, 4], far_recv.at[4], partners[o],
            )
        )
        far.append(group)
    part = pot_rim // 8
    pot_far = [
        remote(
            pot.at[pl.ds(jnp.where(left == 1, quarter - pot_rim, 0) + (2 * x + o) * part, part)],
            pot_v.at[pl.ds(placed(-pot_rim, pot_rim) + pot_rim + (2 * x + o) * part, part)],
            pot_send.at[o], pot_recv, partners[o],
        )
        for o in range(2)
    ]
    mine = pot_v.at[pl.ds(placed(-pot_rim, pot_rim) + pot_rim + (2 * x + core) * part, part)]

    @pl.when(long)
    def _():
        for o in range(2):
            pot_far[o].start()
        for at in range(2):
            for o in range(2):
                far[o][at].start()

    @pl.when(jnp.logical_not(long))
    def _():
        for o in range(2):
            far[o][4].start()

    near = remote(
        orb.at[1 - core], p0.at[pl.ds(core * quarter + rims[0], quarter)],
        near_send.at[0], near_recv.at[0], sibling,
    )
    near_pot = remote(
        pot, pot_v.at[pl.ds(core * quarter + pot_rim, quarter)],
        near_send.at[1], near_recv.at[1], sibling,
    )
    near.start()
    near_pot.start()

    tell(y_line, plane_sem)

    step = 8

    def apply(level, u, blocks):
        scale, weight = scalars[level]

        def body(i, c):
            at = placed(u + i * step, step)
            before = None
            if level > 0:
                before = buffers[level - 1][pl.ds(at + rims[level - 1], step)]
            window = buffers[level][pl.ds(at + rims[level] - REACH, step + 2 * REACH)]
            pairs = filtered_block(
                window, pot_v[pl.ds(at + pot_rim, step)], before, scale, weight, lanes, lines
            )
            if level < DEG - 1:
                buffers[level + 1][pl.ds(at + rims[level + 1], step)] = pairs
            else:
                keep = jnp.where(core == 0, pairs[:, 0], pairs[:, 1])
                give = jnp.where(core == 0, pairs[:, 1], pairs[:, 0])
                out[pl.ds(at + rims[DEG], step), core] = keep
                given[pl.ds(at + rims[DEG], step)] = give
            return c

        lax.fori_loop(0, blocks, body, 0)

    swaps = []

    def spread(u, count):
        start = placed(u, count)
        part = pl.ds(start + rims[DEG], count)
        number = len(swaps)
        swap = remote(
            given.at[part], out.at[part, core], swap_send.at[number], swap_recv.at[number], sibling
        )
        swap.start()
        swaps.append(swap)
        swap.wait_recv()

        def send(i, c):
            at = lax.rem(i + yx, count)
            tile = lax.rem(2 * (base + start + at) + core + 2 * whole, 2 * whole)
            src = out.at[start + rims[DEG] + at]

            @pl.when(tile != own_tile)
            def _():
                peer = {"band": lax.rem(tile, bands), "dom": lax.div(tile, bands)}
                remote(src, recv.at[band], all_send, all_recv, peer).start()

            @pl.when(tile == own_tile)
            def _():
                pltpu.make_async_copy(src, recv.at[band], move_sem.at[3]).start()

            return c

        lax.fori_loop(0, count, send, 0)

    def advance(u):
        for level in range(DEG):
            apply(level, u + level * REACH, 1)
        spread(u + (DEG - 1) * REACH, 8)

    def next_far(at):
        @pl.when(long)
        def _():
            for o in range(2):
                far[o][at - 2].wait_send()
            for o in range(2):
                far[o][at].start()

    load.wait()
    load_pot.wait()
    next_far(2)
    near.wait_recv()
    near_pot.wait_recv()
    next_far(3)
    pl.semaphore_wait(plane_sem, len(y_line))
    tell(z_line, all_sem)
    apply(0, 8, 6)
    apply(1, 14, 4)
    apply(1, 42, 1)
    apply(2, 20, 3)
    pl.semaphore_wait(all_sem, len(z_line))
    spread(20, 24)

    pot_far[0].wait_recv()
    passed = [
        remote(mine, mine, pass_send.at[at], pass_recv.at[at], peer)
        for at, peer in enumerate(x_line)
    ]
    for copy in passed:
        copy.start()

    far[0][4].wait_recv()
    apply(0, slab - 8, 1)
    apply(1, slab - 14, 1)
    apply(2, slab - 20, 1)
    spread(slab - 20, 8)
    for at in range(4):
        if at == 1:
            own_rows.wait()
            gather_rows(1)
            for copy in passed:
                copy.wait_recv()
        if at == 3:
            gather_rows(2)
        far[0][at].wait_recv()
        advance(-8 * at)

    @pl.when(long)
    def _():
        for o in range(2):
            pot_far[o].wait_send()
            for at in range(2, 4):
                far[o][at].wait_send()

    @pl.when(jnp.logical_not(long))
    def _():
        for o in range(2):
            far[o][4].wait_send()

    for copy in (near, near_pot, *passed):
        copy.wait_send()
    for copy in row_copies[2]:
        copy.wait_recv()
    for copies in row_copies:
        for copy in copies:
            copy.wait_send()
    for swap in swaps:
        swap.wait_send()

    def finish(number):
        arrived = recv.at[pl.ds(0, number)]
        pltpu.make_async_copy(arrived, arrived, all_send).wait()
        pltpu.make_async_copy(arrived, arrived, all_recv).wait()

    @pl.when(lax.rem(x, 2) == core)
    def _():
        pltpu.make_async_copy(out.at[0], recv.at[0], move_sem.at[3]).wait()
        finish(bands - 1)

    @pl.when(lax.rem(x, 2) != core)
    def _():
        finish(bands)


def rotate_kernel(recv_v, rows_v, out, out_v, sems):
    high, low = two_parts(jnp.concatenate([rows_v[:, 0], rows_v[:, 1]], axis=0).T)
    matrix = jnp.concatenate([high, high, low], axis=1)
    width = 256
    stores = []
    for at in range(0, 8 * 128, width):
        columns = []
        for r in range(at // 128, (at + width) // 128):
            values = jnp.concatenate([recv_v[:, 0, r], recv_v[:, 1, r]], axis=0)
            high, low = two_parts(values)
            columns.append(jnp.concatenate([high, low, high], axis=0))
        out_v[:, pl.ds(at, width)] = jnp.dot(
            matrix, jnp.concatenate(columns, axis=1), preferred_element_type=jnp.float32
        )
        store = pltpu.make_async_copy(
            out_v.at[:, pl.ds(at, width)], out.at[:, pl.ds(at, width)], sems.at[at // width]
        )
        store.start()
        stores.append(store)
    for store in stores:
        store.wait()


def per_device(bands, orbitals, potential, subspace):
    orbs, planes = orbitals.shape[0], orbitals.shape[1]
    orb = orbitals.reshape(orbs, planes, 2, 8, 128)
    pot = potential.reshape(planes, 2, 8, 128)
    f32 = jnp.float32
    dma = pltpu.SemaphoreType.DMA
    anywhere = pl.BlockSpec(memory_space=pl.ANY)
    slab, shift = 2 * planes, 2 * REACH
    recv, rows = pl.pallas_call(
        functools.partial(filter_kernel, bands),
        out_shape=(
            pltpu.VMEM((bands, orbs, 8, 128), f32),
            pltpu.VMEM((4, 4, 4, orbs, 128), f32),
        ),
        in_specs=[anywhere] * 3,
        out_specs=(anywhere,) * 2,
        scratch_shapes=[
            *[
                pltpu.VMEM((slab + 2 * (shift + REACH * (DEG - level)), 2, 8, 128), f32)
                for level in range(DEG)
            ],
            pltpu.VMEM((slab + 2 * shift, orbs, 8, 128), f32),
            pltpu.VMEM((slab + 2 * shift, 8, 128), f32),
            pltpu.VMEM((slab + 2 * (shift + REACH * (DEG - 1)), 2, 8, 128), f32),
            dma((2,)),
            dma((2,)),
            dma((2, 5)),
            dma((5,)),
            dma((2,)),
            dma,
            dma((7,)),
            dma((7,)),
            dma((6,)),
            dma((6,)),
            dma((4,)),
            dma,
            dma,
            dma((3, 3)),
            dma((3, 3)),
            pltpu.SemaphoreType.REGULAR,
            pltpu.SemaphoreType.REGULAR,
        ],
        compiler_params=pltpu.CompilerParams(
            collective_id=0, has_side_effects=True, vmem_limit_bytes=32 * 2**20
        ),
        name="filter",
    )(*(pltpu.with_memory_space_constraint(a, pltpu.HBM) for a in (orb, pot, subspace)))
    rows = rows.reshape(bands, orbs, 128)
    return pl.pallas_call(
        rotate_kernel,
        out_shape=jax.ShapeDtypeStruct((bands * orbs, 1024), f32),
        in_specs=[pl.BlockSpec(memory_space=pltpu.VMEM)] * 2,
        out_specs=anywhere,
        scratch_shapes=[pltpu.VMEM((bands * orbs, 1024), f32), dma((4,))],
        compiler_params=pltpu.CompilerParams(vmem_limit_bytes=32 * 2**20),
        name="rotate",
    )(*(pltpu.with_memory_space_constraint(a, pltpu.VMEM) for a in (recv, rows)))


def solution(mesh):
    in_specs = (P("band", "dom", None, None), P("dom", None, None), P("band", None))
    out_specs = P(None, ("dom", "band"))
    return jax.shard_map(
        functools.partial(per_device, mesh.shape["band"]),
        mesh=mesh,
        in_specs=in_specs,
        out_specs=out_specs,
        check_vma=False,
    )
```

```python
import functools
import math

import jax
import jax.numpy as jnp
from jax import lax
from jax.experimental import pallas as pl
from jax.experimental.pallas import tpu as pltpu
from jax.sharding import PartitionSpec as P

DEG = 3
REACH = 6
MESH = pl.DeviceIdType.MESH

upper_edge = 10.7
lower_edge = 1.5
bottom_edge = -1.0


def stencil_weights():
    factor_square = math.factorial(6) ** 2
    side_weights = []
    for offset in range(1, 7):
        side_weights.append(
            2.0
            * (-1.0) ** (offset + 1)
            * factor_square
            / (offset * offset * math.factorial(6 - offset) * math.factorial(6 + offset))
        )
    center_weight = -2.0 * sum(side_weights)
    return (center_weight, side_weights)


def filter_scalars(pass_count):
    half_width = (upper_edge - lower_edge) / 2.0
    sigma_now = half_width / (bottom_edge - (upper_edge + lower_edge) / 2.0)
    gamma_value = 2.0 / sigma_now
    scalars = [(sigma_now / half_width, 0.0)]
    for pass_index in range(pass_count - 1):
        sigma_next = 1.0 / (gamma_value - sigma_now)
        scalars.append((2.0 * sigma_next / half_width, sigma_now * sigma_next))
        sigma_now = sigma_next
    return scalars


def two_parts(values):
    high = values.astype(jnp.bfloat16)
    return high, (values - high.astype(jnp.float32)).astype(jnp.bfloat16)


def stencil_matrix(period, axis):
    rows = lax.broadcasted_iota(jnp.int32, (128, 128), 0)
    columns = lax.broadcasted_iota(jnp.int32, (128, 128), 1)
    apart = jnp.abs(rows - columns)
    if period < 128:
        same = jnp.bitwise_or(rows, period - 1) == jnp.bitwise_or(columns, period - 1)
        apart = jnp.where(same, apart, 0)
    apart = jnp.minimum(apart, period - apart)
    matrix = jnp.zeros((128, 128), jnp.float32)
    for k, w in enumerate(stencil_weights()[1], 1):
        matrix = jnp.where(apart == k, jnp.float32(w), matrix)
    high, low = two_parts(matrix)
    return jnp.concatenate([high, high, low], axis=axis)


def filtered_block(window, pot, before, scale, weight, lanes, rows):
    center_weight, side = stencil_weights()
    n = window.shape[0] - 2 * REACH
    mid = window[REACH : REACH + n]
    high, low = two_parts(mid.reshape(n * 16, 128))
    total = jnp.dot(
        jnp.concatenate([high, low, high], axis=1), lanes, preferred_element_type=jnp.float32
    ) + jnp.dot(
        rows, jnp.concatenate([high, low, high], axis=0), preferred_element_type=jnp.float32
    )
    total = total.reshape(n, 2, 8, 128)
    for k in range(1, REACH + 1):
        beside = window[REACH + k : REACH + k + n] + window[REACH - k : REACH - k + n]
        total = total + side[k - 1] * beside
    diag = (-1.5 * center_weight - (upper_edge + lower_edge) / 2.0) * scale
    result = (pot * scale + diag) * mid + (-0.5 * scale) * total
    if before is not None:
        result = result - weight * before
    return result


def filter_kernel(
    bands, orb, pot, sub, recv, rows, p0, p1, p2, out, given, pot_v,
    near_send, near_recv, far_send, far_recv, pot_send, pot_recv, pass_send, pass_recv,
    swap_send, swap_recv, move_sem, all_send, all_recv, row_send, row_recv, plane_sem, all_sem,
):
    quarter = orb.shape[1]
    slab, whole = 2 * quarter, 4 * quarter
    band, dom = lax.axis_index("band"), lax.axis_index("dom")
    core, half = lax.rem(dom, 2), lax.div(dom, 2)
    side = 4
    floor = side * side
    zl, x, yx = lax.div(band, floor), lax.rem(band, side), lax.rem(band, floor)
    shift = 2 * REACH
    left = jnp.where(zl < side // 2, 1, 0)
    long = core == left
    base = half * slab
    own_tile = dom * bands + band
    own_plane = lax.div(own_tile, 2)
    scalars = filter_scalars(DEG)
    buffers = (p0, p1, p2)
    rims = tuple(shift + REACH * (DEG - level) for level in range(DEG + 1))
    pot_rim = rims[1]

    def placed(u, count):
        return jnp.where(left == 1, u, slab - count - u)

    load = pltpu.make_async_copy(
        orb.at[core], p0.at[pl.ds(core * quarter + rims[0], quarter)], move_sem.at[0]
    )
    load.start()
    load_pot = pltpu.make_async_copy(
        pot, pot_v.at[pl.ds(core * quarter + pot_rim, quarter)], move_sem.at[1]
    )
    load_pot.start()

    sibling = {"dom": dom + 1 - 2 * core}
    partners = [{"dom": 2 * (1 - half) + k} for k in range(2)]

    def chip_along(shift):
        there = lax.rem(half * side + zl + shift, 2 * side)
        return {
            "band": lax.rem(there, side) * floor + yx,
            "dom": lax.div(there, side) * 2 + core,
        }

    x_line = [
        {"band": band - x + lax.rem(x + dx, side), "dom": dom if dk == 0 else dom + 1 - 2 * core}
        for dx in range(side)
        for dk in range(2)
    ][1:]
    y = lax.div(yx, side)
    y_line = [{"band": band + side * (lax.rem(y + dy, side) - y)} for dy in range(1, side)]
    z_line = [chip_along(dz) for dz in range(1, 2 * side)]
    other_partner = {"dom": 2 * (1 - half) + 1 - core}
    barrier = pltpu.get_barrier_semaphore()
    entered = (*z_line, other_partner, *x_line, *y_line)

    def tell(peers, semaphore):
        for peer in peers:
            pl.semaphore_signal(semaphore, inc=1, device_id=peer, device_id_type=MESH)

    tell(entered, barrier)
    lanes, lines = stencil_matrix(128, 0), stencil_matrix(16, 1)
    pl.semaphore_wait(barrier, len(entered))

    def remote(src, dst, send_sem, recv_sem, peer):
        return pltpu.make_async_remote_copy(
            src_ref=src, dst_ref=dst, send_sem=send_sem, recv_sem=recv_sem,
            device_id=peer, device_id_type=MESH,
        )

    own_rows = pltpu.make_async_copy(sub, rows.at[zl, y, x], move_sem.at[2])
    own_rows.start()
    row_lines = [
        (rows.at[zl, y, x], [{"band": lax.rem(band + d * floor, bands)} for d in range(1, side)]),
        (rows.at[:, y, x], y_line),
        (rows.at[:, :, x], [{"band": band - x + lax.rem(x + d, side)} for d in range(1, side)]),
    ]
    row_copies = [
        [
            remote(
                sub if stage == 0 else part_rows, part_rows,
                row_send.at[stage, at], row_recv.at[stage, at], peer,
            )
            for at, peer in enumerate(peers)
        ]
        for stage, (part_rows, peers) in enumerate(row_lines)
    ]

    def gather_rows(stage):
        if stage > 0:
            for copy in row_copies[stage - 1]:
                copy.wait_recv()
        for copy in row_copies[stage]:
            copy.start()

    gather_rows(0)
    pieces = [(0, REACH)] + [(REACH + 8 * i, 8) for i in range(3)]
    assert sum(n for _, n in pieces) == rims[0]
    far, far_parts = [], []
    for o in range(2):
        group, group_parts = [], []
        for at, (a, n) in enumerate(pieces + [(slab, REACH)]):
            if a < slab:
                source = jnp.where(left == 1, quarter - a - n, a)
                target = placed(-a - n, n) + rims[0]
            else:
                source = jnp.where(left == 1, 0, quarter - n)
                target = placed(a, n) + rims[0]
            copies = [
                remote(
                    orb.at[o, pl.ds(source + i, size)], p0.at[pl.ds(target + i, size)],
                    far_send.at[o, at], far_recv.at[at], partners[o],
                )
                for size, places in ((n, (0,)), (2, range(0, n, 2)))
                for i in places
            ]
            group.append(copies[0])
            group_parts.append(copies[1:])
        far.append(group)
        far_parts.append(group_parts)
    part = pot_rim // 8
    pot_far = [
        remote(
            pot.at[pl.ds(jnp.where(left == 1, quarter - pot_rim, 0) + (2 * x + o) * part, part)],
            pot_v.at[pl.ds(placed(-pot_rim, pot_rim) + pot_rim + (2 * x + o) * part, part)],
            pot_send.at[o], pot_recv, partners[o],
        )
        for o in range(2)
    ]
    mine = pot_v.at[pl.ds(placed(-pot_rim, pot_rim) + pot_rim + (2 * x + core) * part, part)]

    @pl.when(long)
    def _():
        for o in range(2):
            pot_far[o].start()
        for at in range(4):
            for o in range(2):
                for copy in far_parts[o][at]:
                    copy.start()

    @pl.when(jnp.logical_not(long))
    def _():
        for o in range(2):
            for copy in far_parts[o][4]:
                copy.start()

    near, *near_parts = [
        remote(
            orb.at[1 - core, pl.ds(i, size)],
            p0.at[pl.ds(core * quarter + rims[0] + i, size)],
            near_send.at[0], near_recv.at[0], sibling,
        )
        for size, places in ((quarter, (0,)), (4, range(0, quarter, 4)))
        for i in places
    ]
    near_pot, *near_pot_parts = [
        remote(
            pot.at[pl.ds(i, size)], pot_v.at[pl.ds(core * quarter + pot_rim + i, size)],
            near_send.at[1], near_recv.at[1], sibling,
        )
        for size, places in ((quarter, (0,)), (4, range(0, quarter, 4)))
        for i in places
    ]
    for copy in (*near_parts, *near_pot_parts):
        copy.start()

    tell(y_line, plane_sem)

    step = 8

    def apply(level, u, blocks):
        scale, weight = scalars[level]

        def body(i, c):
            at = placed(u + i * step, step)
            before = None
            if level > 0:
                before = buffers[level - 1][pl.ds(at + rims[level - 1], step)]
            window = buffers[level][pl.ds(at + rims[level] - REACH, step + 2 * REACH)]
            pairs = filtered_block(
                window, pot_v[pl.ds(at + pot_rim, step)], before, scale, weight, lanes, lines
            )
            if level < DEG - 1:
                buffers[level + 1][pl.ds(at + rims[level + 1], step)] = pairs
            else:
                keep = jnp.where(core == 0, pairs[:, 0], pairs[:, 1])
                give = jnp.where(core == 0, pairs[:, 1], pairs[:, 0])
                out[pl.ds(at + rims[DEG], step), core] = keep
                given[pl.ds(at + rims[DEG], step)] = give
            return c

        lax.fori_loop(0, blocks, body, 0)

    swaps = []

    def spread(u, count):
        start = placed(u, count)
        part = pl.ds(start + rims[DEG], count)
        number = len(swaps)
        swap = remote(
            given.at[part], out.at[part, core], swap_send.at[number], swap_recv.at[number], sibling
        )
        swap.start()
        swaps.append(swap)
        swap.wait_recv()

        def send(i, c):
            at = lax.rem(i + yx, count)
            tile = lax.rem(2 * (base + start + at) + core + 2 * whole, 2 * whole)
            src = out.at[start + rims[DEG] + at]

            @pl.when(tile != own_tile)
            def _():
                peer = {"band": lax.rem(tile, bands), "dom": lax.div(tile, bands)}
                remote(src, recv.at[band], all_send, all_recv, peer).start()

            @pl.when(tile == own_tile)
            def _():
                pltpu.make_async_copy(src, recv.at[band], move_sem.at[3]).start()

            return c

        lax.fori_loop(0, count, send, 0)

    def advance(u):
        for level in range(DEG):
            apply(level, u + level * REACH, 1)
        spread(u + (DEG - 1) * REACH, 8)

    load.wait()
    load_pot.wait()
    near.wait_recv()
    near_pot.wait_recv()
    pl.semaphore_wait(plane_sem, len(y_line))
    tell(z_line, all_sem)
    apply(0, 8, 6)
    apply(1, 14, 4)
    apply(1, 42, 1)
    apply(2, 20, 3)
    pl.semaphore_wait(all_sem, len(z_line))
    spread(20, 24)

    pot_far[0].wait_recv()
    passed = [
        remote(mine, mine, pass_send.at[at], pass_recv.at[at], peer)
        for at, peer in enumerate(x_line)
    ]
    for copy in passed:
        copy.start()

    far[0][4].wait_recv()
    apply(0, slab - 8, 1)
    apply(1, slab - 14, 1)
    apply(2, slab - 20, 1)
    spread(slab - 20, 8)
    for at in range(4):
        if at == 1:
            own_rows.wait()
            gather_rows(1)
            for copy in passed:
                copy.wait_recv()
        if at == 3:
            gather_rows(2)
        far[0][at].wait_recv()
        advance(-8 * at)

    @pl.when(long)
    def _():
        for o in range(2):
            pot_far[o].wait_send()
            for at in range(4):
                far[o][at].wait_send()

    @pl.when(jnp.logical_not(long))
    def _():
        for o in range(2):
            far[o][4].wait_send()

    for copy in (near, near_pot, *passed):
        copy.wait_send()
    for copy in row_copies[2]:
        copy.wait_recv()
    for copies in row_copies:
        for copy in copies:
            copy.wait_send()
    for swap in swaps:
        swap.wait_send()

    def finish(number):
        arrived = recv.at[pl.ds(0, number)]
        pltpu.make_async_copy(arrived, arrived, all_send).wait()
        pltpu.make_async_copy(arrived, arrived, all_recv).wait()

    @pl.when(lax.rem(x, 2) == core)
    def _():
        pltpu.make_async_copy(out.at[0], recv.at[0], move_sem.at[3]).wait()
        finish(bands - 1)

    @pl.when(lax.rem(x, 2) != core)
    def _():
        finish(bands)


def rotate_kernel(recv_v, rows_v, out, out_v, sems):
    high, low = two_parts(jnp.concatenate([rows_v[:, 0], rows_v[:, 1]], axis=0).T)
    matrix = jnp.concatenate([high, high, low], axis=1)
    width = 256
    stores = []
    for at in range(0, 8 * 128, width):
        columns = []
        for r in range(at // 128, (at + width) // 128):
            values = jnp.concatenate([recv_v[:, 0, r], recv_v[:, 1, r]], axis=0)
            high, low = two_parts(values)
            columns.append(jnp.concatenate([high, low, high], axis=0))
        out_v[:, pl.ds(at, width)] = jnp.dot(
            matrix, jnp.concatenate(columns, axis=1), preferred_element_type=jnp.float32
        )
        store = pltpu.make_async_copy(
            out_v.at[:, pl.ds(at, width)], out.at[:, pl.ds(at, width)], sems.at[at // width]
        )
        store.start()
        stores.append(store)
    for store in stores:
        store.wait()


def per_device(bands, orbitals, potential, subspace):
    orbs, planes = orbitals.shape[0], orbitals.shape[1]
    orb = orbitals.reshape(orbs, planes, 2, 8, 128)
    pot = potential.reshape(planes, 2, 8, 128)
    f32 = jnp.float32
    dma = pltpu.SemaphoreType.DMA
    anywhere = pl.BlockSpec(memory_space=pl.ANY)
    slab, shift = 2 * planes, 2 * REACH
    recv, rows = pl.pallas_call(
        functools.partial(filter_kernel, bands),
        out_shape=(
            pltpu.VMEM((bands, orbs, 8, 128), f32),
            pltpu.VMEM((4, 4, 4, orbs, 128), f32),
        ),
        in_specs=[anywhere] * 3,
        out_specs=(anywhere,) * 2,
        scratch_shapes=[
            *[
                pltpu.VMEM((slab + 2 * (shift + REACH * (DEG - level)), 2, 8, 128), f32)
                for level in range(DEG)
            ],
            pltpu.VMEM((slab + 2 * shift, orbs, 8, 128), f32),
            pltpu.VMEM((slab + 2 * shift, 8, 128), f32),
            pltpu.VMEM((slab + 2 * (shift + REACH * (DEG - 1)), 2, 8, 128), f32),
            dma((2,)),
            dma((2,)),
            dma((2, 5)),
            dma((5,)),
            dma((2,)),
            dma,
            dma((7,)),
            dma((7,)),
            dma((6,)),
            dma((6,)),
            dma((4,)),
            dma,
            dma,
            dma((3, 3)),
            dma((3, 3)),
            pltpu.SemaphoreType.REGULAR,
            pltpu.SemaphoreType.REGULAR,
        ],
        compiler_params=pltpu.CompilerParams(
            collective_id=0, has_side_effects=True, vmem_limit_bytes=32 * 2**20
        ),
        name="filter",
    )(*(pltpu.with_memory_space_constraint(a, pltpu.HBM) for a in (orb, pot, subspace)))
    rows = rows.reshape(bands, orbs, 128)
    return pl.pallas_call(
        rotate_kernel,
        out_shape=jax.ShapeDtypeStruct((bands * orbs, 1024), f32),
        in_specs=[pl.BlockSpec(memory_space=pltpu.VMEM)] * 2,
        out_specs=anywhere,
        scratch_shapes=[pltpu.VMEM((bands * orbs, 1024), f32), dma((4,))],
        compiler_params=pltpu.CompilerParams(vmem_limit_bytes=32 * 2**20),
        name="rotate",
    )(*(pltpu.with_memory_space_constraint(a, pltpu.VMEM) for a in (recv, rows)))


def solution(mesh):
    in_specs = (P("band", "dom", None, None), P("dom", None, None), P("band", None))
    out_specs = P(None, ("dom", "band"))
    return jax.shard_map(
        functools.partial(per_device, mesh.shape["band"]),
        mesh=mesh,
        in_specs=in_specs,
        out_specs=out_specs,
        check_vma=False,
    )
```

```python
import functools
import math

import jax
import jax.numpy as jnp
from jax import lax
from jax.experimental import pallas as pl
from jax.experimental.pallas import tpu as pltpu
from jax.sharding import PartitionSpec as P

DEG = 3
REACH = 6
MESH = pl.DeviceIdType.MESH

upper_edge = 10.7
lower_edge = 1.5
bottom_edge = -1.0


def stencil_weights():
    factor_square = math.factorial(6) ** 2
    side_weights = []
    for offset in range(1, 7):
        side_weights.append(
            2.0
            * (-1.0) ** (offset + 1)
            * factor_square
            / (offset * offset * math.factorial(6 - offset) * math.factorial(6 + offset))
        )
    center_weight = -2.0 * sum(side_weights)
    return (center_weight, side_weights)


def filter_scalars(pass_count):
    half_width = (upper_edge - lower_edge) / 2.0
    sigma_now = half_width / (bottom_edge - (upper_edge + lower_edge) / 2.0)
    gamma_value = 2.0 / sigma_now
    scalars = [(sigma_now / half_width, 0.0)]
    for pass_index in range(pass_count - 1):
        sigma_next = 1.0 / (gamma_value - sigma_now)
        scalars.append((2.0 * sigma_next / half_width, sigma_now * sigma_next))
        sigma_now = sigma_next
    return scalars


def two_parts(values):
    high = values.astype(jnp.bfloat16)
    return high, (values - high.astype(jnp.float32)).astype(jnp.bfloat16)


def stencil_matrix(size, period, axis):
    rows = lax.broadcasted_iota(jnp.int32, (size, size), 0)
    columns = lax.broadcasted_iota(jnp.int32, (size, size), 1)
    apart = jnp.abs(rows - columns)
    if period < size:
        same = jnp.bitwise_or(rows, period - 1) == jnp.bitwise_or(columns, period - 1)
        apart = jnp.where(same, apart, 0)
    apart = jnp.minimum(apart, period - apart)
    matrix = jnp.zeros((size, size), jnp.float32)
    for k, w in enumerate(stencil_weights()[1], 1):
        matrix = jnp.where(apart == k, jnp.float32(w), matrix)
    high, low = two_parts(matrix)
    return jnp.concatenate([high, high, low], axis=axis)


def filtered_block(window, pot, before, scale, weight, lanes, rows):
    center_weight, side = stencil_weights()
    n = window.shape[0] - 2 * REACH
    mid = window[REACH : REACH + n]
    high, low = two_parts(mid.reshape(n * 16, 128))
    total = jnp.dot(
        jnp.concatenate([high, low, high], axis=1), lanes, preferred_element_type=jnp.float32
    ) + jnp.dot(
        rows, jnp.concatenate([high, low, high], axis=0), preferred_element_type=jnp.float32
    )
    total = total.reshape(n, 2, 8, 128)
    for k in range(1, REACH + 1):
        beside = window[REACH + k : REACH + k + n] + window[REACH - k : REACH - k + n]
        total = total + side[k - 1] * beside
    diag = (-1.5 * center_weight - (upper_edge + lower_edge) / 2.0) * scale
    result = (pot * scale + diag) * mid + (-0.5 * scale) * total
    if before is not None:
        result = result - weight * before
    return result


def filter_kernel(
    bands, orb, pot, sub, recv, rows, p0, p1, p2, out, pot_v,
    near_send, near_recv, far_send, far_recv, pot_send, pot_recv, pass_send, pass_recv,
    move_sem, all_send, all_recv, row_send, row_recv, plane_sem, all_sem,
):
    quarter = orb.shape[1]
    slab, whole = 2 * quarter, 4 * quarter
    band, dom = lax.axis_index("band"), lax.axis_index("dom")
    core, half = lax.rem(dom, 2), lax.div(dom, 2)
    side = 4
    floor = side * side
    zl, x, yx = lax.div(band, floor), lax.rem(band, side), lax.rem(band, floor)
    shift = 2 * REACH
    left = jnp.where(zl < side // 2, 1, 0)
    long = core == left
    base = half * slab
    own_tile = dom * bands + band
    own_plane = lax.div(own_tile, 2)
    scalars = filter_scalars(DEG)
    buffers = (p0, p1, p2)
    rims = tuple(shift + REACH * (DEG - level) for level in range(DEG + 1))
    pot_rim = rims[1]

    def placed(u, count):
        return jnp.where(left == 1, u, slab - count - u)

    load = pltpu.make_async_copy(
        orb.at[core], p0.at[pl.ds(core * quarter + rims[0], quarter)], move_sem.at[0]
    )
    load.start()
    load_pot = pltpu.make_async_copy(
        pot, pot_v.at[pl.ds(core * quarter + pot_rim, quarter)], move_sem.at[1]
    )
    load_pot.start()

    sibling = {"dom": dom + 1 - 2 * core}
    partners = [{"dom": 2 * (1 - half) + k} for k in range(2)]

    def chip_along(shift):
        there = lax.rem(half * side + zl + shift, 2 * side)
        return {
            "band": lax.rem(there, side) * floor + yx,
            "dom": lax.div(there, side) * 2 + core,
        }

    x_line = [
        {"band": band - x + lax.rem(x + dx, side), "dom": dom if dk == 0 else dom + 1 - 2 * core}
        for dx in range(side)
        for dk in range(2)
    ][1:]
    y = lax.div(yx, side)
    y_line = [{"band": band + side * (lax.rem(y + dy, side) - y)} for dy in range(1, side)]
    z_line = [chip_along(dz) for dz in range(1, 2 * side)]
    other_partner = {"dom": 2 * (1 - half) + 1 - core}
    barrier = pltpu.get_barrier_semaphore()
    entered = (*z_line, other_partner, *x_line, *y_line)

    def tell(peers, semaphore):
        for peer in peers:
            pl.semaphore_signal(semaphore, inc=1, device_id=peer, device_id_type=MESH)

    tell(entered, barrier)
    lanes = stencil_matrix(128, 128, 0)
    lines = {n: stencil_matrix(16 * n, 16, 1) for n in (4, 8)}
    pl.semaphore_wait(barrier, len(entered))

    def remote(src, dst, send_sem, recv_sem, peer):
        return pltpu.make_async_remote_copy(
            src_ref=src, dst_ref=dst, send_sem=send_sem, recv_sem=recv_sem,
            device_id=peer, device_id_type=MESH,
        )

    own_rows = pltpu.make_async_copy(sub, rows.at[zl, y, x], move_sem.at[2])
    own_rows.start()
    row_lines = [
        (rows.at[zl, y, x], [{"band": lax.rem(band + d * floor, bands)} for d in range(1, side)]),
        (rows.at[:, y, x], y_line),
        (rows.at[:, :, x], [{"band": band - x + lax.rem(x + d, side)} for d in range(1, side)]),
    ]
    row_copies = [
        [
            remote(
                sub if stage == 0 else part_rows, part_rows,
                row_send.at[stage, at], row_recv.at[stage, at], peer,
            )
            for at, peer in enumerate(peers)
        ]
        for stage, (part_rows, peers) in enumerate(row_lines)
    ]

    def gather_rows(stage):
        if stage > 0:
            for copy in row_copies[stage - 1]:
                copy.wait_recv()
        for copy in row_copies[stage]:
            copy.start()

    gather_rows(0)
    pieces = [(0, 6), (6, 8), (14, 8), (22, 4), (26, 4)]
    assert sum(n for _, n in pieces) == rims[0]
    far = []
    for o in range(2):
        group = []
        for at, (a, n) in enumerate(pieces):
            group.append(
                remote(
                    orb.at[o, pl.ds(jnp.where(left == 1, quarter - a - n, a), n)],
                    p0.at[pl.ds(placed(-a - n, n) + rims[0], n)],
                    far_send.at[o, at], far_recv.at[at], partners[o],
                )
            )
        n = REACH
        group.append(
            remote(
                orb.at[o, pl.ds(jnp.where(left == 1, 0, quarter - n), n)],
                p0.at[pl.ds(placed(slab, n) + rims[0], n)],
                far_send.at[o, 5], far_recv.at[5], partners[o],
            )
        )
        far.append(group)
    part = pot_rim // 8
    pot_far = [
        remote(
            pot.at[pl.ds(jnp.where(left == 1, quarter - pot_rim, 0) + (2 * x + o) * part, part)],
            pot_v.at[pl.ds(placed(-pot_rim, pot_rim) + pot_rim + (2 * x + o) * part, part)],
            pot_send.at[o], pot_recv, partners[o],
        )
        for o in range(2)
    ]
    mine = pot_v.at[pl.ds(placed(-pot_rim, pot_rim) + pot_rim + (2 * x + core) * part, part)]

    @pl.when(long)
    def _():
        for o in range(2):
            pot_far[o].start()
        for at in range(len(pieces)):
            for o in range(2):
                far[o][at].start()

    @pl.when(jnp.logical_not(long))
    def _():
        for o in range(2):
            far[o][5].start()

    near = remote(
        orb.at[1 - core], p0.at[pl.ds(core * quarter + rims[0], quarter)],
        near_send.at[0], near_recv.at[0], sibling,
    )
    near_pot = remote(
        pot, pot_v.at[pl.ds(core * quarter + pot_rim, quarter)],
        near_send.at[1], near_recv.at[1], sibling,
    )
    near.start()
    near_pot.start()

    tell(y_line, plane_sem)

    def apply(level, u, blocks, step=8):
        scale, weight = scalars[level]

        def body(i, c):
            at = placed(u + i * step, step)
            before = None
            if level > 0:
                before = buffers[level - 1][pl.ds(at + rims[level - 1], step)]
            window = buffers[level][pl.ds(at + rims[level] - REACH, step + 2 * REACH)]
            pairs = filtered_block(
                window, pot_v[pl.ds(at + pot_rim, step)], before, scale, weight, lanes, lines[step]
            )
            if level < DEG - 1:
                buffers[level + 1][pl.ds(at + rims[level + 1], step)] = pairs
            else:
                out[pl.ds(2 * (at + rims[DEG]), 2 * step)] = pairs.reshape(2 * step, 8, 128)
            return c

        lax.fori_loop(0, blocks, body, 0)

    row = 2 * band + core

    def spread(u, count):
        start = placed(u, count)
        tiles = 2 * count

        def send(i, c):
            at = lax.rem(i + yx * max(tiles // floor, 1), tiles)
            tile = lax.rem(2 * (base + start) + at + 2 * whole, 2 * whole)
            src = out.at[2 * (start + rims[DEG]) + at]

            @pl.when(tile != own_tile)
            def _():
                peer = {"band": lax.rem(tile, bands), "dom": lax.div(tile, bands)}
                remote(src, recv.at[row], all_send, all_recv, peer).start()

            @pl.when(tile == own_tile)
            def _():
                pltpu.make_async_copy(src, recv.at[row], move_sem.at[3]).start()

            return c

        lax.fori_loop(0, tiles, send, 0)

    def advance(u, n):
        for level in range(DEG):
            apply(level, u + level * REACH, 1, n)
        spread(u + (DEG - 1) * REACH, n)

    load.wait()
    load_pot.wait()
    near.wait_recv()
    near_pot.wait_recv()
    pl.semaphore_wait(plane_sem, len(y_line))
    tell(z_line, all_sem)
    apply(0, 8, 6)
    apply(1, 14, 4)
    apply(1, 42, 1)
    apply(2, 20, 3)
    pl.semaphore_wait(all_sem, len(z_line))
    spread(20, 24)

    pot_far[0].wait_recv()
    passed = [
        remote(mine, mine, pass_send.at[at], pass_recv.at[at], peer)
        for at, peer in enumerate(x_line)
    ]
    for copy in passed:
        copy.start()

    far[0][5].wait_recv()
    apply(0, slab - 8, 1)
    apply(1, slab - 14, 1)
    apply(2, slab - 20, 1)
    spread(slab - 20, 8)
    for at, (u, n) in enumerate(((0, 8), (-8, 8), (-16, 8), (-20, 4), (-24, 4))):
        if at == 1:
            own_rows.wait()
            gather_rows(1)
            for copy in passed:
                copy.wait_recv()
        if at == 3:
            gather_rows(2)
        far[0][at].wait_recv()
        advance(u, n)

    @pl.when(long)
    def _():
        for o in range(2):
            pot_far[o].wait_send()
            for at in range(len(pieces)):
                far[o][at].wait_send()

    @pl.when(jnp.logical_not(long))
    def _():
        for o in range(2):
            far[o][5].wait_send()

    for copy in (near, near_pot, *passed):
        copy.wait_send()
    for copy in row_copies[2]:
        copy.wait_recv()
    for copies in row_copies:
        for copy in copies:
            copy.wait_send()
    pltpu.make_async_copy(out.at[0], recv.at[row], move_sem.at[3]).wait()
    all_but_own = recv.at[pl.ds(0, recv.shape[0] - 1)]
    pltpu.make_async_copy(all_but_own, all_but_own, all_send).wait()
    pltpu.make_async_copy(all_but_own, all_but_own, all_recv).wait()


def rotate_kernel(recv_v, rows_v, out, out_v, sems):
    high, low = two_parts(jnp.concatenate([rows_v[:, 0], rows_v[:, 1]], axis=0).T)
    matrix = jnp.concatenate([high, high, low], axis=1)
    width = 256
    stores = []
    for at in range(0, 8 * 128, width):
        columns = []
        for r in range(at // 128, (at + width) // 128):
            values = jnp.concatenate([recv_v[:, 0, r], recv_v[:, 1, r]], axis=0)
            high, low = two_parts(values)
            columns.append(jnp.concatenate([high, low, high], axis=0))
        out_v[:, pl.ds(at, width)] = jnp.dot(
            matrix, jnp.concatenate(columns, axis=1), preferred_element_type=jnp.float32
        )
        store = pltpu.make_async_copy(
            out_v.at[:, pl.ds(at, width)], out.at[:, pl.ds(at, width)], sems.at[at // width]
        )
        store.start()
        stores.append(store)
    for store in stores:
        store.wait()


def per_device(bands, orbitals, potential, subspace):
    orbs, planes = orbitals.shape[0], orbitals.shape[1]
    orb = orbitals.reshape(orbs, planes, 2, 8, 128)
    pot = potential.reshape(planes, 2, 8, 128)
    f32 = jnp.float32
    dma = pltpu.SemaphoreType.DMA
    anywhere = pl.BlockSpec(memory_space=pl.ANY)
    slab, shift = 2 * planes, 2 * REACH
    recv, rows = pl.pallas_call(
        functools.partial(filter_kernel, bands),
        out_shape=(
            pltpu.VMEM((bands * orbs, 8, 128), f32),
            pltpu.VMEM((4, 4, 4, orbs, 128), f32),
        ),
        in_specs=[anywhere] * 3,
        out_specs=(anywhere,) * 2,
        scratch_shapes=[
            *[
                pltpu.VMEM((slab + 2 * (shift + REACH * (DEG - level)), 2, 8, 128), f32)
                for level in range(DEG)
            ],
            pltpu.VMEM((2 * (slab + 2 * shift), 8, 128), f32),
            pltpu.VMEM((slab + 2 * (shift + REACH * (DEG - 1)), 2, 8, 128), f32),
            dma((2,)),
            dma((2,)),
            dma((2, 6)),
            dma((6,)),
            dma((2,)),
            dma,
            dma((7,)),
            dma((7,)),
            dma((4,)),
            dma,
            dma,
            dma((3, 3)),
            dma((3, 3)),
            pltpu.SemaphoreType.REGULAR,
            pltpu.SemaphoreType.REGULAR,
        ],
        compiler_params=pltpu.CompilerParams(
            collective_id=0, has_side_effects=True, vmem_limit_bytes=32 * 2**20
        ),
        name="filter",
    )(*(pltpu.with_memory_space_constraint(a, pltpu.HBM) for a in (orb, pot, subspace)))
    recv, rows = recv.reshape(bands, orbs, 8, 128), rows.reshape(bands, orbs, 128)
    return pl.pallas_call(
        rotate_kernel,
        out_shape=jax.ShapeDtypeStruct((bands * orbs, 1024), f32),
        in_specs=[pl.BlockSpec(memory_space=pltpu.VMEM)] * 2,
        out_specs=anywhere,
        scratch_shapes=[pltpu.VMEM((bands * orbs, 1024), f32), dma((4,))],
        compiler_params=pltpu.CompilerParams(vmem_limit_bytes=32 * 2**20),
        name="rotate",
    )(*(pltpu.with_memory_space_constraint(a, pltpu.VMEM) for a in (recv, rows)))


def solution(mesh):
    in_specs = (P("band", "dom", None, None), P("dom", None, None), P("band", None))
    out_specs = P(None, ("dom", "band"))
    return jax.shard_map(
        functools.partial(per_device, mesh.shape["band"]),
        mesh=mesh,
        in_specs=in_specs,
        out_specs=out_specs,
        check_vma=False,
    )
```

```python
import functools
import math

import jax
import jax.numpy as jnp
from jax import lax
from jax.experimental import pallas as pl
from jax.experimental.pallas import tpu as pltpu
from jax.sharding import PartitionSpec as P

DEG = 3
REACH = 6
MESH = pl.DeviceIdType.MESH

upper_edge = 10.7
lower_edge = 1.5
bottom_edge = -1.0


def stencil_weights():
    factor_square = math.factorial(6) ** 2
    side_weights = []
    for offset in range(1, 7):
        side_weights.append(
            2.0
            * (-1.0) ** (offset + 1)
            * factor_square
            / (offset * offset * math.factorial(6 - offset) * math.factorial(6 + offset))
        )
    center_weight = -2.0 * sum(side_weights)
    return (center_weight, side_weights)


def filter_scalars(pass_count):
    half_width = (upper_edge - lower_edge) / 2.0
    sigma_now = half_width / (bottom_edge - (upper_edge + lower_edge) / 2.0)
    gamma_value = 2.0 / sigma_now
    scalars = [(sigma_now / half_width, 0.0)]
    for pass_index in range(pass_count - 1):
        sigma_next = 1.0 / (gamma_value - sigma_now)
        scalars.append((2.0 * sigma_next / half_width, sigma_now * sigma_next))
        sigma_now = sigma_next
    return scalars


def two_parts(values):
    high = values.astype(jnp.bfloat16)
    return high, (values - high.astype(jnp.float32)).astype(jnp.bfloat16)


def stencil_matrix(size, period, axis):
    rows = lax.broadcasted_iota(jnp.int32, (size, size), 0)
    columns = lax.broadcasted_iota(jnp.int32, (size, size), 1)
    apart = jnp.abs(rows - columns)
    if period < size:
        same = jnp.bitwise_or(rows, period - 1) == jnp.bitwise_or(columns, period - 1)
        apart = jnp.where(same, apart, 0)
    apart = jnp.minimum(apart, period - apart)
    matrix = jnp.zeros((size, size), jnp.float32)
    for k, w in enumerate(stencil_weights()[1], 1):
        matrix = jnp.where(apart == k, jnp.float32(w), matrix)
    high, low = two_parts(matrix)
    return jnp.concatenate([high, high, low], axis=axis)


def filtered_block(window, pot, before, scale, weight, lanes, rows):
    center_weight, side = stencil_weights()
    n = window.shape[0] - 2 * REACH
    mid = window[REACH : REACH + n]
    high, low = two_parts(mid.reshape(n * 16, 128))
    total = jnp.dot(
        jnp.concatenate([high, low, high], axis=1), lanes, preferred_element_type=jnp.float32
    ) + jnp.dot(
        rows, jnp.concatenate([high, low, high], axis=0), preferred_element_type=jnp.float32
    )
    total = total.reshape(n, 2, 8, 128)
    for k in range(1, REACH + 1):
        beside = window[REACH + k : REACH + k + n] + window[REACH - k : REACH - k + n]
        total = total + side[k - 1] * beside
    diag = (-1.5 * center_weight - (upper_edge + lower_edge) / 2.0) * scale
    result = (pot * scale + diag) * mid + (-0.5 * scale) * total
    if before is not None:
        result = result - weight * before
    return result


def filter_kernel(
    bands, orb, pot, sub, recv, rows, p0, p1, p2, out, pot_v,
    near_send, near_recv, far_send, far_recv, pot_send, pot_recv, pass_send, pass_recv,
    move_sem, all_send, all_recv, row_send, row_recv, plane_sem, all_sem,
):
    quarter = orb.shape[1]
    slab, whole = 2 * quarter, 4 * quarter
    band, dom = lax.axis_index("band"), lax.axis_index("dom")
    core, half = lax.rem(dom, 2), lax.div(dom, 2)
    side = 4
    floor = side * side
    zl, x, yx = lax.div(band, floor), lax.rem(band, side), lax.rem(band, floor)
    shift = 2 * REACH
    left = jnp.where(zl < side // 2, 1, 0)
    long = core == left
    base = half * slab
    own_tile = dom * bands + band
    own_plane = lax.div(own_tile, 2)
    scalars = filter_scalars(DEG)
    buffers = (p0, p1, p2)
    rims = tuple(shift + REACH * (DEG - level) for level in range(DEG + 1))
    pot_rim = rims[1]

    def placed(u, count):
        return jnp.where(left == 1, u, slab - count - u)

    load = pltpu.make_async_copy(
        orb.at[core], p0.at[pl.ds(core * quarter + rims[0], quarter)], move_sem.at[0]
    )
    load.start()
    load_pot = pltpu.make_async_copy(
        pot, pot_v.at[pl.ds(core * quarter + pot_rim, quarter)], move_sem.at[1]
    )
    load_pot.start()

    sibling = {"dom": dom + 1 - 2 * core}
    partners = [{"dom": 2 * (1 - half) + k} for k in range(2)]

    def chip_along(shift):
        there = lax.rem(half * side + zl + shift, 2 * side)
        return {
            "band": lax.rem(there, side) * floor + yx,
            "dom": lax.div(there, side) * 2 + core,
        }

    x_line = [
        {"band": band - x + lax.rem(x + dx, side), "dom": dom if dk == 0 else dom + 1 - 2 * core}
        for dx in range(side)
        for dk in range(2)
    ][1:]
    y = lax.div(yx, side)
    y_line = [{"band": band + side * (lax.rem(y + dy, side) - y)} for dy in range(1, side)]
    z_line = [chip_along(dz) for dz in range(1, 2 * side)]
    other_partner = {"dom": 2 * (1 - half) + 1 - core}
    barrier = pltpu.get_barrier_semaphore()
    entered = (*z_line, other_partner, *x_line, *y_line)

    def tell(peers, semaphore):
        for peer in peers:
            pl.semaphore_signal(semaphore, inc=1, device_id=peer, device_id_type=MESH)

    tell(entered, barrier)
    lanes = stencil_matrix(128, 128, 0)
    lines = {n: stencil_matrix(16 * n, 16, 1) for n in (4, 8)}
    pl.semaphore_wait(barrier, len(entered))

    def remote(src, dst, send_sem, recv_sem, peer):
        return pltpu.make_async_remote_copy(
            src_ref=src, dst_ref=dst, send_sem=send_sem, recv_sem=recv_sem,
            device_id=peer, device_id_type=MESH,
        )

    own_rows = pltpu.make_async_copy(sub, rows.at[zl, y, x], move_sem.at[2])
    own_rows.start()
    row_lines = [
        (rows.at[zl, y, x], [{"band": lax.rem(band + d * floor, bands)} for d in range(1, side)]),
        (rows.at[:, y, x], y_line),
        (rows.at[:, :, x], [{"band": band - x + lax.rem(x + d, side)} for d in range(1, side)]),
    ]
    row_copies = [
        [
            remote(
                sub if stage == 0 else part_rows, part_rows,
                row_send.at[stage, at], row_recv.at[stage, at], peer,
            )
            for at, peer in enumerate(peers)
        ]
        for stage, (part_rows, peers) in enumerate(row_lines)
    ]

    def gather_rows(stage):
        if stage > 0:
            for copy in row_copies[stage - 1]:
                copy.wait_recv()
        for copy in row_copies[stage]:
            copy.start()

    gather_rows(0)
    pieces = [(0, 6), (6, 8), (14, 8), (22, 4), (26, 4)]
    assert sum(n for _, n in pieces) == rims[0]
    far = []
    for o in range(2):
        group = []
        for at, (a, n) in enumerate(pieces):
            group.append(
                remote(
                    orb.at[o, pl.ds(jnp.where(left == 1, quarter - a - n, a), n)],
                    p0.at[pl.ds(placed(-a - n, n) + rims[0], n)],
                    far_send.at[o, at], far_recv.at[at], partners[o],
                )
            )
        n = REACH
        group.append(
            remote(
                orb.at[o, pl.ds(jnp.where(left == 1, 0, quarter - n), n)],
                p0.at[pl.ds(placed(slab, n) + rims[0], n)],
                far_send.at[o, 5], far_recv.at[5], partners[o],
            )
        )
        far.append(group)
    part = pot_rim // 8
    pot_far = [
        remote(
            pot.at[pl.ds(jnp.where(left == 1, quarter - pot_rim, 0) + (2 * x + o) * part, part)],
            pot_v.at[pl.ds(placed(-pot_rim, pot_rim) + pot_rim + (2 * x + o) * part, part)],
            pot_send.at[o], pot_recv, partners[o],
        )
        for o in range(2)
    ]
    mine = pot_v.at[pl.ds(placed(-pot_rim, pot_rim) + pot_rim + (2 * x + core) * part, part)]

    @pl.when(long)
    def _():
        for o in range(2):
            pot_far[o].start()
        for at in range(len(pieces)):
            for o in range(2):
                far[o][at].start()

    @pl.when(jnp.logical_not(long))
    def _():
        for o in range(2):
            far[o][5].start()

    near = remote(
        orb.at[1 - core], p0.at[pl.ds(core * quarter + rims[0], quarter)],
        near_send.at[0], near_recv.at[0], sibling,
    )
    near_pot = remote(
        pot, pot_v.at[pl.ds(core * quarter + pot_rim, quarter)],
        near_send.at[1], near_recv.at[1], sibling,
    )
    near.start()
    near_pot.start()

    tell(y_line, plane_sem)

    def apply(level, u, blocks, step=8):
        scale, weight = scalars[level]

        def body(i, c):
            at = placed(u + i * step, step)
            before = None
            if level > 0:
                before = buffers[level - 1][pl.ds(at + rims[level - 1], step)]
            window = buffers[level][pl.ds(at + rims[level] - REACH, step + 2 * REACH)]
            pairs = filtered_block(
                window, pot_v[pl.ds(at + pot_rim, step)], before, scale, weight, lanes, lines[step]
            )
            if level < DEG - 1:
                buffers[level + 1][pl.ds(at + rims[level + 1], step)] = pairs
            else:
                out[pl.ds(2 * (at + rims[DEG]), 2 * step)] = pairs.reshape(2 * step, 8, 128)
            return c

        lax.fori_loop(0, blocks, body, 0)

    row = 2 * band + core

    def spread(u, count):
        start = placed(u, count)
        tiles = 2 * count

        def send(i, c):
            at = lax.rem(i + yx * max(tiles // floor, 1), tiles)
            tile = lax.rem(2 * (base + start) + at + 2 * whole, 2 * whole)
            src = out.at[2 * (start + rims[DEG]) + at]

            @pl.when(tile != own_tile)
            def _():
                peer = {"band": lax.rem(tile, bands), "dom": lax.div(tile, bands)}
                remote(src, recv.at[row], all_send, all_recv, peer).start()

            @pl.when(tile == own_tile)
            def _():
                pltpu.make_async_copy(src, recv.at[row], move_sem.at[3]).start()

            return c

        lax.fori_loop(0, tiles, send, 0)

    def advance(u, n):
        for level in range(DEG):
            apply(level, u + level * REACH, 1, n)
        spread(u + (DEG - 1) * REACH, n)

    pot_far[0].wait_recv()
    passed = [
        remote(mine, mine, pass_send.at[at], pass_recv.at[at], peer)
        for at, peer in enumerate(x_line)
    ]
    for copy in passed:
        copy.start()

    load.wait()
    load_pot.wait()
    own_rows.wait()
    gather_rows(1)
    near.wait_recv()
    near_pot.wait_recv()
    pl.semaphore_wait(plane_sem, len(y_line))
    tell(z_line, all_sem)
    apply(0, 8, 6)
    apply(1, 14, 4)
    apply(1, 42, 1)
    apply(2, 20, 3)
    gather_rows(2)
    pl.semaphore_wait(all_sem, len(z_line))
    spread(20, 24)

    far[0][5].wait_recv()
    apply(0, slab - 8, 1)
    apply(1, slab - 14, 1)
    apply(2, slab - 20, 1)
    spread(slab - 20, 8)
    for at, (u, n) in enumerate(((0, 8), (-8, 8), (-16, 8), (-20, 4), (-24, 4))):
        if at == 1:
            for copy in passed:
                copy.wait_recv()
        far[0][at].wait_recv()
        advance(u, n)

    @pl.when(long)
    def _():
        for o in range(2):
            pot_far[o].wait_send()
            for at in range(len(pieces)):
                far[o][at].wait_send()

    @pl.when(jnp.logical_not(long))
    def _():
        for o in range(2):
            far[o][5].wait_send()

    for copy in (near, near_pot, *passed):
        copy.wait_send()
    for copy in row_copies[2]:
        copy.wait_recv()
    for copies in row_copies:
        for copy in copies:
            copy.wait_send()
    pltpu.make_async_copy(out.at[0], recv.at[row], move_sem.at[3]).wait()
    all_but_own = recv.at[pl.ds(0, recv.shape[0] - 1)]
    pltpu.make_async_copy(all_but_own, all_but_own, all_send).wait()
    pltpu.make_async_copy(all_but_own, all_but_own, all_recv).wait()


def rotate_kernel(recv_v, rows_v, out, out_v, sems):
    high, low = two_parts(jnp.concatenate([rows_v[:, 0], rows_v[:, 1]], axis=0).T)
    matrix = jnp.concatenate([high, high, low], axis=1)
    width = 256
    stores = []
    for at in range(0, 8 * 128, width):
        columns = []
        for r in range(at // 128, (at + width) // 128):
            values = jnp.concatenate([recv_v[:, 0, r], recv_v[:, 1, r]], axis=0)
            high, low = two_parts(values)
            columns.append(jnp.concatenate([high, low, high], axis=0))
        out_v[:, pl.ds(at, width)] = jnp.dot(
            matrix, jnp.concatenate(columns, axis=1), preferred_element_type=jnp.float32
        )
        store = pltpu.make_async_copy(
            out_v.at[:, pl.ds(at, width)], out.at[:, pl.ds(at, width)], sems.at[at // width]
        )
        store.start()
        stores.append(store)
    for store in stores:
        store.wait()


def per_device(bands, orbitals, potential, subspace):
    orbs, planes = orbitals.shape[0], orbitals.shape[1]
    orb = orbitals.reshape(orbs, planes, 2, 8, 128)
    pot = potential.reshape(planes, 2, 8, 128)
    f32 = jnp.float32
    dma = pltpu.SemaphoreType.DMA
    anywhere = pl.BlockSpec(memory_space=pl.ANY)
    slab, shift = 2 * planes, 2 * REACH
    recv, rows = pl.pallas_call(
        functools.partial(filter_kernel, bands),
        out_shape=(
            pltpu.VMEM((bands * orbs, 8, 128), f32),
            pltpu.VMEM((4, 4, 4, orbs, 128), f32),
        ),
        in_specs=[anywhere] * 3,
        out_specs=(anywhere,) * 2,
        scratch_shapes=[
            *[
                pltpu.VMEM((slab + 2 * (shift + REACH * (DEG - level)), 2, 8, 128), f32)
                for level in range(DEG)
            ],
            pltpu.VMEM((2 * (slab + 2 * shift), 8, 128), f32),
            pltpu.VMEM((slab + 2 * (shift + REACH * (DEG - 1)), 2, 8, 128), f32),
            dma((2,)),
            dma((2,)),
            dma((2, 6)),
            dma((6,)),
            dma((2,)),
            dma,
            dma((7,)),
            dma((7,)),
            dma((4,)),
            dma,
            dma,
            dma((3, 3)),
            dma((3, 3)),
            pltpu.SemaphoreType.REGULAR,
            pltpu.SemaphoreType.REGULAR,
        ],
        compiler_params=pltpu.CompilerParams(
            collective_id=0, has_side_effects=True, vmem_limit_bytes=32 * 2**20
        ),
        name="filter",
    )(*(pltpu.with_memory_space_constraint(a, pltpu.HBM) for a in (orb, pot, subspace)))
    recv, rows = recv.reshape(bands, orbs, 8, 128), rows.reshape(bands, orbs, 128)
    return pl.pallas_call(
        rotate_kernel,
        out_shape=jax.ShapeDtypeStruct((bands * orbs, 1024), f32),
        in_specs=[pl.BlockSpec(memory_space=pltpu.VMEM)] * 2,
        out_specs=anywhere,
        scratch_shapes=[pltpu.VMEM((bands * orbs, 1024), f32), dma((4,))],
        compiler_params=pltpu.CompilerParams(vmem_limit_bytes=32 * 2**20),
        name="rotate",
    )(*(pltpu.with_memory_space_constraint(a, pltpu.VMEM) for a in (recv, rows)))


def solution(mesh):
    in_specs = (P("band", "dom", None, None), P("dom", None, None), P("band", None))
    out_specs = P(None, ("dom", "band"))
    return jax.shard_map(
        functools.partial(per_device, mesh.shape["band"]),
        mesh=mesh,
        in_specs=in_specs,
        out_specs=out_specs,
        check_vma=False,
    )
```

```python
import functools
import math

import jax
import jax.numpy as jnp
from jax import lax
from jax.experimental import pallas as pl
from jax.experimental.pallas import tpu as pltpu
from jax.sharding import PartitionSpec as P

DEG = 3
REACH = 6
MESH = pl.DeviceIdType.MESH

upper_edge = 10.7
lower_edge = 1.5
bottom_edge = -1.0


def stencil_weights():
    factor_square = math.factorial(6) ** 2
    side_weights = []
    for offset in range(1, 7):
        side_weights.append(
            2.0
            * (-1.0) ** (offset + 1)
            * factor_square
            / (offset * offset * math.factorial(6 - offset) * math.factorial(6 + offset))
        )
    center_weight = -2.0 * sum(side_weights)
    return (center_weight, side_weights)


def filter_scalars(pass_count):
    half_width = (upper_edge - lower_edge) / 2.0
    sigma_now = half_width / (bottom_edge - (upper_edge + lower_edge) / 2.0)
    gamma_value = 2.0 / sigma_now
    scalars = [(sigma_now / half_width, 0.0)]
    for pass_index in range(pass_count - 1):
        sigma_next = 1.0 / (gamma_value - sigma_now)
        scalars.append((2.0 * sigma_next / half_width, sigma_now * sigma_next))
        sigma_now = sigma_next
    return scalars


def two_parts(values):
    high = values.astype(jnp.bfloat16)
    return high, (values - high.astype(jnp.float32)).astype(jnp.bfloat16)


def stencil_matrix(size, period, axis):
    rows = lax.broadcasted_iota(jnp.int32, (size, size), 0)
    columns = lax.broadcasted_iota(jnp.int32, (size, size), 1)
    apart = jnp.abs(rows - columns)
    if period < size:
        same = jnp.bitwise_or(rows, period - 1) == jnp.bitwise_or(columns, period - 1)
        apart = jnp.where(same, apart, 0)
    apart = jnp.minimum(apart, period - apart)
    matrix = jnp.zeros((size, size), jnp.float32)
    for k, w in enumerate(stencil_weights()[1], 1):
        matrix = jnp.where(apart == k, jnp.float32(w), matrix)
    high, low = two_parts(matrix)
    return jnp.concatenate([high, high, low], axis=axis)


def filtered_block(window, pot, before, scale, weight, lanes, rows):
    center_weight, side = stencil_weights()
    n = window.shape[0] - 2 * REACH
    mid = window[REACH : REACH + n]
    high, low = two_parts(mid.reshape(n * 16, 128))
    total = jnp.dot(
        jnp.concatenate([high, low, high], axis=1), lanes, preferred_element_type=jnp.float32
    ) + jnp.dot(
        rows, jnp.concatenate([high, low, high], axis=0), preferred_element_type=jnp.float32
    )
    total = total.reshape(n, 2, 8, 128)
    for k in range(1, REACH + 1):
        beside = window[REACH + k : REACH + k + n] + window[REACH - k : REACH - k + n]
        total = total + side[k - 1] * beside
    diag = (-1.5 * center_weight - (upper_edge + lower_edge) / 2.0) * scale
    result = (pot * scale + diag) * mid + (-0.5 * scale) * total
    if before is not None:
        result = result - weight * before
    return result


def filter_kernel(
    bands, orb, pot, sub, recv, rows, p0, p1, p2, out, pot_v,
    near_send, near_recv, far_send, far_recv, pot_send, pot_recv, pass_send, pass_recv,
    move_sem, all_send, all_recv, row_send, row_recv, plane_sem, all_sem,
):
    quarter = orb.shape[1]
    slab, whole = 2 * quarter, 4 * quarter
    band, dom = lax.axis_index("band"), lax.axis_index("dom")
    core, half = lax.rem(dom, 2), lax.div(dom, 2)
    side = 4
    floor = side * side
    zl, x, yx = lax.div(band, floor), lax.rem(band, side), lax.rem(band, floor)
    shift = 2 * REACH
    left = jnp.where(zl < side // 2, 1, 0)
    long = core == left
    base = half * slab
    own_tile = dom * bands + band
    own_plane = lax.div(own_tile, 2)
    scalars = filter_scalars(DEG)
    buffers = (p0, p1, p2)
    rims = tuple(shift + REACH * (DEG - level) for level in range(DEG + 1))
    pot_rim = rims[1]

    def placed(u, count):
        return jnp.where(left == 1, u, slab - count - u)

    load = pltpu.make_async_copy(
        orb.at[core], p0.at[pl.ds(core * quarter + rims[0], quarter)], move_sem.at[0]
    )
    load.start()
    load_pot = pltpu.make_async_copy(
        pot, pot_v.at[pl.ds(core * quarter + pot_rim, quarter)], move_sem.at[1]
    )
    load_pot.start()

    sibling = {"dom": dom + 1 - 2 * core}
    partners = [{"dom": 2 * (1 - half) + k} for k in range(2)]

    def chip_along(shift):
        there = lax.rem(half * side + zl + shift, 2 * side)
        return {
            "band": lax.rem(there, side) * floor + yx,
            "dom": lax.div(there, side) * 2 + core,
        }

    x_line = [
        {"band": band - x + lax.rem(x + dx, side), "dom": dom if dk == 0 else dom + 1 - 2 * core}
        for dx in range(side)
        for dk in range(2)
    ][1:]
    y = lax.div(yx, side)
    y_line = [{"band": band + side * (lax.rem(y + dy, side) - y)} for dy in range(1, side)]
    z_line = [chip_along(dz) for dz in range(1, 2 * side)]
    other_partner = {"dom": 2 * (1 - half) + 1 - core}
    barrier = pltpu.get_barrier_semaphore()
    entered = (*z_line, other_partner, *x_line, *y_line)

    def tell(peers, semaphore):
        for peer in peers:
            pl.semaphore_signal(semaphore, inc=1, device_id=peer, device_id_type=MESH)

    tell(entered, barrier)
    lanes = stencil_matrix(128, 128, 0)
    lines = {n: stencil_matrix(16 * n, 16, 1) for n in (4, 8)}
    pl.semaphore_wait(barrier, len(entered))

    def remote(src, dst, send_sem, recv_sem, peer):
        return pltpu.make_async_remote_copy(
            src_ref=src, dst_ref=dst, send_sem=send_sem, recv_sem=recv_sem,
            device_id=peer, device_id_type=MESH,
        )

    own_rows = pltpu.make_async_copy(sub, rows.at[zl, y, x], move_sem.at[2])
    own_rows.start()
    row_lines = [
        (rows.at[zl, y, x], [{"band": lax.rem(band + d * floor, bands)} for d in range(1, side)]),
        (rows.at[:, y, x], y_line),
        (rows.at[:, :, x], [{"band": band - x + lax.rem(x + d, side)} for d in range(1, side)]),
    ]
    row_copies = [
        [
            remote(
                sub if stage == 0 else part_rows, part_rows,
                row_send.at[stage, at], row_recv.at[stage, at], peer,
            )
            for at, peer in enumerate(peers)
        ]
        for stage, (part_rows, peers) in enumerate(row_lines)
    ]

    def gather_rows(stage):
        if stage > 0:
            for copy in row_copies[stage - 1]:
                copy.wait_recv()
        for copy in row_copies[stage]:
            copy.start()

    gather_rows(0)
    pieces = [(0, 6), (6, 8), (14, 8), (22, 4), (26, 4)]
    assert sum(n for _, n in pieces) == rims[0]
    far = []
    for o in range(2):
        group = []
        for at, (a, n) in enumerate(pieces):
            group.append(
                remote(
                    orb.at[o, pl.ds(jnp.where(left == 1, quarter - a - n, a), n)],
                    p0.at[pl.ds(placed(-a - n, n) + rims[0], n)],
                    far_send.at[o, at], far_recv.at[at], partners[o],
                )
            )
        n = REACH
        group.append(
            remote(
                orb.at[o, pl.ds(jnp.where(left == 1, 0, quarter - n), n)],
                p0.at[pl.ds(placed(slab, n) + rims[0], n)],
                far_send.at[o, 5], far_recv.at[5], partners[o],
            )
        )
        far.append(group)
    part = pot_rim // 8
    pot_far = [
        remote(
            pot.at[pl.ds(jnp.where(left == 1, quarter - pot_rim, 0) + (2 * x + o) * part, part)],
            pot_v.at[pl.ds(placed(-pot_rim, pot_rim) + pot_rim + (2 * x + o) * part, part)],
            pot_send.at[o], pot_recv, partners[o],
        )
        for o in range(2)
    ]
    mine = pot_v.at[pl.ds(placed(-pot_rim, pot_rim) + pot_rim + (2 * x + core) * part, part)]

    @pl.when(long)
    def _():
        for o in range(2):
            pot_far[o].start()
        for at in range(len(pieces)):
            for o in range(2):
                far[o][at].start()

    @pl.when(jnp.logical_not(long))
    def _():
        for o in range(2):
            far[o][5].start()

    near = remote(
        orb.at[1 - core], p0.at[pl.ds(core * quarter + rims[0], quarter)],
        near_send.at[0], near_recv.at[0], sibling,
    )
    near_pot = remote(
        pot, pot_v.at[pl.ds(core * quarter + pot_rim, quarter)],
        near_send.at[1], near_recv.at[1], sibling,
    )
    near.start()
    near_pot.start()

    tell(y_line, plane_sem)

    def apply(level, u, blocks, step=8):
        scale, weight = scalars[level]

        def body(i, c):
            at = placed(u + i * step, step)
            before = None
            if level > 0:
                before = buffers[level - 1][pl.ds(at + rims[level - 1], step)]
            window = buffers[level][pl.ds(at + rims[level] - REACH, step + 2 * REACH)]
            pairs = filtered_block(
                window, pot_v[pl.ds(at + pot_rim, step)], before, scale, weight, lanes, lines[step]
            )
            if level < DEG - 1:
                buffers[level + 1][pl.ds(at + rims[level + 1], step)] = pairs
            else:
                out[pl.ds(2 * (at + rims[DEG]), 2 * step)] = pairs.reshape(2 * step, 8, 128)
            return c

        lax.fori_loop(0, blocks, body, 0, unroll=min(blocks, 3))

    row = 2 * band + core
    offsets = [lax.rem(i + yx, 8) for i in range(8)]

    def spread(u, count):
        start = placed(u, count)
        groups = count // 4

        def send_group(i, c):
            plane = start + 4 * lax.rem(i + yx, groups)
            tile = lax.rem(2 * (base + plane) + 2 * whole, 2 * whole)
            there, first = lax.div(tile, bands), lax.rem(tile, bands)
            place = 2 * (plane + rims[DEG])
            for offset in offsets:
                src, peer = out.at[place + offset], first + offset

                @pl.when((peer != band) | (there != dom))
                def _():
                    remote(
                        src, recv.at[row], all_send, all_recv, {"band": peer, "dom": there}
                    ).start()

                @pl.when((peer == band) & (there == dom))
                def _():
                    pltpu.make_async_copy(src, recv.at[row], move_sem.at[3]).start()

            return c

        lax.fori_loop(0, groups, send_group, 0)

    def advance(u, n):
        for level in range(DEG):
            apply(level, u + level * REACH, 1, n)
        spread(u + (DEG - 1) * REACH, n)

    pot_far[0].wait_recv()
    passed = [
        remote(mine, mine, pass_send.at[at], pass_recv.at[at], peer)
        for at, peer in enumerate(x_line)
    ]
    for copy in passed:
        copy.start()

    load.wait()
    load_pot.wait()
    own_rows.wait()
    gather_rows(1)
    near.wait_recv()
    near_pot.wait_recv()
    pl.semaphore_wait(plane_sem, len(y_line))
    tell(z_line, all_sem)
    apply(0, 8, 6)
    apply(1, 14, 4)
    apply(1, 42, 1)
    apply(2, 20, 3)
    gather_rows(2)
    pl.semaphore_wait(all_sem, len(z_line))
    spread(20, 24)

    far[0][5].wait_recv()
    apply(0, slab - 8, 1)
    apply(1, slab - 14, 1)
    apply(2, slab - 20, 1)
    spread(slab - 20, 8)
    for at, (u, n) in enumerate(((0, 8), (-8, 8), (-16, 8), (-20, 4), (-24, 4))):
        if at == 1:
            for copy in passed:
                copy.wait_recv()
        far[0][at].wait_recv()
        advance(u, n)

    @pl.when(long)
    def _():
        for o in range(2):
            pot_far[o].wait_send()
            for at in range(len(pieces)):
                far[o][at].wait_send()

    @pl.when(jnp.logical_not(long))
    def _():
        for o in range(2):
            far[o][5].wait_send()

    for copy in (near, near_pot, *passed):
        copy.wait_send()
    for copy in row_copies[2]:
        copy.wait_recv()
    for copies in row_copies:
        for copy in copies:
            copy.wait_send()
    pltpu.make_async_copy(out.at[0], recv.at[row], move_sem.at[3]).wait()
    all_but_own = recv.at[pl.ds(0, recv.shape[0] - 1)]
    pltpu.make_async_copy(all_but_own, all_but_own, all_send).wait()
    pltpu.make_async_copy(all_but_own, all_but_own, all_recv).wait()


def rotate_kernel(recv_v, rows_v, out, out_v, sems):
    high, low = two_parts(jnp.concatenate([rows_v[:, 0], rows_v[:, 1]], axis=0).T)
    matrix = jnp.concatenate([high, high, low], axis=1)
    width = 256
    stores = []
    for at in range(0, 8 * 128, width):
        columns = []
        for r in range(at // 128, (at + width) // 128):
            values = jnp.concatenate([recv_v[:, 0, r], recv_v[:, 1, r]], axis=0)
            high, low = two_parts(values)
            columns.append(jnp.concatenate([high, low, high], axis=0))
        out_v[:, pl.ds(at, width)] = jnp.dot(
            matrix, jnp.concatenate(columns, axis=1), preferred_element_type=jnp.float32
        )
        store = pltpu.make_async_copy(
            out_v.at[:, pl.ds(at, width)], out.at[:, pl.ds(at, width)], sems.at[at // width]
        )
        store.start()
        stores.append(store)
    for store in stores:
        store.wait()


def per_device(bands, orbitals, potential, subspace):
    orbs, planes = orbitals.shape[0], orbitals.shape[1]
    orb = orbitals.reshape(orbs, planes, 2, 8, 128)
    pot = potential.reshape(planes, 2, 8, 128)
    f32 = jnp.float32
    dma = pltpu.SemaphoreType.DMA
    anywhere = pl.BlockSpec(memory_space=pl.ANY)
    slab, shift = 2 * planes, 2 * REACH
    recv, rows = pl.pallas_call(
        functools.partial(filter_kernel, bands),
        out_shape=(
            pltpu.VMEM((bands * orbs, 8, 128), f32),
            pltpu.VMEM((4, 4, 4, orbs, 128), f32),
        ),
        in_specs=[anywhere] * 3,
        out_specs=(anywhere,) * 2,
        scratch_shapes=[
            *[
                pltpu.VMEM((slab + 2 * (shift + REACH * (DEG - level)), 2, 8, 128), f32)
                for level in range(DEG)
            ],
            pltpu.VMEM((2 * (slab + 2 * shift), 8, 128), f32),
            pltpu.VMEM((slab + 2 * (shift + REACH * (DEG - 1)), 2, 8, 128), f32),
            dma((2,)),
            dma((2,)),
            dma((2, 6)),
            dma((6,)),
            dma((2,)),
            dma,
            dma((7,)),
            dma((7,)),
            dma((4,)),
            dma,
            dma,
            dma((3, 3)),
            dma((3, 3)),
            pltpu.SemaphoreType.REGULAR,
            pltpu.SemaphoreType.REGULAR,
        ],
        compiler_params=pltpu.CompilerParams(
            collective_id=0, has_side_effects=True, vmem_limit_bytes=32 * 2**20
        ),
        name="filter",
    )(*(pltpu.with_memory_space_constraint(a, pltpu.HBM) for a in (orb, pot, subspace)))
    recv, rows = recv.reshape(bands, orbs, 8, 128), rows.reshape(bands, orbs, 128)
    return pl.pallas_call(
        rotate_kernel,
        out_shape=jax.ShapeDtypeStruct((bands * orbs, 1024), f32),
        in_specs=[pl.BlockSpec(memory_space=pltpu.VMEM)] * 2,
        out_specs=anywhere,
        scratch_shapes=[pltpu.VMEM((bands * orbs, 1024), f32), dma((4,))],
        compiler_params=pltpu.CompilerParams(vmem_limit_bytes=32 * 2**20),
        name="rotate",
    )(*(pltpu.with_memory_space_constraint(a, pltpu.VMEM) for a in (recv, rows)))


def solution(mesh):
    in_specs = (P("band", "dom", None, None), P("dom", None, None), P("band", None))
    out_specs = P(None, ("dom", "band"))
    return jax.shard_map(
        functools.partial(per_device, mesh.shape["band"]),
        mesh=mesh,
        in_specs=in_specs,
        out_specs=out_specs,
        check_vma=False,
    )
```

```python
import functools
import math

import jax
import jax.numpy as jnp
from jax import lax
from jax.experimental import pallas as pl
from jax.experimental.pallas import tpu as pltpu
from jax.sharding import PartitionSpec as P

DEG = 3
REACH = 6
MESH = pl.DeviceIdType.MESH

upper_edge = 10.7
lower_edge = 1.5
bottom_edge = -1.0


def stencil_weights():
    factor_square = math.factorial(6) ** 2
    side_weights = []
    for offset in range(1, 7):
        side_weights.append(
            2.0
            * (-1.0) ** (offset + 1)
            * factor_square
            / (offset * offset * math.factorial(6 - offset) * math.factorial(6 + offset))
        )
    center_weight = -2.0 * sum(side_weights)
    return (center_weight, side_weights)


def filter_scalars(pass_count):
    half_width = (upper_edge - lower_edge) / 2.0
    sigma_now = half_width / (bottom_edge - (upper_edge + lower_edge) / 2.0)
    gamma_value = 2.0 / sigma_now
    scalars = [(sigma_now / half_width, 0.0)]
    for pass_index in range(pass_count - 1):
        sigma_next = 1.0 / (gamma_value - sigma_now)
        scalars.append((2.0 * sigma_next / half_width, sigma_now * sigma_next))
        sigma_now = sigma_next
    return scalars


def two_parts(values):
    high = values.astype(jnp.bfloat16)
    return high, (values - high.astype(jnp.float32)).astype(jnp.bfloat16)


def stencil_matrix(size, period, axis):
    rows = lax.broadcasted_iota(jnp.int32, (size, size), 0)
    columns = lax.broadcasted_iota(jnp.int32, (size, size), 1)
    apart = jnp.abs(rows - columns)
    if period < size:
        same = jnp.bitwise_or(rows, period - 1) == jnp.bitwise_or(columns, period - 1)
        apart = jnp.where(same, apart, 0)
    apart = jnp.minimum(apart, period - apart)
    matrix = jnp.zeros((size, size), jnp.float32)
    for k, w in enumerate(stencil_weights()[1], 1):
        matrix = jnp.where(apart == k, jnp.float32(w), matrix)
    high, low = two_parts(matrix)
    return jnp.concatenate([high, high, low], axis=axis)


def filtered_block(window, pot, before, scale, weight, lanes, rows):
    center_weight, side = stencil_weights()
    n = window.shape[0] - 2 * REACH
    mid = window[REACH : REACH + n]
    high, low = two_parts(mid.reshape(n * 16, 128))
    total = jnp.dot(
        jnp.concatenate([high, low, high], axis=1), lanes, preferred_element_type=jnp.float32
    ) + jnp.dot(
        rows, jnp.concatenate([high, low, high], axis=0), preferred_element_type=jnp.float32
    )
    total = total.reshape(n, 2, 8, 128)
    for k in range(1, REACH + 1):
        beside = window[REACH + k : REACH + k + n] + window[REACH - k : REACH - k + n]
        total = total + side[k - 1] * beside
    diag = (-1.5 * center_weight - (upper_edge + lower_edge) / 2.0) * scale
    result = (pot * scale + diag) * mid + (-0.5 * scale) * total
    if before is not None:
        result = result - weight * before
    return result


def filter_kernel(
    bands, orb, pot, sub, recv, rows, p0, p1, p2, out, pot_v, held,
    near_send, near_recv, far_send, far_recv, held_recv, onward_send, pot_send, pot_recv, pass_send, pass_recv,
    move_sem, all_send, all_recv, row_send, row_recv, plane_sem, all_sem,
):
    quarter = orb.shape[1]
    slab, whole = 2 * quarter, 4 * quarter
    band, dom = lax.axis_index("band"), lax.axis_index("dom")
    core, half = lax.rem(dom, 2), lax.div(dom, 2)
    side = 4
    floor = side * side
    zl, x, yx = lax.div(band, floor), lax.rem(band, side), lax.rem(band, floor)
    shift = 2 * REACH
    left = jnp.where(zl < side // 2, 1, 0)
    long = core == left
    base = half * slab
    own_tile = dom * bands + band
    own_plane = lax.div(own_tile, 2)
    scalars = filter_scalars(DEG)
    buffers = (p0, p1, p2)
    rims = tuple(shift + REACH * (DEG - level) for level in range(DEG + 1))
    pot_rim = rims[1]

    def placed(u, count):
        return jnp.where(left == 1, u, slab - count - u)

    load = pltpu.make_async_copy(
        orb.at[core], p0.at[pl.ds(core * quarter + rims[0], quarter)], move_sem.at[0]
    )
    load.start()
    load_pot = pltpu.make_async_copy(
        pot, pot_v.at[pl.ds(core * quarter + pot_rim, quarter)], move_sem.at[1]
    )
    load_pot.start()

    sibling = {"dom": dom + 1 - 2 * core}
    partners = [{"dom": 2 * (1 - half) + k} for k in range(2)]

    def chip_along(shift):
        there = lax.rem(half * side + zl + shift, 2 * side)
        return {
            "band": lax.rem(there, side) * floor + yx,
            "dom": lax.div(there, side) * 2 + core,
        }

    x_line = [
        {"band": band - x + lax.rem(x + dx, side), "dom": dom if dk == 0 else dom + 1 - 2 * core}
        for dx in range(side)
        for dk in range(2)
    ][1:]
    y = lax.div(yx, side)
    y_line = [{"band": band + side * (lax.rem(y + dy, side) - y)} for dy in range(1, side)]
    z_line = [chip_along(dz) for dz in range(1, 2 * side)]
    other_partner = {"dom": 2 * (1 - half) + 1 - core}
    outer = (y == 0) | (y == side - 1)
    y_far = lax.rem(y + side // 2, side)

    def two_on(half_there, core_there):
        return {"band": zl * floor + y_far * side + x, "dom": 2 * half_there + core_there}

    relay_half = jnp.where(outer, half, 1 - half)
    from_half = jnp.where(outer, 1 - half, half)
    relay_to = two_on(relay_half, 0)
    onward_to = two_on(1 - from_half, 1)
    barrier = pltpu.get_barrier_semaphore()
    entered = (*z_line, other_partner, *x_line, *y_line)

    def tell(peers, semaphore):
        for peer in peers:
            pl.semaphore_signal(semaphore, inc=1, device_id=peer, device_id_type=MESH)

    tell(entered, barrier)

    @pl.when(core == 0)
    def _():
        tell([two_on(from_half, k) for k in range(2)], barrier)

    @pl.when(core == 1)
    def _():
        tell([two_on(1 - relay_half, 0)], barrier)

    lanes = stencil_matrix(128, 128, 0)
    lines = {n: stencil_matrix(16 * n, 16, 1) for n in (4, 8)}
    pl.semaphore_wait(barrier, len(entered) + 2 - core)

    def remote(src, dst, send_sem, recv_sem, peer):
        return pltpu.make_async_remote_copy(
            src_ref=src, dst_ref=dst, send_sem=send_sem, recv_sem=recv_sem,
            device_id=peer, device_id_type=MESH,
        )

    own_rows = pltpu.make_async_copy(sub, rows.at[zl, y, x], move_sem.at[2])
    own_rows.start()
    row_lines = [
        (rows.at[zl, y, x], [{"band": lax.rem(band + d * floor, bands)} for d in range(1, side)]),
        (rows.at[:, y, x], y_line),
        (rows.at[:, :, x], [{"band": band - x + lax.rem(x + d, side)} for d in range(1, side)]),
    ]
    row_copies = [
        [
            remote(
                sub if stage == 0 else part_rows, part_rows,
                row_send.at[stage, at], row_recv.at[stage, at], peer,
            )
            for at, peer in enumerate(peers)
        ]
        for stage, (part_rows, peers) in enumerate(row_lines)
    ]

    def gather_rows(stage):
        if stage > 0:
            for copy in row_copies[stage - 1]:
                copy.wait_recv()
        for copy in row_copies[stage]:
            copy.start()

    gather_rows(0)
    pieces = [(0, 6), (6, 8), (14, 8), (22, 4), (26, 4)]
    assert sum(n for _, n in pieces) == rims[0]
    far, onward = [], []
    for o in range(2):
        group = []
        for at, (a, n) in enumerate(pieces + [(slab, REACH)]):
            if a < slab:
                source = jnp.where(left == 1, quarter - a - n, a)
                place = p0.at[pl.ds(placed(-a - n, n) + rims[0], n)]
            else:
                source = jnp.where(left == 1, 0, quarter - n)
                place = p0.at[pl.ds(placed(a, n) + rims[0], n)]
            mine = orb.at[o, pl.ds(source, n)]
            if o == 0:
                copy = remote(mine, place, far_send.at[o, at], far_recv.at[at], partners[0])
            else:
                slot = held.at[at, pl.ds(0, n)]
                copy = remote(mine, slot, far_send.at[o, at], held_recv.at[at], relay_to)
                onward.append(
                    remote(slot, place, onward_send.at[at], far_recv.at[at], onward_to)
                )
            group.append(copy)
        far.append(group)

    def pass_on(*numbers):
        @pl.when(core == 0)
        def _():
            for at in numbers:
                far[1][at].wait_recv()
                onward[at].start()

    part = pot_rim // 8
    pot_far = [
        remote(
            pot.at[pl.ds(jnp.where(left == 1, quarter - pot_rim, 0) + (2 * x + o) * part, part)],
            pot_v.at[pl.ds(placed(-pot_rim, pot_rim) + pot_rim + (2 * x + o) * part, part)],
            pot_send.at[o], pot_recv, partners[o],
        )
        for o in range(2)
    ]
    mine = pot_v.at[pl.ds(placed(-pot_rim, pot_rim) + pot_rim + (2 * x + core) * part, part)]

    @pl.when(long)
    def _():
        for o in range(2):
            pot_far[o].start()
        for at in range(len(pieces)):
            for o in range(2):
                far[o][at].start()

    @pl.when(jnp.logical_not(long))
    def _():
        for o in range(2):
            far[o][5].start()

    near = remote(
        orb.at[1 - core], p0.at[pl.ds(core * quarter + rims[0], quarter)],
        near_send.at[0], near_recv.at[0], sibling,
    )
    near_pot = remote(
        pot, pot_v.at[pl.ds(core * quarter + pot_rim, quarter)],
        near_send.at[1], near_recv.at[1], sibling,
    )
    near.start()
    near_pot.start()

    tell(y_line, plane_sem)

    def apply(level, u, blocks, step=8):
        scale, weight = scalars[level]

        def body(i, c):
            at = placed(u + i * step, step)
            before = None
            if level > 0:
                before = buffers[level - 1][pl.ds(at + rims[level - 1], step)]
            window = buffers[level][pl.ds(at + rims[level] - REACH, step + 2 * REACH)]
            pairs = filtered_block(
                window, pot_v[pl.ds(at + pot_rim, step)], before, scale, weight, lanes, lines[step]
            )
            if level < DEG - 1:
                buffers[level + 1][pl.ds(at + rims[level + 1], step)] = pairs
            else:
                out[pl.ds(2 * (at + rims[DEG]), 2 * step)] = pairs.reshape(2 * step, 8, 128)
            return c

        lax.fori_loop(0, blocks, body, 0)

    row = 2 * band + core

    def spread(u, count):
        start = placed(u, count)
        tiles = 2 * count

        def send(i, c):
            at = lax.rem(i + yx * max(tiles // floor, 1), tiles)
            tile = lax.rem(2 * (base + start) + at + 2 * whole, 2 * whole)
            src = out.at[2 * (start + rims[DEG]) + at]

            @pl.when(tile != own_tile)
            def _():
                peer = {"band": lax.rem(tile, bands), "dom": lax.div(tile, bands)}
                remote(src, recv.at[row], all_send, all_recv, peer).start()

            @pl.when(tile == own_tile)
            def _():
                pltpu.make_async_copy(src, recv.at[row], move_sem.at[3]).start()

            return c

        lax.fori_loop(0, tiles, send, 0)

    def advance(u, n):
        for level in range(DEG):
            apply(level, u + level * REACH, 1, n)
        spread(u + (DEG - 1) * REACH, n)

    pot_far[0].wait_recv()
    passed = [
        remote(mine, mine, pass_send.at[at], pass_recv.at[at], peer)
        for at, peer in enumerate(x_line)
    ]
    for copy in passed:
        copy.start()

    pass_on(5, 0)
    load.wait()
    load_pot.wait()
    own_rows.wait()
    gather_rows(1)
    pass_on(1)
    near.wait_recv()
    near_pot.wait_recv()
    pass_on(2)
    pl.semaphore_wait(plane_sem, len(y_line))
    tell(z_line, all_sem)
    apply(0, 8, 6)
    pass_on(3, 4)
    apply(1, 14, 4)
    apply(1, 42, 1)
    apply(2, 20, 3)
    gather_rows(2)
    pl.semaphore_wait(all_sem, len(z_line))
    spread(20, 24)

    far[0][5].wait_recv()
    apply(0, slab - 8, 1)
    apply(1, slab - 14, 1)
    apply(2, slab - 20, 1)
    spread(slab - 20, 8)
    for at, (u, n) in enumerate(((0, 8), (-8, 8), (-16, 8), (-20, 4), (-24, 4))):
        if at == 1:
            for copy in passed:
                copy.wait_recv()
        far[0][at].wait_recv()
        advance(u, n)

    @pl.when(long)
    def _():
        for o in range(2):
            pot_far[o].wait_send()
            for at in range(len(pieces)):
                far[o][at].wait_send()

    @pl.when(jnp.logical_not(long))
    def _():
        for o in range(2):
            far[o][5].wait_send()

    @pl.when(core == 0)
    def _():
        for copy in onward:
            copy.wait_send()

    for copy in (near, near_pot, *passed):
        copy.wait_send()
    for copy in row_copies[2]:
        copy.wait_recv()
    for copies in row_copies:
        for copy in copies:
            copy.wait_send()
    pltpu.make_async_copy(out.at[0], recv.at[row], move_sem.at[3]).wait()
    all_but_own = recv.at[pl.ds(0, recv.shape[0] - 1)]
    pltpu.make_async_copy(all_but_own, all_but_own, all_send).wait()
    pltpu.make_async_copy(all_but_own, all_but_own, all_recv).wait()


def rotate_kernel(recv_v, rows_v, out, out_v, sems):
    high, low = two_parts(jnp.concatenate([rows_v[:, 0], rows_v[:, 1]], axis=0).T)
    matrix = jnp.concatenate([high, high, low], axis=1)
    width = 256
    stores = []
    for at in range(0, 8 * 128, width):
        columns = []
        for r in range(at // 128, (at + width) // 128):
            values = jnp.concatenate([recv_v[:, 0, r], recv_v[:, 1, r]], axis=0)
            high, low = two_parts(values)
            columns.append(jnp.concatenate([high, low, high], axis=0))
        out_v[:, pl.ds(at, width)] = jnp.dot(
            matrix, jnp.concatenate(columns, axis=1), preferred_element_type=jnp.float32
        )
        store = pltpu.make_async_copy(
            out_v.at[:, pl.ds(at, width)], out.at[:, pl.ds(at, width)], sems.at[at // width]
        )
        store.start()
        stores.append(store)
    for store in stores:
        store.wait()


def per_device(bands, orbitals, potential, subspace):
    orbs, planes = orbitals.shape[0], orbitals.shape[1]
    orb = orbitals.reshape(orbs, planes, 2, 8, 128)
    pot = potential.reshape(planes, 2, 8, 128)
    f32 = jnp.float32
    dma = pltpu.SemaphoreType.DMA
    anywhere = pl.BlockSpec(memory_space=pl.ANY)
    slab, shift = 2 * planes, 2 * REACH
    recv, rows = pl.pallas_call(
        functools.partial(filter_kernel, bands),
        out_shape=(
            pltpu.VMEM((bands * orbs, 8, 128), f32),
            pltpu.VMEM((4, 4, 4, orbs, 128), f32),
        ),
        in_specs=[anywhere] * 3,
        out_specs=(anywhere,) * 2,
        scratch_shapes=[
            *[
                pltpu.VMEM((slab + 2 * (shift + REACH * (DEG - level)), 2, 8, 128), f32)
                for level in range(DEG)
            ],
            pltpu.VMEM((2 * (slab + 2 * shift), 8, 128), f32),
            pltpu.VMEM((slab + 2 * (shift + REACH * (DEG - 1)), 2, 8, 128), f32),
            pltpu.VMEM((6, 8, 2, 8, 128), f32),
            dma((2,)),
            dma((2,)),
            dma((2, 6)),
            dma((6,)),
            dma((6,)),
            dma((6,)),
            dma((2,)),
            dma,
            dma((7,)),
            dma((7,)),
            dma((4,)),
            dma,
            dma,
            dma((3, 3)),
            dma((3, 3)),
            pltpu.SemaphoreType.REGULAR,
            pltpu.SemaphoreType.REGULAR,
        ],
        compiler_params=pltpu.CompilerParams(
            collective_id=0, has_side_effects=True, vmem_limit_bytes=32 * 2**20
        ),
        name="filter",
    )(*(pltpu.with_memory_space_constraint(a, pltpu.HBM) for a in (orb, pot, subspace)))
    recv, rows = recv.reshape(bands, orbs, 8, 128), rows.reshape(bands, orbs, 128)
    return pl.pallas_call(
        rotate_kernel,
        out_shape=jax.ShapeDtypeStruct((bands * orbs, 1024), f32),
        in_specs=[pl.BlockSpec(memory_space=pltpu.VMEM)] * 2,
        out_specs=anywhere,
        scratch_shapes=[pltpu.VMEM((bands * orbs, 1024), f32), dma((4,))],
        compiler_params=pltpu.CompilerParams(vmem_limit_bytes=32 * 2**20),
        name="rotate",
    )(*(pltpu.with_memory_space_constraint(a, pltpu.VMEM) for a in (recv, rows)))


def solution(mesh):
    in_specs = (P("band", "dom", None, None), P("dom", None, None), P("band", None))
    out_specs = P(None, ("dom", "band"))
    return jax.shard_map(
        functools.partial(per_device, mesh.shape["band"]),
        mesh=mesh,
        in_specs=in_specs,
        out_specs=out_specs,
        check_vma=False,
    )
```

```python
import functools
import math

import jax
import jax.numpy as jnp
from jax import lax
from jax.experimental import pallas as pl
from jax.experimental.pallas import tpu as pltpu
from jax.sharding import PartitionSpec as P

DEG = 3
REACH = 6
MESH = pl.DeviceIdType.MESH

upper_edge = 10.7
lower_edge = 1.5
bottom_edge = -1.0


def stencil_weights():
    factor_square = math.factorial(6) ** 2
    side_weights = []
    for offset in range(1, 7):
        side_weights.append(
            2.0
            * (-1.0) ** (offset + 1)
            * factor_square
            / (offset * offset * math.factorial(6 - offset) * math.factorial(6 + offset))
        )
    center_weight = -2.0 * sum(side_weights)
    return (center_weight, side_weights)


def filter_scalars(pass_count):
    half_width = (upper_edge - lower_edge) / 2.0
    sigma_now = half_width / (bottom_edge - (upper_edge + lower_edge) / 2.0)
    gamma_value = 2.0 / sigma_now
    scalars = [(sigma_now / half_width, 0.0)]
    for pass_index in range(pass_count - 1):
        sigma_next = 1.0 / (gamma_value - sigma_now)
        scalars.append((2.0 * sigma_next / half_width, sigma_now * sigma_next))
        sigma_now = sigma_next
    return scalars


def two_parts(values):
    high = values.astype(jnp.bfloat16)
    return high, (values - high.astype(jnp.float32)).astype(jnp.bfloat16)


def stencil_matrix(size, period, axis):
    rows = lax.broadcasted_iota(jnp.int32, (size, size), 0)
    columns = lax.broadcasted_iota(jnp.int32, (size, size), 1)
    apart = jnp.abs(rows - columns)
    if period < size:
        same = jnp.bitwise_or(rows, period - 1) == jnp.bitwise_or(columns, period - 1)
        apart = jnp.where(same, apart, 0)
    apart = jnp.minimum(apart, period - apart)
    matrix = jnp.zeros((size, size), jnp.float32)
    for k, w in enumerate(stencil_weights()[1], 1):
        matrix = jnp.where(apart == k, jnp.float32(w), matrix)
    high, low = two_parts(matrix)
    return jnp.concatenate([high, high, low], axis=axis)


def filtered_block(window, pot, before, scale, weight, lanes, rows):
    center_weight, side = stencil_weights()
    n = window.shape[0] - 2 * REACH
    mid = window[REACH : REACH + n]
    high, low = two_parts(mid.reshape(n * 16, 128))
    total = jnp.dot(
        jnp.concatenate([high, low, high], axis=1), lanes, preferred_element_type=jnp.float32
    ) + jnp.dot(
        rows, jnp.concatenate([high, low, high], axis=0), preferred_element_type=jnp.float32
    )
    total = total.reshape(n, 2, 8, 128)
    for k in range(1, REACH + 1):
        beside = window[REACH + k : REACH + k + n] + window[REACH - k : REACH - k + n]
        total = total + side[k - 1] * beside
    diag = (-1.5 * center_weight - (upper_edge + lower_edge) / 2.0) * scale
    result = (pot * scale + diag) * mid + (-0.5 * scale) * total
    if before is not None:
        result = result - weight * before
    return result


def filter_kernel(
    bands, orb, pot, sub, recv, rows, p0, p1, p2, out, pot_v,
    near_send, near_recv, far_send, far_recv, pot_send, pot_recv, pass_send, pass_recv,
    move_sem, all_send, all_recv, row_send, row_recv, plane_sem, all_sem,
):
    quarter = orb.shape[1]
    slab, whole = 2 * quarter, 4 * quarter
    band, dom = lax.axis_index("band"), lax.axis_index("dom")
    core, half = lax.rem(dom, 2), lax.div(dom, 2)
    side = 4
    floor = side * side
    zl, x, yx = lax.div(band, floor), lax.rem(band, side), lax.rem(band, floor)
    shift = 2 * REACH
    left = jnp.where(zl < side // 2, 1, 0)
    long = core == left
    base = half * slab
    own_tile = dom * bands + band
    own_plane = lax.div(own_tile, 2)
    scalars = filter_scalars(DEG)
    buffers = (p0, p1, p2)
    rims = tuple(shift + REACH * (DEG - level) for level in range(DEG + 1))
    pot_rim = rims[1]

    def placed(u, count):
        return jnp.where(left == 1, u, slab - count - u)

    load = pltpu.make_async_copy(
        orb.at[core], p0.at[pl.ds(core * quarter + rims[0], quarter)], move_sem.at[0]
    )
    load.start()
    load_pot = pltpu.make_async_copy(
        pot, pot_v.at[pl.ds(core * quarter + pot_rim, quarter)], move_sem.at[1]
    )
    load_pot.start()

    sibling = {"dom": dom + 1 - 2 * core}
    partners = [{"dom": 2 * (1 - half) + k} for k in range(2)]

    def chip_along(shift):
        there = lax.rem(half * side + zl + shift, 2 * side)
        return {
            "band": lax.rem(there, side) * floor + yx,
            "dom": lax.div(there, side) * 2 + core,
        }

    x_line = [
        {"band": band - x + lax.rem(x + dx, side), "dom": dom if dk == 0 else dom + 1 - 2 * core}
        for dx in range(side)
        for dk in range(2)
    ][1:]
    y = lax.div(yx, side)
    y_line = [{"band": band + side * (lax.rem(y + dy, side) - y)} for dy in range(1, side)]
    z_line = [chip_along(dz) for dz in range(1, 2 * side)]
    other_partner = {"dom": 2 * (1 - half) + 1 - core}
    barrier = pltpu.get_barrier_semaphore()
    entered = (*z_line, other_partner, *x_line, *y_line)

    def tell(peers, semaphore):
        for peer in peers:
            pl.semaphore_signal(semaphore, inc=1, device_id=peer, device_id_type=MESH)

    tell(entered, barrier)
    lanes = stencil_matrix(128, 128, 0)
    lines = stencil_matrix(128, 16, 1)
    pl.semaphore_wait(barrier, len(entered))

    def remote(src, dst, send_sem, recv_sem, peer):
        return pltpu.make_async_remote_copy(
            src_ref=src, dst_ref=dst, send_sem=send_sem, recv_sem=recv_sem,
            device_id=peer, device_id_type=MESH,
        )

    own_rows = pltpu.make_async_copy(sub, rows.at[zl, y, x], move_sem.at[2])
    own_rows.start()
    row_lines = [
        (rows.at[zl, y, x], [{"band": lax.rem(band + d * floor, bands)} for d in range(1, side)]),
        (rows.at[:, y, x], y_line),
        (rows.at[:, :, x], [{"band": band - x + lax.rem(x + d, side)} for d in range(1, side)]),
    ]
    row_copies = [
        [
            remote(
                sub if stage == 0 else part_rows, part_rows,
                row_send.at[stage, at], row_recv.at[stage, at], peer,
            )
            for at, peer in enumerate(peers)
        ]
        for stage, (part_rows, peers) in enumerate(row_lines)
    ]

    def gather_rows(stage):
        if stage > 0:
            for copy in row_copies[stage - 1]:
                copy.wait_recv()
        for copy in row_copies[stage]:
            copy.start()

    gather_rows(0)
    pieces = [(0, 6), (6, 8), (14, 8), (22, 8)]
    assert sum(n for _, n in pieces) == rims[0]
    far = []
    for o in range(2):
        group = []
        for at, (a, n) in enumerate(pieces):
            group.append(
                remote(
                    orb.at[o, pl.ds(jnp.where(left == 1, quarter - a - n, a), n)],
                    p0.at[pl.ds(placed(-a - n, n) + rims[0], n)],
                    far_send.at[o, at], far_recv.at[at], partners[o],
                )
            )
        n = REACH
        group.append(
            remote(
                orb.at[o, pl.ds(jnp.where(left == 1, 0, quarter - n), n)],
                p0.at[pl.ds(placed(slab, n) + rims[0], n)],
                far_send.at[o, 4], far_recv.at[4], partners[o],
            )
        )
        far.append(group)
    part = pot_rim // 8
    pot_far = [
        remote(
            pot.at[pl.ds(jnp.where(left == 1, quarter - pot_rim, 0) + (2 * x + o) * part, part)],
            pot_v.at[pl.ds(placed(-pot_rim, pot_rim) + pot_rim + (2 * x + o) * part, part)],
            pot_send.at[o], pot_recv, partners[o],
        )
        for o in range(2)
    ]
    mine = pot_v.at[pl.ds(placed(-pot_rim, pot_rim) + pot_rim + (2 * x + core) * part, part)]

    @pl.when(long)
    def _():
        for o in range(2):
            pot_far[o].start()
        for at in range(len(pieces)):
            for o in range(2):
                far[o][at].start()

    @pl.when(jnp.logical_not(long))
    def _():
        for o in range(2):
            far[o][4].start()

    near = remote(
        orb.at[1 - core], p0.at[pl.ds(core * quarter + rims[0], quarter)],
        near_send.at[0], near_recv.at[0], sibling,
    )
    near_pot = remote(
        pot, pot_v.at[pl.ds(core * quarter + pot_rim, quarter)],
        near_send.at[1], near_recv.at[1], sibling,
    )
    near.start()
    near_pot.start()

    tell(y_line, plane_sem)

    step = 8

    def apply(level, *places):
        scale, weight = scalars[level]
        begins = [placed(u, step) for u in places]
        results = []
        for at in begins:
            before = None
            if level > 0:
                before = buffers[level - 1][pl.ds(at + rims[level - 1], step)]
            window = buffers[level][pl.ds(at + rims[level] - REACH, step + 2 * REACH)]
            pairs = filtered_block(
                window, pot_v[pl.ds(at + pot_rim, step)], before, scale, weight, lanes, lines
            )
            results.append(pairs)
        for at, pairs in zip(begins, results):
            if level < DEG - 1:
                buffers[level + 1][pl.ds(at + rims[level + 1], step)] = pairs
            else:
                out[pl.ds(2 * (at + rims[DEG]), 2 * step)] = pairs.reshape(2 * step, 8, 128)

    row = 2 * band + core

    def spread(u, count):
        start = placed(u, count)
        tiles = 2 * count

        def send(i, c):
            at = lax.rem(i + yx * max(tiles // floor, 1), tiles)
            tile = lax.rem(2 * (base + start) + at + 2 * whole, 2 * whole)
            src = out.at[2 * (start + rims[DEG]) + at]

            @pl.when(tile != own_tile)
            def _():
                peer = {"band": lax.rem(tile, bands), "dom": lax.div(tile, bands)}
                remote(src, recv.at[row], all_send, all_recv, peer).start()

            @pl.when(tile == own_tile)
            def _():
                pltpu.make_async_copy(src, recv.at[row], move_sem.at[3]).start()

            return c

        lax.fori_loop(0, tiles, send, 0)

    pot_far[0].wait_recv()
    passed = [
        remote(mine, mine, pass_send.at[at], pass_recv.at[at], peer)
        for at, peer in enumerate(x_line)
    ]
    for copy in passed:
        copy.start()

    load.wait()
    load_pot.wait()
    own_rows.wait()
    gather_rows(1)
    near.wait_recv()
    near_pot.wait_recv()
    pl.semaphore_wait(plane_sem, len(y_line))
    tell(z_line, all_sem)
    apply(0, 8, 16, 24)
    apply(0, 32, 40, 48)
    apply(1, 14, 22)
    apply(1, 30, 38, 42)
    apply(2, 20, 28, 36)
    gather_rows(2)
    pl.semaphore_wait(all_sem, len(z_line))
    spread(20, 24)

    for at in (4, 0, 1):
        far[0][at].wait_recv()
    for copy in passed:
        copy.wait_recv()
    apply(0, -8, 0, slab - 8)
    apply(1, -2, 6, slab - 14)
    apply(2, 4, 12, slab - 20)
    for u in (4, 12, slab - 20):
        spread(u, 8)
    for at in (2, 3):
        far[0][at].wait_recv()
    apply(0, -24, -16)
    apply(1, -18, -10)
    apply(2, -12, -4)
    spread(-12, 8)
    spread(-4, 8)

    @pl.when(long)
    def _():
        for o in range(2):
            pot_far[o].wait_send()
            for at in range(len(pieces)):
                far[o][at].wait_send()

    @pl.when(jnp.logical_not(long))
    def _():
        for o in range(2):
            far[o][4].wait_send()

    for copy in (near, near_pot, *passed):
        copy.wait_send()
    for copy in row_copies[2]:
        copy.wait_recv()
    for copies in row_copies:
        for copy in copies:
            copy.wait_send()
    pltpu.make_async_copy(out.at[0], recv.at[row], move_sem.at[3]).wait()
    all_but_own = recv.at[pl.ds(0, recv.shape[0] - 1)]
    pltpu.make_async_copy(all_but_own, all_but_own, all_send).wait()
    pltpu.make_async_copy(all_but_own, all_but_own, all_recv).wait()


def rotate_kernel(recv_v, rows_v, out, out_v, sems):
    high, low = two_parts(jnp.concatenate([rows_v[:, 0], rows_v[:, 1]], axis=0).T)
    matrix = jnp.concatenate([high, high, low], axis=1)
    width = 256
    stores = []
    for at in range(0, 8 * 128, width):
        columns = []
        for r in range(at // 128, (at + width) // 128):
            values = jnp.concatenate([recv_v[:, 0, r], recv_v[:, 1, r]], axis=0)
            high, low = two_parts(values)
            columns.append(jnp.concatenate([high, low, high], axis=0))
        out_v[:, pl.ds(at, width)] = jnp.dot(
            matrix, jnp.concatenate(columns, axis=1), preferred_element_type=jnp.float32
        )
        store = pltpu.make_async_copy(
            out_v.at[:, pl.ds(at, width)], out.at[:, pl.ds(at, width)], sems.at[at // width]
        )
        store.start()
        stores.append(store)
    for store in stores:
        store.wait()


def per_device(bands, orbitals, potential, subspace):
    orbs, planes = orbitals.shape[0], orbitals.shape[1]
    orb = orbitals.reshape(orbs, planes, 2, 8, 128)
    pot = potential.reshape(planes, 2, 8, 128)
    f32 = jnp.float32
    dma = pltpu.SemaphoreType.DMA
    anywhere = pl.BlockSpec(memory_space=pl.ANY)
    slab, shift = 2 * planes, 2 * REACH
    recv, rows = pl.pallas_call(
        functools.partial(filter_kernel, bands),
        out_shape=(
            pltpu.VMEM((bands * orbs, 8, 128), f32),
            pltpu.VMEM((4, 4, 4, orbs, 128), f32),
        ),
        in_specs=[anywhere] * 3,
        out_specs=(anywhere,) * 2,
        scratch_shapes=[
            *[
                pltpu.VMEM((slab + 2 * (shift + REACH * (DEG - level)), 2, 8, 128), f32)
                for level in range(DEG)
            ],
            pltpu.VMEM((2 * (slab + 2 * shift), 8, 128), f32),
            pltpu.VMEM((slab + 2 * (shift + REACH * (DEG - 1)), 2, 8, 128), f32),
            dma((2,)),
            dma((2,)),
            dma((2, 5)),
            dma((5,)),
            dma((2,)),
            dma,
            dma((7,)),
            dma((7,)),
            dma((4,)),
            dma,
            dma,
            dma((3, 3)),
            dma((3, 3)),
            pltpu.SemaphoreType.REGULAR,
            pltpu.SemaphoreType.REGULAR,
        ],
        compiler_params=pltpu.CompilerParams(
            collective_id=0, has_side_effects=True, vmem_limit_bytes=32 * 2**20
        ),
        name="filter",
    )(*(pltpu.with_memory_space_constraint(a, pltpu.HBM) for a in (orb, pot, subspace)))
    recv, rows = recv.reshape(bands, orbs, 8, 128), rows.reshape(bands, orbs, 128)
    return pl.pallas_call(
        rotate_kernel,
        out_shape=jax.ShapeDtypeStruct((bands * orbs, 1024), f32),
        in_specs=[pl.BlockSpec(memory_space=pltpu.VMEM)] * 2,
        out_specs=anywhere,
        scratch_shapes=[pltpu.VMEM((bands * orbs, 1024), f32), dma((4,))],
        compiler_params=pltpu.CompilerParams(vmem_limit_bytes=32 * 2**20),
        name="rotate",
    )(*(pltpu.with_memory_space_constraint(a, pltpu.VMEM) for a in (recv, rows)))


def solution(mesh):
    in_specs = (P("band", "dom", None, None), P("dom", None, None), P("band", None))
    out_specs = P(None, ("dom", "band"))
    return jax.shard_map(
        functools.partial(per_device, mesh.shape["band"]),
        mesh=mesh,
        in_specs=in_specs,
        out_specs=out_specs,
        check_vma=False,
    )
```

```python
import functools
import math

import jax
import jax.numpy as jnp
from jax import lax
from jax.experimental import pallas as pl
from jax.experimental.pallas import tpu as pltpu
from jax.sharding import PartitionSpec as P

DEG = 3
REACH = 6
MESH = pl.DeviceIdType.MESH

upper_edge = 10.7
lower_edge = 1.5
bottom_edge = -1.0


def stencil_weights():
    factor_square = math.factorial(6) ** 2
    side_weights = []
    for offset in range(1, 7):
        side_weights.append(
            2.0
            * (-1.0) ** (offset + 1)
            * factor_square
            / (offset * offset * math.factorial(6 - offset) * math.factorial(6 + offset))
        )
    center_weight = -2.0 * sum(side_weights)
    return (center_weight, side_weights)


def filter_scalars(pass_count):
    half_width = (upper_edge - lower_edge) / 2.0
    sigma_now = half_width / (bottom_edge - (upper_edge + lower_edge) / 2.0)
    gamma_value = 2.0 / sigma_now
    scalars = [(sigma_now / half_width, 0.0)]
    for pass_index in range(pass_count - 1):
        sigma_next = 1.0 / (gamma_value - sigma_now)
        scalars.append((2.0 * sigma_next / half_width, sigma_now * sigma_next))
        sigma_now = sigma_next
    return scalars


def two_parts(values):
    high = values.astype(jnp.bfloat16)
    return high, (values - high.astype(jnp.float32)).astype(jnp.bfloat16)


def stencil_matrix(size, period, axis):
    rows = lax.broadcasted_iota(jnp.int32, (size, size), 0)
    columns = lax.broadcasted_iota(jnp.int32, (size, size), 1)
    apart = jnp.abs(rows - columns)
    if period < size:
        same = jnp.bitwise_or(rows, period - 1) == jnp.bitwise_or(columns, period - 1)
        apart = jnp.where(same, apart, 0)
    apart = jnp.minimum(apart, period - apart)
    matrix = jnp.zeros((size, size), jnp.float32)
    for k, w in enumerate(stencil_weights()[1], 1):
        matrix = jnp.where(apart == k, jnp.float32(w), matrix)
    high, low = two_parts(matrix)
    return jnp.concatenate([high, high, low], axis=axis)


def filtered_block(window, pot, before, scale, weight, lanes, rows):
    center_weight, side = stencil_weights()
    n = window.shape[0] - 2 * REACH
    mid = window[REACH : REACH + n]
    high, low = two_parts(mid.reshape(n * 16, 128))
    total = jnp.dot(
        jnp.concatenate([high, low, high], axis=1), lanes, preferred_element_type=jnp.float32
    ) + jnp.dot(
        rows, jnp.concatenate([high, low, high], axis=0), preferred_element_type=jnp.float32
    )
    total = total.reshape(n, 2, 8, 128)
    for k in range(1, REACH + 1):
        beside = window[REACH + k : REACH + k + n] + window[REACH - k : REACH - k + n]
        total = total + side[k - 1] * beside
    diag = (-1.5 * center_weight - (upper_edge + lower_edge) / 2.0) * scale
    result = (pot * scale + diag) * mid + (-0.5 * scale) * total
    if before is not None:
        result = result - weight * before
    return result


def filter_kernel(
    bands, orb, pot, sub, recv, matrix, rows, p0, p1, p2, out, pot_v,
    near_send, near_recv, far_send, far_recv, pot_send, pot_recv, pair_send, pair_recv, pass_send, pass_recv,
    move_sem, all_send, all_recv, row_send, row_recv, plane_sem, all_sem,
):
    quarter = orb.shape[1]
    slab, whole = 2 * quarter, 4 * quarter
    band, dom = lax.axis_index("band"), lax.axis_index("dom")
    core, half = lax.rem(dom, 2), lax.div(dom, 2)
    side = 4
    floor = side * side
    zl, x, yx = lax.div(band, floor), lax.rem(band, side), lax.rem(band, floor)
    shift = 2 * REACH
    left = jnp.where(zl < side // 2, 1, 0)
    long = core == left
    base = half * slab
    own_tile = dom * bands + band
    own_plane = lax.div(own_tile, 2)
    scalars = filter_scalars(DEG)
    buffers = (p0, p1, p2)
    rims = tuple(shift + REACH * (DEG - level) for level in range(DEG + 1))
    pot_rim = rims[1]

    def placed(u, count):
        return jnp.where(left == 1, u, slab - count - u)

    load = pltpu.make_async_copy(
        orb.at[core], p0.at[pl.ds(core * quarter + rims[0], quarter)], move_sem.at[0]
    )
    load.start()
    load_pot = pltpu.make_async_copy(
        pot, pot_v.at[pl.ds(core * quarter + pot_rim, quarter)], move_sem.at[1]
    )
    load_pot.start()

    sibling = {"dom": dom + 1 - 2 * core}
    partners = [{"dom": 2 * (1 - half) + k} for k in range(2)]

    def chip_along(shift):
        there = lax.rem(half * side + zl + shift, 2 * side)
        return {
            "band": lax.rem(there, side) * floor + yx,
            "dom": lax.div(there, side) * 2 + core,
        }

    x_line = [
        {"band": band - x + lax.rem(x + dx, side), "dom": dom if dk == 0 else dom + 1 - 2 * core}
        for dx in range(side)
        for dk in range(2)
    ][1:]
    y = lax.div(yx, side)
    y_line = [{"band": band + side * (lax.rem(y + dy, side) - y)} for dy in range(1, side)]
    z_line = [chip_along(dz) for dz in range(1, 2 * side)]
    other_partner = {"dom": 2 * (1 - half) + 1 - core}
    barrier = pltpu.get_barrier_semaphore()
    entered = (*z_line, other_partner, *x_line, *y_line)

    def tell(peers, semaphore):
        for peer in peers:
            pl.semaphore_signal(semaphore, inc=1, device_id=peer, device_id_type=MESH)

    tell(entered, barrier)
    lanes = stencil_matrix(128, 128, 0)
    lines = {n: stencil_matrix(16 * n, 16, 1) for n in (4, 8)}
    pl.semaphore_wait(barrier, len(entered))

    def remote(src, dst, send_sem, recv_sem, peer):
        return pltpu.make_async_remote_copy(
            src_ref=src, dst_ref=dst, send_sem=send_sem, recv_sem=recv_sem,
            device_id=peer, device_id_type=MESH,
        )

    own_rows = pltpu.make_async_copy(sub, rows.at[zl, y, x], move_sem.at[2])
    own_rows.start()
    row_lines = [
        (rows.at[zl, y, x], [{"band": lax.rem(band + d * floor, bands)} for d in range(1, side)]),
        (rows.at[:, y, x], y_line),
        (rows.at[:, :, x], [{"band": band - x + lax.rem(x + d, side)} for d in range(1, side)]),
    ]
    row_copies = [
        [
            remote(
                sub if stage == 0 else part_rows, part_rows,
                row_send.at[stage, at], row_recv.at[stage, at], peer,
            )
            for at, peer in enumerate(peers)
        ]
        for stage, (part_rows, peers) in enumerate(row_lines)
    ]

    def gather_rows(stage):
        if stage > 0:
            for copy in row_copies[stage - 1]:
                copy.wait_recv()
        for copy in row_copies[stage]:
            copy.start()

    gather_rows(0)
    pieces = [(0, 6), (6, 8), (14, 8), (22, 4), (26, 4)]
    assert sum(n for _, n in pieces) == rims[0]
    far = []
    for o in range(2):
        group = []
        for at, (a, n) in enumerate(pieces):
            group.append(
                remote(
                    orb.at[o, pl.ds(jnp.where(left == 1, quarter - a - n, a), n)],
                    p0.at[pl.ds(placed(-a - n, n) + rims[0], n)],
                    far_send.at[o, at], far_recv.at[at], partners[o],
                )
            )
        n = REACH
        group.append(
            remote(
                orb.at[o, pl.ds(jnp.where(left == 1, 0, quarter - n), n)],
                p0.at[pl.ds(placed(slab, n) + rims[0], n)],
                far_send.at[o, 5], far_recv.at[5], partners[o],
            )
        )
        far.append(group)
    part = pot_rim // 8
    parity = lax.rem(y, 2)
    pot_far = [
        remote(
            pot.at[
                pl.ds(jnp.where(left == 1, quarter - pot_rim, 0) + (2 * x + o) * part, part), parity
            ],
            pot_v.at[
                pl.ds(placed(-pot_rim, pot_rim) + pot_rim + (2 * x + o) * part, part), parity
            ],
            pot_send.at[o], pot_recv, partners[o],
        )
        for o in range(2)
    ]
    mine = pot_v.at[pl.ds(placed(-pot_rim, pot_rim) + pot_rim + (2 * x + core) * part, part)]

    @pl.when(long)
    def _():
        for o in range(2):
            pot_far[o].start()
        for at in range(len(pieces)):
            for o in range(2):
                far[o][at].start()

    @pl.when(jnp.logical_not(long))
    def _():
        for o in range(2):
            far[o][5].start()

    near = remote(
        orb.at[1 - core], p0.at[pl.ds(core * quarter + rims[0], quarter)],
        near_send.at[0], near_recv.at[0], sibling,
    )
    near_pot = remote(
        pot, pot_v.at[pl.ds(core * quarter + pot_rim, quarter)],
        near_send.at[1], near_recv.at[1], sibling,
    )
    near.start()
    near_pot.start()

    tell(y_line, plane_sem)

    def apply(level, u, blocks, step=8):
        scale, weight = scalars[level]

        def body(i, c):
            at = placed(u + i * step, step)
            before = None
            if level > 0:
                before = buffers[level - 1][pl.ds(at + rims[level - 1], step)]
            window = buffers[level][pl.ds(at + rims[level] - REACH, step + 2 * REACH)]
            pairs = filtered_block(
                window, pot_v[pl.ds(at + pot_rim, step)], before, scale, weight, lanes, lines[step]
            )
            if level < DEG - 1:
                buffers[level + 1][pl.ds(at + rims[level + 1], step)] = pairs
            else:
                out[pl.ds(2 * (at + rims[DEG]), 2 * step)] = pairs.reshape(2 * step, 8, 128)
            return c

        lax.fori_loop(0, blocks, body, 0)

    row = 2 * band + core

    def spread(u, count):
        start = placed(u, count)
        tiles = 2 * count

        def send(i, c):
            at = lax.rem(i + yx * max(tiles // floor, 1), tiles)
            tile = lax.rem(2 * (base + start) + at + 2 * whole, 2 * whole)
            src = out.at[2 * (start + rims[DEG]) + at]

            @pl.when(tile != own_tile)
            def _():
                peer = {"band": lax.rem(tile, bands), "dom": lax.div(tile, bands)}
                remote(src, recv.at[row], all_send, all_recv, peer).start()

            @pl.when(tile == own_tile)
            def _():
                pltpu.make_async_copy(src, recv.at[row], move_sem.at[3]).start()

            return c

        lax.fori_loop(0, tiles, send, 0)

    def advance(u, n):
        for level in range(DEG):
            apply(level, u + level * REACH, 1, n)
        spread(u + (DEG - 1) * REACH, n)

    part_half = pot_v.at[
        pl.ds(placed(-pot_rim, pot_rim) + pot_rim + (2 * x + core) * part, part), parity
    ]
    pot_pair = remote(
        part_half, part_half, pair_send, pair_recv, {"band": band + side * (1 - 2 * parity)}
    )
    pot_far[0].wait_recv()
    pot_pair.start()
    pot_pair.wait_recv()
    passed = [
        remote(mine, mine, pass_send.at[at], pass_recv.at[at], peer)
        for at, peer in enumerate(x_line)
    ]
    for copy in passed:
        copy.start()

    load.wait()
    load_pot.wait()
    own_rows.wait()
    gather_rows(1)
    near.wait_recv()
    near_pot.wait_recv()
    pl.semaphore_wait(plane_sem, len(y_line))
    tell(z_line, all_sem)
    apply(0, 8, 6)
    apply(1, 14, 4)
    apply(1, 42, 1)
    apply(2, 20, 3)
    gather_rows(2)
    pl.semaphore_wait(all_sem, len(z_line))
    spread(20, 24)

    far[0][5].wait_recv()
    apply(0, slab - 8, 1)
    apply(1, slab - 14, 1)
    apply(2, slab - 20, 1)
    spread(slab - 20, 8)
    for at, (u, n) in enumerate(((0, 8), (-8, 8), (-16, 8), (-20, 4), (-24, 4))):
        if at == 3:
            for copy in row_copies[2]:
                copy.wait_recv()
            high, low = two_parts(
                jnp.concatenate(
                    [rows[:, :, :, k].reshape(bands, 2 * bands) for k in range(2)], axis=0
                ).T
            )
            matrix[...] = jnp.concatenate([high, high, low], axis=1)
        if at == 1:
            for copy in passed:
                copy.wait_recv()
        far[0][at].wait_recv()
        advance(u, n)

    @pl.when(long)
    def _():
        for o in range(2):
            pot_far[o].wait_send()
            for at in range(len(pieces)):
                far[o][at].wait_send()

    @pl.when(jnp.logical_not(long))
    def _():
        for o in range(2):
            far[o][5].wait_send()

    for copy in (near, near_pot, pot_pair, *passed):
        copy.wait_send()
    for copies in row_copies:
        for copy in copies:
            copy.wait_send()
    pltpu.make_async_copy(out.at[0], recv.at[row], move_sem.at[3]).wait()
    all_but_own = recv.at[pl.ds(0, recv.shape[0] - 1)]
    pltpu.make_async_copy(all_but_own, all_but_own, all_send).wait()
    pltpu.make_async_copy(all_but_own, all_but_own, all_recv).wait()


def rotate_kernel(recv_v, matrix_v, out, out_v, sems):
    matrix = matrix_v[...]
    width = 256
    stores = []
    for at in range(0, 8 * 128, width):
        columns = []
        for r in range(at // 128, (at + width) // 128):
            values = jnp.concatenate([recv_v[:, 0, r], recv_v[:, 1, r]], axis=0)
            high, low = two_parts(values)
            columns.append(jnp.concatenate([high, low, high], axis=0))
        out_v[:, pl.ds(at, width)] = jnp.dot(
            matrix, jnp.concatenate(columns, axis=1), preferred_element_type=jnp.float32
        )
        store = pltpu.make_async_copy(
            out_v.at[:, pl.ds(at, width)], out.at[:, pl.ds(at, width)], sems.at[at // width]
        )
        store.start()
        stores.append(store)
    for store in stores:
        store.wait()


def per_device(bands, orbitals, potential, subspace):
    orbs, planes = orbitals.shape[0], orbitals.shape[1]
    orb = orbitals.reshape(orbs, planes, 2, 8, 128)
    pot = potential.reshape(planes, 2, 8, 128)
    f32 = jnp.float32
    dma = pltpu.SemaphoreType.DMA
    anywhere = pl.BlockSpec(memory_space=pl.ANY)
    slab, shift = 2 * planes, 2 * REACH
    recv, matrix = pl.pallas_call(
        functools.partial(filter_kernel, bands),
        out_shape=(
            pltpu.VMEM((bands * orbs, 8, 128), f32),
            pltpu.VMEM((bands * orbs, 3 * bands * orbs), jnp.bfloat16),
        ),
        in_specs=[anywhere] * 3,
        out_specs=(anywhere, pl.BlockSpec(memory_space=pltpu.VMEM)),
        scratch_shapes=[
            pltpu.VMEM((4, 4, 4, orbs, 128), f32),
            *[
                pltpu.VMEM((slab + 2 * (shift + REACH * (DEG - level)), 2, 8, 128), f32)
                for level in range(DEG)
            ],
            pltpu.VMEM((2 * (slab + 2 * shift), 8, 128), f32),
            pltpu.VMEM((slab + 2 * (shift + REACH * (DEG - 1)), 2, 8, 128), f32),
            dma((2,)),
            dma((2,)),
            dma((2, 6)),
            dma((6,)),
            dma((2,)),
            dma,
            dma,
            dma,
            dma((7,)),
            dma((7,)),
            dma((4,)),
            dma,
            dma,
            dma((3, 3)),
            dma((3, 3)),
            pltpu.SemaphoreType.REGULAR,
            pltpu.SemaphoreType.REGULAR,
        ],
        compiler_params=pltpu.CompilerParams(
            collective_id=0, has_side_effects=True, vmem_limit_bytes=32 * 2**20
        ),
        name="filter",
    )(*(pltpu.with_memory_space_constraint(a, pltpu.HBM) for a in (orb, pot, subspace)))
    recv = recv.reshape(bands, orbs, 8, 128)
    return pl.pallas_call(
        rotate_kernel,
        out_shape=jax.ShapeDtypeStruct((bands * orbs, 1024), f32),
        in_specs=[pl.BlockSpec(memory_space=pltpu.VMEM)] * 2,
        out_specs=anywhere,
        scratch_shapes=[pltpu.VMEM((bands * orbs, 1024), f32), dma((4,))],
        compiler_params=pltpu.CompilerParams(vmem_limit_bytes=32 * 2**20),
        name="rotate",
    )(*(pltpu.with_memory_space_constraint(a, pltpu.VMEM) for a in (recv, matrix)))


def solution(mesh):
    in_specs = (P("band", "dom", None, None), P("dom", None, None), P("band", None))
    out_specs = P(None, ("dom", "band"))
    return jax.shard_map(
        functools.partial(per_device, mesh.shape["band"]),
        mesh=mesh,
        in_specs=in_specs,
        out_specs=out_specs,
        check_vma=False,
    )
```

```python
import functools
import math

import jax
import jax.numpy as jnp
from jax import lax
from jax.experimental import pallas as pl
from jax.experimental.pallas import tpu as pltpu
from jax.sharding import PartitionSpec as P

DEG = 3
REACH = 6
MESH = pl.DeviceIdType.MESH

upper_edge = 10.7
lower_edge = 1.5
bottom_edge = -1.0


def stencil_weights():
    factor_square = math.factorial(6) ** 2
    side_weights = []
    for offset in range(1, 7):
        side_weights.append(
            2.0
            * (-1.0) ** (offset + 1)
            * factor_square
            / (offset * offset * math.factorial(6 - offset) * math.factorial(6 + offset))
        )
    center_weight = -2.0 * sum(side_weights)
    return (center_weight, side_weights)


def filter_scalars(pass_count):
    half_width = (upper_edge - lower_edge) / 2.0
    sigma_now = half_width / (bottom_edge - (upper_edge + lower_edge) / 2.0)
    gamma_value = 2.0 / sigma_now
    scalars = [(sigma_now / half_width, 0.0)]
    for pass_index in range(pass_count - 1):
        sigma_next = 1.0 / (gamma_value - sigma_now)
        scalars.append((2.0 * sigma_next / half_width, sigma_now * sigma_next))
        sigma_now = sigma_next
    return scalars


def two_parts(values):
    high = values.astype(jnp.bfloat16)
    return high, (values - high.astype(jnp.float32)).astype(jnp.bfloat16)


def stencil_matrix(size, period, axis):
    rows = lax.broadcasted_iota(jnp.int32, (size, size), 0)
    columns = lax.broadcasted_iota(jnp.int32, (size, size), 1)
    apart = jnp.abs(rows - columns)
    if period < size:
        same = jnp.bitwise_or(rows, period - 1) == jnp.bitwise_or(columns, period - 1)
        apart = jnp.where(same, apart, 0)
    apart = jnp.minimum(apart, period - apart)
    matrix = jnp.zeros((size, size), jnp.float32)
    for k, w in enumerate(stencil_weights()[1], 1):
        matrix = jnp.where(apart == k, jnp.float32(w), matrix)
    high, low = two_parts(matrix)
    return jnp.concatenate([high, high, low], axis=axis)


def filtered_block(window, pot, before, scale, weight, lanes, rows):
    center_weight, side = stencil_weights()
    n = window.shape[0] - 2 * REACH
    mid = window[REACH : REACH + n]
    high, low = two_parts(mid.reshape(n * 16, 128))
    total = jnp.dot(
        jnp.concatenate([high, low, high], axis=1), lanes, preferred_element_type=jnp.float32
    ) + jnp.dot(
        rows, jnp.concatenate([high, low, high], axis=0), preferred_element_type=jnp.float32
    )
    total = total.reshape(n, 2, 8, 128)
    for k in range(1, REACH + 1):
        beside = window[REACH + k : REACH + k + n] + window[REACH - k : REACH - k + n]
        total = total + side[k - 1] * beside
    diag = (-1.5 * center_weight - (upper_edge + lower_edge) / 2.0) * scale
    result = (pot * scale + diag) * mid + (-0.5 * scale) * total
    if before is not None:
        result = result - weight * before
    return result


def filter_kernel(
    bands, orb, pot, sub, recv, rows, p0, p1, p2, out, pot_v, held,
    near_send, near_recv, far_send, far_recv, onward_send, onward_recv, pot_send, pot_recv, pass_send, pass_recv,
    move_sem, all_send, all_recv, row_send, row_recv, plane_sem, all_sem,
):
    quarter = orb.shape[1]
    slab, whole = 2 * quarter, 4 * quarter
    band, dom = lax.axis_index("band"), lax.axis_index("dom")
    core, half = lax.rem(dom, 2), lax.div(dom, 2)
    side = 4
    floor = side * side
    zl, x, yx = lax.div(band, floor), lax.rem(band, side), lax.rem(band, floor)
    shift = 2 * REACH
    left = jnp.where(zl < side // 2, 1, 0)
    long = core == left
    base = half * slab
    own_tile = dom * bands + band
    own_plane = lax.div(own_tile, 2)
    scalars = filter_scalars(DEG)
    buffers = (p0, p1, p2)
    rims = tuple(shift + REACH * (DEG - level) for level in range(DEG + 1))
    pot_rim = rims[1]

    def placed(u, count):
        return jnp.where(left == 1, u, slab - count - u)

    load = pltpu.make_async_copy(
        orb.at[core], p0.at[pl.ds(core * quarter + rims[0], quarter)], move_sem.at[0]
    )
    load.start()
    load_pot = pltpu.make_async_copy(
        pot, pot_v.at[pl.ds(core * quarter + pot_rim, quarter)], move_sem.at[1]
    )
    load_pot.start()

    sibling = {"dom": dom + 1 - 2 * core}
    partners = [{"dom": 2 * (1 - half) + k} for k in range(2)]

    def chip_along(shift, core_there=core):
        there = lax.rem(half * side + zl + shift + 2 * side, 2 * side)
        return {
            "band": lax.rem(there, side) * floor + yx,
            "dom": lax.div(there, side) * 2 + core_there,
        }

    relays = [chip_along(2 - 4 * o, o) for o in range(2)]
    onward_to = chip_along(2 - 4 * core)

    x_line = [
        {"band": band - x + lax.rem(x + dx, side), "dom": dom if dk == 0 else dom + 1 - 2 * core}
        for dx in range(side)
        for dk in range(2)
    ][1:]
    y = lax.div(yx, side)
    y_line = [{"band": band + side * (lax.rem(y + dy, side) - y)} for dy in range(1, side)]
    z_line = [chip_along(dz) for dz in range(1, 2 * side)]
    other_partner = {"dom": 2 * (1 - half) + 1 - core}
    barrier = pltpu.get_barrier_semaphore()
    entered = (*z_line, other_partner, chip_along(4 * core - 2, 1 - core), *x_line, *y_line)

    def tell(peers, semaphore):
        for peer in peers:
            pl.semaphore_signal(semaphore, inc=1, device_id=peer, device_id_type=MESH)

    tell(entered, barrier)
    lanes = stencil_matrix(128, 128, 0)
    lines = {n: stencil_matrix(16 * n, 16, 1) for n in (4, 8)}
    pl.semaphore_wait(barrier, len(entered))

    def remote(src, dst, send_sem, recv_sem, peer):
        return pltpu.make_async_remote_copy(
            src_ref=src, dst_ref=dst, send_sem=send_sem, recv_sem=recv_sem,
            device_id=peer, device_id_type=MESH,
        )

    own_rows = pltpu.make_async_copy(sub, rows.at[zl, y, x], move_sem.at[2])
    own_rows.start()
    row_lines = [
        (rows.at[zl, y, x], [{"band": lax.rem(band + d * floor, bands)} for d in range(1, side)]),
        (rows.at[:, y, x], y_line),
        (rows.at[:, :, x], [{"band": band - x + lax.rem(x + d, side)} for d in range(1, side)]),
    ]
    row_copies = [
        [
            remote(
                sub if stage == 0 else part_rows, part_rows,
                row_send.at[stage, at], row_recv.at[stage, at], peer,
            )
            for at, peer in enumerate(peers)
        ]
        for stage, (part_rows, peers) in enumerate(row_lines)
    ]

    def gather_rows(stage):
        if stage > 0:
            for copy in row_copies[stage - 1]:
                copy.wait_recv()
        for copy in row_copies[stage]:
            copy.start()

    gather_rows(0)
    pieces = [(0, 6), (6, 8), (14, 8), (22, 4), (26, 4)]
    assert sum(n for _, n in pieces) == rims[0]
    far, onward = [[], []], []
    for at, (a, n) in enumerate(pieces + [(slab, REACH)]):
        if a < slab:
            u, source = -a - n, jnp.where(left == 1, quarter - a - n, a)
        else:
            u, source = a, jnp.where(left == 1, 0, quarter - n)
        slot = held.at[at, pl.ds(0, n)]
        for o in range(2):
            far[o].append(
                remote(
                    orb.at[o, pl.ds(source, n)], slot,
                    far_send.at[o, at], far_recv.at[at], relays[o],
                )
            )
        place = jnp.where(left == 1, slab - n - u, u) + rims[0]
        onward.append(
            remote(
                slot, p0.at[pl.ds(place, n)],
                onward_send.at[at], onward_recv.at[at], onward_to,
            )
        )

    part = pot_rim // 8
    pot_far = [
        remote(
            pot.at[pl.ds(jnp.where(left == 1, quarter - pot_rim, 0) + (2 * x + o) * part, part)],
            pot_v.at[pl.ds(placed(-pot_rim, pot_rim) + pot_rim + (2 * x + o) * part, part)],
            pot_send.at[o], pot_recv, partners[o],
        )
        for o in range(2)
    ]
    mine = pot_v.at[pl.ds(placed(-pot_rim, pot_rim) + pot_rim + (2 * x + core) * part, part)]

    @pl.when(long)
    def _():
        for o in range(2):
            pot_far[o].start()
        for at in range(len(pieces)):
            for o in range(2):
                far[o][at].start()

    @pl.when(jnp.logical_not(long))
    def _():
        for o in range(2):
            far[o][5].start()

    near = remote(
        orb.at[1 - core], p0.at[pl.ds(core * quarter + rims[0], quarter)],
        near_send.at[0], near_recv.at[0], sibling,
    )
    near_pot = remote(
        pot, pot_v.at[pl.ds(core * quarter + pot_rim, quarter)],
        near_send.at[1], near_recv.at[1], sibling,
    )
    near.start()
    near_pot.start()

    tell(y_line, plane_sem)

    def apply(level, u, blocks, step=8):
        scale, weight = scalars[level]

        def body(i, c):
            at = placed(u + i * step, step)
            before = None
            if level > 0:
                before = buffers[level - 1][pl.ds(at + rims[level - 1], step)]
            window = buffers[level][pl.ds(at + rims[level] - REACH, step + 2 * REACH)]
            pairs = filtered_block(
                window, pot_v[pl.ds(at + pot_rim, step)], before, scale, weight, lanes, lines[step]
            )
            if level < DEG - 1:
                buffers[level + 1][pl.ds(at + rims[level + 1], step)] = pairs
            else:
                out[pl.ds(2 * (at + rims[DEG]), 2 * step)] = pairs.reshape(2 * step, 8, 128)
            return c

        lax.fori_loop(0, blocks, body, 0)

    row = 2 * band + core

    def spread(u, count):
        start = placed(u, count)
        tiles = 2 * count

        def send(i, c):
            at = lax.rem(i + yx * max(tiles // floor, 1), tiles)
            tile = lax.rem(2 * (base + start) + at + 2 * whole, 2 * whole)
            src = out.at[2 * (start + rims[DEG]) + at]

            @pl.when(tile != own_tile)
            def _():
                peer = {"band": lax.rem(tile, bands), "dom": lax.div(tile, bands)}
                remote(src, recv.at[row], all_send, all_recv, peer).start()

            @pl.when(tile == own_tile)
            def _():
                pltpu.make_async_copy(src, recv.at[row], move_sem.at[3]).start()

            return c

        lax.fori_loop(0, tiles, send, 0)

    def advance(u, n):
        for level in range(DEG):
            apply(level, u + level * REACH, 1, n)
        spread(u + (DEG - 1) * REACH, n)

    pot_far[0].wait_recv()
    passed = [
        remote(mine, mine, pass_send.at[at], pass_recv.at[at], peer)
        for at, peer in enumerate(x_line)
    ]
    for copy in passed:
        copy.start()

    def pass_on(*numbers):
        for at in numbers:
            far[0][at].wait_recv()
            onward[at].start()

    pass_on(5, 0, 1)
    load.wait()
    load_pot.wait()
    own_rows.wait()
    gather_rows(1)
    near.wait_recv()
    near_pot.wait_recv()
    pass_on(2, 3, 4)
    pl.semaphore_wait(plane_sem, len(y_line))
    tell(z_line, all_sem)
    apply(0, 8, 6)
    apply(1, 14, 4)
    apply(1, 42, 1)
    apply(2, 20, 3)
    gather_rows(2)
    pl.semaphore_wait(all_sem, len(z_line))
    spread(20, 24)

    onward[5].wait_recv()
    apply(0, slab - 8, 1)
    apply(1, slab - 14, 1)
    apply(2, slab - 20, 1)
    spread(slab - 20, 8)
    for at, (u, n) in enumerate(((0, 8), (-8, 8), (-16, 8), (-20, 4), (-24, 4))):
        if at == 1:
            for copy in passed:
                copy.wait_recv()
        onward[at].wait_recv()
        advance(u, n)

    @pl.when(long)
    def _():
        for o in range(2):
            pot_far[o].wait_send()
            for at in range(len(pieces)):
                far[o][at].wait_send()

    @pl.when(jnp.logical_not(long))
    def _():
        for o in range(2):
            far[o][5].wait_send()

    for copy in (near, near_pot, *onward, *passed):
        copy.wait_send()
    for copy in row_copies[2]:
        copy.wait_recv()
    for copies in row_copies:
        for copy in copies:
            copy.wait_send()
    pltpu.make_async_copy(out.at[0], recv.at[row], move_sem.at[3]).wait()
    all_but_own = recv.at[pl.ds(0, recv.shape[0] - 1)]
    pltpu.make_async_copy(all_but_own, all_but_own, all_send).wait()
    pltpu.make_async_copy(all_but_own, all_but_own, all_recv).wait()


def rotate_kernel(recv_v, rows_v, out, out_v, sems):
    high, low = two_parts(jnp.concatenate([rows_v[:, 0], rows_v[:, 1]], axis=0).T)
    matrix = jnp.concatenate([high, high, low], axis=1)
    width = 256
    stores = []
    for at in range(0, 8 * 128, width):
        columns = []
        for r in range(at // 128, (at + width) // 128):
            values = jnp.concatenate([recv_v[:, 0, r], recv_v[:, 1, r]], axis=0)
            high, low = two_parts(values)
            columns.append(jnp.concatenate([high, low, high], axis=0))
        out_v[:, pl.ds(at, width)] = jnp.dot(
            matrix, jnp.concatenate(columns, axis=1), preferred_element_type=jnp.float32
        )
        store = pltpu.make_async_copy(
            out_v.at[:, pl.ds(at, width)], out.at[:, pl.ds(at, width)], sems.at[at // width]
        )
        store.start()
        stores.append(store)
    for store in stores:
        store.wait()


def per_device(bands, orbitals, potential, subspace):
    orbs, planes = orbitals.shape[0], orbitals.shape[1]
    orb = orbitals.reshape(orbs, planes, 2, 8, 128)
    pot = potential.reshape(planes, 2, 8, 128)
    f32 = jnp.float32
    dma = pltpu.SemaphoreType.DMA
    anywhere = pl.BlockSpec(memory_space=pl.ANY)
    slab, shift = 2 * planes, 2 * REACH
    recv, rows = pl.pallas_call(
        functools.partial(filter_kernel, bands),
        out_shape=(
            pltpu.VMEM((bands * orbs, 8, 128), f32),
            pltpu.VMEM((4, 4, 4, orbs, 128), f32),
        ),
        in_specs=[anywhere] * 3,
        out_specs=(anywhere,) * 2,
        scratch_shapes=[
            *[
                pltpu.VMEM((slab + 2 * (shift + REACH * (DEG - level)), 2, 8, 128), f32)
                for level in range(DEG)
            ],
            pltpu.VMEM((2 * (slab + 2 * shift), 8, 128), f32),
            pltpu.VMEM((slab + 2 * (shift + REACH * (DEG - 1)), 2, 8, 128), f32),
            pltpu.VMEM((6, 8, 2, 8, 128), f32),
            dma((2,)),
            dma((2,)),
            dma((2, 6)),
            dma((6,)),
            dma((6,)),
            dma((6,)),
            dma((2,)),
            dma,
            dma((7,)),
            dma((7,)),
            dma((4,)),
            dma,
            dma,
            dma((3, 3)),
            dma((3, 3)),
            pltpu.SemaphoreType.REGULAR,
            pltpu.SemaphoreType.REGULAR,
        ],
        compiler_params=pltpu.CompilerParams(
            collective_id=0, has_side_effects=True, vmem_limit_bytes=32 * 2**20
        ),
        name="filter",
    )(*(pltpu.with_memory_space_constraint(a, pltpu.HBM) for a in (orb, pot, subspace)))
    recv, rows = recv.reshape(bands, orbs, 8, 128), rows.reshape(bands, orbs, 128)
    return pl.pallas_call(
        rotate_kernel,
        out_shape=jax.ShapeDtypeStruct((bands * orbs, 1024), f32),
        in_specs=[pl.BlockSpec(memory_space=pltpu.VMEM)] * 2,
        out_specs=anywhere,
        scratch_shapes=[pltpu.VMEM((bands * orbs, 1024), f32), dma((4,))],
        compiler_params=pltpu.CompilerParams(vmem_limit_bytes=32 * 2**20),
        name="rotate",
    )(*(pltpu.with_memory_space_constraint(a, pltpu.VMEM) for a in (recv, rows)))


def solution(mesh):
    in_specs = (P("band", "dom", None, None), P("dom", None, None), P("band", None))
    out_specs = P(None, ("dom", "band"))
    return jax.shard_map(
        functools.partial(per_device, mesh.shape["band"]),
        mesh=mesh,
        in_specs=in_specs,
        out_specs=out_specs,
        check_vma=False,
    )
```

```python
import functools
import math

import jax
import jax.numpy as jnp
from jax import lax
from jax.experimental import pallas as pl
from jax.experimental.pallas import tpu as pltpu
from jax.sharding import PartitionSpec as P

DEG = 3
REACH = 6
MESH = pl.DeviceIdType.MESH

upper_edge = 10.7
lower_edge = 1.5
bottom_edge = -1.0


def stencil_weights():
    factor_square = math.factorial(6) ** 2
    side_weights = []
    for offset in range(1, 7):
        side_weights.append(
            2.0
            * (-1.0) ** (offset + 1)
            * factor_square
            / (offset * offset * math.factorial(6 - offset) * math.factorial(6 + offset))
        )
    center_weight = -2.0 * sum(side_weights)
    return (center_weight, side_weights)


def filter_scalars(pass_count):
    half_width = (upper_edge - lower_edge) / 2.0
    sigma_now = half_width / (bottom_edge - (upper_edge + lower_edge) / 2.0)
    gamma_value = 2.0 / sigma_now
    scalars = [(sigma_now / half_width, 0.0)]
    for pass_index in range(pass_count - 1):
        sigma_next = 1.0 / (gamma_value - sigma_now)
        scalars.append((2.0 * sigma_next / half_width, sigma_now * sigma_next))
        sigma_now = sigma_next
    return scalars


def two_parts(values):
    high = values.astype(jnp.bfloat16)
    return high, (values - high.astype(jnp.float32)).astype(jnp.bfloat16)


def stencil_matrix(size, period, axis):
    rows = lax.broadcasted_iota(jnp.int32, (size, size), 0)
    columns = lax.broadcasted_iota(jnp.int32, (size, size), 1)
    apart = jnp.abs(rows - columns)
    if period < size:
        same = jnp.bitwise_or(rows, period - 1) == jnp.bitwise_or(columns, period - 1)
        apart = jnp.where(same, apart, 0)
    apart = jnp.minimum(apart, period - apart)
    matrix = jnp.zeros((size, size), jnp.float32)
    for k, w in enumerate(stencil_weights()[1], 1):
        matrix = jnp.where(apart == k, jnp.float32(w), matrix)
    high, low = two_parts(matrix)
    return jnp.concatenate([high, high, low], axis=axis)


def filtered_block(window, pot, before, scale, weight, lanes, rows):
    center_weight, side = stencil_weights()
    n = window.shape[0] - 2 * REACH
    mid = window[REACH : REACH + n]
    high, low = two_parts(mid.reshape(n * 16, 128))
    total = jnp.dot(
        jnp.concatenate([high, low, high], axis=1), lanes, preferred_element_type=jnp.float32
    ) + jnp.dot(
        rows, jnp.concatenate([high, low, high], axis=0), preferred_element_type=jnp.float32
    )
    total = total.reshape(n, 2, 8, 128)
    for k in range(1, REACH + 1):
        beside = window[REACH + k : REACH + k + n] + window[REACH - k : REACH - k + n]
        total = total + side[k - 1] * beside
    diag = (-1.5 * center_weight - (upper_edge + lower_edge) / 2.0) * scale
    result = (pot * scale + diag) * mid + (-0.5 * scale) * total
    if before is not None:
        result = result - weight * before
    return result


def filter_kernel(
    bands, orb, pot, sub, recv, rows, p0, p1, p2, out, pot_v,
    near_send, near_recv, far_send, far_recv, pot_send, pot_recv, pass_send, pass_recv,
    move_sem, all_send, all_recv, row_send, row_recv, plane_sem, all_sem,
):
    quarter = orb.shape[1]
    slab, whole = 2 * quarter, 4 * quarter
    band, dom = lax.axis_index("band"), lax.axis_index("dom")
    core, half = lax.rem(dom, 2), lax.div(dom, 2)
    side = 4
    floor = side * side
    zl, x, yx = lax.div(band, floor), lax.rem(band, side), lax.rem(band, floor)
    shift = 2 * REACH
    left = jnp.where(zl < side // 2, 1, 0)
    long = core == left
    base = half * slab
    own_tile = dom * bands + band
    own_plane = lax.div(own_tile, 2)
    scalars = filter_scalars(DEG)
    buffers = (p0, p1, p2)
    rims = tuple(shift + REACH * (DEG - level) for level in range(DEG + 1))
    pot_rim = rims[1]

    def placed(u, count):
        return jnp.where(left == 1, u, slab - count - u)

    load = pltpu.make_async_copy(
        orb.at[core], p0.at[pl.ds(core * quarter + rims[0], quarter)], move_sem.at[0]
    )
    load.start()
    load_pot = pltpu.make_async_copy(
        pot, pot_v.at[pl.ds(core * quarter + pot_rim, quarter)], move_sem.at[1]
    )
    load_pot.start()

    sibling = {"dom": dom + 1 - 2 * core}
    partners = [{"dom": 2 * (1 - half) + k} for k in range(2)]

    def chip_along(shift):
        there = lax.rem(half * side + zl + shift, 2 * side)
        return {
            "band": lax.rem(there, side) * floor + yx,
            "dom": lax.div(there, side) * 2 + core,
        }

    x_line = [
        {"band": band - x + lax.rem(x + dx, side), "dom": dom if dk == 0 else dom + 1 - 2 * core}
        for dx in range(side)
        for dk in range(2)
    ][1:]
    y = lax.div(yx, side)
    y_line = [{"band": band + side * (lax.rem(y + dy, side) - y)} for dy in range(1, side)]
    z_line = [chip_along(dz) for dz in range(1, 2 * side)]
    other_partner = {"dom": 2 * (1 - half) + 1 - core}
    barrier = pltpu.get_barrier_semaphore()
    entered = (*z_line, other_partner, *x_line, *y_line)

    def tell(peers, semaphore):
        for peer in peers:
            pl.semaphore_signal(semaphore, inc=1, device_id=peer, device_id_type=MESH)

    tell(entered, barrier)
    lanes = stencil_matrix(128, 128, 0)
    lines = {n: stencil_matrix(16 * n, 16, 1) for n in (4, 8)}
    pl.semaphore_wait(barrier, len(entered))

    def remote(src, dst, send_sem, recv_sem, peer):
        return pltpu.make_async_remote_copy(
            src_ref=src, dst_ref=dst, send_sem=send_sem, recv_sem=recv_sem,
            device_id=peer, device_id_type=MESH,
        )

    own_rows = pltpu.make_async_copy(sub, rows.at[zl, y, x], move_sem.at[2])
    own_rows.start()
    row_lines = [
        (rows.at[zl, y, x], [{"band": lax.rem(band + d * floor, bands)} for d in range(1, side)]),
        (rows.at[:, y, x], y_line),
        (rows.at[:, :, x], [{"band": band - x + lax.rem(x + d, side)} for d in range(1, side)]),
    ]
    row_copies = [
        [
            remote(
                sub if stage == 0 else part_rows, part_rows,
                row_send.at[stage, at], row_recv.at[stage, at], peer,
            )
            for at, peer in enumerate(peers)
        ]
        for stage, (part_rows, peers) in enumerate(row_lines)
    ]

    def gather_rows(stage):
        if stage > 0:
            for copy in row_copies[stage - 1]:
                copy.wait_recv()
        for copy in row_copies[stage]:
            copy.start()

    gather_rows(0)
    pieces = [(0, 6), (6, 8), (14, 8), (22, 4), (26, 4)]
    assert sum(n for _, n in pieces) == rims[0]
    far = []
    for o in range(2):
        group = []
        for at, (a, n) in enumerate(pieces):
            group.append(
                remote(
                    orb.at[o, pl.ds(jnp.where(left == 1, quarter - a - n, a), n)],
                    p0.at[pl.ds(placed(-a - n, n) + rims[0], n)],
                    far_send.at[o, at], far_recv.at[at], partners[o],
                )
            )
        n = REACH
        group.append(
            remote(
                orb.at[o, pl.ds(jnp.where(left == 1, 0, quarter - n), n)],
                p0.at[pl.ds(placed(slab, n) + rims[0], n)],
                far_send.at[o, 5], far_recv.at[5], partners[o],
            )
        )
        far.append(group)
    part = pot_rim // 8
    pot_far = [
        remote(
            pot.at[pl.ds(jnp.where(left == 1, quarter - pot_rim, 0) + (2 * x + o) * part, part)],
            pot_v.at[pl.ds(placed(-pot_rim, pot_rim) + pot_rim + (2 * x + o) * part, part)],
            pot_send.at[o], pot_recv, partners[o],
        )
        for o in range(2)
    ]
    mine = pot_v.at[pl.ds(placed(-pot_rim, pot_rim) + pot_rim + (2 * x + core) * part, part)]

    @pl.when(long)
    def _():
        for o in range(2):
            pot_far[o].start()
        for at in range(3):
            for o in range(2):
                far[o][at].start()

    def send_last():
        for at in range(3, len(pieces)):
            for o in range(2):
                far[o][at].start()

    inner = (zl != 0) & (zl != side - 1)
    pl.when(long & inner)(send_last)

    @pl.when(jnp.logical_not(long))
    def _():
        for o in range(2):
            far[o][5].start()

    near = remote(
        orb.at[1 - core], p0.at[pl.ds(core * quarter + rims[0], quarter)],
        near_send.at[0], near_recv.at[0], sibling,
    )
    near_pot = remote(
        pot, pot_v.at[pl.ds(core * quarter + pot_rim, quarter)],
        near_send.at[1], near_recv.at[1], sibling,
    )
    near.start()
    near_pot.start()

    tell(y_line, plane_sem)

    def apply(level, u, blocks, step=8):
        scale, weight = scalars[level]

        def body(i, c):
            at = placed(u + i * step, step)
            before = None
            if level > 0:
                before = buffers[level - 1][pl.ds(at + rims[level - 1], step)]
            window = buffers[level][pl.ds(at + rims[level] - REACH, step + 2 * REACH)]
            pairs = filtered_block(
                window, pot_v[pl.ds(at + pot_rim, step)], before, scale, weight, lanes, lines[step]
            )
            if level < DEG - 1:
                buffers[level + 1][pl.ds(at + rims[level + 1], step)] = pairs
            else:
                out[pl.ds(2 * (at + rims[DEG]), 2 * step)] = pairs.reshape(2 * step, 8, 128)
            return c

        lax.fori_loop(0, blocks, body, 0)

    row = 2 * band + core

    def spread(u, count):
        start = placed(u, count)
        tiles = 2 * count

        def send(i, c):
            at = lax.rem(i + yx * max(tiles // floor, 1), tiles)
            tile = lax.rem(2 * (base + start) + at + 2 * whole, 2 * whole)
            src = out.at[2 * (start + rims[DEG]) + at]

            @pl.when(tile != own_tile)
            def _():
                peer = {"band": lax.rem(tile, bands), "dom": lax.div(tile, bands)}
                remote(src, recv.at[row], all_send, all_recv, peer).start()

            @pl.when(tile == own_tile)
            def _():
                pltpu.make_async_copy(src, recv.at[row], move_sem.at[3]).start()

            return c

        lax.fori_loop(0, tiles, send, 0)

    def advance(u, n):
        for level in range(DEG):
            apply(level, u + level * REACH, 1, n)
        spread(u + (DEG - 1) * REACH, n)

    pot_far[0].wait_recv()
    passed = [
        remote(mine, mine, pass_send.at[at], pass_recv.at[at], peer)
        for at, peer in enumerate(x_line)
    ]
    for copy in passed:
        copy.start()

    load.wait()
    load_pot.wait()
    own_rows.wait()
    gather_rows(1)
    near.wait_recv()
    near_pot.wait_recv()
    pl.when(long & jnp.logical_not(inner))(send_last)
    pl.semaphore_wait(plane_sem, len(y_line))
    tell(z_line, all_sem)
    apply(0, 8, 6)
    apply(1, 14, 4)
    apply(1, 42, 1)
    apply(2, 20, 3)
    gather_rows(2)
    pl.semaphore_wait(all_sem, len(z_line))
    spread(20, 24)

    far[0][5].wait_recv()
    apply(0, slab - 8, 1)
    apply(1, slab - 14, 1)
    apply(2, slab - 20, 1)
    spread(slab - 20, 8)
    for at, (u, n) in enumerate(((0, 8), (-8, 8), (-16, 8), (-20, 4), (-24, 4))):
        if at == 1:
            for copy in passed:
                copy.wait_recv()
        far[0][at].wait_recv()
        advance(u, n)

    @pl.when(long)
    def _():
        for o in range(2):
            pot_far[o].wait_send()
            for at in range(len(pieces)):
                far[o][at].wait_send()

    @pl.when(jnp.logical_not(long))
    def _():
        for o in range(2):
            far[o][5].wait_send()

    for copy in (near, near_pot, *passed):
        copy.wait_send()
    for copy in row_copies[2]:
        copy.wait_recv()
    for copies in row_copies:
        for copy in copies:
            copy.wait_send()
    pltpu.make_async_copy(out.at[0], recv.at[row], move_sem.at[3]).wait()
    all_but_own = recv.at[pl.ds(0, recv.shape[0] - 1)]
    pltpu.make_async_copy(all_but_own, all_but_own, all_send).wait()
    pltpu.make_async_copy(all_but_own, all_but_own, all_recv).wait()


def rotate_kernel(recv_v, rows_v, out, out_v, sems):
    high, low = two_parts(jnp.concatenate([rows_v[:, 0], rows_v[:, 1]], axis=0).T)
    matrix = jnp.concatenate([high, high, low], axis=1)
    width = 256
    stores = []
    for at in range(0, 8 * 128, width):
        columns = []
        for r in range(at // 128, (at + width) // 128):
            values = jnp.concatenate([recv_v[:, 0, r], recv_v[:, 1, r]], axis=0)
            high, low = two_parts(values)
            columns.append(jnp.concatenate([high, low, high], axis=0))
        out_v[:, pl.ds(at, width)] = jnp.dot(
            matrix, jnp.concatenate(columns, axis=1), preferred_element_type=jnp.float32
        )
        store = pltpu.make_async_copy(
            out_v.at[:, pl.ds(at, width)], out.at[:, pl.ds(at, width)], sems.at[at // width]
        )
        store.start()
        stores.append(store)
    for store in stores:
        store.wait()


def per_device(bands, orbitals, potential, subspace):
    orbs, planes = orbitals.shape[0], orbitals.shape[1]
    orb = orbitals.reshape(orbs, planes, 2, 8, 128)
    pot = potential.reshape(planes, 2, 8, 128)
    f32 = jnp.float32
    dma = pltpu.SemaphoreType.DMA
    anywhere = pl.BlockSpec(memory_space=pl.ANY)
    slab, shift = 2 * planes, 2 * REACH
    recv, rows = pl.pallas_call(
        functools.partial(filter_kernel, bands),
        out_shape=(
            pltpu.VMEM((bands * orbs, 8, 128), f32),
            pltpu.VMEM((4, 4, 4, orbs, 128), f32),
        ),
        in_specs=[anywhere] * 3,
        out_specs=(anywhere,) * 2,
        scratch_shapes=[
            *[
                pltpu.VMEM((slab + 2 * (shift + REACH * (DEG - level)), 2, 8, 128), f32)
                for level in range(DEG)
            ],
            pltpu.VMEM((2 * (slab + 2 * shift), 8, 128), f32),
            pltpu.VMEM((slab + 2 * (shift + REACH * (DEG - 1)), 2, 8, 128), f32),
            dma((2,)),
            dma((2,)),
            dma((2, 6)),
            dma((6,)),
            dma((2,)),
            dma,
            dma((7,)),
            dma((7,)),
            dma((4,)),
            dma,
            dma,
            dma((3, 3)),
            dma((3, 3)),
            pltpu.SemaphoreType.REGULAR,
            pltpu.SemaphoreType.REGULAR,
        ],
        compiler_params=pltpu.CompilerParams(
            collective_id=0, has_side_effects=True, vmem_limit_bytes=32 * 2**20
        ),
        name="filter",
    )(*(pltpu.with_memory_space_constraint(a, pltpu.HBM) for a in (orb, pot, subspace)))
    recv, rows = recv.reshape(bands, orbs, 8, 128), rows.reshape(bands, orbs, 128)
    return pl.pallas_call(
        rotate_kernel,
        out_shape=jax.ShapeDtypeStruct((bands * orbs, 1024), f32),
        in_specs=[pl.BlockSpec(memory_space=pltpu.VMEM)] * 2,
        out_specs=anywhere,
        scratch_shapes=[pltpu.VMEM((bands * orbs, 1024), f32), dma((4,))],
        compiler_params=pltpu.CompilerParams(vmem_limit_bytes=32 * 2**20),
        name="rotate",
    )(*(pltpu.with_memory_space_constraint(a, pltpu.VMEM) for a in (recv, rows)))


def solution(mesh):
    in_specs = (P("band", "dom", None, None), P("dom", None, None), P("band", None))
    out_specs = P(None, ("dom", "band"))
    return jax.shard_map(
        functools.partial(per_device, mesh.shape["band"]),
        mesh=mesh,
        in_specs=in_specs,
        out_specs=out_specs,
        check_vma=False,
    )
```

```python
import functools
import math

import jax
import jax.numpy as jnp
from jax import lax
from jax.experimental import pallas as pl
from jax.experimental.pallas import tpu as pltpu
from jax.sharding import PartitionSpec as P

DEG = 3
REACH = 6
MESH = pl.DeviceIdType.MESH

upper_edge = 10.7
lower_edge = 1.5
bottom_edge = -1.0


def stencil_weights():
    factor_square = math.factorial(6) ** 2
    side_weights = []
    for offset in range(1, 7):
        side_weights.append(
            2.0
            * (-1.0) ** (offset + 1)
            * factor_square
            / (offset * offset * math.factorial(6 - offset) * math.factorial(6 + offset))
        )
    center_weight = -2.0 * sum(side_weights)
    return (center_weight, side_weights)


def filter_scalars(pass_count):
    half_width = (upper_edge - lower_edge) / 2.0
    sigma_now = half_width / (bottom_edge - (upper_edge + lower_edge) / 2.0)
    gamma_value = 2.0 / sigma_now
    scalars = [(sigma_now / half_width, 0.0)]
    for pass_index in range(pass_count - 1):
        sigma_next = 1.0 / (gamma_value - sigma_now)
        scalars.append((2.0 * sigma_next / half_width, sigma_now * sigma_next))
        sigma_now = sigma_next
    return scalars


def two_parts(values):
    high = values.astype(jnp.bfloat16)
    return high, (values - high.astype(jnp.float32)).astype(jnp.bfloat16)


def stencil_matrix(size, period, axis):
    rows = lax.broadcasted_iota(jnp.int32, (size, size), 0)
    columns = lax.broadcasted_iota(jnp.int32, (size, size), 1)
    apart = jnp.abs(rows - columns)
    if period < size:
        same = jnp.bitwise_or(rows, period - 1) == jnp.bitwise_or(columns, period - 1)
        apart = jnp.where(same, apart, 0)
    apart = jnp.minimum(apart, period - apart)
    matrix = jnp.zeros((size, size), jnp.float32)
    for k, w in enumerate(stencil_weights()[1], 1):
        matrix = jnp.where(apart == k, jnp.float32(w), matrix)
    high, low = two_parts(matrix)
    return jnp.concatenate([high, high, low], axis=axis)


def filtered_block(window, pot, before, scale, weight, lanes, rows):
    center_weight, side = stencil_weights()
    n = window.shape[0] - 2 * REACH
    mid = window[REACH : REACH + n]
    high, low = two_parts(mid.reshape(n * 16, 128))
    total = jnp.dot(
        jnp.concatenate([high, low, high], axis=1), lanes, preferred_element_type=jnp.float32
    ) + jnp.dot(
        rows, jnp.concatenate([high, low, high], axis=0), preferred_element_type=jnp.float32
    )
    total = total.reshape(n, 2, 8, 128)
    for k in range(1, REACH + 1):
        beside = window[REACH + k : REACH + k + n] + window[REACH - k : REACH - k + n]
        total = total + side[k - 1] * beside
    diag = (-1.5 * center_weight - (upper_edge + lower_edge) / 2.0) * scale
    result = (pot * scale + diag) * mid + (-0.5 * scale) * total
    if before is not None:
        result = result - weight * before
    return result


def filter_kernel(
    bands, orb, pot, sub, recv, rows, p0, p1, p2, out, pot_v,
    near_send, near_recv, far_send, far_recv, pot_send, pot_recv, pass_send, pass_recv,
    move_sem, all_send, all_recv, row_send, row_recv, plane_sem, all_sem,
):
    quarter = orb.shape[1]
    slab, whole = 2 * quarter, 4 * quarter
    band, dom = lax.axis_index("band"), lax.axis_index("dom")
    core, half = lax.rem(dom, 2), lax.div(dom, 2)
    side = 4
    floor = side * side
    zl, x, yx = lax.div(band, floor), lax.rem(band, side), lax.rem(band, floor)
    shift = 2 * REACH
    left = jnp.where(zl < side // 2, 1, 0)
    long = core == left
    base = half * slab
    own_tile = dom * bands + band
    own_plane = lax.div(own_tile, 2)
    scalars = filter_scalars(DEG)
    buffers = (p0, p1, p2)
    rims = tuple(shift + REACH * (DEG - level) for level in range(DEG + 1))
    pot_rim = rims[1]

    def placed(u, count):
        return jnp.where(left == 1, u, slab - count - u)

    load = pltpu.make_async_copy(
        orb.at[core], p0.at[pl.ds(core * quarter + rims[0], quarter)], move_sem.at[0]
    )
    load.start()
    load_pot = pltpu.make_async_copy(
        pot, pot_v.at[pl.ds(core * quarter + pot_rim, quarter)], move_sem.at[1]
    )
    load_pot.start()

    sibling = {"dom": dom + 1 - 2 * core}
    partners = [{"dom": 2 * (1 - half) + k} for k in range(2)]

    def chip_along(shift):
        there = lax.rem(half * side + zl + shift, 2 * side)
        return {
            "band": lax.rem(there, side) * floor + yx,
            "dom": lax.div(there, side) * 2 + core,
        }

    x_line = [
        {"band": band - x + lax.rem(x + dx, side), "dom": dom if dk == 0 else dom + 1 - 2 * core}
        for dx in range(side)
        for dk in range(2)
    ][1:]
    y = lax.div(yx, side)
    y_line = [{"band": band + side * (lax.rem(y + dy, side) - y)} for dy in range(1, side)]
    z_line = [chip_along(dz) for dz in range(1, 2 * side)]
    other_partner = {"dom": 2 * (1 - half) + 1 - core}
    barrier = pltpu.get_barrier_semaphore()
    entered = (*z_line, other_partner, *x_line, *y_line)

    def tell(peers, semaphore):
        for peer in peers:
            pl.semaphore_signal(semaphore, inc=1, device_id=peer, device_id_type=MESH)

    tell(entered, barrier)
    lanes = stencil_matrix(128, 128, 0)
    lines = {n: stencil_matrix(16 * n, 16, 1) for n in (4, 8)}
    pl.semaphore_wait(barrier, len(entered))

    def remote(src, dst, send_sem, recv_sem, peer):
        return pltpu.make_async_remote_copy(
            src_ref=src, dst_ref=dst, send_sem=send_sem, recv_sem=recv_sem,
            device_id=peer, device_id_type=MESH,
        )

    own_rows = pltpu.make_async_copy(sub, rows.at[zl, y, x], move_sem.at[2])
    own_rows.start()
    row_lines = [
        (rows.at[zl, y, x], [{"band": lax.rem(band + d * floor, bands)} for d in range(1, side)]),
        (rows.at[:, y, x], y_line),
        (rows.at[:, :, x], [{"band": band - x + lax.rem(x + d, side)} for d in range(1, side)]),
    ]
    row_copies = [
        [
            remote(
                sub if stage == 0 else part_rows, part_rows,
                row_send.at[stage, at], row_recv.at[stage, at], peer,
            )
            for at, peer in enumerate(peers)
        ]
        for stage, (part_rows, peers) in enumerate(row_lines)
    ]

    def gather_rows(stage):
        if stage > 0:
            for copy in row_copies[stage - 1]:
                copy.wait_recv()
        for copy in row_copies[stage]:
            copy.start()

    gather_rows(0)
    pieces = [(0, 6), (6, 8), (14, 8), (22, 4), (26, 4)]
    assert sum(n for _, n in pieces) == rims[0]
    far = []
    for o in range(2):
        group = []
        for at, (a, n) in enumerate(pieces):
            group.append(
                remote(
                    orb.at[o, pl.ds(jnp.where(left == 1, quarter - a - n, a), n)],
                    p0.at[pl.ds(placed(-a - n, n) + rims[0], n)],
                    far_send.at[o, at], far_recv.at[at], partners[o],
                )
            )
        n = REACH
        group.append(
            remote(
                orb.at[o, pl.ds(jnp.where(left == 1, 0, quarter - n), n)],
                p0.at[pl.ds(placed(slab, n) + rims[0], n)],
                far_send.at[o, 5], far_recv.at[5], partners[o],
            )
        )
        far.append(group)
    part = pot_rim // 8
    pot_far = [
        remote(
            pot.at[pl.ds(jnp.where(left == 1, quarter - pot_rim, 0) + (2 * x + o) * part, part)],
            pot_v.at[pl.ds(placed(-pot_rim, pot_rim) + pot_rim + (2 * x + o) * part, part)],
            pot_send.at[o], pot_recv, partners[o],
        )
        for o in range(2)
    ]
    mine = pot_v.at[pl.ds(placed(-pot_rim, pot_rim) + pot_rim + (2 * x + core) * part, part)]

    @pl.when(long)
    def _():
        for o in range(2):
            pot_far[o].start()
        for at in range(len(pieces)):
            for o in range(2):
                far[o][at].start()

    @pl.when(jnp.logical_not(long))
    def _():
        for o in range(2):
            far[o][5].start()

    near = remote(
        orb.at[1 - core], p0.at[pl.ds(core * quarter + rims[0], quarter)],
        near_send.at[0], near_recv.at[0], sibling,
    )
    near_pot = remote(
        pot, pot_v.at[pl.ds(core * quarter + pot_rim, quarter)],
        near_send.at[1], near_recv.at[1], sibling,
    )
    near.start()
    near_pot.start()

    tell(y_line, plane_sem)

    def apply(level, u, blocks, step=8):
        scale, weight = scalars[level]

        def body(i, c):
            at = placed(u + i * step, step)
            before = None
            if level > 0:
                before = buffers[level - 1][pl.ds(at + rims[level - 1], step)]
            window = buffers[level][pl.ds(at + rims[level] - REACH, step + 2 * REACH)]
            pairs = filtered_block(
                window, pot_v[pl.ds(at + pot_rim, step)], before, scale, weight, lanes, lines[step]
            )
            if level < DEG - 1:
                buffers[level + 1][pl.ds(at + rims[level + 1], step)] = pairs
            else:
                out[pl.ds(2 * (at + rims[DEG]), 2 * step)] = pairs.reshape(2 * step, 8, 128)
            return c

        lax.fori_loop(0, blocks, body, 0, unroll=min(blocks, 3))

    row = 2 * band + core
    offsets = [lax.rem(i + yx, 8) for i in range(8)]

    def spread(u, count):
        start = placed(u, count)
        groups = count // 4

        def send_group(i, c):
            plane = start + 4 * lax.rem(i + yx, groups)
            tile = lax.rem(2 * (base + plane) + 2 * whole, 2 * whole)
            there, first = lax.div(tile, bands), lax.rem(tile, bands)
            place = 2 * (plane + rims[DEG])
            for offset in offsets:
                src, peer = out.at[place + offset], first + offset

                @pl.when((peer != band) | (there != dom))
                def _():
                    remote(
                        src, recv.at[row], all_send, all_recv, {"band": peer, "dom": there}
                    ).start()

                @pl.when((peer == band) & (there == dom))
                def _():
                    pltpu.make_async_copy(src, recv.at[row], move_sem.at[3]).start()

            return c

        lax.fori_loop(0, groups, send_group, 0)

    def advance(u, n):
        for level in range(DEG):
            apply(level, u + level * REACH, 1, n)
        spread(u + (DEG - 1) * REACH, n)

    pot_far[0].wait_recv()
    passed = [
        remote(mine, mine, pass_send.at[at], pass_recv.at[at], peer)
        for at, peer in enumerate(x_line)
    ]
    for copy in passed:
        copy.start()

    load.wait()
    load_pot.wait()
    own_rows.wait()
    gather_rows(1)

    def two_blocks(first):
        apply(0, jnp.where(left == 1, first, slab - 16 - first), 2)

    two_blocks(core * quarter + 8)
    near.wait_recv()
    near_pot.wait_recv()
    pl.semaphore_wait(plane_sem, len(y_line))
    tell(z_line, all_sem)
    two_blocks((1 - core) * quarter + 8)
    apply(0, 24, 2)
    apply(1, 14, 4)
    apply(1, 42, 1)
    apply(2, 20, 3)
    gather_rows(2)
    pl.semaphore_wait(all_sem, len(z_line))
    spread(20, 24)

    far[0][5].wait_recv()
    apply(0, slab - 8, 1)
    apply(1, slab - 14, 1)
    apply(2, slab - 20, 1)
    spread(slab - 20, 8)
    for at, (u, n) in enumerate(((0, 8), (-8, 8), (-16, 8), (-20, 4), (-24, 4))):
        if at == 1:
            for copy in passed:
                copy.wait_recv()
        far[0][at].wait_recv()
        advance(u, n)

    @pl.when(long)
    def _():
        for o in range(2):
            pot_far[o].wait_send()
            for at in range(len(pieces)):
                far[o][at].wait_send()

    @pl.when(jnp.logical_not(long))
    def _():
        for o in range(2):
            far[o][5].wait_send()

    for copy in (near, near_pot, *passed):
        copy.wait_send()
    for copy in row_copies[2]:
        copy.wait_recv()
    for copies in row_copies:
        for copy in copies:
            copy.wait_send()
    pltpu.make_async_copy(out.at[0], recv.at[row], move_sem.at[3]).wait()
    all_but_own = recv.at[pl.ds(0, recv.shape[0] - 1)]
    pltpu.make_async_copy(all_but_own, all_but_own, all_send).wait()
    pltpu.make_async_copy(all_but_own, all_but_own, all_recv).wait()


def rotate_kernel(recv_v, rows_v, out, out_v, sems):
    high, low = two_parts(jnp.concatenate([rows_v[:, 0], rows_v[:, 1]], axis=0).T)
    matrix = jnp.concatenate([high, high, low], axis=1)
    width = 256
    stores = []
    for at in range(0, 8 * 128, width):
        columns = []
        for r in range(at // 128, (at + width) // 128):
            values = jnp.concatenate([recv_v[:, 0, r], recv_v[:, 1, r]], axis=0)
            high, low = two_parts(values)
            columns.append(jnp.concatenate([high, low, high], axis=0))
        out_v[:, pl.ds(at, width)] = jnp.dot(
            matrix, jnp.concatenate(columns, axis=1), preferred_element_type=jnp.float32
        )
        store = pltpu.make_async_copy(
            out_v.at[:, pl.ds(at, width)], out.at[:, pl.ds(at, width)], sems.at[at // width]
        )
        store.start()
        stores.append(store)
    for store in stores:
        store.wait()


def per_device(bands, orbitals, potential, subspace):
    orbs, planes = orbitals.shape[0], orbitals.shape[1]
    orb = orbitals.reshape(orbs, planes, 2, 8, 128)
    pot = potential.reshape(planes, 2, 8, 128)
    f32 = jnp.float32
    dma = pltpu.SemaphoreType.DMA
    anywhere = pl.BlockSpec(memory_space=pl.ANY)
    slab, shift = 2 * planes, 2 * REACH
    recv, rows = pl.pallas_call(
        functools.partial(filter_kernel, bands),
        out_shape=(
            pltpu.VMEM((bands * orbs, 8, 128), f32),
            pltpu.VMEM((4, 4, 4, orbs, 128), f32),
        ),
        in_specs=[anywhere] * 3,
        out_specs=(anywhere,) * 2,
        scratch_shapes=[
            *[
                pltpu.VMEM((slab + 2 * (shift + REACH * (DEG - level)), 2, 8, 128), f32)
                for level in range(DEG)
            ],
            pltpu.VMEM((2 * (slab + 2 * shift), 8, 128), f32),
            pltpu.VMEM((slab + 2 * (shift + REACH * (DEG - 1)), 2, 8, 128), f32),
            dma((2,)),
            dma((2,)),
            dma((2, 6)),
            dma((6,)),
            dma((2,)),
            dma,
            dma((7,)),
            dma((7,)),
            dma((4,)),
            dma,
            dma,
            dma((3, 3)),
            dma((3, 3)),
            pltpu.SemaphoreType.REGULAR,
            pltpu.SemaphoreType.REGULAR,
        ],
        compiler_params=pltpu.CompilerParams(
            collective_id=0, has_side_effects=True, vmem_limit_bytes=32 * 2**20
        ),
        name="filter",
    )(*(pltpu.with_memory_space_constraint(a, pltpu.HBM) for a in (orb, pot, subspace)))
    recv, rows = recv.reshape(bands, orbs, 8, 128), rows.reshape(bands, orbs, 128)
    return pl.pallas_call(
        rotate_kernel,
        out_shape=jax.ShapeDtypeStruct((bands * orbs, 1024), f32),
        in_specs=[pl.BlockSpec(memory_space=pltpu.VMEM)] * 2,
        out_specs=anywhere,
        scratch_shapes=[pltpu.VMEM((bands * orbs, 1024), f32), dma((4,))],
        compiler_params=pltpu.CompilerParams(vmem_limit_bytes=32 * 2**20),
        name="rotate",
    )(*(pltpu.with_memory_space_constraint(a, pltpu.VMEM) for a in (recv, rows)))


def solution(mesh):
    in_specs = (P("band", "dom", None, None), P("dom", None, None), P("band", None))
    out_specs = P(None, ("dom", "band"))
    return jax.shard_map(
        functools.partial(per_device, mesh.shape["band"]),
        mesh=mesh,
        in_specs=in_specs,
        out_specs=out_specs,
        check_vma=False,
    )
```

```python
import functools
import math

import jax
import jax.numpy as jnp
from jax import lax
from jax.experimental import pallas as pl
from jax.experimental.pallas import tpu as pltpu
from jax.sharding import PartitionSpec as P

DEG = 3
REACH = 6
MESH = pl.DeviceIdType.MESH

upper_edge = 10.7
lower_edge = 1.5
bottom_edge = -1.0


def stencil_weights():
    factor_square = math.factorial(6) ** 2
    side_weights = []
    for offset in range(1, 7):
        side_weights.append(
            2.0
            * (-1.0) ** (offset + 1)
            * factor_square
            / (offset * offset * math.factorial(6 - offset) * math.factorial(6 + offset))
        )
    center_weight = -2.0 * sum(side_weights)
    return (center_weight, side_weights)


def filter_scalars(pass_count):
    half_width = (upper_edge - lower_edge) / 2.0
    sigma_now = half_width / (bottom_edge - (upper_edge + lower_edge) / 2.0)
    gamma_value = 2.0 / sigma_now
    scalars = [(sigma_now / half_width, 0.0)]
    for pass_index in range(pass_count - 1):
        sigma_next = 1.0 / (gamma_value - sigma_now)
        scalars.append((2.0 * sigma_next / half_width, sigma_now * sigma_next))
        sigma_now = sigma_next
    return scalars


def two_parts(values):
    high = values.astype(jnp.bfloat16)
    return high, (values - high.astype(jnp.float32)).astype(jnp.bfloat16)


def stencil_matrix(size, period, axis):
    rows = lax.broadcasted_iota(jnp.int32, (size, size), 0)
    columns = lax.broadcasted_iota(jnp.int32, (size, size), 1)
    apart = jnp.abs(rows - columns)
    if period < size:
        same = jnp.bitwise_or(rows, period - 1) == jnp.bitwise_or(columns, period - 1)
        apart = jnp.where(same, apart, 0)
    apart = jnp.minimum(apart, period - apart)
    matrix = jnp.zeros((size, size), jnp.float32)
    for k, w in enumerate(stencil_weights()[1], 1):
        matrix = jnp.where(apart == k, jnp.float32(w), matrix)
    high, low = two_parts(matrix)
    return jnp.concatenate([high, high, low], axis=axis)


def filtered_block(window, pot, before, scale, weight, lanes, rows):
    center_weight, side = stencil_weights()
    n = window.shape[0] - 2 * REACH
    mid = window[REACH : REACH + n]
    high, low = two_parts(mid.reshape(n * 16, 128))
    total = jnp.dot(
        jnp.concatenate([high, low, high], axis=1), lanes, preferred_element_type=jnp.float32
    ) + jnp.dot(
        rows, jnp.concatenate([high, low, high], axis=0), preferred_element_type=jnp.float32
    )
    total = total.reshape(n, 2, 8, 128)
    for k in range(1, REACH + 1):
        beside = window[REACH + k : REACH + k + n] + window[REACH - k : REACH - k + n]
        total = total + side[k - 1] * beside
    diag = (-1.5 * center_weight - (upper_edge + lower_edge) / 2.0) * scale
    result = (pot * scale + diag) * mid + (-0.5 * scale) * total
    if before is not None:
        result = result - weight * before
    return result


def filter_kernel(
    bands, orb, pot, sub, recv, rows, p0, p1, p2, out, pot_v,
    near_send, near_recv, far_send, far_recv, pot_send, pot_recv, pass_send, pass_recv,
    move_sem, all_send, all_recv, row_send, row_recv, plane_sem, all_sem,
):
    quarter = orb.shape[1]
    slab, whole = 2 * quarter, 4 * quarter
    band, dom = lax.axis_index("band"), lax.axis_index("dom")
    core, half = lax.rem(dom, 2), lax.div(dom, 2)
    side = 4
    floor = side * side
    zl, x, yx = lax.div(band, floor), lax.rem(band, side), lax.rem(band, floor)
    shift = 2 * REACH
    left = jnp.where(zl < side // 2, 1, 0)
    long = core == left
    base = half * slab
    own_tile = dom * bands + band
    own_plane = lax.div(own_tile, 2)
    scalars = filter_scalars(DEG)
    buffers = (p0, p1, p2)
    rims = tuple(shift + REACH * (DEG - level) for level in range(DEG + 1))
    pot_rim = rims[1]

    def placed(u, count):
        return jnp.where(left == 1, u, slab - count - u)

    load = pltpu.make_async_copy(
        orb.at[core], p0.at[pl.ds(core * quarter + rims[0], quarter)], move_sem.at[0]
    )
    load.start()
    load_pot = pltpu.make_async_copy(
        pot, pot_v.at[pl.ds(core * quarter + pot_rim, quarter)], move_sem.at[1]
    )
    load_pot.start()

    sibling = {"dom": dom + 1 - 2 * core}
    partners = [{"dom": 2 * (1 - half) + k} for k in range(2)]

    def chip_along(shift):
        there = lax.rem(half * side + zl + shift, 2 * side)
        return {
            "band": lax.rem(there, side) * floor + yx,
            "dom": lax.div(there, side) * 2 + core,
        }

    x_line = [
        {"band": band - x + lax.rem(x + dx, side), "dom": dom if dk == 0 else dom + 1 - 2 * core}
        for dx in range(side)
        for dk in range(2)
    ][1:]
    y = lax.div(yx, side)
    y_line = [{"band": band + side * (lax.rem(y + dy, side) - y)} for dy in range(1, side)]
    z_line = [chip_along(dz) for dz in range(1, 2 * side)]
    other_partner = {"dom": 2 * (1 - half) + 1 - core}
    barrier = pltpu.get_barrier_semaphore()
    entered = (*z_line, other_partner, *x_line, *y_line)

    def tell(peers, semaphore):
        for peer in peers:
            pl.semaphore_signal(semaphore, inc=1, device_id=peer, device_id_type=MESH)

    tell(entered, barrier)
    lanes = stencil_matrix(128, 128, 0)
    lines = {n: stencil_matrix(16 * n, 16, 1) for n in (4, 8)}
    pl.semaphore_wait(barrier, len(entered))

    def remote(src, dst, send_sem, recv_sem, peer):
        return pltpu.make_async_remote_copy(
            src_ref=src, dst_ref=dst, send_sem=send_sem, recv_sem=recv_sem,
            device_id=peer, device_id_type=MESH,
        )

    own_rows = pltpu.make_async_copy(sub, rows.at[zl, y, x], move_sem.at[2])
    own_rows.start()
    row_lines = [
        (rows.at[zl, y, x], [{"band": lax.rem(band + d * floor, bands)} for d in range(1, side)]),
        (rows.at[:, y, x], y_line),
        (rows.at[:, :, x], [{"band": band - x + lax.rem(x + d, side)} for d in range(1, side)]),
    ]
    row_copies = [
        [
            remote(
                sub if stage == 0 else part_rows, part_rows,
                row_send.at[stage, at], row_recv.at[stage, at], peer,
            )
            for at, peer in enumerate(peers)
        ]
        for stage, (part_rows, peers) in enumerate(row_lines)
    ]

    def gather_rows(stage):
        if stage > 0:
            for copy in row_copies[stage - 1]:
                copy.wait_recv()
        for copy in row_copies[stage]:
            copy.start()

    gather_rows(0)
    pieces = [(0, 6), (6, 8), (14, 8), (22, 4), (26, 4)]
    assert sum(n for _, n in pieces) == rims[0]
    far = []
    for o in range(2):
        group = []
        for at, (a, n) in enumerate(pieces):
            group.append(
                remote(
                    orb.at[o, pl.ds(jnp.where(left == 1, quarter - a - n, a), n)],
                    p0.at[pl.ds(placed(-a - n, n) + rims[0], n)],
                    far_send.at[o, at], far_recv.at[at], partners[o],
                )
            )
        n = REACH
        group.append(
            remote(
                orb.at[o, pl.ds(jnp.where(left == 1, 0, quarter - n), n)],
                p0.at[pl.ds(placed(slab, n) + rims[0], n)],
                far_send.at[o, 5], far_recv.at[5], partners[o],
            )
        )
        far.append(group)
    part = pot_rim // 8
    pot_far = [
        remote(
            pot.at[pl.ds(jnp.where(left == 1, quarter - pot_rim, 0) + (2 * x + o) * part, part)],
            pot_v.at[pl.ds(placed(-pot_rim, pot_rim) + pot_rim + (2 * x + o) * part, part)],
            pot_send.at[o], pot_recv, partners[o],
        )
        for o in range(2)
    ]
    mine = pot_v.at[pl.ds(placed(-pot_rim, pot_rim) + pot_rim + (2 * x + core) * part, part)]

    @pl.when(long)
    def _():
        for o in range(2):
            pot_far[o].start()
        for at in range(3):
            for o in range(2):
                far[o][at].start()

    def send_last():
        for at in range(3, len(pieces)):
            for o in range(2):
                far[o][at].start()

    inner = (zl != 0) & (zl != side - 1)
    pl.when(long & inner)(send_last)

    @pl.when(jnp.logical_not(long))
    def _():
        for o in range(2):
            far[o][5].start()

    near = remote(
        orb.at[1 - core], p0.at[pl.ds(core * quarter + rims[0], quarter)],
        near_send.at[0], near_recv.at[0], sibling,
    )
    near_pot = remote(
        pot, pot_v.at[pl.ds(core * quarter + pot_rim, quarter)],
        near_send.at[1], near_recv.at[1], sibling,
    )
    near.start()
    near_pot.start()

    tell(y_line, plane_sem)

    def apply(level, u, blocks, step=8):
        scale, weight = scalars[level]

        def body(i, c):
            at = placed(u + i * step, step)
            before = None
            if level > 0:
                before = buffers[level - 1][pl.ds(at + rims[level - 1], step)]
            window = buffers[level][pl.ds(at + rims[level] - REACH, step + 2 * REACH)]
            pairs = filtered_block(
                window, pot_v[pl.ds(at + pot_rim, step)], before, scale, weight, lanes, lines[step]
            )
            if level < DEG - 1:
                buffers[level + 1][pl.ds(at + rims[level + 1], step)] = pairs
            else:
                out[pl.ds(2 * (at + rims[DEG]), 2 * step)] = pairs.reshape(2 * step, 8, 128)
            return c

        lax.fori_loop(0, blocks, body, 0, unroll=min(blocks, 3))

    row = 2 * band + core

    def spread(u, count):
        start = placed(u, count)
        tiles = 2 * count

        def send(i, c):
            at = lax.rem(i + yx * max(tiles // floor, 1), tiles)
            tile = lax.rem(2 * (base + start) + at + 2 * whole, 2 * whole)
            src = out.at[2 * (start + rims[DEG]) + at]

            @pl.when(tile != own_tile)
            def _():
                peer = {"band": lax.rem(tile, bands), "dom": lax.div(tile, bands)}
                remote(src, recv.at[row], all_send, all_recv, peer).start()

            @pl.when(tile == own_tile)
            def _():
                pltpu.make_async_copy(src, recv.at[row], move_sem.at[3]).start()

            return c

        lax.fori_loop(0, tiles, send, 0)

    def advance(u, n):
        for level in range(DEG):
            apply(level, u + level * REACH, 1, n)
        spread(u + (DEG - 1) * REACH, n)

    pot_far[0].wait_recv()
    passed = [
        remote(mine, mine, pass_send.at[at], pass_recv.at[at], peer)
        for at, peer in enumerate(x_line)
    ]
    for copy in passed:
        copy.start()

    load.wait()
    load_pot.wait()
    own_rows.wait()
    gather_rows(1)

    def two_blocks(first):
        apply(0, jnp.where(left == 1, first, slab - 16 - first), 2)

    two_blocks(core * quarter + 8)
    near.wait_recv()
    near_pot.wait_recv()
    pl.when(long & jnp.logical_not(inner))(send_last)
    pl.semaphore_wait(plane_sem, len(y_line))
    tell(z_line, all_sem)
    two_blocks((1 - core) * quarter + 8)
    apply(0, 24, 2)
    apply(1, 14, 4)
    apply(1, 42, 1)
    apply(2, 20, 3)
    gather_rows(2)
    pl.semaphore_wait(all_sem, len(z_line))
    spread(20, 24)

    far[0][5].wait_recv()
    apply(0, slab - 8, 1)
    apply(1, slab - 14, 1)
    apply(2, slab - 20, 1)
    spread(slab - 20, 8)
    for at, (u, n) in enumerate(((0, 8), (-8, 8), (-16, 8), (-20, 4), (-24, 4))):
        if at == 1:
            for copy in passed:
                copy.wait_recv()
        far[0][at].wait_recv()
        advance(u, n)

    @pl.when(long)
    def _():
        for o in range(2):
            pot_far[o].wait_send()
            for at in range(len(pieces)):
                far[o][at].wait_send()

    @pl.when(jnp.logical_not(long))
    def _():
        for o in range(2):
            far[o][5].wait_send()

    for copy in (near, near_pot, *passed):
        copy.wait_send()
    for copy in row_copies[2]:
        copy.wait_recv()
    for copies in row_copies:
        for copy in copies:
            copy.wait_send()
    pltpu.make_async_copy(out.at[0], recv.at[row], move_sem.at[3]).wait()
    all_but_own = recv.at[pl.ds(0, recv.shape[0] - 1)]
    pltpu.make_async_copy(all_but_own, all_but_own, all_send).wait()
    pltpu.make_async_copy(all_but_own, all_but_own, all_recv).wait()


def rotate_kernel(recv_v, rows_v, out, out_v, sems):
    high, low = two_parts(jnp.concatenate([rows_v[:, 0], rows_v[:, 1]], axis=0).T)
    matrix = jnp.concatenate([high, high, low], axis=1)
    width = 256
    stores = []
    for at in range(0, 8 * 128, width):
        columns = []
        for r in range(at // 128, (at + width) // 128):
            values = jnp.concatenate([recv_v[:, 0, r], recv_v[:, 1, r]], axis=0)
            high, low = two_parts(values)
            columns.append(jnp.concatenate([high, low, high], axis=0))
        out_v[:, pl.ds(at, width)] = jnp.dot(
            matrix, jnp.concatenate(columns, axis=1), preferred_element_type=jnp.float32
        )
        store = pltpu.make_async_copy(
            out_v.at[:, pl.ds(at, width)], out.at[:, pl.ds(at, width)], sems.at[at // width]
        )
        store.start()
        stores.append(store)
    for store in stores:
        store.wait()


def per_device(bands, orbitals, potential, subspace):
    orbs, planes = orbitals.shape[0], orbitals.shape[1]
    orb = orbitals.reshape(orbs, planes, 2, 8, 128)
    pot = potential.reshape(planes, 2, 8, 128)
    f32 = jnp.float32
    dma = pltpu.SemaphoreType.DMA
    anywhere = pl.BlockSpec(memory_space=pl.ANY)
    slab, shift = 2 * planes, 2 * REACH
    recv, rows = pl.pallas_call(
        functools.partial(filter_kernel, bands),
        out_shape=(
            pltpu.VMEM((bands * orbs, 8, 128), f32),
            pltpu.VMEM((4, 4, 4, orbs, 128), f32),
        ),
        in_specs=[anywhere] * 3,
        out_specs=(anywhere,) * 2,
        scratch_shapes=[
            *[
                pltpu.VMEM((slab + 2 * (shift + REACH * (DEG - level)), 2, 8, 128), f32)
                for level in range(DEG)
            ],
            pltpu.VMEM((2 * (slab + 2 * shift), 8, 128), f32),
            pltpu.VMEM((slab + 2 * (shift + REACH * (DEG - 1)), 2, 8, 128), f32),
            dma((2,)),
            dma((2,)),
            dma((2, 6)),
            dma((6,)),
            dma((2,)),
            dma,
            dma((7,)),
            dma((7,)),
            dma((4,)),
            dma,
            dma,
            dma((3, 3)),
            dma((3, 3)),
            pltpu.SemaphoreType.REGULAR,
            pltpu.SemaphoreType.REGULAR,
        ],
        compiler_params=pltpu.CompilerParams(
            collective_id=0, has_side_effects=True, vmem_limit_bytes=32 * 2**20
        ),
        name="filter",
    )(*(pltpu.with_memory_space_constraint(a, pltpu.HBM) for a in (orb, pot, subspace)))
    recv, rows = recv.reshape(bands, orbs, 8, 128), rows.reshape(bands, orbs, 128)
    return pl.pallas_call(
        rotate_kernel,
        out_shape=jax.ShapeDtypeStruct((bands * orbs, 1024), f32),
        in_specs=[pl.BlockSpec(memory_space=pltpu.VMEM)] * 2,
        out_specs=anywhere,
        scratch_shapes=[pltpu.VMEM((bands * orbs, 1024), f32), dma((4,))],
        compiler_params=pltpu.CompilerParams(vmem_limit_bytes=32 * 2**20),
        name="rotate",
    )(*(pltpu.with_memory_space_constraint(a, pltpu.VMEM) for a in (recv, rows)))


def solution(mesh):
    in_specs = (P("band", "dom", None, None), P("dom", None, None), P("band", None))
    out_specs = P(None, ("dom", "band"))
    return jax.shard_map(
        functools.partial(per_device, mesh.shape["band"]),
        mesh=mesh,
        in_specs=in_specs,
        out_specs=out_specs,
        check_vma=False,
    )
```

```python
import functools
import math

import jax
import jax.numpy as jnp
from jax import lax
from jax.experimental import pallas as pl
from jax.experimental.pallas import tpu as pltpu
from jax.sharding import PartitionSpec as P

DEG = 3
REACH = 6
MESH = pl.DeviceIdType.MESH

upper_edge = 10.7
lower_edge = 1.5
bottom_edge = -1.0


def stencil_weights():
    factor_square = math.factorial(6) ** 2
    side_weights = []
    for offset in range(1, 7):
        side_weights.append(
            2.0
            * (-1.0) ** (offset + 1)
            * factor_square
            / (offset * offset * math.factorial(6 - offset) * math.factorial(6 + offset))
        )
    center_weight = -2.0 * sum(side_weights)
    return (center_weight, side_weights)


def filter_scalars(pass_count):
    half_width = (upper_edge - lower_edge) / 2.0
    sigma_now = half_width / (bottom_edge - (upper_edge + lower_edge) / 2.0)
    gamma_value = 2.0 / sigma_now
    scalars = [(sigma_now / half_width, 0.0)]
    for pass_index in range(pass_count - 1):
        sigma_next = 1.0 / (gamma_value - sigma_now)
        scalars.append((2.0 * sigma_next / half_width, sigma_now * sigma_next))
        sigma_now = sigma_next
    return scalars


def two_parts(values):
    high = values.astype(jnp.bfloat16)
    return high, (values - high.astype(jnp.float32)).astype(jnp.bfloat16)


def stencil_matrix(size, period, axis):
    rows = lax.broadcasted_iota(jnp.int32, (size, size), 0)
    columns = lax.broadcasted_iota(jnp.int32, (size, size), 1)
    apart = jnp.abs(rows - columns)
    if period < size:
        same = jnp.bitwise_or(rows, period - 1) == jnp.bitwise_or(columns, period - 1)
        apart = jnp.where(same, apart, 0)
    apart = jnp.minimum(apart, period - apart)
    matrix = jnp.zeros((size, size), jnp.float32)
    for k, w in enumerate(stencil_weights()[1], 1):
        matrix = jnp.where(apart == k, jnp.float32(w), matrix)
    high, low = two_parts(matrix)
    return jnp.concatenate([high, high, low], axis=axis)


def filtered_block(window, pot, before, scale, weight, lanes, rows):
    center_weight, side = stencil_weights()
    n = window.shape[0] - 2 * REACH
    mid = window[REACH : REACH + n]
    high, low = two_parts(mid.reshape(n * 16, 128))
    total = jnp.dot(
        jnp.concatenate([high, low, high], axis=1), lanes, preferred_element_type=jnp.float32
    ) + jnp.dot(
        rows, jnp.concatenate([high, low, high], axis=0), preferred_element_type=jnp.float32
    )
    total = total.reshape(n, 2, 8, 128)
    for k in range(1, REACH + 1):
        beside = window[REACH + k : REACH + k + n] + window[REACH - k : REACH - k + n]
        total = total + side[k - 1] * beside
    diag = (-1.5 * center_weight - (upper_edge + lower_edge) / 2.0) * scale
    result = (pot * scale + diag) * mid + (-0.5 * scale) * total
    if before is not None:
        result = result - weight * before
    return result


def filter_kernel(
    bands, orb, pot, sub, recv, rows, p0, p1, p2, out, pot_v,
    near_send, near_recv, far_send, far_recv, pot_send, pot_recv, pass_send, pass_recv,
    move_sem, all_send, all_recv, row_send, row_recv, plane_sem, all_sem,
):
    quarter = orb.shape[1]
    slab, whole = 2 * quarter, 4 * quarter
    band, dom = lax.axis_index("band"), lax.axis_index("dom")
    core, half = lax.rem(dom, 2), lax.div(dom, 2)
    side = 4
    floor = side * side
    zl, x, yx = lax.div(band, floor), lax.rem(band, side), lax.rem(band, floor)
    shift = 2 * REACH
    left = jnp.where(zl < side // 2, 1, 0)
    long = core == left
    base = half * slab
    own_tile = dom * bands + band
    own_plane = lax.div(own_tile, 2)
    scalars = filter_scalars(DEG)
    buffers = (p0, p1, p2)
    rims = tuple(shift + REACH * (DEG - level) for level in range(DEG + 1))
    pot_rim = rims[1]

    def placed(u, count):
        return jnp.where(left == 1, u, slab - count - u)

    load = pltpu.make_async_copy(
        orb.at[core], p0.at[pl.ds(core * quarter + rims[0], quarter)], move_sem.at[0]
    )
    load.start()
    load_pot = pltpu.make_async_copy(
        pot, pot_v.at[pl.ds(core * quarter + pot_rim, quarter)], move_sem.at[1]
    )
    load_pot.start()

    sibling = {"dom": dom + 1 - 2 * core}
    partners = [{"dom": 2 * (1 - half) + k} for k in range(2)]

    def chip_along(shift):
        there = lax.rem(half * side + zl + shift, 2 * side)
        return {
            "band": lax.rem(there, side) * floor + yx,
            "dom": lax.div(there, side) * 2 + core,
        }

    x_line = [
        {"band": band - x + lax.rem(x + dx, side), "dom": dom if dk == 0 else dom + 1 - 2 * core}
        for dx in range(side)
        for dk in range(2)
    ][1:]
    y = lax.div(yx, side)
    y_line = [{"band": band + side * (lax.rem(y + dy, side) - y)} for dy in range(1, side)]
    z_line = [chip_along(dz) for dz in range(1, 2 * side)]
    other_partner = {"dom": 2 * (1 - half) + 1 - core}
    barrier = pltpu.get_barrier_semaphore()
    entered = (*z_line, other_partner, *x_line, *y_line)

    def tell(peers, semaphore):
        for peer in peers:
            pl.semaphore_signal(semaphore, inc=1, device_id=peer, device_id_type=MESH)

    tell(entered, barrier)
    lanes = stencil_matrix(128, 128, 0)
    lines = {n: stencil_matrix(16 * n, 16, 1) for n in (4, 8)}
    pl.semaphore_wait(barrier, len(entered))

    def remote(src, dst, send_sem, recv_sem, peer):
        return pltpu.make_async_remote_copy(
            src_ref=src, dst_ref=dst, send_sem=send_sem, recv_sem=recv_sem,
            device_id=peer, device_id_type=MESH,
        )

    own_rows = pltpu.make_async_copy(sub, rows.at[zl, y, x], move_sem.at[2])
    own_rows.start()
    row_lines = [
        (rows.at[zl, y, x], [{"band": lax.rem(band + d * floor, bands)} for d in range(1, side)]),
        (rows.at[:, y, x], y_line),
        (rows.at[:, :, x], [{"band": band - x + lax.rem(x + d, side)} for d in range(1, side)]),
    ]
    row_copies = [
        [
            remote(
                sub if stage == 0 else part_rows, part_rows,
                row_send.at[stage, at], row_recv.at[stage, at], peer,
            )
            for at, peer in enumerate(peers)
        ]
        for stage, (part_rows, peers) in enumerate(row_lines)
    ]

    def gather_rows(stage):
        if stage > 0:
            for copy in row_copies[stage - 1]:
                copy.wait_recv()
        for copy in row_copies[stage]:
            copy.start()

    gather_rows(0)
    pieces = [(0, 6), (6, 8), (14, 8), (22, 4), (26, 4)]
    assert sum(n for _, n in pieces) == rims[0]
    far = []
    for o in range(2):
        group = []
        for at, (a, n) in enumerate(pieces):
            group.append(
                remote(
                    orb.at[o, pl.ds(jnp.where(left == 1, quarter - a - n, a), n)],
                    p0.at[pl.ds(placed(-a - n, n) + rims[0], n)],
                    far_send.at[o, at], far_recv.at[at], partners[o],
                )
            )
        n = REACH
        group.append(
            remote(
                orb.at[o, pl.ds(jnp.where(left == 1, 0, quarter - n), n)],
                p0.at[pl.ds(placed(slab, n) + rims[0], n)],
                far_send.at[o, 5], far_recv.at[5], partners[o],
            )
        )
        far.append(group)
    part = pot_rim // 8
    pot_far = [
        remote(
            pot.at[pl.ds(jnp.where(left == 1, quarter - pot_rim, 0) + (2 * x + o) * part, part)],
            pot_v.at[pl.ds(placed(-pot_rim, pot_rim) + pot_rim + (2 * x + o) * part, part)],
            pot_send.at[o], pot_recv, partners[o],
        )
        for o in range(2)
    ]
    mine = pot_v.at[pl.ds(placed(-pot_rim, pot_rim) + pot_rim + (2 * x + core) * part, part)]

    @pl.when(long)
    def _():
        for o in range(2):
            pot_far[o].start()
        for at in range(3):
            for o in range(2):
                far[o][at].start()

    def send_last():
        for at in range(3, len(pieces)):
            for o in range(2):
                far[o][at].start()

    inner = (zl != 0) & (zl != side - 1)
    pl.when(long & inner)(send_last)

    @pl.when(jnp.logical_not(long))
    def _():
        for o in range(2):
            far[o][5].start()

    near = remote(
        orb.at[1 - core], p0.at[pl.ds(core * quarter + rims[0], quarter)],
        near_send.at[0], near_recv.at[0], sibling,
    )
    near_pot = remote(
        pot, pot_v.at[pl.ds(core * quarter + pot_rim, quarter)],
        near_send.at[1], near_recv.at[1], sibling,
    )
    near.start()
    near_pot.start()

    tell(y_line, plane_sem)

    def apply(level, u, blocks, step=8):
        scale, weight = scalars[level]

        def body(i, c):
            at = placed(u + i * step, step)
            before = None
            if level > 0:
                before = buffers[level - 1][pl.ds(at + rims[level - 1], step)]
            window = buffers[level][pl.ds(at + rims[level] - REACH, step + 2 * REACH)]
            pairs = filtered_block(
                window, pot_v[pl.ds(at + pot_rim, step)], before, scale, weight, lanes, lines[step]
            )
            if level < DEG - 1:
                buffers[level + 1][pl.ds(at + rims[level + 1], step)] = pairs
            else:
                out[pl.ds(2 * (at + rims[DEG]), 2 * step)] = pairs.reshape(2 * step, 8, 128)
            return c

        lax.fori_loop(0, blocks, body, 0)

    row = 2 * band + core

    def spread(u, count):
        start = placed(u, count)
        tiles = 2 * count

        def send(i, c):
            at = lax.rem(i + yx * max(tiles // floor, 1) + 4 * zl + 2 * core, tiles)
            tile = lax.rem(2 * (base + start) + at + 2 * whole, 2 * whole)
            src = out.at[2 * (start + rims[DEG]) + at]

            @pl.when(tile != own_tile)
            def _():
                peer = {"band": lax.rem(tile, bands), "dom": lax.div(tile, bands)}
                remote(src, recv.at[row], all_send, all_recv, peer).start()

            @pl.when(tile == own_tile)
            def _():
                pltpu.make_async_copy(src, recv.at[row], move_sem.at[3]).start()

            return c

        lax.fori_loop(0, tiles, send, 0)

    def advance(u, n):
        for level in range(DEG):
            apply(level, u + level * REACH, 1, n)
        spread(u + (DEG - 1) * REACH, n)

    pot_far[0].wait_recv()
    passed = [
        remote(mine, mine, pass_send.at[at], pass_recv.at[at], peer)
        for at, peer in enumerate(x_line)
    ]
    for copy in passed:
        copy.start()

    load.wait()
    load_pot.wait()
    own_rows.wait()
    gather_rows(1)
    near.wait_recv()
    near_pot.wait_recv()
    pl.when(long & jnp.logical_not(inner))(send_last)
    pl.semaphore_wait(plane_sem, len(y_line))
    tell(z_line, all_sem)
    apply(0, 8, 6)
    apply(1, 14, 4)
    apply(1, 42, 1)
    apply(2, 20, 3)
    gather_rows(2)
    pl.semaphore_wait(all_sem, len(z_line))
    spread(20, 24)

    far[0][5].wait_recv()
    apply(0, slab - 8, 1)
    apply(1, slab - 14, 1)
    apply(2, slab - 20, 1)
    spread(slab - 20, 8)
    for at, (u, n) in enumerate(((0, 8), (-8, 8), (-16, 8), (-20, 4), (-24, 4))):
        if at == 1:
            for copy in passed:
                copy.wait_recv()
        far[0][at].wait_recv()
        advance(u, n)

    @pl.when(long)
    def _():
        for o in range(2):
            pot_far[o].wait_send()
            for at in range(len(pieces)):
                far[o][at].wait_send()

    @pl.when(jnp.logical_not(long))
    def _():
        for o in range(2):
            far[o][5].wait_send()

    for copy in (near, near_pot, *passed):
        copy.wait_send()
    for copy in row_copies[2]:
        copy.wait_recv()
    for copies in row_copies:
        for copy in copies:
            copy.wait_send()
    pltpu.make_async_copy(out.at[0], recv.at[row], move_sem.at[3]).wait()
    all_but_own = recv.at[pl.ds(0, recv.shape[0] - 1)]
    pltpu.make_async_copy(all_but_own, all_but_own, all_send).wait()
    pltpu.make_async_copy(all_but_own, all_but_own, all_recv).wait()


def rotate_kernel(recv_v, rows_v, out, out_v, sems):
    high, low = two_parts(jnp.concatenate([rows_v[:, 0], rows_v[:, 1]], axis=0).T)
    matrix = jnp.concatenate([high, high, low], axis=1)
    width = 256
    stores = []
    for at in range(0, 8 * 128, width):
        columns = []
        for r in range(at // 128, (at + width) // 128):
            values = jnp.concatenate([recv_v[:, 0, r], recv_v[:, 1, r]], axis=0)
            high, low = two_parts(values)
            columns.append(jnp.concatenate([high, low, high], axis=0))
        out_v[:, pl.ds(at, width)] = jnp.dot(
            matrix, jnp.concatenate(columns, axis=1), preferred_element_type=jnp.float32
        )
        store = pltpu.make_async_copy(
            out_v.at[:, pl.ds(at, width)], out.at[:, pl.ds(at, width)], sems.at[at // width]
        )
        store.start()
        stores.append(store)
    for store in stores:
        store.wait()


def per_device(bands, orbitals, potential, subspace):
    orbs, planes = orbitals.shape[0], orbitals.shape[1]
    orb = orbitals.reshape(orbs, planes, 2, 8, 128)
    pot = potential.reshape(planes, 2, 8, 128)
    f32 = jnp.float32
    dma = pltpu.SemaphoreType.DMA
    anywhere = pl.BlockSpec(memory_space=pl.ANY)
    slab, shift = 2 * planes, 2 * REACH
    recv, rows = pl.pallas_call(
        functools.partial(filter_kernel, bands),
        out_shape=(
            pltpu.VMEM((bands * orbs, 8, 128), f32),
            pltpu.VMEM((4, 4, 4, orbs, 128), f32),
        ),
        in_specs=[anywhere] * 3,
        out_specs=(anywhere,) * 2,
        scratch_shapes=[
            *[
                pltpu.VMEM((slab + 2 * (shift + REACH * (DEG - level)), 2, 8, 128), f32)
                for level in range(DEG)
            ],
            pltpu.VMEM((2 * (slab + 2 * shift), 8, 128), f32),
            pltpu.VMEM((slab + 2 * (shift + REACH * (DEG - 1)), 2, 8, 128), f32),
            dma((2,)),
            dma((2,)),
            dma((2, 6)),
            dma((6,)),
            dma((2,)),
            dma,
            dma((7,)),
            dma((7,)),
            dma((4,)),
            dma,
            dma,
            dma((3, 3)),
            dma((3, 3)),
            pltpu.SemaphoreType.REGULAR,
            pltpu.SemaphoreType.REGULAR,
        ],
        compiler_params=pltpu.CompilerParams(
            collective_id=0, has_side_effects=True, vmem_limit_bytes=32 * 2**20
        ),
        name="filter",
    )(*(pltpu.with_memory_space_constraint(a, pltpu.HBM) for a in (orb, pot, subspace)))
    recv, rows = recv.reshape(bands, orbs, 8, 128), rows.reshape(bands, orbs, 128)
    return pl.pallas_call(
        rotate_kernel,
        out_shape=jax.ShapeDtypeStruct((bands * orbs, 1024), f32),
        in_specs=[pl.BlockSpec(memory_space=pltpu.VMEM)] * 2,
        out_specs=anywhere,
        scratch_shapes=[pltpu.VMEM((bands * orbs, 1024), f32), dma((4,))],
        compiler_params=pltpu.CompilerParams(vmem_limit_bytes=32 * 2**20),
        name="rotate",
    )(*(pltpu.with_memory_space_constraint(a, pltpu.VMEM) for a in (recv, rows)))


def solution(mesh):
    in_specs = (P("band", "dom", None, None), P("dom", None, None), P("band", None))
    out_specs = P(None, ("dom", "band"))
    return jax.shard_map(
        functools.partial(per_device, mesh.shape["band"]),
        mesh=mesh,
        in_specs=in_specs,
        out_specs=out_specs,
        check_vma=False,
    )
```

```python
import functools
import math

import jax
import jax.numpy as jnp
from jax import lax
from jax.experimental import pallas as pl
from jax.experimental.pallas import tpu as pltpu
from jax.sharding import PartitionSpec as P

DEG = 3
REACH = 6
MESH = pl.DeviceIdType.MESH

upper_edge = 10.7
lower_edge = 1.5
bottom_edge = -1.0


def stencil_weights():
    factor_square = math.factorial(6) ** 2
    side_weights = []
    for offset in range(1, 7):
        side_weights.append(
            2.0
            * (-1.0) ** (offset + 1)
            * factor_square
            / (offset * offset * math.factorial(6 - offset) * math.factorial(6 + offset))
        )
    center_weight = -2.0 * sum(side_weights)
    return (center_weight, side_weights)


def filter_scalars(pass_count):
    half_width = (upper_edge - lower_edge) / 2.0
    sigma_now = half_width / (bottom_edge - (upper_edge + lower_edge) / 2.0)
    gamma_value = 2.0 / sigma_now
    scalars = [(sigma_now / half_width, 0.0)]
    for pass_index in range(pass_count - 1):
        sigma_next = 1.0 / (gamma_value - sigma_now)
        scalars.append((2.0 * sigma_next / half_width, sigma_now * sigma_next))
        sigma_now = sigma_next
    return scalars


def two_parts(values):
    high = values.astype(jnp.bfloat16)
    return high, (values - high.astype(jnp.float32)).astype(jnp.bfloat16)


def stencil_matrix(size, period, axis):
    rows = lax.broadcasted_iota(jnp.int32, (size, size), 0)
    columns = lax.broadcasted_iota(jnp.int32, (size, size), 1)
    apart = jnp.abs(rows - columns)
    if period < size:
        same = jnp.bitwise_or(rows, period - 1) == jnp.bitwise_or(columns, period - 1)
        apart = jnp.where(same, apart, 0)
    apart = jnp.minimum(apart, period - apart)
    matrix = jnp.zeros((size, size), jnp.float32)
    for k, w in enumerate(stencil_weights()[1], 1):
        matrix = jnp.where(apart == k, jnp.float32(w), matrix)
    high, low = two_parts(matrix)
    return jnp.concatenate([high, high, low], axis=axis)


def filtered_block(window, pot, before, scale, weight, lanes, rows):
    center_weight, side = stencil_weights()
    n = window.shape[0] - 2 * REACH
    mid = window[REACH : REACH + n]
    high, low = two_parts(mid.reshape(n * 16, 128))
    total = jnp.dot(
        jnp.concatenate([high, low, high], axis=1), lanes, preferred_element_type=jnp.float32
    ) + jnp.dot(
        rows, jnp.concatenate([high, low, high], axis=0), preferred_element_type=jnp.float32
    )
    total = total.reshape(n, 2, 8, 128)
    for k in range(1, REACH + 1):
        beside = window[REACH + k : REACH + k + n] + window[REACH - k : REACH - k + n]
        total = total + side[k - 1] * beside
    diag = (-1.5 * center_weight - (upper_edge + lower_edge) / 2.0) * scale
    result = (pot * scale + diag) * mid + (-0.5 * scale) * total
    if before is not None:
        result = result - weight * before
    return result


def filter_kernel(
    bands, orb, pot, sub, recv, rows, p0, p1, p2, out, pot_v,
    near_send, near_recv, far_send, far_recv, pot_send, pot_recv, pass_send, pass_recv,
    move_sem, all_send, all_recv, row_send, row_recv, plane_sem, all_sem,
):
    quarter = orb.shape[1]
    slab, whole = 2 * quarter, 4 * quarter
    band, dom = lax.axis_index("band"), lax.axis_index("dom")
    core, half = lax.rem(dom, 2), lax.div(dom, 2)
    side = 4
    floor = side * side
    zl, x, yx = lax.div(band, floor), lax.rem(band, side), lax.rem(band, floor)
    shift = 2 * REACH
    left = jnp.where(zl < side // 2, 1, 0)
    long = core == left
    base = half * slab
    own_tile = dom * bands + band
    own_plane = lax.div(own_tile, 2)
    scalars = filter_scalars(DEG)
    buffers = (p0, p1, p2)
    rims = tuple(shift + REACH * (DEG - level) for level in range(DEG + 1))
    pot_rim = rims[1]

    def placed(u, count):
        return jnp.where(left == 1, u, slab - count - u)

    load = pltpu.make_async_copy(
        orb.at[core], p0.at[pl.ds(core * quarter + rims[0], quarter)], move_sem.at[0]
    )
    load.start()
    load_pot = pltpu.make_async_copy(
        pot, pot_v.at[pl.ds(core * quarter + pot_rim, quarter)], move_sem.at[1]
    )
    load_pot.start()

    sibling = {"dom": dom + 1 - 2 * core}
    partners = [{"dom": 2 * (1 - half) + k} for k in range(2)]

    def chip_along(shift):
        there = lax.rem(half * side + zl + shift, 2 * side)
        return {
            "band": lax.rem(there, side) * floor + yx,
            "dom": lax.div(there, side) * 2 + core,
        }

    x_line = [
        {"band": band - x + lax.rem(x + dx, side), "dom": dom if dk == 0 else dom + 1 - 2 * core}
        for dx in range(side)
        for dk in range(2)
    ][1:]
    y = lax.div(yx, side)
    y_line = [{"band": band + side * (lax.rem(y + dy, side) - y)} for dy in range(1, side)]
    z_line = [chip_along(dz) for dz in range(1, 2 * side)]
    other_partner = {"dom": 2 * (1 - half) + 1 - core}
    barrier = pltpu.get_barrier_semaphore()
    entered = (*z_line, other_partner, *x_line, *y_line)

    def tell(peers, semaphore):
        for peer in peers:
            pl.semaphore_signal(semaphore, inc=1, device_id=peer, device_id_type=MESH)

    tell(entered, barrier)
    lanes = stencil_matrix(128, 128, 0)
    lines = {n: stencil_matrix(16 * n, 16, 1) for n in (4, 8)}
    pl.semaphore_wait(barrier, len(entered))

    def remote(src, dst, send_sem, recv_sem, peer):
        return pltpu.make_async_remote_copy(
            src_ref=src, dst_ref=dst, send_sem=send_sem, recv_sem=recv_sem,
            device_id=peer, device_id_type=MESH,
        )

    own_rows = pltpu.make_async_copy(sub, rows.at[zl, y, x], move_sem.at[2])
    own_rows.start()
    row_lines = [
        (rows.at[zl, y, x], [{"band": lax.rem(band + d * floor, bands)} for d in range(1, side)]),
        (rows.at[:, y, x], y_line),
        (rows.at[:, :, x], [{"band": band - x + lax.rem(x + d, side)} for d in range(1, side)]),
    ]
    row_copies = [
        [
            remote(
                sub if stage == 0 else part_rows, part_rows,
                row_send.at[stage, at], row_recv.at[stage, at], peer,
            )
            for at, peer in enumerate(peers)
        ]
        for stage, (part_rows, peers) in enumerate(row_lines)
    ]

    def gather_rows(stage):
        if stage > 0:
            for copy in row_copies[stage - 1]:
                copy.wait_recv()
        for copy in row_copies[stage]:
            copy.start()

    gather_rows(0)
    pieces = [(0, 6), (6, 8), (14, 8), (22, 4), (26, 4)]
    assert sum(n for _, n in pieces) == rims[0]
    far = []
    for o in range(2):
        group = []
        for at, (a, n) in enumerate(pieces):
            group.append(
                remote(
                    orb.at[o, pl.ds(jnp.where(left == 1, quarter - a - n, a), n)],
                    p0.at[pl.ds(placed(-a - n, n) + rims[0], n)],
                    far_send.at[o, at], far_recv.at[at], partners[o],
                )
            )
        n = REACH
        group.append(
            remote(
                orb.at[o, pl.ds(jnp.where(left == 1, 0, quarter - n), n)],
                p0.at[pl.ds(placed(slab, n) + rims[0], n)],
                far_send.at[o, 5], far_recv.at[5], partners[o],
            )
        )
        far.append(group)
    part = pot_rim // 8
    pot_far = [
        remote(
            pot.at[pl.ds(jnp.where(left == 1, quarter - pot_rim, 0) + (2 * x + o) * part, part)],
            pot_v.at[pl.ds(placed(-pot_rim, pot_rim) + pot_rim + (2 * x + o) * part, part)],
            pot_send.at[o], pot_recv, partners[o],
        )
        for o in range(2)
    ]
    mine = pot_v.at[pl.ds(placed(-pot_rim, pot_rim) + pot_rim + (2 * x + core) * part, part)]

    @pl.when(long)
    def _():
        for o in range(2):
            pot_far[o].start()
        for at in range(3):
            for o in range(2):
                far[o][at].start()

    def send_last():
        for at in range(3, len(pieces)):
            for o in range(2):
                far[o][at].start()

    inner = (zl != 0) & (zl != side - 1)
    pl.when(long & inner)(send_last)

    @pl.when(jnp.logical_not(long))
    def _():
        for o in range(2):
            far[o][5].start()

    near = remote(
        orb.at[1 - core], p0.at[pl.ds(core * quarter + rims[0], quarter)],
        near_send.at[0], near_recv.at[0], sibling,
    )
    near_pot = remote(
        pot, pot_v.at[pl.ds(core * quarter + pot_rim, quarter)],
        near_send.at[1], near_recv.at[1], sibling,
    )
    near.start()
    near_pot.start()

    tell(y_line, plane_sem)

    def apply(level, u, blocks, step=8):
        scale, weight = scalars[level]

        def body(i, c):
            at = placed(u + i * step, step)
            before = None
            if level > 0:
                before = buffers[level - 1][pl.ds(at + rims[level - 1], step)]
            window = buffers[level][pl.ds(at + rims[level] - REACH, step + 2 * REACH)]
            pairs = filtered_block(
                window, pot_v[pl.ds(at + pot_rim, step)], before, scale, weight, lanes, lines[step]
            )
            if level < DEG - 1:
                buffers[level + 1][pl.ds(at + rims[level + 1], step)] = pairs
            else:
                out[pl.ds(2 * (at + rims[DEG]), 2 * step)] = pairs.reshape(2 * step, 8, 128)
            return c

        lax.fori_loop(0, blocks, body, 0)

    row = 2 * band + core

    def spread(u, count, first=0, last=None):
        start = placed(u, count)
        tiles = 2 * count

        def send(i, c):
            at = lax.rem(i + yx * max(tiles // floor, 1) + 4 * zl + 2 * core, tiles)
            tile = lax.rem(2 * (base + start) + at + 2 * whole, 2 * whole)
            src = out.at[2 * (start + rims[DEG]) + at]

            @pl.when(tile != own_tile)
            def _():
                peer = {"band": lax.rem(tile, bands), "dom": lax.div(tile, bands)}
                remote(src, recv.at[row], all_send, all_recv, peer).start()

            @pl.when(tile == own_tile)
            def _():
                pltpu.make_async_copy(src, recv.at[row], move_sem.at[3]).start()

            return c

        lax.fori_loop(first, tiles if last is None else last, send, 0)

    def advance(u, n):
        for level in range(DEG):
            apply(level, u + level * REACH, 1, n)
        spread(u + (DEG - 1) * REACH, n)

    pot_far[0].wait_recv()
    passed = [
        remote(mine, mine, pass_send.at[at], pass_recv.at[at], peer)
        for at, peer in enumerate(x_line)
    ]
    for copy in passed:
        copy.start()

    load.wait()
    load_pot.wait()
    own_rows.wait()
    gather_rows(1)
    near.wait_recv()
    near_pot.wait_recv()
    pl.when(long & jnp.logical_not(inner))(send_last)
    pl.semaphore_wait(plane_sem, len(y_line))
    tell(z_line, all_sem)
    apply(0, 8, 6)
    apply(1, 14, 4)
    apply(1, 42, 1)
    apply(2, 20, 3)
    gather_rows(2)
    pl.semaphore_wait(all_sem, len(z_line))
    spread(20, 24, 0, 24)

    far[0][5].wait_recv()
    apply(0, slab - 8, 1)
    apply(1, slab - 14, 1)
    apply(2, slab - 20, 1)
    spread(slab - 20, 8)
    for at, (u, n) in enumerate(((0, 8), (-8, 8), (-16, 8), (-20, 4), (-24, 4))):
        if at == 1:
            for copy in passed:
                copy.wait_recv()
        far[0][at].wait_recv()
        advance(u, n)
        if at == 2:
            spread(20, 24, 24, 48)

    @pl.when(long)
    def _():
        for o in range(2):
            pot_far[o].wait_send()
            for at in range(len(pieces)):
                far[o][at].wait_send()

    @pl.when(jnp.logical_not(long))
    def _():
        for o in range(2):
            far[o][5].wait_send()

    for copy in (near, near_pot, *passed):
        copy.wait_send()
    for copy in row_copies[2]:
        copy.wait_recv()
    for copies in row_copies:
        for copy in copies:
            copy.wait_send()
    pltpu.make_async_copy(out.at[0], recv.at[row], move_sem.at[3]).wait()
    all_but_own = recv.at[pl.ds(0, recv.shape[0] - 1)]
    pltpu.make_async_copy(all_but_own, all_but_own, all_send).wait()
    pltpu.make_async_copy(all_but_own, all_but_own, all_recv).wait()


def rotate_kernel(recv_v, rows_v, out, out_v, sems):
    high, low = two_parts(jnp.concatenate([rows_v[:, 0], rows_v[:, 1]], axis=0).T)
    matrix = jnp.concatenate([high, high, low], axis=1)
    width = 256
    stores = []
    for at in range(0, 8 * 128, width):
        columns = []
        for r in range(at // 128, (at + width) // 128):
            values = jnp.concatenate([recv_v[:, 0, r], recv_v[:, 1, r]], axis=0)
            high, low = two_parts(values)
            columns.append(jnp.concatenate([high, low, high], axis=0))
        out_v[:, pl.ds(at, width)] = jnp.dot(
            matrix, jnp.concatenate(columns, axis=1), preferred_element_type=jnp.float32
        )
        store = pltpu.make_async_copy(
            out_v.at[:, pl.ds(at, width)], out.at[:, pl.ds(at, width)], sems.at[at // width]
        )
        store.start()
        stores.append(store)
    for store in stores:
        store.wait()


def per_device(bands, orbitals, potential, subspace):
    orbs, planes = orbitals.shape[0], orbitals.shape[1]
    orb = orbitals.reshape(orbs, planes, 2, 8, 128)
    pot = potential.reshape(planes, 2, 8, 128)
    f32 = jnp.float32
    dma = pltpu.SemaphoreType.DMA
    anywhere = pl.BlockSpec(memory_space=pl.ANY)
    slab, shift = 2 * planes, 2 * REACH
    recv, rows = pl.pallas_call(
        functools.partial(filter_kernel, bands),
        out_shape=(
            pltpu.VMEM((bands * orbs, 8, 128), f32),
            pltpu.VMEM((4, 4, 4, orbs, 128), f32),
        ),
        in_specs=[anywhere] * 3,
        out_specs=(anywhere,) * 2,
        scratch_shapes=[
            *[
                pltpu.VMEM((slab + 2 * (shift + REACH * (DEG - level)), 2, 8, 128), f32)
                for level in range(DEG)
            ],
            pltpu.VMEM((2 * (slab + 2 * shift), 8, 128), f32),
            pltpu.VMEM((slab + 2 * (shift + REACH * (DEG - 1)), 2, 8, 128), f32),
            dma((2,)),
            dma((2,)),
            dma((2, 6)),
            dma((6,)),
            dma((2,)),
            dma,
            dma((7,)),
            dma((7,)),
            dma((4,)),
            dma,
            dma,
            dma((3, 3)),
            dma((3, 3)),
            pltpu.SemaphoreType.REGULAR,
            pltpu.SemaphoreType.REGULAR,
        ],
        compiler_params=pltpu.CompilerParams(
            collective_id=0, has_side_effects=True, vmem_limit_bytes=32 * 2**20
        ),
        name="filter",
    )(*(pltpu.with_memory_space_constraint(a, pltpu.HBM) for a in (orb, pot, subspace)))
    recv, rows = recv.reshape(bands, orbs, 8, 128), rows.reshape(bands, orbs, 128)
    return pl.pallas_call(
        rotate_kernel,
        out_shape=jax.ShapeDtypeStruct((bands * orbs, 1024), f32),
        in_specs=[pl.BlockSpec(memory_space=pltpu.VMEM)] * 2,
        out_specs=anywhere,
        scratch_shapes=[pltpu.VMEM((bands * orbs, 1024), f32), dma((4,))],
        compiler_params=pltpu.CompilerParams(vmem_limit_bytes=32 * 2**20),
        name="rotate",
    )(*(pltpu.with_memory_space_constraint(a, pltpu.VMEM) for a in (recv, rows)))


def solution(mesh):
    in_specs = (P("band", "dom", None, None), P("dom", None, None), P("band", None))
    out_specs = P(None, ("dom", "band"))
    return jax.shard_map(
        functools.partial(per_device, mesh.shape["band"]),
        mesh=mesh,
        in_specs=in_specs,
        out_specs=out_specs,
        check_vma=False,
    )
```

```python
import functools
import math

import jax
import jax.numpy as jnp
from jax import lax
from jax.experimental import pallas as pl
from jax.experimental.pallas import tpu as pltpu
from jax.sharding import PartitionSpec as P

DEG = 3
REACH = 6
MESH = pl.DeviceIdType.MESH

upper_edge = 10.7
lower_edge = 1.5
bottom_edge = -1.0


def stencil_weights():
    factor_square = math.factorial(6) ** 2
    side_weights = []
    for offset in range(1, 7):
        side_weights.append(
            2.0
            * (-1.0) ** (offset + 1)
            * factor_square
            / (offset * offset * math.factorial(6 - offset) * math.factorial(6 + offset))
        )
    center_weight = -2.0 * sum(side_weights)
    return (center_weight, side_weights)


def filter_scalars(pass_count):
    half_width = (upper_edge - lower_edge) / 2.0
    sigma_now = half_width / (bottom_edge - (upper_edge + lower_edge) / 2.0)
    gamma_value = 2.0 / sigma_now
    scalars = [(sigma_now / half_width, 0.0)]
    for pass_index in range(pass_count - 1):
        sigma_next = 1.0 / (gamma_value - sigma_now)
        scalars.append((2.0 * sigma_next / half_width, sigma_now * sigma_next))
        sigma_now = sigma_next
    return scalars


def two_parts(values):
    high = values.astype(jnp.bfloat16)
    return high, (values - high.astype(jnp.float32)).astype(jnp.bfloat16)


def stencil_matrix(size, period, axis):
    rows = lax.broadcasted_iota(jnp.int32, (size, size), 0)
    columns = lax.broadcasted_iota(jnp.int32, (size, size), 1)
    apart = jnp.abs(rows - columns)
    if period < size:
        same = jnp.bitwise_or(rows, period - 1) == jnp.bitwise_or(columns, period - 1)
        apart = jnp.where(same, apart, 0)
    apart = jnp.minimum(apart, period - apart)
    matrix = jnp.zeros((size, size), jnp.float32)
    for k, w in enumerate(stencil_weights()[1], 1):
        matrix = jnp.where(apart == k, jnp.float32(w), matrix)
    high, low = two_parts(matrix)
    return jnp.concatenate([high, high, low], axis=axis)


def filtered_block(window, pot, before, scale, weight, lanes, rows):
    center_weight, side = stencil_weights()
    n = window.shape[0] - 2 * REACH
    mid = window[REACH : REACH + n]
    high, low = two_parts(mid.reshape(n * 16, 128))
    total = jnp.dot(
        jnp.concatenate([high, low, high], axis=1), lanes, preferred_element_type=jnp.float32
    ) + jnp.dot(
        rows, jnp.concatenate([high, low, high], axis=0), preferred_element_type=jnp.float32
    )
    total = total.reshape(n, 2, 8, 128)
    for k in range(1, REACH + 1):
        beside = window[REACH + k : REACH + k + n] + window[REACH - k : REACH - k + n]
        total = total + side[k - 1] * beside
    diag = (-1.5 * center_weight - (upper_edge + lower_edge) / 2.0) * scale
    result = (pot * scale + diag) * mid + (-0.5 * scale) * total
    if before is not None:
        result = result - weight * before
    return result


def filter_kernel(
    bands, orb, pot, sub, recv, rows, p0, p1, p2, out, pot_v,
    near_send, near_recv, far_send, far_recv, pot_send, pot_recv, pass_send, pass_recv,
    move_sem, all_send, all_recv, row_send, row_recv, plane_sem, all_sem,
):
    quarter = orb.shape[1]
    slab, whole = 2 * quarter, 4 * quarter
    band, dom = lax.axis_index("band"), lax.axis_index("dom")
    core, half = lax.rem(dom, 2), lax.div(dom, 2)
    side = 4
    floor = side * side
    zl, x, yx = lax.div(band, floor), lax.rem(band, side), lax.rem(band, floor)
    shift = 2 * REACH
    left = jnp.where(zl < side // 2, 1, 0)
    long = core == left
    base = half * slab
    own_tile = dom * bands + band
    own_plane = lax.div(own_tile, 2)
    scalars = filter_scalars(DEG)
    buffers = (p0, p1, p2)
    rims = tuple(shift + REACH * (DEG - level) for level in range(DEG + 1))
    pot_rim = rims[1]

    def placed(u, count):
        return jnp.where(left == 1, u, slab - count - u)

    load = pltpu.make_async_copy(
        orb.at[core], p0.at[pl.ds(core * quarter + rims[0], quarter)], move_sem.at[0]
    )
    load.start()
    load_pot = pltpu.make_async_copy(
        pot, pot_v.at[pl.ds(core * quarter + pot_rim, quarter)], move_sem.at[1]
    )
    load_pot.start()

    sibling = {"dom": dom + 1 - 2 * core}
    partners = [{"dom": 2 * (1 - half) + k} for k in range(2)]

    def chip_along(shift):
        there = lax.rem(half * side + zl + shift, 2 * side)
        return {
            "band": lax.rem(there, side) * floor + yx,
            "dom": lax.div(there, side) * 2 + core,
        }

    x_line = [
        {"band": band - x + lax.rem(x + dx, side), "dom": dom if dk == 0 else dom + 1 - 2 * core}
        for dx in range(side)
        for dk in range(2)
    ][1:]
    y = lax.div(yx, side)
    y_line = [{"band": band + side * (lax.rem(y + dy, side) - y)} for dy in range(1, side)]
    z_line = [chip_along(dz) for dz in range(1, 2 * side)]
    other_partner = {"dom": 2 * (1 - half) + 1 - core}
    barrier = pltpu.get_barrier_semaphore()
    entered = (*z_line, other_partner, *x_line, *y_line)

    def tell(peers, semaphore):
        for peer in peers:
            pl.semaphore_signal(semaphore, inc=1, device_id=peer, device_id_type=MESH)

    tell(entered, barrier)
    lanes = stencil_matrix(128, 128, 0)
    lines = {n: stencil_matrix(16 * n, 16, 1) for n in (4, 8)}
    pl.semaphore_wait(barrier, len(entered))

    def remote(src, dst, send_sem, recv_sem, peer):
        return pltpu.make_async_remote_copy(
            src_ref=src, dst_ref=dst, send_sem=send_sem, recv_sem=recv_sem,
            device_id=peer, device_id_type=MESH,
        )

    own_rows = pltpu.make_async_copy(sub, rows.at[zl, y, x], move_sem.at[2])
    own_rows.start()
    row_lines = [
        (rows.at[zl, y, x], [{"band": lax.rem(band + d * floor, bands)} for d in range(1, side)]),
        (rows.at[:, y, x], y_line),
        (rows.at[:, :, x], [{"band": band - x + lax.rem(x + d, side)} for d in range(1, side)]),
    ]
    row_copies = [
        [
            remote(
                sub if stage == 0 else part_rows, part_rows,
                row_send.at[stage, at], row_recv.at[stage, at], peer,
            )
            for at, peer in enumerate(peers)
        ]
        for stage, (part_rows, peers) in enumerate(row_lines)
    ]

    def gather_rows(stage):
        if stage > 0:
            for copy in row_copies[stage - 1]:
                copy.wait_recv()
        for copy in row_copies[stage]:
            copy.start()

    gather_rows(0)
    pieces = [(0, 6), (6, 8), (14, 8), (22, 4), (26, 4)]
    assert sum(n for _, n in pieces) == rims[0]
    far = []
    for o in range(2):
        group = []
        for at, (a, n) in enumerate(pieces):
            group.append(
                remote(
                    orb.at[o, pl.ds(jnp.where(left == 1, quarter - a - n, a), n)],
                    p0.at[pl.ds(placed(-a - n, n) + rims[0], n)],
                    far_send.at[o, at], far_recv.at[at], partners[o],
                )
            )
        n = REACH
        group.append(
            remote(
                orb.at[o, pl.ds(jnp.where(left == 1, 0, quarter - n), n)],
                p0.at[pl.ds(placed(slab, n) + rims[0], n)],
                far_send.at[o, 5], far_recv.at[5], partners[o],
            )
        )
        far.append(group)
    part = pot_rim // 8
    pot_far = [
        remote(
            pot.at[pl.ds(jnp.where(left == 1, quarter - pot_rim, 0) + (2 * x + o) * part, part)],
            pot_v.at[pl.ds(placed(-pot_rim, pot_rim) + pot_rim + (2 * x + o) * part, part)],
            pot_send.at[o], pot_recv, partners[o],
        )
        for o in range(2)
    ]
    mine = pot_v.at[pl.ds(placed(-pot_rim, pot_rim) + pot_rim + (2 * x + core) * part, part)]

    @pl.when(long)
    def _():
        for o in range(2):
            pot_far[o].start()
        for at in range(3):
            for o in range(2):
                far[o][at].start()

    def send_last():
        for at in range(3, len(pieces)):
            for o in range(2):
                far[o][at].start()

    inner = (zl != 0) & (zl != side - 1)
    pl.when(long & inner)(send_last)

    @pl.when(jnp.logical_not(long))
    def _():
        for o in range(2):
            far[o][5].start()

    near = remote(
        orb.at[1 - core], p0.at[pl.ds(core * quarter + rims[0], quarter)],
        near_send.at[0], near_recv.at[0], sibling,
    )
    near_pot = remote(
        pot, pot_v.at[pl.ds(core * quarter + pot_rim, quarter)],
        near_send.at[1], near_recv.at[1], sibling,
    )
    near.start()
    near_pot.start()

    tell(y_line, plane_sem)

    def apply(level, u, blocks, step=8):
        scale, weight = scalars[level]

        def body(i, c):
            at = placed(u + i * step, step)
            before = None
            if level > 0:
                before = buffers[level - 1][pl.ds(at + rims[level - 1], step)]
            window = buffers[level][pl.ds(at + rims[level] - REACH, step + 2 * REACH)]
            pairs = filtered_block(
                window, pot_v[pl.ds(at + pot_rim, step)], before, scale, weight, lanes, lines[step]
            )
            if level < DEG - 1:
                buffers[level + 1][pl.ds(at + rims[level + 1], step)] = pairs
            else:
                out[pl.ds(2 * (at + rims[DEG]), 2 * step)] = pairs.reshape(2 * step, 8, 128)
            return c

        lax.fori_loop(0, blocks, body, 0, unroll=min(blocks, 3))

    row = 2 * band + core

    def spread(u, count):
        start = placed(u, count)
        tiles = 2 * count

        def send(i, c):
            at = lax.rem(i + yx * max(tiles // floor, 1) + 4 * zl + 2 * core, tiles)
            tile = lax.rem(2 * (base + start) + at + 2 * whole, 2 * whole)
            src = out.at[2 * (start + rims[DEG]) + at]

            @pl.when(tile != own_tile)
            def _():
                peer = {"band": lax.rem(tile, bands), "dom": lax.div(tile, bands)}
                remote(src, recv.at[row], all_send, all_recv, peer).start()

            @pl.when(tile == own_tile)
            def _():
                pltpu.make_async_copy(src, recv.at[row], move_sem.at[3]).start()

            return c

        lax.fori_loop(0, tiles, send, 0)

    def advance(u, n):
        for level in range(DEG):
            apply(level, u + level * REACH, 1, n)
        spread(u + (DEG - 1) * REACH, n)

    pot_far[0].wait_recv()
    passed = [
        remote(mine, mine, pass_send.at[at], pass_recv.at[at], peer)
        for at, peer in enumerate(x_line)
    ]
    for copy in passed:
        copy.start()

    load.wait()
    load_pot.wait()
    own_rows.wait()
    gather_rows(1)

    def two_blocks(first):
        apply(0, jnp.where(left == 1, first, slab - 16 - first), 2)

    two_blocks(core * quarter + 8)
    near.wait_recv()
    near_pot.wait_recv()
    pl.when(long & jnp.logical_not(inner))(send_last)
    pl.semaphore_wait(plane_sem, len(y_line))
    tell(z_line, all_sem)
    two_blocks((1 - core) * quarter + 8)
    apply(0, 24, 2)
    apply(1, 14, 4)
    apply(1, 42, 1)
    apply(2, 20, 3)
    gather_rows(2)
    pl.semaphore_wait(all_sem, len(z_line))
    spread(20, 24)

    far[0][5].wait_recv()
    apply(0, slab - 8, 1)
    apply(1, slab - 14, 1)
    apply(2, slab - 20, 1)
    spread(slab - 20, 8)
    for at, (u, n) in enumerate(((0, 8), (-8, 8), (-16, 8), (-20, 4), (-24, 4))):
        if at == 1:
            for copy in passed:
                copy.wait_recv()
        far[0][at].wait_recv()
        advance(u, n)

    @pl.when(long)
    def _():
        for o in range(2):
            pot_far[o].wait_send()
            for at in range(len(pieces)):
                far[o][at].wait_send()

    @pl.when(jnp.logical_not(long))
    def _():
        for o in range(2):
            far[o][5].wait_send()

    for copy in (near, near_pot, *passed):
        copy.wait_send()
    for copy in row_copies[2]:
        copy.wait_recv()
    for copies in row_copies:
        for copy in copies:
            copy.wait_send()
    pltpu.make_async_copy(out.at[0], recv.at[row], move_sem.at[3]).wait()
    all_but_own = recv.at[pl.ds(0, recv.shape[0] - 1)]
    pltpu.make_async_copy(all_but_own, all_but_own, all_send).wait()
    pltpu.make_async_copy(all_but_own, all_but_own, all_recv).wait()


def rotate_kernel(recv_v, rows_v, out, out_v, sems):
    high, low = two_parts(jnp.concatenate([rows_v[:, 0], rows_v[:, 1]], axis=0).T)
    matrix = jnp.concatenate([high, high, low], axis=1)
    width = 256
    stores = []
    for at in range(0, 8 * 128, width):
        columns = []
        for r in range(at // 128, (at + width) // 128):
            values = jnp.concatenate([recv_v[:, 0, r], recv_v[:, 1, r]], axis=0)
            high, low = two_parts(values)
            columns.append(jnp.concatenate([high, low, high], axis=0))
        out_v[:, pl.ds(at, width)] = jnp.dot(
            matrix, jnp.concatenate(columns, axis=1), preferred_element_type=jnp.float32
        )
        store = pltpu.make_async_copy(
            out_v.at[:, pl.ds(at, width)], out.at[:, pl.ds(at, width)], sems.at[at // width]
        )
        store.start()
        stores.append(store)
    for store in stores:
        store.wait()


def per_device(bands, orbitals, potential, subspace):
    orbs, planes = orbitals.shape[0], orbitals.shape[1]
    orb = orbitals.reshape(orbs, planes, 2, 8, 128)
    pot = potential.reshape(planes, 2, 8, 128)
    f32 = jnp.float32
    dma = pltpu.SemaphoreType.DMA
    anywhere = pl.BlockSpec(memory_space=pl.ANY)
    slab, shift = 2 * planes, 2 * REACH
    recv, rows = pl.pallas_call(
        functools.partial(filter_kernel, bands),
        out_shape=(
            pltpu.VMEM((bands * orbs, 8, 128), f32),
            pltpu.VMEM((4, 4, 4, orbs, 128), f32),
        ),
        in_specs=[anywhere] * 3,
        out_specs=(anywhere,) * 2,
        scratch_shapes=[
            *[
                pltpu.VMEM((slab + 2 * (shift + REACH * (DEG - level)), 2, 8, 128), f32)
                for level in range(DEG)
            ],
            pltpu.VMEM((2 * (slab + 2 * shift), 8, 128), f32),
            pltpu.VMEM((slab + 2 * (shift + REACH * (DEG - 1)), 2, 8, 128), f32),
            dma((2,)),
            dma((2,)),
            dma((2, 6)),
            dma((6,)),
            dma((2,)),
            dma,
            dma((7,)),
            dma((7,)),
            dma((4,)),
            dma,
            dma,
            dma((3, 3)),
            dma((3, 3)),
            pltpu.SemaphoreType.REGULAR,
            pltpu.SemaphoreType.REGULAR,
        ],
        compiler_params=pltpu.CompilerParams(
            collective_id=0, has_side_effects=True, vmem_limit_bytes=32 * 2**20
        ),
        name="filter",
    )(*(pltpu.with_memory_space_constraint(a, pltpu.HBM) for a in (orb, pot, subspace)))
    recv, rows = recv.reshape(bands, orbs, 8, 128), rows.reshape(bands, orbs, 128)
    return pl.pallas_call(
        rotate_kernel,
        out_shape=jax.ShapeDtypeStruct((bands * orbs, 1024), f32),
        in_specs=[pl.BlockSpec(memory_space=pltpu.VMEM)] * 2,
        out_specs=anywhere,
        scratch_shapes=[pltpu.VMEM((bands * orbs, 1024), f32), dma((4,))],
        compiler_params=pltpu.CompilerParams(vmem_limit_bytes=32 * 2**20),
        name="rotate",
    )(*(pltpu.with_memory_space_constraint(a, pltpu.VMEM) for a in (recv, rows)))


def solution(mesh):
    in_specs = (P("band", "dom", None, None), P("dom", None, None), P("band", None))
    out_specs = P(None, ("dom", "band"))
    return jax.shard_map(
        functools.partial(per_device, mesh.shape["band"]),
        mesh=mesh,
        in_specs=in_specs,
        out_specs=out_specs,
        check_vma=False,
    )
```
